32 devices in a mesh: gx: 8 (over z, x), gy: 4 (over y, core).
Axes of the slice: x: 2, y: 2, z: 4, core: 2. Of those that a mesh axis runs over, the one named last changes fastest.
Arguments:
- features: bfloat16 [128, 8, 8, 8, 128], P(('gx', 'gy')), may hold values from -6 to 6
- out_grad: bfloat16 [128, 8, 8, 8, 128], P(('gx', 'gy')), may hold values from -6 to 6
- kernel: bfloat16 [27, 128, 128], replicated, may hold values from -0.109375 to 0.109375
- voxel_mask: int32 [128, 512], P(('gx', 'gy')), may hold values from 0 to 1, as said below
- neighbours: int32 [128, 27], P(('gx', 'gy')), may hold values from 0 to 16, as said below
- face_sends: int32 [128, 2], P(('gx', 'gy')), may hold values from 0 to 4, as said below
- edge_sends: int32 [128, 1], P(('gx', 'gy')), may hold values from 0 to 4, as said below
Outputs:
- output: bfloat16 [128, 8, 8, 8, 128], P(('gx', 'gy'))
- input_grad: bfloat16 [128, 8, 8, 8, 128], P(('gx', 'gy'))
- weight_grad: float32 [27, 128, 128], replicated
The draws below stay inside these ranges and needn't reach their ends.
Inputs may be any that keep to these rules, and one draw needn't show every extreme that they name: `voxel_mask`: zero in every voxel of a slot that holds no brick; in a slot that holds a brick each voxel is one or zero. neighbours[s, 9 (n_x + 1) + 3 (n_y + 1) + n_z + 1] is the index in the device's pool of the brick at brick offset n from slot s's brick, or 16 where that position lies outside the volume or holds no brick; the entry for offset (0,0,0) is the slot's own number; all other entries of a slot that holds no brick are 16. Each column of brick positions holds at most 1 bricks. `face_sends`: row 4 t + j lists, in increasing order, the device's slots whose bricks lie in its brick columns next to the side (-1,0), (1,0), (0,-1), (0,1) numbered j, then 4 for the rest. `edge_sends`: row 4 t + j lists, in increasing order, the device's slots whose bricks lie in its brick column at the corner (-1,-1), (-1,1), (1,-1), (1,1) numbered j, then 4 for the rest.
All inputs are finite; a program needn't handle non-finite values.
Results may differ from the reference program's by a relative error of at most 0.001.
Values may be sent and summed in bfloat16 or wider, within the bound.
No kernel may reach another device: no remote copies, remote signals or barrier semaphores. Data moves between devices by JAX's collectives and lax.ppermute only.
A program may use at most 192 MiB of HBM per device.

```python
import math
import jax
import jax.numpy as jnp
import numpy as np
from jax import lax

CHANNELS = 128
COLUMN_CAP = 1
DEPTH = 8
BRICKS = 4
FACE_CAP = 2
EDGE_CAP = 1
POOL = 17
SLOTS = 128
VOXELS = 65536
N_GX = 8
N_GY = 4


DIRECTIONS = ((-1, 0), (1, 0), (0, -1), (0, 1), (-1, -1), (-1, 1), (1, -1), (1, 1))


def brick_layout(key):
    column_cap = COLUMN_CAP
    bricks_dev = 4 * column_cap
    face_cap = 2 * column_cap
    edge_cap = column_cap
    grid_x = N_GX
    grid_y = N_GY
    depth = DEPTH
    places = 4 * depth
    zero_entry = bricks_dev + 4 * face_cap + 4 * edge_cap
    base_key = jax.random.fold_in(key, 7)
    key_count, key_full, key_place, key_order, key_voxel = jax.random.split(base_key, 5)
    counts = jax.random.randint(key_count, (grid_x, grid_y, 4), 0, column_cap + 1)
    chosen = jax.random.randint(key_full, (), 0, grid_x * grid_y)
    device_ids = jnp.arange(grid_x * grid_y).reshape(grid_x, grid_y)
    counts = jnp.where((device_ids == chosen)[:, :, None], column_cap, counts)
    scores = jax.random.randint(key_place, (grid_x, grid_y, 4, depth), 0, 1 << 20) * depth + jnp.arange(depth)
    ranks = jnp.argsort(jnp.argsort(scores, axis=-1), axis=-1)
    occupied = (ranks < counts[..., None]).reshape(grid_x, grid_y, places)
    order_scores = jax.random.randint(key_order, (grid_x, grid_y, places), 0, 1 << 20) * places + jnp.arange(places)
    order_scores = jnp.where(occupied, order_scores, (1 << 20) * places + jnp.arange(places))
    ordering = jnp.argsort(order_scores, axis=-1)
    slot_of_place = jnp.argsort(ordering, axis=-1)
    place_of_slot = ordering[..., :bricks_dev]
    slot_live = jnp.take_along_axis(occupied, place_of_slot, axis=-1)
    column = place_of_slot // depth
    column_x = column // 2
    column_y = column % 2
    level = place_of_slot % depth
    voxels = jax.random.randint(key_voxel, (grid_x, grid_y, bricks_dev, 512), 0, 2) * slot_live[..., None].astype(jnp.int32)
    toward_x = jnp.array([d[0] for d in DIRECTIONS], jnp.int32)[:, None]
    toward_y = jnp.array([d[1] for d in DIRECTIONS], jnp.int32)[:, None]
    match_x = (toward_x == 0) | (column_x[:, :, None, :] == (toward_x > 0).astype(jnp.int32))
    match_y = (toward_y == 0) | (column_y[:, :, None, :] == (toward_y > 0).astype(jnp.int32))
    matches = slot_live[:, :, None, :] & match_x & match_y
    slot_index = jnp.arange(bricks_dev)
    list_keys = jnp.where(matches, slot_index, bricks_dev + slot_index)
    listed = jnp.sort(list_keys, axis=-1)
    listed = jnp.where(listed < bricks_dev, listed, bricks_dev)
    face_lists = listed[:, :, :4, :face_cap].reshape(-1, face_cap)
    edge_lists = listed[:, :, 4:, :edge_cap].reshape(-1, edge_cap)
    list_rank = jnp.cumsum(matches.astype(jnp.int32), axis=-1) - 1
    offset_table = np.array([(i, j, k) for i in (-1, 0, 1) for j in (-1, 0, 1) for k in (-1, 0, 1)], np.int32)
    offset_x = jnp.asarray(offset_table[:, 0])
    offset_y = jnp.asarray(offset_table[:, 1])
    offset_z = jnp.asarray(offset_table[:, 2])
    grid_a = jnp.arange(grid_x)[:, None, None, None]
    grid_b = jnp.arange(grid_y)[None, :, None, None]
    whole_x = 2 * grid_a + column_x[..., None] + offset_x
    whole_y = 2 * grid_b + column_y[..., None] + offset_y
    whole_z = level[..., None] + offset_z
    inside = (whole_x >= 0) & (whole_x < 2 * grid_x) & (whole_y >= 0) & (whole_y < 2 * grid_y) & (whole_z >= 0) & (whole_z < depth)
    clamp_x = jnp.clip(whole_x, 0, 2 * grid_x - 1)
    clamp_y = jnp.clip(whole_y, 0, 2 * grid_y - 1)
    clamp_z = jnp.clip(whole_z, 0, depth - 1)
    source_a = clamp_x // 2
    source_b = clamp_y // 2
    source_place = (clamp_x % 2 * 2 + clamp_y % 2) * depth + clamp_z
    present = occupied[source_a, source_b, source_place]
    source_slot = slot_of_place[source_a, source_b, source_place]
    step_a = source_a - grid_a
    step_b = source_b - grid_b
    base_table = np.zeros((3, 3), np.int32)
    direction_table = np.zeros((3, 3), np.int32)
    faces_list = DIRECTIONS[:4]
    edges_list = DIRECTIONS[4:]
    for position in range(4):
        source = faces_list[position]
        base_table[source[0] + 1, source[1] + 1] = bricks_dev + position * face_cap
        direction_table[source[0] + 1, source[1] + 1] = DIRECTIONS.index((-source[0], -source[1]))
        source = edges_list[position]
        base_table[source[0] + 1, source[1] + 1] = bricks_dev + 4 * face_cap + position * edge_cap
        direction_table[source[0] + 1, source[1] + 1] = DIRECTIONS.index((-source[0], -source[1]))
    block_base = jnp.asarray(base_table)[step_a + 1, step_b + 1]
    block_direction = jnp.asarray(direction_table)[step_a + 1, step_b + 1]
    rank_there = list_rank[source_a, source_b, block_direction, source_slot]
    entries = jnp.where((step_a == 0) & (step_b == 0), source_slot, block_base + rank_there)
    entries = jnp.where(inside & present & slot_live[..., None], entries, zero_entry)
    center = (offset_x == 0) & (offset_y == 0) & (offset_z == 0)
    entries = jnp.where(center, jnp.broadcast_to(slot_index[:, None], entries.shape), entries)
    return (voxels.reshape(-1, 512).astype(jnp.int32), entries.reshape(-1, 27).astype(jnp.int32), face_lists.astype(jnp.int32), edge_lists.astype(jnp.int32))


def draw_voxel_mask(key, part):
    return brick_layout(key)[0]


def draw_neighbours(key, part):
    return brick_layout(key)[1]


def draw_face_sends(key, part):
    return brick_layout(key)[2]


def draw_edge_sends(key, part):
    return brick_layout(key)[3]


def steps_of(own_key, shape, cuts, low, high):
    factor_of = 1.0
    for dim, blocks in cuts:
        steps = jax.random.uniform(jax.random.fold_in(jax.random.fold_in(own_key, 6), dim), (blocks,), jnp.float32, low / len(cuts), high / len(cuts))
        factor_of = factor_of * jnp.repeat(jnp.exp(steps), shape[dim] // blocks).reshape((-1,) + (1,) * (len(shape) - 1 - dim))
    return factor_of


def noise(key, shape, width, limit, cuts=(), held_as=jnp.bfloat16):
    values = width * jax.random.normal(key, shape, jnp.float32)
    if cuts:
        values = values * steps_of(key, shape, cuts, -0.22, 0.18)
    return jnp.clip(values, -limit, limit).astype(held_as)


def setup_inputs(seed: int = 0) -> dict:
    key_list = jax.random.split(jax.random.key(seed), 8)
    features = noise(key_list[0], (SLOTS, 8, 8, 8, CHANNELS), 1.0, 6.0, ((0, 32),))
    out_grad = noise(key_list[1], (SLOTS, 8, 8, 8, CHANNELS), 1.0, 6.0, ((0, 32),))
    kernel = noise(key_list[2], (27, CHANNELS, CHANNELS), (27 * CHANNELS) ** -0.5, 0.109375)
    voxel_mask = draw_voxel_mask(jax.random.fold_in(key_list[7], 71), 0)
    neighbours = draw_neighbours(jax.random.fold_in(key_list[7], 71), 0)
    face_sends = draw_face_sends(jax.random.fold_in(key_list[7], 71), 0)
    edge_sends = draw_edge_sends(jax.random.fold_in(key_list[7], 71), 0)
    return {"features": features, "out_grad": out_grad, "kernel": kernel, "voxel_mask": voxel_mask, "neighbours": neighbours, "face_sends": face_sends, "edge_sends": edge_sends}


def cell_range(step):
    if step < 0:
        return slice(7, 8)
    if step > 0:
        return slice(0, 1)
    return slice(0, 8)

def padded_bricks(extended, indices):
    layers_x = []
    for step_x in (-1, 0, 1):
        layers_y = []
        for step_y in (-1, 0, 1):
            layers_z = []
            for step_z in (-1, 0, 1):
                column = 9 * (step_x + 1) + 3 * (step_y + 1) + step_z + 1
                picked = jnp.take(extended, indices[:, column], axis=0)
                layers_z.append(picked[:, cell_range(step_x), cell_range(step_y), cell_range(step_z)])
            layers_y.append(jnp.concatenate(layers_z, axis=3))
        layers_x.append(jnp.concatenate(layers_y, axis=2))
    return jnp.concatenate(layers_x, axis=1)

def shifted_columns(padded, step_x, direction):
    row_count = padded.shape[0] * 512
    channels = padded.shape[-1]
    pieces = []
    low_x = 1 + direction * step_x
    for step_y in (-1, 0, 1):
        for step_z in (-1, 0, 1):
            low_y = 1 + direction * step_y
            low_z = 1 + direction * step_z
            pieces.append(padded[:, low_x:low_x + 8, low_y:low_y + 8, low_z:low_z + 8].reshape(row_count, channels))
    return jnp.concatenate(pieces, axis=1)

def global_slots(neighbours, face_sends, edge_sends):
    slot_ids = jnp.arange(SLOTS, dtype=jnp.int32)
    device = slot_ids // BRICKS
    grid_a = (device // N_GY)[:, None]
    grid_b = (device % N_GY)[:, None]

    def remote_slot(offset, capacity, steps_a, steps_b, reverse_index, lists):
        position = jnp.clip(offset, 0, 4 * capacity - 1)
        block_index = position // capacity
        place_index = position % capacity
        source_a = grid_a + steps_a[block_index]
        source_b = grid_b + steps_b[block_index]
        inside = (source_a >= 0) & (source_a < N_GX) & (source_b >= 0) & (source_b < N_GY)
        source = jnp.clip(source_a, 0, N_GX - 1) * N_GY + jnp.clip(source_b, 0, N_GY - 1)
        listed = lists[source * 4 + reverse_index[block_index], place_index]
        return jnp.where(inside & (listed < BRICKS), source * BRICKS + listed, SLOTS)
    face_part = remote_slot(neighbours - BRICKS, FACE_CAP, jnp.array([-1, 1, 0, 0], jnp.int32), jnp.array([0, 0, -1, 1], jnp.int32), jnp.array([1, 0, 3, 2], jnp.int32), face_sends)
    edge_part = remote_slot(neighbours - BRICKS - 4 * FACE_CAP, EDGE_CAP, jnp.array([-1, -1, 1, 1], jnp.int32), jnp.array([-1, 1, -1, 1], jnp.int32), jnp.array([3, 2, 1, 0], jnp.int32), edge_sends)
    local_slot = device[:, None] * BRICKS + neighbours
    result = jnp.where(neighbours < BRICKS, local_slot, jnp.where(neighbours < BRICKS + 4 * FACE_CAP, face_part, jnp.where(neighbours < POOL - 1, edge_part, SLOTS)))
    return result.astype(jnp.int32)

def reference(features, out_grad, kernel, voxel_mask, neighbours, face_sends, edge_sends):
    channels = CHANNELS
    devices = N_GX * N_GY
    mask_brick = voxel_mask.astype(jnp.bfloat16).reshape(SLOTS, 8, 8, 8, 1)
    active = features * mask_brick
    masked_grad = out_grad * mask_brick
    zero_brick = jnp.zeros((1, 8, 8, 8, channels), jnp.bfloat16)
    active_ext = jnp.concatenate([active, zero_brick], axis=0)
    grad_ext = jnp.concatenate([masked_grad, zero_brick], axis=0)
    table = global_slots(neighbours, face_sends, edge_sends)
    forward_rows = kernel.reshape(3, 9 * channels, channels)
    backward_rows = jnp.transpose(kernel.reshape(3, 9, channels, channels), (0, 1, 3, 2)).reshape(3, 9 * channels, channels)
    row_count = BRICKS * 512

    def per_device(kernel_sum, device):
        indices = lax.dynamic_slice_in_dim(table, device * BRICKS, BRICKS, 0)
        mask_rows = lax.dynamic_slice_in_dim(voxel_mask, device * BRICKS, BRICKS, 0).reshape(row_count, 1).astype(jnp.float32)
        grad_rows = lax.dynamic_slice_in_dim(masked_grad, device * BRICKS, BRICKS, 0).reshape(row_count, channels)
        padded = padded_bricks(active_ext, indices)
        padded_grad = padded_bricks(grad_ext, indices)
        running_sum = jnp.zeros((row_count, channels), jnp.float32)
        back_sum = jnp.zeros((row_count, channels), jnp.float32)
        kernel_parts = []
        for step_x in (-1, 0, 1):
            columns = shifted_columns(padded, step_x, 1)
            running_sum = running_sum + jnp.dot(columns, forward_rows[step_x + 1], preferred_element_type=jnp.float32)
            kernel_parts.append(lax.dot_general(columns, grad_rows, (((0,), (0,)), ((), ())), preferred_element_type=jnp.float32))
            back_columns = shifted_columns(padded_grad, step_x, -1)
            back_sum = back_sum + jnp.dot(back_columns, backward_rows[step_x + 1], preferred_element_type=jnp.float32)
        out_rows = (running_sum * mask_rows).astype(jnp.bfloat16).reshape(BRICKS, 8, 8, 8, channels)
        grad_out = (back_sum * mask_rows).astype(jnp.bfloat16).reshape(BRICKS, 8, 8, 8, channels)
        kernel_sum = kernel_sum + jnp.stack(kernel_parts).reshape(27, channels, channels)
        return (kernel_sum, (out_rows, grad_out))
    start_sum = jnp.zeros((27, channels, channels), jnp.float32)
    weight_sum, stacked = lax.scan(per_device, start_sum, jnp.arange(devices, dtype=jnp.int32))
    output = stacked[0].reshape(SLOTS, 8, 8, 8, channels)
    input_grad = stacked[1].reshape(SLOTS, 8, 8, 8, channels)
    return (output, input_grad, weight_sum / math.sqrt(VOXELS))
```

```python
import math

import jax
import jax.numpy as jnp
from jax import lax
from jax.experimental import pallas as pl
from jax.experimental.pallas import tpu as pltpu
from jax.sharding import PartitionSpec as P

FACES = ((-1, 0), (1, 0), (0, -1), (0, 1))
EDGES = ((-1, -1), (-1, 1), (1, -1), (1, 1))
C = 128
SLOTS = 4
FACE = 2
ZERO = SLOTS + 4 * FACE + 4
ROWS = 27 * C
VMEM_LIMIT = 50 * 1024 * 1024


def vmem():
    return pl.BlockSpec(memory_space=pltpu.VMEM)


def smem():
    return pl.BlockSpec(memory_space=pltpu.SMEM)


def mask_columns(mask_ref, s):
    m = mask_ref[...].astype(jnp.float32)
    pick = (lax.broadcasted_iota(jnp.int32, (SLOTS, C), 0) == s).astype(jnp.float32)
    return lax.dot_general(m, pick, (((0,), (0,)), ((), ())), preferred_element_type=jnp.float32)


def pack_kernel(face_ref, edge_ref, feat_ref, grad_ref, mask_ref, *refs):
    act_ref, grd_ref = refs[0:2]
    face_out = refs[2:6]
    edge_out = refs[6:10]
    full = refs[10]
    for s in range(SLOTS):
        rows = mask_columns(mask_ref, s)
        for f, (src, dst) in enumerate(((feat_ref, act_ref), (grad_ref, grd_ref))):
            masked = src[s].astype(jnp.float32) * rows
            full[f, s] = masked.reshape(8, 8, 8, C)
            dst[s] = masked.astype(jnp.bfloat16)
    for position, (ex, ey) in enumerate(FACES):
        for f in range(2):
            for r in range(FACE):
                entry = face_ref[position, r]
                slot = jnp.minimum(entry, SLOTS - 1)
                live = entry < SLOTS
                if ex != 0:
                    layer = full[f, slot, 7 if ex > 0 else 0]
                else:
                    layer = full[f, slot, :, 7 if ey > 0 else 0]
                layer = jnp.where(live, layer, 0.0)
                face_out[position][pl.ds((f * FACE + r) * 64, 64)] = layer.reshape(64, C).astype(jnp.bfloat16)
    for position, (ex, ey) in enumerate(EDGES):
        lines = []
        for f in range(2):
            entry = edge_ref[position, 0]
            slot = jnp.minimum(entry, SLOTS - 1)
            line = full[f, slot, 7 if ex > 0 else 0, 7 if ey > 0 else 0]
            lines.append(jnp.where(entry < SLOTS, line, 0.0))
        edge_out[position][...] = jnp.concatenate(lines, axis=0).astype(jnp.bfloat16)


def pack(features, out_grad, mask, face_sends, edge_sends):
    face = jax.ShapeDtypeStruct((2 * FACE * 64, C), jnp.bfloat16)
    edge = jax.ShapeDtypeStruct((16, C), jnp.bfloat16)
    brick = jax.ShapeDtypeStruct((SLOTS, 512, C), jnp.bfloat16)
    return pl.pallas_call(
        pack_kernel,
        out_shape=[brick, brick] + [face] * 4 + [edge] * 4,
        in_specs=[smem(), smem()] + [vmem()] * 3,
        out_specs=[vmem()] * 10,
        scratch_shapes=[pltpu.VMEM((2, SLOTS, 8, 8, 8, C), jnp.float32)],
        compiler_params=pltpu.CompilerParams(vmem_limit_bytes=VMEM_LIMIT),
        name="pack",
    )(face_sends, edge_sends, features, out_grad, mask)


def fill_layers(f, bricks, faces, edges, lx, ly, corners):
    zero_layer = jnp.zeros((8, 8, C), jnp.float32)
    for s in range(SLOTS):
        for side, at in ((0, 7), (1, 0)):
            lx[side, s] = bricks[s, pl.ds(64 * at, 64)].astype(jnp.float32).reshape(8, 8, C)
        whole = bricks[s].astype(jnp.float32).reshape(8, 8, 8, C)
        for side, at in ((0, 7), (1, 0)):
            ly[side, s] = whole[:, at]
    for side in range(2):
        for r in range(FACE):
            rows = pl.ds((f * FACE + r) * 64, 64)
            lx[side, SLOTS + r] = faces[side][rows].astype(jnp.float32).reshape(8, 8, C)
            ly[side, SLOTS + r] = faces[2 + side][rows].astype(jnp.float32).reshape(8, 8, C)
        lx[side, SLOTS + FACE] = zero_layer
        ly[side, SLOTS + FACE] = zero_layer
    for sx in range(2):
        for sy in range(2):
            ax = 0 if sx else 7
            ay = 0 if sy else 7
            c = 2 * sx + sy
            for s in range(SLOTS):
                corners[c, s] = lx[sx, s, ay]
            for r in range(FACE):
                corners[c, SLOTS + r] = lx[sx, SLOTS + r, ay]
                corners[c, SLOTS + FACE + r] = ly[sy, SLOTS + r, ax]
            corners[c, SLOTS + 2 * FACE] = edges[c][...].astype(jnp.float32)[8 * f : 8 * f + 8]
            corners[c, SLOTS + 2 * FACE + 1] = jnp.zeros((8, C), jnp.float32)


def build_columns(s, bricks, near, lx, ly, corners, wide, v):
    line = lax.broadcasted_iota(jnp.int32, (8, C), 0)

    def spread(cells, at_x, at_y, depth):
        if depth is None:
            keep = ((line >= 1), None, (line <= 6))
        else:
            same = depth == 0
            keep = (
                (same & (line >= 1)) | ((depth == -1) & (line == 0)),
                same & (line >= 0),
                (same & (line <= 6)) | ((depth == 1) & (line == 7)),
            )
        flat = cells.reshape(-1, 8, C)
        for k in range(3):
            moved = flat if k == 1 else pltpu.roll(flat, 1 if k == 0 else 7, 1)
            if keep[k] is not None:
                moved = jnp.where(keep[k][None], moved, 0.0)
            wide[k, at_x, at_y] = moved.reshape(cells.shape)

    def column(nx, ny):
        base = 9 * (nx + 1) + 3 * (ny + 1)
        low, mid, high = near[s, base], near[s, base + 1], near[s, base + 2]
        entry = jnp.minimum(jnp.minimum(low, mid), high)
        depth = jnp.where(low < ZERO, -1, jnp.where(high < ZERO, 1, 0))
        return entry, depth

    middle = pl.ds(1, 8)
    spread(bricks[s].astype(jnp.float32).reshape(8, 8, 8, C), middle, middle, None)
    for side, n in ((0, -1), (1, 1)):
        edge_at = pl.ds(0 if n < 0 else 9, 1)
        entry, depth = column(n, 0)
        place = jnp.where(entry < SLOTS, entry, jnp.clip(entry - FACE * side, 0, SLOTS + FACE))
        spread(lx[side, place].reshape(1, 8, 8, C), edge_at, middle, depth)
        entry, depth = column(0, n)
        place = jnp.where(entry < SLOTS, entry, jnp.clip(entry - FACE * (2 + side), 0, SLOTS + FACE))
        spread(ly[side, place].reshape(8, 1, 8, C), middle, edge_at, depth)
    for sx in range(2):
        for sy in range(2):
            entry, depth = column(2 * sx - 1, 2 * sy - 1)
            first_x = SLOTS + FACE * sx
            first_y = SLOTS + FACE * (2 + sy)
            own_edge = SLOTS + 4 * FACE + 2 * sx + sy
            in_x = (entry >= first_x) & (entry < first_x + FACE)
            in_y = (entry >= first_y) & (entry < first_y + FACE)
            place = jnp.where(entry == own_edge, SLOTS + 2 * FACE, SLOTS + 2 * FACE + 1)
            place = jnp.where(in_y, SLOTS + FACE + entry - first_y, place)
            place = jnp.where(in_x, SLOTS + entry - first_x, place)
            place = jnp.where(entry < SLOTS, entry, place)
            spread(corners[2 * sx + sy, place].reshape(1, 1, 8, C), pl.ds(9 * sx, 1), pl.ds(9 * sy, 1), depth)
    for y in range(3):
        for z in range(3):
            cells = wide[z, :, pl.ds(y, 8)].reshape(10, 64, C).astype(jnp.bfloat16)
            v[s, :, :, pl.ds((3 * y + z) * C, C)] = cells


def columns_scratch():
    return [
        pltpu.VMEM((2, SLOTS + FACE + 1, 8, 8, C), jnp.float32),
        pltpu.VMEM((2, SLOTS + FACE + 1, 8, 8, C), jnp.float32),
        pltpu.VMEM((4, SLOTS + 2 * FACE + 2, 8, C), jnp.float32),
        pltpu.VMEM((3, 10, 10, 8, C), jnp.float32),
        pltpu.VMEM((SLOTS, 10, 64, 9 * C), jnp.bfloat16),
    ]


def weight_kernel(parts, take, near, act, grd, *refs):
    faces, edges = refs[0:4], refs[4:8]
    out = refs[8]
    lx, ly, corners, wide, v, total = refs[9:]
    fill_layers(0, act, faces, edges, lx, ly, corners)

    def per_slot(s, carry):
        build_columns(s, act, near, lx, ly, corners, wide, v)
        return carry

    lax.fori_loop(0, SLOTS, per_slot, 0)
    rows = grd[...].reshape(SLOTS * 512, C)
    for x in range(3):
        for j in range(9):
            cells = v[:, pl.ds(x, 8), :, pl.ds(j * C, C)].reshape(SLOTS * 512, C)
            total[pl.ds((9 * x + j) * C, C)] = lax.dot_general(
                cells, rows, (((0,), (0,)), ((), ())), preferred_element_type=jnp.float32
            )
    if parts * take > ROWS:
        total[pl.ds(ROWS, parts * take - ROWS)] = jnp.zeros((parts * take - ROWS, C), jnp.float32)
    peak = jnp.max(jnp.abs(total[...]))
    power = jnp.clip(jnp.ceil(jnp.log2(jnp.full((8, C), peak))), -100.0, 100.0)
    scale = jnp.exp2(14.0 - power)
    held = out.shape[1]
    for p in range(parts):
        out[p, pl.ds(0, take)] = total[pl.ds(p * take, take)] * scale[0:1]
        out[p, pl.ds(take, held - take)] = jnp.broadcast_to(power[0:1], (held - take, C))


def weight_terms(parts, take, held, near, act, grd, faces, edges):
    return pl.pallas_call(
        lambda *refs: weight_kernel(parts, take, *refs),
        out_shape=jax.ShapeDtypeStruct((parts, held, C), jnp.float32),
        in_specs=[smem()] + [vmem()] * 10,
        out_specs=vmem(),
        scratch_shapes=columns_scratch() + [pltpu.VMEM((parts * take, C), jnp.float32)],
        compiler_params=pltpu.CompilerParams(vmem_limit_bytes=VMEM_LIMIT),
        cost_estimate=pl.CostEstimate(flops=2 * 2048 * ROWS * C, bytes_accessed=6 << 20, transcendentals=0),
        name="weight_terms",
    )(near, act, grd, *faces, *edges)


def products_kernel(near, mask_ref, kernel_ref, act, grd, *refs):
    faces, edges = refs[0:4], refs[4:8]
    outs = refs[8:10]
    lx, ly, corners, wide, v, flipped = refs[10:]
    for o in range(27):
        flipped[pl.ds((26 - o) * C, C)] = kernel_ref[pl.ds(o * C, C)].T
    for f, (bricks, weights) in enumerate(((act, kernel_ref), (grd, flipped))):
        fill_layers(f, bricks, faces, edges, lx, ly, corners)

        def per_slot(s, carry):
            build_columns(s, bricks, near, lx, ly, corners, wide, v)
            total = jnp.zeros((512, C), jnp.float32)
            for x in range(3):
                cells = v[s, pl.ds(x, 8)].reshape(512, 9 * C)
                total += jnp.dot(cells, weights[pl.ds(x * 9 * C, 9 * C)], preferred_element_type=jnp.float32)
            outs[f][s] = (total * mask_columns(mask_ref, s)).astype(jnp.bfloat16)
            return carry

        lax.fori_loop(0, SLOTS, per_slot, 0)


def products(near, mask, kernel, act, grd, faces, edges):
    brick = jax.ShapeDtypeStruct((SLOTS, 512, C), jnp.bfloat16)
    return pl.pallas_call(
        products_kernel,
        out_shape=[brick, brick],
        in_specs=[smem()] + [vmem()] * 12,
        out_specs=[vmem()] * 2,
        scratch_shapes=columns_scratch() + [pltpu.VMEM((ROWS, C), jnp.bfloat16)],
        compiler_params=pltpu.CompilerParams(vmem_limit_bytes=VMEM_LIMIT),
        cost_estimate=pl.CostEstimate(flops=4 * 2048 * ROWS * C, bytes_accessed=8 << 20, transcendentals=0),
        name="products",
    )(near, mask, kernel, act, grd, *faces, *edges)


def exchange(face_out, edge_out):
    size_x, size_y = lax.axis_size("gx"), lax.axis_size("gy")

    def moved(value, by_x, by_y):
        pairs = []
        for a in range(size_x):
            for b in range(size_y):
                if 0 <= a + by_x < size_x and 0 <= b + by_y < size_y:
                    pairs.append((a * size_y + b, (a + by_x) * size_y + b + by_y))
        return lax.ppermute(value, ("gx", "gy"), pairs)

    faces = [moved(face_out[p ^ 1], -ex, -ey) for p, (ex, ey) in enumerate(FACES)]
    edges = [moved(edge_out[3 - p], -ex, -ey) for p, (ex, ey) in enumerate(EDGES)]
    return faces, edges


def unscaled(blocks, take):
    wide = blocks.astype(jnp.float32)
    return wide[:, :take] * jnp.exp2(wide[:, take : take + 1] - 14.0)


def total_weights(terms, take):
    parts, held, _ = terms.shape
    arrived = lax.all_to_all(terms.astype(jnp.float16), ("gx", "gy"), 0, 0, tiled=True)
    mine = jnp.sum(unscaled(arrived, take), axis=0)
    power = jnp.clip(jnp.ceil(jnp.log2(jnp.max(jnp.abs(mine)))), -100.0, 100.0)
    scaled = jnp.concatenate(
        [mine * jnp.exp2(14.0 - power), jnp.full((held - take, C), power, jnp.float32)], axis=0
    ).astype(jnp.float16)
    copies = jnp.broadcast_to(scaled[None], (parts, held, C))
    gathered = lax.all_to_all(copies, ("gx", "gy"), 0, 0, tiled=True)
    return unscaled(gathered, take).reshape(parts * take, C)[:ROWS]


def local(features, out_grad, kernel, voxel_mask, neighbours, face_sends, edge_sends):
    parts = lax.axis_size("gx") * lax.axis_size("gy")
    take = -(-ROWS // parts)
    held = -(-(take + 1) // 16) * 16
    act, grd, *sends = pack(
        features.reshape(SLOTS, 512, C), out_grad.reshape(SLOTS, 512, C), voxel_mask, face_sends, edge_sends
    )
    faces, edges = exchange(sends[:4], sends[4:])
    terms = weight_terms(parts, take, held, neighbours, act, grd, faces, edges)
    weight = total_weights(terms, take)
    output, input_grad = products(
        neighbours, voxel_mask, kernel.reshape(ROWS, C), act, grd, faces, edges
    )
    scale = 1.0 / math.sqrt(parts * SLOTS * 512)
    shape = (SLOTS, 8, 8, 8, C)
    return (
        output.reshape(shape),
        input_grad.reshape(shape),
        (weight * scale).reshape(27, C, C),
    )


def solution(mesh):
    spec = P(("gx", "gy"))
    return jax.shard_map(
        local,
        mesh=mesh,
        in_specs=(spec, spec, P(), spec, spec, spec, spec),
        out_specs=(spec, spec, P()),
        check_vma=False,
    )
```

```python
import math

import jax
import jax.numpy as jnp
from jax import lax
from jax.experimental import pallas as pl
from jax.experimental.pallas import tpu as pltpu
from jax.sharding import PartitionSpec as P

FACES = ((-1, 0), (1, 0), (0, -1), (0, 1))
EDGES = ((-1, -1), (-1, 1), (1, -1), (1, 1))
C = 128
SLOTS = 4
FACE = 2
ZERO = SLOTS + 4 * FACE + 4
ROWS = 27 * C
FACE_ROWS = 2 * FACE * 64
SEND_ROWS = FACE_ROWS + 32
HALF = ROWS // 2
VMEM_LIMIT = 50 * 1024 * 1024


def vmem():
    return pl.BlockSpec(memory_space=pltpu.VMEM)


def smem():
    return pl.BlockSpec(memory_space=pltpu.SMEM)


def mask_columns(mask_ref, s):
    m = mask_ref[...].astype(jnp.float32)
    pick = (lax.broadcasted_iota(jnp.int32, (SLOTS, C), 0) == s).astype(jnp.float32)
    return lax.dot_general(m, pick, (((0,), (0,)), ((), ())), preferred_element_type=jnp.float32)


def parity(axis):
    return lax.rem(lax.axis_index(axis), 2)


def side_of(k, odd):
    return 1 - odd if k == 0 else odd


def pack_kernel(face_ref, edge_ref, feat_hbm, grad_hbm, mask_hbm, act_ref, grd_ref, *refs):
    y_out, x_out = refs[0:2], refs[2:4]
    raw, mask_ref, full, sems = refs[4:]
    copies = [
        pltpu.make_async_copy(mask_hbm, mask_ref, sems.at[0]),
        pltpu.make_async_copy(feat_hbm, raw.at[0], sems.at[1]),
        pltpu.make_async_copy(grad_hbm, raw.at[1], sems.at[2]),
    ]
    for copy in copies:
        copy.start()
    for copy in copies:
        copy.wait()
    for s in range(SLOTS):
        rows = mask_columns(mask_ref, s)
        for f, dst in enumerate((act_ref, grd_ref)):
            masked = raw[f, s].astype(jnp.float32) * rows
            full[f, s] = masked.reshape(8, 8, 8, C)
            dst[s] = masked.astype(jnp.bfloat16)
    for axis, outs in enumerate((x_out, y_out)):
        odd = parity("gy" if axis else "gx")
        for k in range(2):
            side = side_of(k, odd)
            for f in range(2):
                for r in range(FACE):
                    entry = face_ref[r, 2 * axis + side]
                    slot = jnp.clip(entry, 0, SLOTS - 1)
                    layer = full[f, slot, :, 7 * side] if axis else full[f, slot, 7 * side]
                    layer = jnp.where(entry < SLOTS, layer, 0.0)
                    outs[k][pl.ds((f * FACE + r) * 64, 64)] = layer.reshape(64, C).astype(jnp.bfloat16)
            for far in range(2):
                if axis == 0:
                    outs[k][pl.ds(FACE_ROWS + 16 * far, 16)] = jnp.zeros((16, C), jnp.bfloat16)
                    continue
                entry = edge_ref[0, 2 * far + side]
                slot = jnp.clip(entry, 0, SLOTS - 1)
                lines = [full[f, slot, 7 * far, 7 * side] for f in range(2)]
                lines = jnp.where(entry < SLOTS, jnp.concatenate(lines, axis=0), 0.0)
                outs[k][pl.ds(FACE_ROWS + 16 * far, 16)] = lines.astype(jnp.bfloat16)


def pack(features, out_grad, mask, face_sends, edge_sends):
    send = jax.ShapeDtypeStruct((SEND_ROWS, C), jnp.bfloat16)
    brick = jax.ShapeDtypeStruct((SLOTS, 512, C), jnp.bfloat16)
    return pl.pallas_call(
        pack_kernel,
        out_shape=[brick, brick] + [send] * 4,
        in_specs=[smem(), smem()] + [pl.BlockSpec(memory_space=pl.ANY)] * 3,
        out_specs=[vmem()] * 6,
        scratch_shapes=[
            pltpu.VMEM((2, SLOTS, 512, C), jnp.bfloat16),
            pltpu.VMEM((SLOTS, 512), jnp.int32),
            pltpu.VMEM((2, SLOTS, 8, 8, 8, C), jnp.float32),
            pltpu.SemaphoreType.DMA((3,)),
        ],
        compiler_params=pltpu.CompilerParams(vmem_limit_bytes=VMEM_LIMIT),
        name="pack",
    )(face_sends.T, edge_sends.T, features, out_grad, mask)


def forward_kernel(x0, x1, y0, y1, out0, out1):
    odd_x, odd_y = parity("gx"), parity("gy")
    for k, out in enumerate((out0, out1)):
        far = side_of(k, odd_x)
        for j, came in enumerate((y0, y1)):
            source = side_of(j, odd_y)
            rows = came[pl.ds(pl.multiple_of(FACE_ROWS + 16 * far, 16), 16)]
            out[pl.ds(pl.multiple_of(FACE_ROWS + 16 * source, 16), 16)] = rows
        out[pl.ds(0, FACE_ROWS)] = (x0, x1)[k][pl.ds(0, FACE_ROWS)]


def forward_corners(x_send, y_came):
    send = jax.ShapeDtypeStruct((SEND_ROWS, C), jnp.bfloat16)
    return pl.pallas_call(
        forward_kernel,
        out_shape=[send] * 2,
        in_specs=[vmem()] * 4,
        out_specs=[vmem()] * 2,
        compiler_params=pltpu.CompilerParams(vmem_limit_bytes=VMEM_LIMIT),
        name="forward_corners",
    )(*x_send, *y_came)


def fill_layers(f, bricks, x_came, y_came, lx, ly, corners):
    odd_x, odd_y = parity("gx"), parity("gy")
    zero_layer = jnp.zeros((8, 8, C), jnp.float32)
    for s in range(SLOTS):
        whole = bricks[s].astype(jnp.float32).reshape(8, 8, 8, C)
        for side, at in ((0, 7), (1, 0)):
            lx[side, s] = whole[at]
            ly[side, s] = whole[:, at]
    for came, odd, dst in ((x_came, odd_x, lx), (y_came, odd_y, ly)):
        for k in range(2):
            side = side_of(k, odd)
            for r in range(FACE):
                rows = came[k][pl.ds((f * FACE + r) * 64, 64)]
                dst[side, SLOTS + r] = rows.astype(jnp.float32).reshape(8, 8, C)
            dst[k, SLOTS + FACE] = zero_layer
    for k in range(2):
        side = side_of(k, odd_x)
        for j in range(2):
            rows = x_came[k][pl.ds(FACE_ROWS + 16 * j, 16)].astype(jnp.float32)
            corners[2 * side + j, SLOTS + 2 * FACE] = rows[8 * f : 8 * f + 8]
    for sx in range(2):
        for sy in range(2):
            ax = 0 if sx else 7
            ay = 0 if sy else 7
            c = 2 * sx + sy
            for s in range(SLOTS):
                corners[c, s] = lx[sx, s, ay]
            for r in range(FACE):
                corners[c, SLOTS + r] = lx[sx, SLOTS + r, ay]
                corners[c, SLOTS + FACE + r] = ly[sy, SLOTS + r, ax]
            corners[c, SLOTS + 2 * FACE + 1] = jnp.zeros((8, C), jnp.float32)


def build_columns(s, bricks, near, lx, ly, corners, wide, v):
    line = lax.broadcasted_iota(jnp.int32, (8, C), 0)

    def spread(cells, at_x, at_y, depth):
        if depth is None:
            keep = ((line >= 1), None, (line <= 6))
        else:
            same = depth == 0
            keep = (
                (same & (line >= 1)) | ((depth == -1) & (line == 0)),
                same & (line >= 0),
                (same & (line <= 6)) | ((depth == 1) & (line == 7)),
            )
        flat = cells.reshape(-1, 8, C)
        for k in range(3):
            moved = flat if k == 1 else pltpu.roll(flat, 1 if k == 0 else 7, 1)
            if keep[k] is not None:
                moved = jnp.where(keep[k][None], moved, 0.0)
            wide[k, at_x, at_y] = moved.reshape(cells.shape)

    def column(nx, ny):
        base = 9 * (nx + 1) + 3 * (ny + 1)
        low, mid, high = near[s, base], near[s, base + 1], near[s, base + 2]
        entry = jnp.minimum(jnp.minimum(low, mid), high)
        depth = jnp.where(low < ZERO, -1, jnp.where(high < ZERO, 1, 0))
        return entry, depth

    middle = pl.ds(1, 8)
    spread(bricks[s].astype(jnp.float32).reshape(8, 8, 8, C), middle, middle, None)
    for side, n in ((0, -1), (1, 1)):
        edge_at = pl.ds(0 if n < 0 else 9, 1)
        entry, depth = column(n, 0)
        place = jnp.where(entry < SLOTS, entry, jnp.clip(entry - FACE * side, 0, SLOTS + FACE))
        spread(lx[side, place].reshape(1, 8, 8, C), edge_at, middle, depth)
        entry, depth = column(0, n)
        place = jnp.where(entry < SLOTS, entry, jnp.clip(entry - FACE * (2 + side), 0, SLOTS + FACE))
        spread(ly[side, place].reshape(8, 1, 8, C), middle, edge_at, depth)
    for sx in range(2):
        for sy in range(2):
            entry, depth = column(2 * sx - 1, 2 * sy - 1)
            first_x = SLOTS + FACE * sx
            first_y = SLOTS + FACE * (2 + sy)
            own_edge = SLOTS + 4 * FACE + 2 * sx + sy
            in_x = (entry >= first_x) & (entry < first_x + FACE)
            in_y = (entry >= first_y) & (entry < first_y + FACE)
            place = jnp.where(entry == own_edge, SLOTS + 2 * FACE, SLOTS + 2 * FACE + 1)
            place = jnp.where(in_y, SLOTS + FACE + entry - first_y, place)
            place = jnp.where(in_x, SLOTS + entry - first_x, place)
            place = jnp.where(entry < SLOTS, entry, place)
            spread(corners[2 * sx + sy, place].reshape(1, 1, 8, C), pl.ds(9 * sx, 1), pl.ds(9 * sy, 1), depth)
    for y in range(3):
        for z in range(3):
            cells = wide[z, :, pl.ds(y, 8)].reshape(10, 64, C).astype(jnp.bfloat16)
            v[s, :, :, pl.ds((3 * y + z) * C, C)] = cells


def columns_scratch():
    return [
        pltpu.VMEM((2, SLOTS + FACE + 1, 8, 8, C), jnp.float32),
        pltpu.VMEM((2, SLOTS + FACE + 1, 8, 8, C), jnp.float32),
        pltpu.VMEM((4, SLOTS + 2 * FACE + 2, 8, C), jnp.float32),
        pltpu.VMEM((3, 10, 10, 8, C), jnp.float32),
        pltpu.VMEM((SLOTS, 10, 64, 9 * C), jnp.bfloat16),
    ]


def weight_kernel(near, act, grd, x0, x1, y0, y1, keep, send, lx, ly, corners, wide, v, total):
    fill_layers(0, act, (x0, x1), (y0, y1), lx, ly, corners)

    def per_slot(s, carry):
        build_columns(s, act, near, lx, ly, corners, wide, v)
        return carry

    lax.fori_loop(0, SLOTS, per_slot, 0)
    rows = grd[...].reshape(SLOTS * 512, C)
    for x in range(3):
        for j in range(9):
            cells = v[:, pl.ds(x, 8), :, pl.ds(j * C, C)].reshape(SLOTS * 512, C)
            total[pl.ds((9 * x + j) * C, C)] = lax.dot_general(
                cells, rows, (((0,), (0,)), ((), ())), preferred_element_type=jnp.float32
            )
    core = parity("gy")
    keep[...] = total[pl.ds(pl.multiple_of(core * HALF, 8), HALF)]
    send[...] = total[pl.ds(pl.multiple_of((1 - core) * HALF, 8), HALF)]


def weight_terms(near, act, grd, x_came, y_came):
    half = jax.ShapeDtypeStruct((HALF, C), jnp.float32)
    return pl.pallas_call(
        weight_kernel,
        out_shape=[half, half],
        in_specs=[smem()] + [vmem()] * 6,
        out_specs=[vmem()] * 2,
        scratch_shapes=columns_scratch() + [pltpu.VMEM((ROWS, C), jnp.float32)],
        compiler_params=pltpu.CompilerParams(vmem_limit_bytes=VMEM_LIMIT),
        cost_estimate=pl.CostEstimate(flops=2 * 2048 * ROWS * C, bytes_accessed=6 << 20, transcendentals=0),
        name="weight_terms",
    )(near, act, grd, *x_came, *y_came)


def power_of(values):
    peak = jnp.max(jnp.abs(values))
    return jnp.clip(jnp.ceil(jnp.log2(jnp.full((8, C), peak))), -100.0, 100.0)[0:1]


def merge_kernel(groups, take, keep, came, out, total):
    held = out.shape[1]
    total[pl.ds(0, HALF)] = keep[...] + came[...]
    if groups * take > HALF:
        total[pl.ds(HALF, groups * take - HALF)] = jnp.zeros((groups * take - HALF, C), jnp.float32)
    power = power_of(total[...])
    scale = jnp.exp2(14.0 - power)
    for p in range(groups):
        out[p, pl.ds(0, take)] = total[pl.ds(p * take, take)] * scale
        out[p, pl.ds(take, held - take)] = jnp.broadcast_to(power, (held - take, C))


def merge(groups, take, held, keep, came):
    return pl.pallas_call(
        lambda *refs: merge_kernel(groups, take, *refs),
        out_shape=jax.ShapeDtypeStruct((groups, held, C), jnp.float32),
        in_specs=[vmem()] * 2,
        out_specs=vmem(),
        scratch_shapes=[pltpu.VMEM((groups * take, C), jnp.float32)],
        compiler_params=pltpu.CompilerParams(vmem_limit_bytes=VMEM_LIMIT),
        name="merge",
    )(keep, came)


def sum_kernel(take, blocks, out):
    groups, held, _ = blocks.shape
    total = jnp.zeros((take, C), jnp.float32)
    for p in range(groups):
        total += blocks[p, pl.ds(0, take)] * jnp.exp2(blocks[p, pl.ds(take, 1)] - 14.0)
    power = power_of(total)
    total = total * jnp.exp2(14.0 - power)
    for p in range(groups):
        out[p, pl.ds(0, take)] = total
        out[p, pl.ds(take, held - take)] = jnp.broadcast_to(power, (held - take, C))


def sum_blocks(take, blocks):
    return pl.pallas_call(
        lambda *refs: sum_kernel(take, *refs),
        out_shape=jax.ShapeDtypeStruct(blocks.shape, jnp.float32),
        in_specs=[vmem()],
        out_specs=vmem(),
        compiler_params=pltpu.CompilerParams(vmem_limit_bytes=VMEM_LIMIT),
        name="sum_blocks",
    )(blocks)


def decode_kernel(take, scale, mine, other, out):
    core = parity("gy")
    groups = mine.shape[0]
    for half, blocks in ((core, mine), (1 - core, other)):
        for p in range(groups):
            rows = min(take, HALF - p * take)
            if rows > 0:
                factor = jnp.exp2(blocks[p, pl.ds(take, 1)] - 14.0) * scale
                out[half, pl.ds(p * take, rows)] = blocks[p, pl.ds(0, rows)] * factor


def decode(take, scale, mine, other):
    return pl.pallas_call(
        lambda *refs: decode_kernel(take, scale, *refs),
        out_shape=jax.ShapeDtypeStruct((2, HALF, C), jnp.float32),
        in_specs=[vmem()] * 2,
        out_specs=vmem(),
        compiler_params=pltpu.CompilerParams(vmem_limit_bytes=VMEM_LIMIT),
        name="decode",
    )(mine, other)


def product_kernel(f, near, mask_ref, kernel_ref, bricks, x0, x1, y0, y1, out, lx, ly, corners, wide, v, *flipped):
    weights = kernel_ref
    if f == 1:
        weights = flipped[0]
        for o in range(27):
            weights[pl.ds((26 - o) * C, C)] = kernel_ref[pl.ds(o * C, C)].T
    fill_layers(f, bricks, (x0, x1), (y0, y1), lx, ly, corners)

    def per_slot(s, carry):
        build_columns(s, bricks, near, lx, ly, corners, wide, v)
        total = jnp.zeros((512, C), jnp.float32)
        for x in range(3):
            cells = v[s, pl.ds(x, 8)].reshape(512, 9 * C)
            total += jnp.dot(cells, weights[pl.ds(x * 9 * C, 9 * C)], preferred_element_type=jnp.float32)
        out[s] = (total * mask_columns(mask_ref, s)).astype(jnp.bfloat16)
        return carry

    lax.fori_loop(0, SLOTS, per_slot, 0)


def product(f, near, mask, kernel, bricks, x_came, y_came):
    return pl.pallas_call(
        lambda *refs: product_kernel(f, *refs),
        out_shape=jax.ShapeDtypeStruct((SLOTS, 512, C), jnp.bfloat16),
        in_specs=[smem()] + [vmem()] * 7,
        out_specs=vmem(),
        scratch_shapes=columns_scratch() + ([pltpu.VMEM((ROWS, C), jnp.bfloat16)] if f else []),
        compiler_params=pltpu.CompilerParams(vmem_limit_bytes=VMEM_LIMIT),
        cost_estimate=pl.CostEstimate(flops=2 * 2048 * ROWS * C, bytes_accessed=4 << 20, transcendentals=0),
        name=("output_product", "input_grad_product")[f],
    )(near, mask, kernel, bricks, *x_came, *y_came)


def swapped(value, axis, k):
    pairs = []
    for low in range(k, lax.axis_size(axis) - 1, 2):
        pairs += [(low, low + 1), (low + 1, low)]
    return lax.ppermute(value, axis, pairs)


def local(features, out_grad, kernel, voxel_mask, neighbours, face_sends, edge_sends):
    size_x, size_y = lax.axis_size("gx"), lax.axis_size("gy")
    parts = size_x * size_y
    groups = parts // 2
    take = -(-HALF // groups)
    held = -(-(take + 1) // 16) * 16
    same_core = [[i for i in range(parts) if i % size_y % 2 == core] for core in range(2)]

    def spread(blocks):
        return lax.all_to_all(
            blocks.astype(jnp.float16), ("gx", "gy"), 0, 0, axis_index_groups=same_core, tiled=True
        )

    act, grd, y0, y1, x0, x1 = pack(
        features.reshape(SLOTS, 512, C), out_grad.reshape(SLOTS, 512, C), voxel_mask, face_sends, edge_sends
    )
    y_came = [swapped(y0, "gy", 0), swapped(y1, "gy", 1)]
    x0, x1 = forward_corners((x0, x1), y_came)
    x_came = [swapped(x0, "gx", 0), swapped(x1, "gx", 1)]
    keep, send = weight_terms(neighbours, act, grd, x_came, y_came)
    blocks = merge(groups, take, held, keep, swapped(send, "gy", 0))
    mine = spread(sum_blocks(take, spread(blocks).astype(jnp.float32)))
    other = swapped(mine, "gy", 0)
    scale = 1.0 / math.sqrt(parts * SLOTS * 512)
    weight = decode(take, scale, mine.astype(jnp.float32), other.astype(jnp.float32))
    rows = kernel.reshape(ROWS, C)
    output = product(0, neighbours, voxel_mask, rows, act, x_came, y_came)
    input_grad = product(1, neighbours, voxel_mask, rows, grd, x_came, y_came)
    shape = (SLOTS, 8, 8, 8, C)
    return output.reshape(shape), input_grad.reshape(shape), weight.reshape(27, C, C)


def solution(mesh):
    spec = P(("gx", "gy"))
    return jax.shard_map(
        local,
        mesh=mesh,
        in_specs=(spec, spec, P(), spec, spec, spec, spec),
        out_specs=(spec, spec, P()),
        check_vma=False,
    )
```

```python
import math

import jax
import jax.numpy as jnp
from jax import lax
from jax.experimental import pallas as pl
from jax.experimental.pallas import tpu as pltpu
from jax.sharding import PartitionSpec as P

FACES = ((-1, 0), (1, 0), (0, -1), (0, 1))
EDGES = ((-1, -1), (-1, 1), (1, -1), (1, 1))
C = 128
SLOTS = 4
FACE = 2
ZERO = SLOTS + 4 * FACE + 4
ROWS = 27 * C
FACE_ROWS = 2 * FACE * 64
SEND_ROWS = FACE_ROWS + 32
HALF = ROWS // 2
VMEM_LIMIT = 50 * 1024 * 1024


def vmem():
    return pl.BlockSpec(memory_space=pltpu.VMEM)


def hbm():
    return pl.BlockSpec(memory_space=pltpu.HBM)


def fetched(*pairs):
    copies = [pltpu.make_async_copy(src, dst, sem) for src, dst, sem in pairs]
    for copy in copies:
        copy.start()
    for copy in copies:
        copy.wait()


def mask_columns(mask_ref, s):
    m = mask_ref[...].astype(jnp.float32)
    pick = (lax.broadcasted_iota(jnp.int32, (SLOTS, C), 0) == s).astype(jnp.float32)
    return lax.dot_general(m, pick, (((0,), (0,)), ((), ())), preferred_element_type=jnp.float32)


def parity(axis):
    return lax.rem(lax.axis_index(axis), 2)


def side_of(k, odd):
    return 1 - odd if k == 0 else odd


def pack_kernel(face_hbm, edge_hbm, feat_hbm, grad_hbm, mask_hbm, act_ref, grd_ref, *refs):
    y_out, x_out = refs[0:2], refs[2:4]
    face_ref, edge_ref, raw, mask_ref, full, sems = refs[4:]
    fetched(
        (mask_hbm, mask_ref, sems.at[0]),
        (feat_hbm, raw.at[0], sems.at[1]),
        (grad_hbm, raw.at[1], sems.at[2]),
        (face_hbm, face_ref, sems.at[3]),
        (edge_hbm, edge_ref, sems.at[4]),
    )
    for s in range(SLOTS):
        rows = mask_columns(mask_ref, s)
        for f, dst in enumerate((act_ref, grd_ref)):
            masked = raw[f, s].astype(jnp.float32) * rows
            full[f, s] = masked.reshape(8, 8, 8, C)
            dst[s] = masked.astype(jnp.bfloat16)
    for axis, outs in enumerate((x_out, y_out)):
        odd = parity("gy" if axis else "gx")
        for k in range(2):
            side = side_of(k, odd)
            for f in range(2):
                for r in range(FACE):
                    entry = face_ref[r, 2 * axis + side]
                    slot = jnp.clip(entry, 0, SLOTS - 1)
                    layer = full[f, slot, :, 7 * side] if axis else full[f, slot, 7 * side]
                    layer = jnp.where(entry < SLOTS, layer, 0.0)
                    outs[k][pl.ds((f * FACE + r) * 64, 64)] = layer.reshape(64, C).astype(jnp.bfloat16)
            for far in range(2):
                if axis == 0:
                    outs[k][pl.ds(FACE_ROWS + 16 * far, 16)] = jnp.zeros((16, C), jnp.bfloat16)
                    continue
                entry = edge_ref[0, 2 * far + side]
                slot = jnp.clip(entry, 0, SLOTS - 1)
                lines = [full[f, slot, 7 * far, 7 * side] for f in range(2)]
                lines = jnp.where(entry < SLOTS, jnp.concatenate(lines, axis=0), 0.0)
                outs[k][pl.ds(FACE_ROWS + 16 * far, 16)] = lines.astype(jnp.bfloat16)


def pack(features, out_grad, mask, face_sends, edge_sends):
    send = jax.ShapeDtypeStruct((SEND_ROWS, C), jnp.bfloat16)
    brick = jax.ShapeDtypeStruct((SLOTS, 512, C), jnp.bfloat16)
    return pl.pallas_call(
        pack_kernel,
        out_shape=[brick, brick] + [send] * 4,
        in_specs=[hbm()] * 5,
        out_specs=[vmem()] * 6,
        scratch_shapes=[
            pltpu.SMEM((FACE, 4), jnp.int32),
            pltpu.SMEM((1, 4), jnp.int32),
            pltpu.VMEM((2, SLOTS, 512, C), jnp.bfloat16),
            pltpu.VMEM((SLOTS, 512), jnp.int32),
            pltpu.VMEM((2, SLOTS, 8, 8, 8, C), jnp.float32),
            pltpu.SemaphoreType.DMA((5,)),
        ],
        compiler_params=pltpu.CompilerParams(vmem_limit_bytes=VMEM_LIMIT),
        name="pack",
    )(face_sends.T, edge_sends.T, features, out_grad, mask)


def forward_kernel(x0, x1, y0, y1, out0, out1):
    odd_x, odd_y = parity("gx"), parity("gy")
    for k, out in enumerate((out0, out1)):
        far = side_of(k, odd_x)
        for j, came in enumerate((y0, y1)):
            source = side_of(j, odd_y)
            rows = came[pl.ds(pl.multiple_of(FACE_ROWS + 16 * far, 16), 16)]
            out[pl.ds(pl.multiple_of(FACE_ROWS + 16 * source, 16), 16)] = rows
        out[pl.ds(0, FACE_ROWS)] = (x0, x1)[k][pl.ds(0, FACE_ROWS)]


def forward_corners(x_send, y_came):
    send = jax.ShapeDtypeStruct((SEND_ROWS, C), jnp.bfloat16)
    return pl.pallas_call(
        forward_kernel,
        out_shape=[send] * 2,
        in_specs=[vmem()] * 4,
        out_specs=[vmem()] * 2,
        compiler_params=pltpu.CompilerParams(vmem_limit_bytes=VMEM_LIMIT),
        name="forward_corners",
    )(*x_send, *y_came)


def fill_own(bricks, lx, ly, corners):
    for s in range(SLOTS):
        whole = bricks[s].astype(jnp.float32).reshape(8, 8, 8, C)
        for side, at in ((0, 7), (1, 0)):
            lx[side, s] = whole[at]
            ly[side, s] = whole[:, at]
            for other, far in ((0, 7), (1, 0)):
                corners[2 * side + other, s] = whole[at, far]


def fill_zero(lx, ly, corners, first):
    for ref in (lx, ly, corners):
        count = ref.shape[1] - first
        ref[:, pl.ds(first, count)] = jnp.zeros((ref.shape[0], count) + ref.shape[2:], jnp.float32)


def fill_came(f, x_came, y_came, lx, ly, corners):
    odd_x, odd_y = parity("gx"), parity("gy")
    for came, odd, dst in ((x_came, odd_x, lx), (y_came, odd_y, ly)):
        for k in range(2):
            side = side_of(k, odd)
            for r in range(FACE):
                rows = came[k][pl.ds((f * FACE + r) * 64, 64)]
                dst[side, SLOTS + r] = rows.astype(jnp.float32).reshape(8, 8, C)
            dst[k, SLOTS + FACE] = jnp.zeros((8, 8, C), jnp.float32)
    for k in range(2):
        side = side_of(k, odd_x)
        for j in range(2):
            rows = x_came[k][pl.ds(FACE_ROWS + 16 * j, 16)].astype(jnp.float32)
            corners[2 * side + j, SLOTS + 2 * FACE] = rows[8 * f : 8 * f + 8]
    for sx in range(2):
        for sy in range(2):
            c = 2 * sx + sy
            for r in range(FACE):
                corners[c, SLOTS + r] = lx[sx, SLOTS + r, 0 if sy else 7]
                corners[c, SLOTS + FACE + r] = ly[sy, SLOTS + r, 0 if sx else 7]
            corners[c, SLOTS + 2 * FACE + 1] = jnp.zeros((8, C), jnp.float32)


def build_columns(s, bricks, near, lx, ly, corners, wide, which):
    line = lax.broadcasted_iota(jnp.int32, (8, C), 0)

    def spread(cells, at_x, at_y, depth):
        if depth is None:
            keep = ((line >= 1), None, (line <= 6))
        else:
            same = depth == 0
            keep = (
                (same & (line >= 1)) | ((depth == -1) & (line == 0)),
                same & (line >= 0),
                (same & (line <= 6)) | ((depth == 1) & (line == 7)),
            )
        flat = cells.reshape(-1, 8, C)
        for k in range(3):
            moved = flat if k == 1 else pltpu.roll(flat, 1 if k == 0 else 7, 1)
            if keep[k] is not None:
                moved = jnp.where(keep[k][None], moved, 0.0)
            wide[k, at_x, at_y] = moved.reshape(cells.shape)

    def column(nx, ny):
        base = 9 * (nx + 1) + 3 * (ny + 1)
        low, mid, high = near[s, base], near[s, base + 1], near[s, base + 2]
        entry = jnp.minimum(jnp.minimum(low, mid), high)
        depth = jnp.where(low < ZERO, -1, jnp.where(high < ZERO, 1, 0))
        if which == "own":
            depth = jnp.where(entry < SLOTS, depth, 2)
        if which == "rim":
            depth = jnp.where(entry < SLOTS, 2, depth)
        return entry, depth

    middle = pl.ds(1, 8)
    if which != "rim":
        spread(bricks[s].astype(jnp.float32).reshape(8, 8, 8, C), middle, middle, None)
    for side, n in ((0, -1), (1, 1)):
        edge_at = pl.ds(0 if n < 0 else 9, 1)
        entry, depth = column(n, 0)
        place = jnp.where(entry < SLOTS, entry, jnp.clip(entry - FACE * side, 0, SLOTS + FACE))
        spread(lx[side, place].reshape(1, 8, 8, C), edge_at, middle, depth)
        entry, depth = column(0, n)
        place = jnp.where(entry < SLOTS, entry, jnp.clip(entry - FACE * (2 + side), 0, SLOTS + FACE))
        spread(ly[side, place].reshape(8, 1, 8, C), middle, edge_at, depth)
    for sx in range(2):
        for sy in range(2):
            entry, depth = column(2 * sx - 1, 2 * sy - 1)
            first_x = SLOTS + FACE * sx
            first_y = SLOTS + FACE * (2 + sy)
            own_edge = SLOTS + 4 * FACE + 2 * sx + sy
            in_x = (entry >= first_x) & (entry < first_x + FACE)
            in_y = (entry >= first_y) & (entry < first_y + FACE)
            place = jnp.where(entry == own_edge, SLOTS + 2 * FACE, SLOTS + 2 * FACE + 1)
            place = jnp.where(in_y, SLOTS + FACE + entry - first_y, place)
            place = jnp.where(in_x, SLOTS + entry - first_x, place)
            place = jnp.where(entry < SLOTS, entry, place)
            spread(corners[2 * sx + sy, place].reshape(1, 1, 8, C), pl.ds(9 * sx, 1), pl.ds(9 * sy, 1), depth)


def stack_columns(s, wide, v):
    for y in range(3):
        for z in range(3):
            cells = wide[z, :, pl.ds(y, 8)].reshape(10, 64, C).astype(jnp.bfloat16)
            v[s, :, :, pl.ds((3 * y + z) * C, C)] = cells


def columns_scratch():
    return [
        pltpu.VMEM((2, SLOTS + FACE + 1, 8, 8, C), jnp.float32),
        pltpu.VMEM((2, SLOTS + FACE + 1, 8, 8, C), jnp.float32),
        pltpu.VMEM((4, SLOTS + 2 * FACE + 2, 8, C), jnp.float32),
        pltpu.VMEM((3, 10, 10, 8, C), jnp.float32),
        pltpu.SMEM((SLOTS, 27), jnp.int32),
        pltpu.SemaphoreType.DMA(()),
    ]


def inner_kernel(near_hbm, act, grd, out, lx, ly, corners, wide, near, sem, v):
    fetched((near_hbm, near, sem))
    fill_own(act, lx, ly, corners)
    fill_zero(lx, ly, corners, SLOTS)

    def per_slot(s, carry):
        build_columns(s, act, near, lx, ly, corners, wide, "own")
        stack_columns(s, wide, v)
        return carry

    lax.fori_loop(0, SLOTS, per_slot, 0)
    rows = grd[...].reshape(SLOTS * 512, C)
    for x in range(3):
        for j in range(9):
            cells = v[:, pl.ds(x, 8), :, pl.ds(j * C, C)].reshape(SLOTS * 512, C)
            out[pl.ds((9 * x + j) * C, C)] = lax.dot_general(
                cells, rows, (((0,), (0,)), ((), ())), preferred_element_type=jnp.float32
            )


def inner_terms(near, act, grd):
    return pl.pallas_call(
        inner_kernel,
        out_shape=jax.ShapeDtypeStruct((ROWS, C), jnp.float32),
        in_specs=[hbm()] + [vmem()] * 2,
        out_specs=vmem(),
        scratch_shapes=columns_scratch() + [pltpu.VMEM((SLOTS, 10, 64, 9 * C), jnp.bfloat16)],
        compiler_params=pltpu.CompilerParams(vmem_limit_bytes=VMEM_LIMIT),
        cost_estimate=pl.CostEstimate(flops=2 * 2048 * ROWS * C, bytes_accessed=6 << 20, transcendentals=0),
        name="inner_terms",
    )(near, act, grd)


def rim_kernel(near_hbm, inner, grd, x0, x1, y0, y1, keep, send, lx, ly, corners, wide, near, sem, vx, vy, total):
    fetched((near_hbm, near, sem))
    fill_came(0, (x0, x1), (y0, y1), lx, ly, corners)
    for s in range(SLOTS):
        build_columns(s, None, near, lx, ly, corners, wide, "rim")
        rows = pl.ds(64 * s, 64)
        for side in range(2):
            for j in range(9):
                cells = wide[j % 3, 9 * side, pl.ds(j // 3, 8)]
                vx[side, rows, pl.ds(j * C, C)] = cells.reshape(64, C).astype(jnp.bfloat16)
        for z in range(3):
            for sx in range(2):
                for sy in range(2):
                    wide[z, 9 * sx, 9 * sy] = jnp.zeros((8, C), jnp.float32)
        for side in range(2):
            for j in range(9):
                cells = wide[j % 3, pl.ds(j // 3, 8), 9 * side]
                vy[side, rows, pl.ds(j * C, C)] = cells.reshape(64, C).astype(jnp.bfloat16)
    grads = grd[...]
    lines = grads.astype(jnp.float32).reshape(SLOTS, 8, 8, 8, C)

    def term(v, side, j, rows):
        return lax.dot_general(
            v[side, :, pl.ds(j * C, C)], rows, (((0,), (0,)), ((), ())), preferred_element_type=jnp.float32
        )

    rows_x = [grads[:, 448 * side : 448 * side + 64].reshape(SLOTS * 64, C) for side in range(2)]
    rows_y = [lines[:, :, 7 * side].reshape(SLOTS * 64, C).astype(jnp.bfloat16) for side in range(2)]
    for x in range(3):
        for y in range(3):
            for z in range(3):
                at = pl.ds((9 * x + 3 * y + z) * C, C)
                value = inner[at]
                if x != 1:
                    value += term(vx, x // 2, 3 * y + z, rows_x[x // 2])
                if y != 1:
                    value += term(vy, y // 2, 3 * x + z, rows_y[y // 2])
                total[at] = value
    core = parity("gy")
    keep[...] = total[pl.ds(pl.multiple_of(core * HALF, 8), HALF)]
    send[...] = total[pl.ds(pl.multiple_of((1 - core) * HALF, 8), HALF)]


def rim_terms(near, inner, grd, x_came, y_came):
    half = jax.ShapeDtypeStruct((HALF, C), jnp.float32)
    side = pltpu.VMEM((2, SLOTS * 64, 9 * C), jnp.bfloat16)
    return pl.pallas_call(
        rim_kernel,
        out_shape=[half, half],
        in_specs=[hbm()] + [vmem()] * 6,
        out_specs=[vmem()] * 2,
        scratch_shapes=columns_scratch() + [side, side, pltpu.VMEM((ROWS, C), jnp.float32)],
        compiler_params=pltpu.CompilerParams(vmem_limit_bytes=VMEM_LIMIT),
        cost_estimate=pl.CostEstimate(flops=2 * 256 * 36 * C * C, bytes_accessed=6 << 20, transcendentals=0),
        name="rim_terms",
    )(near, inner, grd, *x_came, *y_came)


def power_of(values):
    peak = jnp.max(jnp.abs(values))
    return jnp.clip(jnp.ceil(jnp.log2(jnp.full((8, C), peak))), -100.0, 100.0)[0:1]


def merge_kernel(groups, take, keep, came, out, total):
    held = out.shape[1]
    total[pl.ds(0, HALF)] = keep[...] + came[...]
    if groups * take > HALF:
        total[pl.ds(HALF, groups * take - HALF)] = jnp.zeros((groups * take - HALF, C), jnp.float32)
    power = power_of(total[...])
    scale = jnp.exp2(14.0 - power)
    for p in range(groups):
        out[p, pl.ds(0, take)] = total[pl.ds(p * take, take)] * scale
        out[p, pl.ds(take, held - take)] = jnp.broadcast_to(power, (held - take, C))


def merge(groups, take, held, keep, came):
    return pl.pallas_call(
        lambda *refs: merge_kernel(groups, take, *refs),
        out_shape=jax.ShapeDtypeStruct((groups, held, C), jnp.float32),
        in_specs=[vmem()] * 2,
        out_specs=vmem(),
        scratch_shapes=[pltpu.VMEM((groups * take, C), jnp.float32)],
        compiler_params=pltpu.CompilerParams(vmem_limit_bytes=VMEM_LIMIT),
        name="merge",
    )(keep, came)


def sum_kernel(take, blocks, out):
    groups, held, _ = blocks.shape
    total = jnp.zeros((take, C), jnp.float32)
    for p in range(groups):
        total += blocks[p, pl.ds(0, take)] * jnp.exp2(blocks[p, pl.ds(take, 1)] - 14.0)
    power = power_of(total)
    total = total * jnp.exp2(14.0 - power)
    for p in range(groups):
        out[p, pl.ds(0, take)] = total
        out[p, pl.ds(take, held - take)] = jnp.broadcast_to(power, (held - take, C))


def sum_blocks(take, blocks):
    return pl.pallas_call(
        lambda *refs: sum_kernel(take, *refs),
        out_shape=jax.ShapeDtypeStruct(blocks.shape, jnp.float32),
        in_specs=[vmem()],
        out_specs=vmem(),
        compiler_params=pltpu.CompilerParams(vmem_limit_bytes=VMEM_LIMIT),
        name="sum_blocks",
    )(blocks)


def decode_kernel(take, scale, mine, other, out):
    core = parity("gy")
    groups = mine.shape[0]
    for half, blocks in ((core, mine), (1 - core, other)):
        for p in range(groups):
            rows = min(take, HALF - p * take)
            if rows > 0:
                factor = jnp.exp2(blocks[p, pl.ds(take, 1)] - 14.0) * scale
                out[half, pl.ds(p * take, rows)] = blocks[p, pl.ds(0, rows)] * factor


def decode(take, scale, mine, other):
    return pl.pallas_call(
        lambda *refs: decode_kernel(take, scale, *refs),
        out_shape=jax.ShapeDtypeStruct((2, HALF, C), jnp.float32),
        in_specs=[vmem()] * 2,
        out_specs=vmem(),
        compiler_params=pltpu.CompilerParams(vmem_limit_bytes=VMEM_LIMIT),
        name="decode",
    )(mine, other)


def product_kernel(f, near_hbm, mask_ref, kernel_ref, bricks, x0, x1, y0, y1, out, *refs):
    lx, ly, corners, wide, near, sem, v, *flipped = refs
    fetched((near_hbm, near, sem))
    weights = kernel_ref
    if f == 1:
        weights = flipped[0]
        for o in range(27):
            weights[pl.ds((26 - o) * C, C)] = kernel_ref[pl.ds(o * C, C)].T
    fill_own(bricks, lx, ly, corners)
    fill_came(f, (x0, x1), (y0, y1), lx, ly, corners)

    def per_slot(s, carry):
        build_columns(s, bricks, near, lx, ly, corners, wide, "all")
        stack_columns(s, wide, v)
        total = jnp.zeros((512, C), jnp.float32)
        for x in range(3):
            cells = v[s, pl.ds(x, 8)].reshape(512, 9 * C)
            total += jnp.dot(cells, weights[pl.ds(x * 9 * C, 9 * C)], preferred_element_type=jnp.float32)
        out[s] = (total * mask_columns(mask_ref, s)).astype(jnp.bfloat16)
        return carry

    lax.fori_loop(0, SLOTS, per_slot, 0)


def product(f, near, mask, kernel, bricks, x_came, y_came):
    return pl.pallas_call(
        lambda *refs: product_kernel(f, *refs),
        out_shape=jax.ShapeDtypeStruct((SLOTS, 512, C), jnp.bfloat16),
        in_specs=[hbm()] + [vmem()] * 7,
        out_specs=vmem(),
        scratch_shapes=columns_scratch()
        + [pltpu.VMEM((SLOTS, 10, 64, 9 * C), jnp.bfloat16)]
        + ([pltpu.VMEM((ROWS, C), jnp.bfloat16)] if f else []),
        compiler_params=pltpu.CompilerParams(vmem_limit_bytes=VMEM_LIMIT),
        cost_estimate=pl.CostEstimate(flops=2 * 2048 * ROWS * C, bytes_accessed=4 << 20, transcendentals=0),
        name=("output_product", "input_grad_product")[f],
    )(near, mask, kernel, bricks, *x_came, *y_came)


def swapped(value, axis, k):
    pairs = []
    for low in range(k, lax.axis_size(axis) - 1, 2):
        pairs += [(low, low + 1), (low + 1, low)]
    return lax.ppermute(value, axis, pairs)


def local(features, out_grad, kernel, voxel_mask, neighbours, face_sends, edge_sends):
    size_x, size_y = lax.axis_size("gx"), lax.axis_size("gy")
    parts = size_x * size_y
    groups = parts // 2
    take = -(-HALF // groups)
    held = -(-(take + 1) // 16) * 16
    same_core = [[i for i in range(parts) if i % size_y % 2 == core] for core in range(2)]

    def spread(blocks):
        return lax.all_to_all(blocks, ("gx", "gy"), 0, 0, axis_index_groups=same_core, tiled=True)

    act, grd, y0, y1, x0, x1 = pack(
        features.reshape(SLOTS, 512, C), out_grad.reshape(SLOTS, 512, C), voxel_mask, face_sends, edge_sends
    )
    y_came = [swapped(y0, "gy", 0), swapped(y1, "gy", 1)]
    x0, x1 = forward_corners((x0, x1), y_came)
    x_came = [swapped(x0, "gx", 0), swapped(x1, "gx", 1)]
    inner = inner_terms(neighbours, act, grd)
    keep, send = rim_terms(neighbours, inner, grd, x_came, y_came)
    blocks = merge(groups, take, held, keep, swapped(send, "gy", 0)).astype(jnp.float16)
    rows = kernel.reshape(ROWS, C)
    blocks, act = lax.optimization_barrier((blocks, act))
    output = product(0, neighbours, voxel_mask, rows, act, x_came, y_came)
    arrived, output = lax.optimization_barrier((spread(blocks), output))
    copies = sum_blocks(take, arrived.astype(jnp.float32)).astype(jnp.float16)
    copies, grd = lax.optimization_barrier((copies, grd))
    input_grad = product(1, neighbours, voxel_mask, rows, grd, x_came, y_came)
    mine, input_grad = lax.optimization_barrier((spread(copies), input_grad))
    other = swapped(mine, "gy", 0)
    scale = 1.0 / math.sqrt(parts * SLOTS * 512)
    weight = decode(take, scale, mine.astype(jnp.float32), other.astype(jnp.float32))
    shape = (SLOTS, 8, 8, 8, C)
    return output.reshape(shape), input_grad.reshape(shape), weight.reshape(27, C, C)


def solution(mesh):
    spec = P(("gx", "gy"))
    return jax.shard_map(
        local,
        mesh=mesh,
        in_specs=(spec, spec, P(), spec, spec, spec, spec),
        out_specs=(spec, spec, P()),
        check_vma=False,
    )
```

```python
import math

import jax
import jax.numpy as jnp
from jax import lax
from jax.experimental import pallas as pl
from jax.experimental.pallas import tpu as pltpu
from jax.sharding import PartitionSpec as P

FACES = ((-1, 0), (1, 0), (0, -1), (0, 1))
EDGES = ((-1, -1), (-1, 1), (1, -1), (1, 1))
C = 128
SLOTS = 4
FACE = 2
ZERO = SLOTS + 4 * FACE + 4
ROWS = 27 * C
FACE_ROWS = 2 * FACE * 64
X_ROWS = FACE_ROWS + 32
Y_ROWS = FACE_ROWS + 48
HALF = ROWS // 2
VMEM_LIMIT = 32 * 1024 * 1024
PACK_LIMIT = 60 * 1024 * 1024


def vmem():
    return pl.BlockSpec(memory_space=pltpu.VMEM)


def hbm():
    return pl.BlockSpec(memory_space=pltpu.HBM)


def fetched(*pairs):
    copies = [pltpu.make_async_copy(src, dst, sem) for src, dst, sem in pairs]
    for copy in copies:
        copy.start()
    for copy in copies:
        copy.wait()


def mask_columns(mask_ref, s):
    m = mask_ref[...].astype(jnp.float32)
    pick = (lax.broadcasted_iota(jnp.int32, (SLOTS, C), 0) == s).astype(jnp.float32)
    return lax.dot_general(m, pick, (((0,), (0,)), ((), ())), preferred_element_type=jnp.float32)


def parity(axis):
    return lax.rem(lax.axis_index(axis), 2)


def side_of(k, odd):
    return 1 - odd if k == 0 else odd


def shifts(cells, same, below, above):
    line = lax.broadcasted_iota(jnp.int32, cells.shape, cells.ndim - 2)
    axis = cells.ndim - 2
    up = jnp.where((same & (line >= 1)) | (below & (line == 0)), pltpu.roll(cells, 1, axis), 0.0)
    down = jnp.where((same & (line <= 6)) | (above & (line == 7)), pltpu.roll(cells, 7, axis), 0.0)
    return up, jnp.where(same, cells, 0.0), down


def pack_kernel(face_hbm, edge_hbm, near_hbm, feat_hbm, grad_hbm, mask_hbm, act_ref, grd_ref, *refs):
    y_out, x_out = refs[0:2], refs[2:4]
    face_ref, edge_ref, near, raw, mask_ref, full, sems = refs[4:]
    fetched(
        (mask_hbm, mask_ref, sems.at[0]),
        (feat_hbm, raw.at[0], sems.at[1]),
        (grad_hbm, raw.at[1], sems.at[2]),
        (face_hbm, face_ref, sems.at[3]),
        (edge_hbm, edge_ref, sems.at[4]),
        (near_hbm, near, sems.at[5]),
    )
    for s in range(SLOTS):
        rows = mask_columns(mask_ref, s)
        for f, dst in enumerate((act_ref, grd_ref)):
            masked = raw[f, s].astype(jnp.float32) * rows
            full[f, s] = masked.reshape(8, 8, 8, C)
            dst[s] = masked.astype(jnp.bfloat16)
    for axis, outs in enumerate((x_out, y_out)):
        odd = parity("gy" if axis else "gx")
        for k in range(2):
            side = side_of(k, odd)
            for f in range(2):
                for r in range(FACE):
                    entry = face_ref[r, 2 * axis + side]
                    slot = jnp.clip(entry, 0, SLOTS - 1)
                    layer = full[f, slot, :, 7 * side] if axis else full[f, slot, 7 * side]
                    layer = jnp.where(entry < SLOTS, layer, 0.0)
                    outs[k][pl.ds((f * FACE + r) * 64, 64)] = layer.reshape(64, C).astype(jnp.bfloat16)
            lines = []
            for far in range(2):
                corner = 2 * far + side if axis else 2 * side + far
                entry = edge_ref[0, corner]
                slot = jnp.clip(entry, 0, SLOTS - 1)
                live = entry < SLOTS
                at_x, at_y = (7 * far, 7 * side) if axis else (7 * side, 7 * far)
                if axis == 0:
                    for f in range(2):
                        lines.append(jnp.where(live, full[f, slot, at_x, at_y], 0.0))
                    continue
                base = 18 * far + 6 * side
                low, mid, high = near[slot, base], near[slot, base + 1], near[slot, base + 2]
                up, same, down = shifts(
                    full[1, slot, at_x, at_y],
                    live & (mid < ZERO),
                    live & (high < ZERO),
                    live & (low < ZERO),
                )
                lines += [down, same, up]
            lines = jnp.concatenate(lines, axis=0).astype(jnp.bfloat16)
            outs[k][pl.ds(FACE_ROWS, lines.shape[0])] = lines


def pack(features, out_grad, mask, near, face_sends, edge_sends):
    sends = [jax.ShapeDtypeStruct((rows, C), jnp.bfloat16) for rows in (Y_ROWS, Y_ROWS, X_ROWS, X_ROWS)]
    brick = jax.ShapeDtypeStruct((SLOTS, 512, C), jnp.bfloat16)
    return pl.pallas_call(
        pack_kernel,
        out_shape=[brick, brick] + sends,
        in_specs=[hbm()] * 6,
        out_specs=[vmem()] * 6,
        scratch_shapes=[
            pltpu.SMEM((FACE, 4), jnp.int32),
            pltpu.SMEM((1, 4), jnp.int32),
            pltpu.SMEM((SLOTS, 27), jnp.int32),
            pltpu.VMEM((2, SLOTS, 512, C), jnp.bfloat16),
            pltpu.VMEM((SLOTS, 512), jnp.int32),
            pltpu.VMEM((2, SLOTS, 8, 8, 8, C), jnp.float32),
            pltpu.SemaphoreType.DMA((6,)),
        ],
        compiler_params=pltpu.CompilerParams(vmem_limit_bytes=PACK_LIMIT),
        name="pack",
    )(face_sends.T, edge_sends.T, near, features, out_grad, mask)


def forward_kernel(x0, x1, out0, out1):
    odd_x, odd_y = parity("gx"), parity("gy")
    for k, out in enumerate((out0, out1)):
        far = side_of(k, odd_y)
        for j, came in enumerate((x0, x1)):
            source = side_of(j, odd_x)
            rows = came[pl.ds(pl.multiple_of(FACE_ROWS + 16 * far, 16), 16)]
            out[pl.ds(pl.multiple_of(16 * source, 16), 16)] = rows


def forward_corners(x_came):
    send = jax.ShapeDtypeStruct((32, C), jnp.bfloat16)
    return pl.pallas_call(
        forward_kernel,
        out_shape=[send] * 2,
        in_specs=[vmem()] * 2,
        out_specs=[vmem()] * 2,
        compiler_params=pltpu.CompilerParams(vmem_limit_bytes=VMEM_LIMIT),
        name="forward_corners",
    )(*x_came)


def fill_own(bricks, lx, ly, corners):
    for s in range(SLOTS):
        whole = bricks[s].astype(jnp.float32).reshape(8, 8, 8, C)
        for side, at in ((0, 7), (1, 0)):
            lx[side, s] = whole[at]
            ly[side, s] = whole[:, at]
            for other, far in ((0, 7), (1, 0)):
                corners[2 * side + other, s] = whole[at, far]


def fill_zero(lx, ly, corners, first):
    for ref in (lx, ly, corners):
        count = ref.shape[1] - first
        ref[:, pl.ds(first, count)] = jnp.zeros((ref.shape[0], count) + ref.shape[2:], jnp.float32)


def fill_came(f, x_came, y_came, edges, lx, ly, corners):
    odd_x, odd_y = parity("gx"), parity("gy")
    for came, odd, dst in ((x_came, odd_x, lx), (y_came, odd_y, ly)):
        for k in range(2):
            side = side_of(k, odd)
            for r in range(FACE):
                rows = came[k][pl.ds((f * FACE + r) * 64, 64)]
                dst[side, SLOTS + r] = rows.astype(jnp.float32).reshape(8, 8, C)
            dst[k, SLOTS + FACE] = jnp.zeros((8, 8, C), jnp.float32)
    for k, came in enumerate(edges):
        side = side_of(k, odd_y)
        for j in range(2):
            rows = came[pl.ds(16 * j, 16)].astype(jnp.float32)
            corners[2 * j + side, SLOTS + 2 * FACE] = rows[8 * f : 8 * f + 8]
    for sx in range(2):
        for sy in range(2):
            c = 2 * sx + sy
            for r in range(FACE):
                corners[c, SLOTS + r] = lx[sx, SLOTS + r, 0 if sy else 7]
                corners[c, SLOTS + FACE + r] = ly[sy, SLOTS + r, 0 if sx else 7]
            corners[c, SLOTS + 2 * FACE + 1] = jnp.zeros((8, C), jnp.float32)


def build_columns(s, bricks, near, lx, ly, corners, wide, which):
    def spread(cells, at_x, at_y, depth):
        flat = cells.reshape(-1, 8, C)
        for k, moved in enumerate(shifts(flat, depth == 0, depth == -1, depth == 1)):
            wide[k, at_x, at_y] = moved.reshape(cells.shape)

    def column(nx, ny):
        base = 9 * (nx + 1) + 3 * (ny + 1)
        low, mid, high = near[s, base], near[s, base + 1], near[s, base + 2]
        entry = jnp.minimum(jnp.minimum(low, mid), high)
        depth = jnp.where(low < ZERO, -1, jnp.where(high < ZERO, 1, 0))
        if which == "own":
            depth = jnp.where(entry < SLOTS, depth, 2)
        if which == "rim":
            depth = jnp.where((entry >= SLOTS) & (entry < SLOTS + 4 * FACE), depth, 2)
        return entry, depth

    middle = pl.ds(1, 8)
    if which != "rim":
        spread(bricks[s].astype(jnp.float32).reshape(8, 8, 8, C), middle, middle, 0)
    for side, n in ((0, -1), (1, 1)):
        edge_at = pl.ds(0 if n < 0 else 9, 1)
        entry, depth = column(n, 0)
        place = jnp.where(entry < SLOTS, entry, jnp.clip(entry - FACE * side, 0, SLOTS + FACE))
        spread(lx[side, place].reshape(1, 8, 8, C), edge_at, middle, depth)
        entry, depth = column(0, n)
        place = jnp.where(entry < SLOTS, entry, jnp.clip(entry - FACE * (2 + side), 0, SLOTS + FACE))
        spread(ly[side, place].reshape(8, 1, 8, C), middle, edge_at, depth)
    for sx in range(2):
        for sy in range(2):
            entry, depth = column(2 * sx - 1, 2 * sy - 1)
            first_x = SLOTS + FACE * sx
            first_y = SLOTS + FACE * (2 + sy)
            own_edge = SLOTS + 4 * FACE + 2 * sx + sy
            in_x = (entry >= first_x) & (entry < first_x + FACE)
            in_y = (entry >= first_y) & (entry < first_y + FACE)
            place = jnp.where(entry == own_edge, SLOTS + 2 * FACE, SLOTS + 2 * FACE + 1)
            place = jnp.where(in_y, SLOTS + FACE + entry - first_y, place)
            place = jnp.where(in_x, SLOTS + entry - first_x, place)
            place = jnp.where(entry < SLOTS, entry, place)
            spread(corners[2 * sx + sy, place].reshape(1, 1, 8, C), pl.ds(9 * sx, 1), pl.ds(9 * sy, 1), depth)


def stack_columns(s, wide, v):
    for y in range(3):
        for z in range(3):
            cells = wide[z, :, pl.ds(y, 8)].reshape(10, 64, C).astype(jnp.bfloat16)
            v[s, :, :, pl.ds((3 * y + z) * C, C)] = cells


def columns_scratch():
    return [
        pltpu.VMEM((2, SLOTS + FACE + 1, 8, 8, C), jnp.float32),
        pltpu.VMEM((2, SLOTS + FACE + 1, 8, 8, C), jnp.float32),
        pltpu.VMEM((4, SLOTS + 2 * FACE + 2, 8, C), jnp.float32),
        pltpu.VMEM((3, 10, 10, 8, C), jnp.float32),
        pltpu.SMEM((SLOTS, 27), jnp.int32),
        pltpu.SemaphoreType.DMA(()),
    ]


def inner_kernel(near_hbm, act, grd, out, lx, ly, corners, wide, near, sem, v):
    fetched((near_hbm, near, sem))
    fill_own(act, lx, ly, corners)
    fill_zero(lx, ly, corners, SLOTS)

    def per_slot(s, carry):
        build_columns(s, act, near, lx, ly, corners, wide, "own")
        stack_columns(s, wide, v)
        return carry

    lax.fori_loop(0, SLOTS, per_slot, 0)
    rows = grd[...].reshape(SLOTS * 512, C)
    for x in range(3):
        cells = v[:, pl.ds(x, 8)].reshape(SLOTS * 512, 9 * C)
        out[pl.ds(9 * x * C, 9 * C)] = lax.dot_general(
            cells, rows, (((0,), (0,)), ((), ())), preferred_element_type=jnp.float32
        )


def inner_terms(near, act, grd):
    return pl.pallas_call(
        inner_kernel,
        out_shape=jax.ShapeDtypeStruct((ROWS, C), jnp.float32),
        in_specs=[hbm()] + [vmem()] * 2,
        out_specs=vmem(),
        scratch_shapes=columns_scratch() + [pltpu.VMEM((SLOTS, 10, 64, 9 * C), jnp.bfloat16)],
        compiler_params=pltpu.CompilerParams(vmem_limit_bytes=VMEM_LIMIT),
        cost_estimate=pl.CostEstimate(flops=2 * 2048 * ROWS * C, bytes_accessed=6 << 20, transcendentals=0),
        name="inner_terms",
    )(near, act, grd)


def rim_kernel(near_hbm, inner, grd, x0, x1, y0, y1, keep, send, lx, ly, corners, wide, near, sem, *refs):
    vx, vy, ends_a, ends_g, total = refs
    fetched((near_hbm, near, sem))
    fill_came(0, (x0, x1), (y0, y1), (), lx, ly, corners)
    for k, came in enumerate((x0, x1)):
        side = side_of(k, parity("gx"))
        for j in range(2):
            ends_a[side, j] = came[pl.ds(FACE_ROWS + 16 * j, 16)].astype(jnp.float32)[0:8]
    for k, came in enumerate((y0, y1)):
        side = side_of(k, parity("gy"))
        ends_g[side] = came[pl.ds(FACE_ROWS, 48)].astype(jnp.float32).reshape(2, 3, 8, C)
    for s in range(SLOTS):
        build_columns(s, None, near, lx, ly, corners, wide, "rim")
        rows = pl.ds(64 * s, 64)
        for side in range(2):
            for j in range(9):
                cells = wide[j % 3, 9 * side, pl.ds(j // 3, 8)]
                vx[side, rows, pl.ds(j * C, C)] = cells.reshape(64, C).astype(jnp.bfloat16)
        for z in range(3):
            for sx in range(2):
                for sy in range(2):
                    wide[z, 9 * sx, 9 * sy] = jnp.zeros((8, C), jnp.float32)
        for side in range(2):
            for j in range(9):
                cells = wide[j % 3, pl.ds(j // 3, 8), 9 * side]
                vy[side, rows, pl.ds(j * C, C)] = cells.reshape(64, C).astype(jnp.bfloat16)
    grads = grd[...]
    lines = grads.astype(jnp.float32).reshape(SLOTS, 8, 8, 8, C)

    def term(cells, rows):
        return lax.dot_general(cells, rows, (((0,), (0,)), ((), ())), preferred_element_type=jnp.float32)

    def end(line):
        return jnp.concatenate([line, jnp.zeros((8, C), jnp.float32)], axis=0).astype(jnp.bfloat16)

    side_x, side_y = [], []
    for side in range(2):
        rows = grads[:, 448 * side : 448 * side + 64].reshape(SLOTS * 64, C)
        side_x.append(term(vx[side], rows))
        rows = lines[:, :, 7 * side].reshape(SLOTS * 64, C).astype(jnp.bfloat16)
        side_y.append(term(vy[side], rows))
    for x in range(3):
        for y in range(3):
            for z in range(3):
                at = pl.ds((9 * x + 3 * y + z) * C, C)
                value = inner[at]
                if x != 1:
                    value += side_x[x // 2][(3 * y + z) * C : (3 * y + z + 1) * C]
                if y != 1:
                    value += side_y[y // 2][(3 * x + z) * C : (3 * x + z + 1) * C]
                if x != 1 and y != 1:
                    sx, sy = x // 2, 1 - y // 2
                    value += term(end(ends_a[sx, sy]), end(ends_g[sy, sx, z]))
                total[at] = value
    core = parity("gy")
    keep[...] = total[pl.ds(pl.multiple_of(core * HALF, 8), HALF)]
    send[...] = total[pl.ds(pl.multiple_of((1 - core) * HALF, 8), HALF)]


def rim_terms(near, inner, grd, x_came, y_came):
    half = jax.ShapeDtypeStruct((HALF, C), jnp.float32)
    side = pltpu.VMEM((2, SLOTS * 64, 9 * C), jnp.bfloat16)
    return pl.pallas_call(
        rim_kernel,
        out_shape=[half, half],
        in_specs=[hbm()] + [vmem()] * 6,
        out_specs=[vmem()] * 2,
        scratch_shapes=columns_scratch()
        + [
            side,
            side,
            pltpu.VMEM((2, 2, 8, C), jnp.float32),
            pltpu.VMEM((2, 2, 3, 8, C), jnp.float32),
            pltpu.VMEM((ROWS, C), jnp.float32),
        ],
        compiler_params=pltpu.CompilerParams(vmem_limit_bytes=VMEM_LIMIT),
        cost_estimate=pl.CostEstimate(flops=2 * 256 * 36 * C * C, bytes_accessed=6 << 20, transcendentals=0),
        name="rim_terms",
    )(near, inner, grd, *x_came, *y_came)


def power_of(values):
    peak = jnp.max(jnp.abs(values))
    return jnp.clip(jnp.ceil(jnp.log2(jnp.full((8, C), peak))), -100.0, 100.0)[0:1]


def merge_kernel(groups, take, keep, came, out, total):
    held = out.shape[1]
    total[pl.ds(0, HALF)] = keep[...] + came[...]
    if groups * take > HALF:
        total[pl.ds(HALF, groups * take - HALF)] = jnp.zeros((groups * take - HALF, C), jnp.float32)
    power = power_of(total[...])
    scale = jnp.exp2(14.0 - power)
    for p in range(groups):
        out[p, pl.ds(0, take)] = total[pl.ds(p * take, take)] * scale
        out[p, pl.ds(take, held - take)] = jnp.broadcast_to(power, (held - take, C))


def merge(groups, take, held, keep, came):
    return pl.pallas_call(
        lambda *refs: merge_kernel(groups, take, *refs),
        out_shape=jax.ShapeDtypeStruct((groups, held, C), jnp.float32),
        in_specs=[vmem()] * 2,
        out_specs=vmem(),
        scratch_shapes=[pltpu.VMEM((groups * take, C), jnp.float32)],
        compiler_params=pltpu.CompilerParams(vmem_limit_bytes=VMEM_LIMIT),
        name="merge",
    )(keep, came)


def sum_kernel(take, blocks, out):
    groups, held, _ = blocks.shape
    total = jnp.zeros((take, C), jnp.float32)
    for p in range(groups):
        total += blocks[p, pl.ds(0, take)] * jnp.exp2(blocks[p, pl.ds(take, 1)] - 14.0)
    power = power_of(total)
    total = total * jnp.exp2(14.0 - power)
    for p in range(groups):
        out[p, pl.ds(0, take)] = total
        out[p, pl.ds(take, held - take)] = jnp.broadcast_to(power, (held - take, C))


def sum_blocks(take, blocks):
    return pl.pallas_call(
        lambda *refs: sum_kernel(take, *refs),
        out_shape=jax.ShapeDtypeStruct(blocks.shape, jnp.float32),
        in_specs=[vmem()],
        out_specs=vmem(),
        compiler_params=pltpu.CompilerParams(vmem_limit_bytes=VMEM_LIMIT),
        name="sum_blocks",
    )(blocks)


def decode_kernel(take, scale, own, blocks, *refs):
    out, half, sem = refs[-3:]
    groups = blocks.shape[0]
    for p in range(groups):
        rows = min(take, HALF - p * take)
        if rows > 0:
            factor = jnp.exp2(blocks[p, pl.ds(take, 1)] - 14.0) * scale
            half[pl.ds(p * take, rows)] = blocks[p, pl.ds(0, rows)] * factor
    core = parity("gy")
    fetched((half, out.at[core if own else 1 - core], sem))


def decode(take, scale, blocks, begun=None):
    rest = () if begun is None else (begun,)
    return pl.pallas_call(
        lambda *refs: decode_kernel(take, scale, not rest, *refs),
        out_shape=jax.ShapeDtypeStruct((2, HALF, C), jnp.float32),
        in_specs=[vmem()] + [hbm()] * len(rest),
        out_specs=hbm(),
        scratch_shapes=[pltpu.VMEM((HALF, C), jnp.float32), pltpu.SemaphoreType.DMA(())],
        input_output_aliases={1: 0} if rest else {},
        compiler_params=pltpu.CompilerParams(vmem_limit_bytes=VMEM_LIMIT),
        name="decode_other" if rest else "decode_own",
    )(blocks, *rest)


def product_kernel(f, near_hbm, mask_ref, kernel_ref, bricks, x0, x1, y0, y1, e0, e1, out, *refs):
    lx, ly, corners, wide, near, sem, v, *flipped = refs
    fetched((near_hbm, near, sem))
    weights = kernel_ref
    if f == 1:
        weights = flipped[0]
        for o in range(27):
            weights[pl.ds((26 - o) * C, C)] = kernel_ref[pl.ds(o * C, C)].T
    fill_own(bricks, lx, ly, corners)
    fill_came(f, (x0, x1), (y0, y1), (e0, e1), lx, ly, corners)

    def per_slot(s, carry):
        build_columns(s, bricks, near, lx, ly, corners, wide, "all")
        stack_columns(s, wide, v)
        total = jnp.zeros((512, C), jnp.float32)
        for x in range(3):
            cells = v[s, pl.ds(x, 8)].reshape(512, 9 * C)
            total += jnp.dot(cells, weights[pl.ds(x * 9 * C, 9 * C)], preferred_element_type=jnp.float32)
        out[s] = (total * mask_columns(mask_ref, s)).astype(jnp.bfloat16)
        return carry

    lax.fori_loop(0, SLOTS, per_slot, 0)


def product(f, near, mask, kernel, bricks, x_came, y_came, edges):
    return pl.pallas_call(
        lambda *refs: product_kernel(f, *refs),
        out_shape=jax.ShapeDtypeStruct((SLOTS, 512, C), jnp.bfloat16),
        in_specs=[hbm()] + [vmem()] * 9,
        out_specs=vmem(),
        scratch_shapes=columns_scratch()
        + [pltpu.VMEM((SLOTS, 10, 64, 9 * C), jnp.bfloat16)]
        + ([pltpu.VMEM((ROWS, C), jnp.bfloat16)] if f else []),
        compiler_params=pltpu.CompilerParams(vmem_limit_bytes=VMEM_LIMIT),
        cost_estimate=pl.CostEstimate(flops=2 * 2048 * ROWS * C, bytes_accessed=4 << 20, transcendentals=0),
        name=("output_product", "input_grad_product")[f],
    )(near, mask, kernel, bricks, *x_came, *y_came, *edges)


def swapped(value, axis, k):
    pairs = []
    for low in range(k, lax.axis_size(axis) - 1, 2):
        pairs += [(low, low + 1), (low + 1, low)]
    return lax.ppermute(value, axis, pairs)


def local(features, out_grad, kernel, voxel_mask, neighbours, face_sends, edge_sends):
    size_x, size_y = lax.axis_size("gx"), lax.axis_size("gy")
    parts = size_x * size_y
    groups = parts // 2
    take = -(-HALF // groups)
    held = -(-(take + 1) // 16) * 16
    same_core = [[i for i in range(parts) if i % size_y % 2 == core] for core in range(2)]

    def spread(blocks):
        return lax.all_to_all(blocks, ("gx", "gy"), 0, 0, axis_index_groups=same_core, tiled=True)

    act, grd, y0, y1, x0, x1 = pack(
        features.reshape(SLOTS, 512, C),
        out_grad.reshape(SLOTS, 512, C),
        voxel_mask,
        neighbours,
        face_sends,
        edge_sends,
    )
    y1, x1 = swapped(y1, "gy", 1), swapped(x1, "gx", 1)
    x0, y0 = swapped(x0, "gx", 0), swapped(y0, "gy", 0)
    x_came, y_came = [x0, x1], [y0, y1]
    inner = inner_terms(neighbours, act, grd)
    keep, send = rim_terms(neighbours, inner, grd, x_came, y_came)
    blocks = merge(groups, take, held, keep, swapped(send, "gy", 0)).astype(jnp.float16)
    rows = kernel.reshape(ROWS, C)
    blocks, act, x_came = lax.optimization_barrier((blocks, act, x_came))
    e0, e1 = forward_corners(x_came)
    edges = [swapped(e0, "gy", 0), swapped(e1, "gy", 1)]
    output = product(0, neighbours, voxel_mask, rows, act, x_came, y_came, edges)
    arrived, output = lax.optimization_barrier((spread(blocks), output))
    copies = sum_blocks(take, arrived.astype(jnp.float32)).astype(jnp.float16)
    copies, grd = lax.optimization_barrier((copies, grd))
    input_grad = product(1, neighbours, voxel_mask, rows, grd, x_came, y_came, edges)
    mine, input_grad = lax.optimization_barrier((spread(copies), input_grad))
    other = swapped(mine, "gy", 0)
    scale = 1.0 / math.sqrt(parts * SLOTS * 512)
    weight = decode(take, scale, mine.astype(jnp.float32))
    weight = decode(take, scale, other.astype(jnp.float32), weight)
    shape = (SLOTS, 8, 8, 8, C)
    return output.reshape(shape), input_grad.reshape(shape), weight.reshape(27, C, C)


def solution(mesh):
    spec = P(("gx", "gy"))
    return jax.shard_map(
        local,
        mesh=mesh,
        in_specs=(spec, spec, P(), spec, spec, spec, spec),
        out_specs=(spec, spec, P()),
        check_vma=False,
    )
```

```python
import math

import jax
import jax.numpy as jnp
from jax import lax
from jax.experimental import pallas as pl
from jax.experimental.pallas import tpu as pltpu
from jax.sharding import PartitionSpec as P

FACES = ((-1, 0), (1, 0), (0, -1), (0, 1))
EDGES = ((-1, -1), (-1, 1), (1, -1), (1, 1))
C = 128
SLOTS = 4
FACE = 2
ZERO = SLOTS + 4 * FACE + 4
ROWS = 27 * C
FACE_ROWS = 2 * FACE * 64
X_ROWS = FACE_ROWS + 32
Y_ROWS = FACE_ROWS + 48
HALF = ROWS // 2
VMEM_LIMIT = 32 * 1024 * 1024
PACK_LIMIT = 60 * 1024 * 1024


def vmem():
    return pl.BlockSpec(memory_space=pltpu.VMEM)


def hbm():
    return pl.BlockSpec(memory_space=pltpu.HBM)


def fetched(*pairs):
    copies = [pltpu.make_async_copy(src, dst, sem) for src, dst, sem in pairs]
    for copy in copies:
        copy.start()
    for copy in copies:
        copy.wait()


def mask_columns(mask_ref, s):
    m = mask_ref[...].astype(jnp.float32)
    pick = (lax.broadcasted_iota(jnp.int32, (SLOTS, C), 0) == s).astype(jnp.float32)
    return lax.dot_general(m, pick, (((0,), (0,)), ((), ())), preferred_element_type=jnp.float32)


def parity(axis):
    return lax.rem(lax.axis_index(axis), 2)


def side_of(k, odd):
    return 1 - odd if k == 0 else odd


def shifts(cells, same, below, above):
    line = lax.broadcasted_iota(jnp.int32, cells.shape, cells.ndim - 2)
    axis = cells.ndim - 2
    up = jnp.where((same & (line >= 1)) | (below & (line == 0)), pltpu.roll(cells, 1, axis), 0.0)
    down = jnp.where((same & (line <= 6)) | (above & (line == 7)), pltpu.roll(cells, 7, axis), 0.0)
    return up, jnp.where(same, cells, 0.0), down


def pack_kernel(face_hbm, edge_hbm, near_hbm, feat_hbm, grad_hbm, mask_hbm, act_ref, grd_ref, *refs):
    y_out, x_out = refs[0:2], refs[2:4]
    face_ref, edge_ref, near, raw, mask_ref, full, sems = refs[4:]
    fetched(
        (mask_hbm, mask_ref, sems.at[0]),
        (feat_hbm, raw.at[0], sems.at[1]),
        (grad_hbm, raw.at[1], sems.at[2]),
        (face_hbm, face_ref, sems.at[3]),
        (edge_hbm, edge_ref, sems.at[4]),
        (near_hbm, near, sems.at[5]),
    )
    for s in range(SLOTS):
        rows = mask_columns(mask_ref, s)
        for f, dst in enumerate((act_ref, grd_ref)):
            masked = raw[f, s].astype(jnp.float32) * rows
            full[f, s] = masked.reshape(8, 8, 8, C)
            dst[s] = masked.astype(jnp.bfloat16)
    for axis, outs in enumerate((x_out, y_out)):
        odd = parity("gy" if axis else "gx")
        for k in range(2):
            side = side_of(k, odd)
            for f in range(2):
                for r in range(FACE):
                    entry = face_ref[r, 2 * axis + side]
                    slot = jnp.clip(entry, 0, SLOTS - 1)
                    layer = full[f, slot, :, 7 * side] if axis else full[f, slot, 7 * side]
                    layer = jnp.where(entry < SLOTS, layer, 0.0)
                    outs[k][pl.ds((f * FACE + r) * 64, 64)] = layer.reshape(64, C).astype(jnp.bfloat16)
            lines = []
            for far in range(2):
                corner = 2 * far + side if axis else 2 * side + far
                entry = edge_ref[0, corner]
                slot = jnp.clip(entry, 0, SLOTS - 1)
                live = entry < SLOTS
                at_x, at_y = (7 * far, 7 * side) if axis else (7 * side, 7 * far)
                if axis == 0:
                    for f in range(2):
                        lines.append(jnp.where(live, full[f, slot, at_x, at_y], 0.0))
                    continue
                base = 18 * far + 6 * side
                low, mid, high = near[slot, base], near[slot, base + 1], near[slot, base + 2]
                up, same, down = shifts(
                    full[1, slot, at_x, at_y],
                    live & (mid < ZERO),
                    live & (high < ZERO),
                    live & (low < ZERO),
                )
                lines += [down, same, up]
            lines = jnp.concatenate(lines, axis=0).astype(jnp.bfloat16)
            outs[k][pl.ds(FACE_ROWS, lines.shape[0])] = lines


def pack(features, out_grad, mask, near, face_sends, edge_sends):
    sends = [jax.ShapeDtypeStruct((rows, C), jnp.bfloat16) for rows in (Y_ROWS, Y_ROWS, X_ROWS, X_ROWS)]
    brick = jax.ShapeDtypeStruct((SLOTS, 512, C), jnp.bfloat16)
    return pl.pallas_call(
        pack_kernel,
        out_shape=[brick, brick] + sends,
        in_specs=[hbm()] * 6,
        out_specs=[vmem()] * 6,
        scratch_shapes=[
            pltpu.SMEM((FACE, 4), jnp.int32),
            pltpu.SMEM((1, 4), jnp.int32),
            pltpu.SMEM((SLOTS, 27), jnp.int32),
            pltpu.VMEM((2, SLOTS, 512, C), jnp.bfloat16),
            pltpu.VMEM((SLOTS, 512), jnp.int32),
            pltpu.VMEM((2, SLOTS, 8, 8, 8, C), jnp.float32),
            pltpu.SemaphoreType.DMA((6,)),
        ],
        compiler_params=pltpu.CompilerParams(vmem_limit_bytes=PACK_LIMIT),
        name="pack",
    )(face_sends.T, edge_sends.T, near, features, out_grad, mask)


def parts_of(ref):
    rows = ref.shape[0] // 2
    return ref.at[pl.ds(0, rows)], ref.at[pl.ds(rows, rows)]


def join_kernel(x0, x1, y0, y1, x_out, y_out):
    for out, pair in ((x_out, (x0, x1)), (y_out, (y0, y1))):
        for k, dst in enumerate(parts_of(out)):
            dst[...] = pair[k][...]


def join(x0, x1, y0, y1):
    outs = [jax.ShapeDtypeStruct((2 * rows, C), jnp.bfloat16) for rows in (X_ROWS, Y_ROWS)]
    return pl.pallas_call(
        join_kernel,
        out_shape=outs,
        in_specs=[vmem()] * 4,
        out_specs=[vmem()] * 2,
        compiler_params=pltpu.CompilerParams(vmem_limit_bytes=VMEM_LIMIT),
        name="join_sides",
    )(x0, x1, y0, y1)


def forward_kernel(x_came, out0, out1):
    odd_x, odd_y = parity("gx"), parity("gy")
    for k, out in enumerate((out0, out1)):
        far = side_of(k, odd_y)
        for j, came in enumerate(parts_of(x_came)):
            source = side_of(j, odd_x)
            rows = came[pl.ds(pl.multiple_of(FACE_ROWS + 16 * far, 16), 16)]
            out[pl.ds(pl.multiple_of(16 * source, 16), 16)] = rows


def forward_corners(x_came):
    send = jax.ShapeDtypeStruct((32, C), jnp.bfloat16)
    return pl.pallas_call(
        forward_kernel,
        out_shape=[send] * 2,
        in_specs=[vmem()],
        out_specs=[vmem()] * 2,
        compiler_params=pltpu.CompilerParams(vmem_limit_bytes=VMEM_LIMIT),
        name="forward_corners",
    )(x_came)


def fill_own(bricks, lx, ly, corners):
    for s in range(SLOTS):
        whole = bricks[s].astype(jnp.float32).reshape(8, 8, 8, C)
        for side, at in ((0, 7), (1, 0)):
            lx[side, s] = whole[at]
            ly[side, s] = whole[:, at]
            for other, far in ((0, 7), (1, 0)):
                corners[2 * side + other, s] = whole[at, far]


def fill_zero(lx, ly, corners, first):
    for ref in (lx, ly, corners):
        count = ref.shape[1] - first
        ref[:, pl.ds(first, count)] = jnp.zeros((ref.shape[0], count) + ref.shape[2:], jnp.float32)


def fill_came(f, x_came, y_came, edges, lx, ly, corners):
    odd_x, odd_y = parity("gx"), parity("gy")
    for came, odd, dst in ((x_came, odd_x, lx), (y_came, odd_y, ly)):
        for k, part in enumerate(parts_of(came)):
            side = side_of(k, odd)
            for r in range(FACE):
                rows = part[pl.ds((f * FACE + r) * 64, 64)]
                dst[side, SLOTS + r] = rows.astype(jnp.float32).reshape(8, 8, C)
            dst[k, SLOTS + FACE] = jnp.zeros((8, 8, C), jnp.float32)
    for k, came in enumerate(edges):
        side = side_of(k, odd_y)
        for j in range(2):
            rows = came[pl.ds(16 * j, 16)].astype(jnp.float32)
            corners[2 * j + side, SLOTS + 2 * FACE] = rows[8 * f : 8 * f + 8]
    for sx in range(2):
        for sy in range(2):
            c = 2 * sx + sy
            for r in range(FACE):
                corners[c, SLOTS + r] = lx[sx, SLOTS + r, 0 if sy else 7]
                corners[c, SLOTS + FACE + r] = ly[sy, SLOTS + r, 0 if sx else 7]
            corners[c, SLOTS + 2 * FACE + 1] = jnp.zeros((8, C), jnp.float32)


def build_columns(s, bricks, near, lx, ly, corners, wide, which):
    def spread(cells, at_x, at_y, depth):
        flat = cells.reshape(-1, 8, C)
        for k, moved in enumerate(shifts(flat, depth == 0, depth == -1, depth == 1)):
            wide[k, at_x, at_y] = moved.reshape(cells.shape)

    def column(nx, ny):
        base = 9 * (nx + 1) + 3 * (ny + 1)
        low, mid, high = near[s, base], near[s, base + 1], near[s, base + 2]
        entry = jnp.minimum(jnp.minimum(low, mid), high)
        depth = jnp.where(low < ZERO, -1, jnp.where(high < ZERO, 1, 0))
        if which == "own":
            depth = jnp.where(entry < SLOTS, depth, 2)
        if which == "rim":
            depth = jnp.where((entry >= SLOTS) & (entry < SLOTS + 4 * FACE), depth, 2)
        return entry, depth

    middle = pl.ds(1, 8)
    if which != "rim":
        spread(bricks[s].astype(jnp.float32).reshape(8, 8, 8, C), middle, middle, 0)
    for side, n in ((0, -1), (1, 1)):
        edge_at = pl.ds(0 if n < 0 else 9, 1)
        entry, depth = column(n, 0)
        place = jnp.where(entry < SLOTS, entry, jnp.clip(entry - FACE * side, 0, SLOTS + FACE))
        spread(lx[side, place].reshape(1, 8, 8, C), edge_at, middle, depth)
        entry, depth = column(0, n)
        place = jnp.where(entry < SLOTS, entry, jnp.clip(entry - FACE * (2 + side), 0, SLOTS + FACE))
        spread(ly[side, place].reshape(8, 1, 8, C), middle, edge_at, depth)
    for sx in range(2):
        for sy in range(2):
            entry, depth = column(2 * sx - 1, 2 * sy - 1)
            first_x = SLOTS + FACE * sx
            first_y = SLOTS + FACE * (2 + sy)
            own_edge = SLOTS + 4 * FACE + 2 * sx + sy
            in_x = (entry >= first_x) & (entry < first_x + FACE)
            in_y = (entry >= first_y) & (entry < first_y + FACE)
            place = jnp.where(entry == own_edge, SLOTS + 2 * FACE, SLOTS + 2 * FACE + 1)
            place = jnp.where(in_y, SLOTS + FACE + entry - first_y, place)
            place = jnp.where(in_x, SLOTS + entry - first_x, place)
            place = jnp.where(entry < SLOTS, entry, place)
            spread(corners[2 * sx + sy, place].reshape(1, 1, 8, C), pl.ds(9 * sx, 1), pl.ds(9 * sy, 1), depth)


def stack_columns(s, wide, v):
    for y in range(3):
        for z in range(3):
            cells = wide[z, :, pl.ds(y, 8)].reshape(10, 64, C).astype(jnp.bfloat16)
            v[s, :, :, pl.ds((3 * y + z) * C, C)] = cells


def columns_scratch():
    return [
        pltpu.VMEM((2, SLOTS + FACE + 1, 8, 8, C), jnp.float32),
        pltpu.VMEM((2, SLOTS + FACE + 1, 8, 8, C), jnp.float32),
        pltpu.VMEM((4, SLOTS + 2 * FACE + 2, 8, C), jnp.float32),
        pltpu.VMEM((3, 10, 10, 8, C), jnp.float32),
        pltpu.SMEM((SLOTS, 27), jnp.int32),
        pltpu.SemaphoreType.DMA(()),
    ]


def columns_kernel(near_hbm, act, v, lx, ly, corners, wide, near, sem):
    fetched((near_hbm, near, sem))
    fill_own(act, lx, ly, corners)
    fill_zero(lx, ly, corners, SLOTS)

    def per_slot(s, carry):
        build_columns(s, act, near, lx, ly, corners, wide, "own")
        stack_columns(s, wide, v)
        return carry

    lax.fori_loop(0, SLOTS, per_slot, 0)


def own_columns(near, act):
    return pl.pallas_call(
        columns_kernel,
        out_shape=jax.ShapeDtypeStruct((SLOTS, 10, 64, 9 * C), jnp.bfloat16),
        in_specs=[hbm(), vmem()],
        out_specs=vmem(),
        scratch_shapes=columns_scratch(),
        compiler_params=pltpu.CompilerParams(vmem_limit_bytes=VMEM_LIMIT),
        cost_estimate=pl.CostEstimate(flops=1 << 24, bytes_accessed=6 << 20, transcendentals=0),
        name="own_columns",
    )(near, act)


def inner_kernel(v, grd, out, turned):
    for s in range(SLOTS):
        for q in range(4):
            turned[:, pl.ds((4 * s + q) * C, C)] = grd[s, pl.ds(q * C, C)].T
    for x in range(3):
        cells = v[:, pl.ds(x, 8)].reshape(SLOTS * 512, 9 * C)
        terms = jnp.dot(turned[...], cells, preferred_element_type=jnp.float32)
        for j in range(9):
            out[pl.ds((9 * x + j) * C, C)] = terms[:, j * C : (j + 1) * C].T


def inner_terms(v, grd):
    return pl.pallas_call(
        inner_kernel,
        out_shape=jax.ShapeDtypeStruct((ROWS, C), jnp.float32),
        in_specs=[vmem()] * 2,
        out_specs=vmem(),
        scratch_shapes=[pltpu.VMEM((C, SLOTS * 512), jnp.bfloat16)],
        compiler_params=pltpu.CompilerParams(vmem_limit_bytes=VMEM_LIMIT),
        cost_estimate=pl.CostEstimate(flops=2 * 2048 * ROWS * C, bytes_accessed=6 << 20, transcendentals=0),
        name="inner_terms",
    )(v, grd)


def rim_kernel(near_hbm, inner, grd, x_ref, y_ref, keep, send, lx, ly, corners, wide, near, sem, *refs):
    vx, vy, ends_a, ends_g, total = refs
    fetched((near_hbm, near, sem))
    fill_came(0, x_ref, y_ref, (), lx, ly, corners)
    for k, came in enumerate(parts_of(x_ref)):
        side = side_of(k, parity("gx"))
        for j in range(2):
            ends_a[side, j] = came[pl.ds(FACE_ROWS + 16 * j, 16)].astype(jnp.float32)[0:8]
    for k, came in enumerate(parts_of(y_ref)):
        side = side_of(k, parity("gy"))
        ends_g[side] = came[pl.ds(FACE_ROWS, 48)].astype(jnp.float32).reshape(2, 3, 8, C)
    for s in range(SLOTS):
        build_columns(s, None, near, lx, ly, corners, wide, "rim")
        rows = pl.ds(64 * s, 64)
        for side in range(2):
            for j in range(9):
                cells = wide[j % 3, 9 * side, pl.ds(j // 3, 8)]
                vx[side, rows, pl.ds(j * C, C)] = cells.reshape(64, C).astype(jnp.bfloat16)
        for z in range(3):
            for sx in range(2):
                for sy in range(2):
                    wide[z, 9 * sx, 9 * sy] = jnp.zeros((8, C), jnp.float32)
        for side in range(2):
            for j in range(9):
                cells = wide[j % 3, pl.ds(j // 3, 8), 9 * side]
                vy[side, rows, pl.ds(j * C, C)] = cells.reshape(64, C).astype(jnp.bfloat16)
    grads = grd[...]
    lines = grads.astype(jnp.float32).reshape(SLOTS, 8, 8, 8, C)

    def term(cells, rows):
        return lax.dot_general(cells, rows, (((0,), (0,)), ((), ())), preferred_element_type=jnp.float32)

    def end(line):
        return jnp.concatenate([line, jnp.zeros((8, C), jnp.float32)], axis=0).astype(jnp.bfloat16)

    side_x, side_y = [], []
    for side in range(2):
        rows = grads[:, 448 * side : 448 * side + 64].reshape(SLOTS * 64, C)
        side_x.append(term(vx[side], rows))
        rows = lines[:, :, 7 * side].reshape(SLOTS * 64, C).astype(jnp.bfloat16)
        side_y.append(term(vy[side], rows))
    for x in range(3):
        for y in range(3):
            for z in range(3):
                at = pl.ds((9 * x + 3 * y + z) * C, C)
                value = inner[at]
                if x != 1:
                    value += side_x[x // 2][(3 * y + z) * C : (3 * y + z + 1) * C]
                if y != 1:
                    value += side_y[y // 2][(3 * x + z) * C : (3 * x + z + 1) * C]
                if x != 1 and y != 1:
                    sx, sy = x // 2, 1 - y // 2
                    value += term(end(ends_a[sx, sy]), end(ends_g[sy, sx, z]))
                total[at] = value
    core = parity("gy")
    keep[...] = total[pl.ds(pl.multiple_of(core * HALF, 8), HALF)]
    send[...] = total[pl.ds(pl.multiple_of((1 - core) * HALF, 8), HALF)]


def rim_terms(near, inner, grd, x_came, y_came):
    half = jax.ShapeDtypeStruct((HALF, C), jnp.float32)
    side = pltpu.VMEM((2, SLOTS * 64, 9 * C), jnp.bfloat16)
    return pl.pallas_call(
        rim_kernel,
        out_shape=[half, half],
        in_specs=[hbm()] + [vmem()] * 4,
        out_specs=[vmem()] * 2,
        scratch_shapes=columns_scratch()
        + [
            side,
            side,
            pltpu.VMEM((2, 2, 8, C), jnp.float32),
            pltpu.VMEM((2, 2, 3, 8, C), jnp.float32),
            pltpu.VMEM((ROWS, C), jnp.float32),
        ],
        compiler_params=pltpu.CompilerParams(vmem_limit_bytes=VMEM_LIMIT),
        cost_estimate=pl.CostEstimate(flops=2 * 256 * 36 * C * C, bytes_accessed=6 << 20, transcendentals=0),
        name="rim_terms",
    )(near, inner, grd, x_came, y_came)


def power_of(values):
    peak = jnp.max(jnp.abs(values))
    return jnp.clip(jnp.ceil(jnp.log2(jnp.full((8, C), peak))), -100.0, 100.0)[0:1]


def merge_kernel(groups, take, keep, came, out, total):
    held = out.shape[1]
    total[pl.ds(0, HALF)] = keep[...] + came[...]
    if groups * take > HALF:
        total[pl.ds(HALF, groups * take - HALF)] = jnp.zeros((groups * take - HALF, C), jnp.float32)
    power = power_of(total[...])
    scale = jnp.exp2(14.0 - power)
    for p in range(groups):
        out[p, pl.ds(0, take)] = total[pl.ds(p * take, take)] * scale
        out[p, pl.ds(take, held - take)] = jnp.broadcast_to(power, (held - take, C))


def merge(groups, take, held, keep, came):
    return pl.pallas_call(
        lambda *refs: merge_kernel(groups, take, *refs),
        out_shape=jax.ShapeDtypeStruct((groups, held, C), jnp.float32),
        in_specs=[vmem()] * 2,
        out_specs=vmem(),
        scratch_shapes=[pltpu.VMEM((groups * take, C), jnp.float32)],
        compiler_params=pltpu.CompilerParams(vmem_limit_bytes=VMEM_LIMIT),
        name="merge",
    )(keep, came)


def sum_kernel(take, blocks, out):
    groups, held, _ = blocks.shape
    total = jnp.zeros((take, C), jnp.float32)
    for p in range(groups):
        total += blocks[p, pl.ds(0, take)] * jnp.exp2(blocks[p, pl.ds(take, 1)] - 14.0)
    power = power_of(total)
    total = total * jnp.exp2(14.0 - power)
    for p in range(groups):
        out[p, pl.ds(0, take)] = total
        out[p, pl.ds(take, held - take)] = jnp.broadcast_to(power, (held - take, C))


def sum_blocks(take, blocks):
    return pl.pallas_call(
        lambda *refs: sum_kernel(take, *refs),
        out_shape=jax.ShapeDtypeStruct(blocks.shape, jnp.float32),
        in_specs=[vmem()],
        out_specs=vmem(),
        compiler_params=pltpu.CompilerParams(vmem_limit_bytes=VMEM_LIMIT),
        name="sum_blocks",
    )(blocks)


def decode_kernel(take, scale, own, blocks, *refs):
    out, half, sem = refs[-3:]
    groups = blocks.shape[0]
    for p in range(groups):
        rows = min(take, HALF - p * take)
        if rows > 0:
            factor = jnp.exp2(blocks[p, pl.ds(take, 1)] - 14.0) * scale
            half[pl.ds(p * take, rows)] = blocks[p, pl.ds(0, rows)] * factor
    core = parity("gy")
    fetched((half, out.at[core if own else 1 - core], sem))


def decode(take, scale, blocks, begun=None):
    rest = () if begun is None else (begun,)
    return pl.pallas_call(
        lambda *refs: decode_kernel(take, scale, not rest, *refs),
        out_shape=jax.ShapeDtypeStruct((2, HALF, C), jnp.float32),
        in_specs=[vmem()] + [hbm()] * len(rest),
        out_specs=hbm(),
        scratch_shapes=[pltpu.VMEM((HALF, C), jnp.float32), pltpu.SemaphoreType.DMA(())],
        input_output_aliases={1: 0} if rest else {},
        compiler_params=pltpu.CompilerParams(vmem_limit_bytes=VMEM_LIMIT),
        name="decode_other" if rest else "decode_own",
    )(blocks, *rest)


def product_kernel(f, near_hbm, mask_ref, kernel_ref, bricks, x_ref, y_ref, e0, e1, out, *refs):
    lx, ly, corners, wide, near, sem, v, *flipped = refs
    fetched((near_hbm, near, sem))
    weights = kernel_ref
    if f == 1:
        weights = flipped[0]
        for o in range(27):
            weights[pl.ds((26 - o) * C, C)] = kernel_ref[pl.ds(o * C, C)].T
    fill_own(bricks, lx, ly, corners)
    fill_came(f, x_ref, y_ref, (e0, e1), lx, ly, corners)

    def per_slot(s, carry):
        build_columns(s, bricks, near, lx, ly, corners, wide, "all")
        stack_columns(s, wide, v)
        total = jnp.zeros((512, C), jnp.float32)
        for x in range(3):
            cells = v[s, pl.ds(x, 8)].reshape(512, 9 * C)
            total += jnp.dot(cells, weights[pl.ds(x * 9 * C, 9 * C)], preferred_element_type=jnp.float32)
        out[s] = (total * mask_columns(mask_ref, s)).astype(jnp.bfloat16)
        return carry

    lax.fori_loop(0, SLOTS, per_slot, 0)


def product(f, near, mask, kernel, bricks, x_came, y_came, edges):
    return pl.pallas_call(
        lambda *refs: product_kernel(f, *refs),
        out_shape=jax.ShapeDtypeStruct((SLOTS, 512, C), jnp.bfloat16),
        in_specs=[hbm()] + [vmem()] * 7,
        out_specs=vmem(),
        scratch_shapes=columns_scratch()
        + [pltpu.VMEM((SLOTS, 10, 64, 9 * C), jnp.bfloat16)]
        + ([pltpu.VMEM((ROWS, C), jnp.bfloat16)] if f else []),
        compiler_params=pltpu.CompilerParams(vmem_limit_bytes=VMEM_LIMIT),
        cost_estimate=pl.CostEstimate(flops=2 * 2048 * ROWS * C, bytes_accessed=4 << 20, transcendentals=0),
        name=("output_product", "input_grad_product")[f],
    )(near, mask, kernel, bricks, x_came, y_came, *edges)


def swapped(value, axis, k):
    pairs = []
    for low in range(k, lax.axis_size(axis) - 1, 2):
        pairs += [(low, low + 1), (low + 1, low)]
    return lax.ppermute(value, axis, pairs)


def hopped(value, axis):
    size = lax.axis_size(axis)
    pairs = [(i, i + 2) for i in range(1, size - 2, 2)] + [(i, i - 2) for i in range(2, size, 2)]
    return lax.ppermute(value, axis, pairs)


def local(features, out_grad, kernel, voxel_mask, neighbours, face_sends, edge_sends):
    size_x, size_y = lax.axis_size("gx"), lax.axis_size("gy")
    parts = size_x * size_y
    groups = parts // 2
    take = -(-HALF // groups)
    held = -(-(take + 1) // 16) * 16
    same_core = [[i for i in range(parts) if i % size_y % 2 == core] for core in range(2)]

    def spread(blocks):
        return lax.all_to_all(blocks, ("gx", "gy"), 0, 0, axis_index_groups=same_core, tiled=True)

    act, grd, y0, y1, x0, x1 = pack(
        features.reshape(SLOTS, 512, C),
        out_grad.reshape(SLOTS, 512, C),
        voxel_mask,
        neighbours,
        face_sends,
        edge_sends,
    )
    x1, y1 = hopped(x1, "gx"), hopped(y1, "gy")
    v = own_columns(neighbours, act)
    x1, y1, v = lax.optimization_barrier((x1, y1, v))
    x_came, y_came = join(x0, x1, y0, y1)
    x_came, y_came = swapped(x_came, "gx", 0), swapped(y_came, "gy", 0)
    inner = inner_terms(v, grd)
    keep, send = rim_terms(neighbours, inner, grd, x_came, y_came)
    blocks = merge(groups, take, held, keep, swapped(send, "gy", 0)).astype(jnp.float16)
    rows = kernel.reshape(ROWS, C)
    blocks, act, x_came = lax.optimization_barrier((blocks, act, x_came))
    e0, e1 = forward_corners(x_came)
    edges = [swapped(e0, "gy", 0), swapped(e1, "gy", 1)]
    output = product(0, neighbours, voxel_mask, rows, act, x_came, y_came, edges)
    arrived, output = lax.optimization_barrier((spread(blocks), output))
    copies = sum_blocks(take, arrived.astype(jnp.float32)).astype(jnp.float16)
    copies, grd = lax.optimization_barrier((copies, grd))
    input_grad = product(1, neighbours, voxel_mask, rows, grd, x_came, y_came, edges)
    mine, input_grad = lax.optimization_barrier((spread(copies), input_grad))
    other = swapped(mine, "gy", 0)
    scale = 1.0 / math.sqrt(parts * SLOTS * 512)
    weight = decode(take, scale, mine.astype(jnp.float32))
    weight = decode(take, scale, other.astype(jnp.float32), weight)
    shape = (SLOTS, 8, 8, 8, C)
    return output.reshape(shape), input_grad.reshape(shape), weight.reshape(27, C, C)


def solution(mesh):
    spec = P(("gx", "gy"))
    return jax.shard_map(
        local,
        mesh=mesh,
        in_specs=(spec, spec, P(), spec, spec, spec, spec),
        out_specs=(spec, spec, P()),
        check_vma=False,
    )
```

```python
import math

import jax
import jax.numpy as jnp
from jax import lax
from jax.experimental import pallas as pl
from jax.experimental.pallas import tpu as pltpu
from jax.sharding import PartitionSpec as P

FACES = ((-1, 0), (1, 0), (0, -1), (0, 1))
EDGES = ((-1, -1), (-1, 1), (1, -1), (1, 1))
C = 128
SLOTS = 4
FACE = 2
ZERO = SLOTS + 4 * FACE + 4
ROWS = 27 * C
FACE_ROWS = FACE * 64
X_ROWS = FACE_ROWS + 32
Y_ROWS = FACE_ROWS + 48
HALF = ROWS // 2
VMEM_LIMIT = 32 * 1024 * 1024
PACK_LIMIT = 60 * 1024 * 1024


def vmem():
    return pl.BlockSpec(memory_space=pltpu.VMEM)


def hbm():
    return pl.BlockSpec(memory_space=pltpu.HBM)


def fetching(*pairs):
    copies = [pltpu.make_async_copy(src, dst, sem) for src, dst, sem in pairs]
    for copy in copies:
        copy.start()
    return copies


def fetched(*pairs):
    for copy in fetching(*pairs):
        copy.wait()


def mask_columns(mask_ref, s):
    m = mask_ref[...].astype(jnp.float32)
    pick = (lax.broadcasted_iota(jnp.int32, (SLOTS, C), 0) == s).astype(jnp.float32)
    return lax.dot_general(m, pick, (((0,), (0,)), ((), ())), preferred_element_type=jnp.float32)


def parity(axis):
    return lax.rem(lax.axis_index(axis), 2)


def side_of(k, odd):
    return 1 - odd if k == 0 else odd


def shifts(cells, same, below, above):
    line = lax.broadcasted_iota(jnp.int32, cells.shape, cells.ndim - 2)
    axis = cells.ndim - 2
    up = jnp.where((same & (line >= 1)) | (below & (line == 0)), pltpu.roll(cells, 1, axis), 0.0)
    down = jnp.where((same & (line <= 6)) | (above & (line == 7)), pltpu.roll(cells, 7, axis), 0.0)
    return up, jnp.where(same, cells, 0.0), down


def pack_kernel(face_hbm, edge_hbm, near_hbm, feat_hbm, grad_hbm, mask_hbm, act_ref, grd_ref, *refs):
    y_out, x_out = refs[0:2], refs[2:4]
    face_ref, edge_ref, near, raw, mask_ref, full, sems = refs[4:]
    fetched(
        (mask_hbm, mask_ref, sems.at[0]),
        (feat_hbm, raw.at[0], sems.at[1]),
        (grad_hbm, raw.at[1], sems.at[2]),
        (face_hbm, face_ref, sems.at[3]),
        (edge_hbm, edge_ref, sems.at[4]),
        (near_hbm, near, sems.at[5]),
    )
    for s in range(SLOTS):
        rows = mask_columns(mask_ref, s)
        for f, dst in enumerate((act_ref, grd_ref)):
            masked = raw[f, s].astype(jnp.float32) * rows
            full[f, s] = masked.reshape(8, 8, 8, C)
            dst[s] = masked.astype(jnp.bfloat16)
    for axis, outs in enumerate((x_out, y_out)):
        odd = parity("gy" if axis else "gx")
        for k in range(2):
            side = side_of(k, odd)
            for f in range(2):
                for r in range(FACE):
                    entry = face_ref[r, 2 * axis + side]
                    slot = jnp.clip(entry, 0, SLOTS - 1)
                    layer = full[f, slot, :, 7 * side] if axis else full[f, slot, 7 * side]
                    layer = jnp.where(entry < SLOTS, layer, 0.0)
                    first = f * (Y_ROWS if axis else X_ROWS) + r * 64
                    outs[k][pl.ds(first, 64)] = layer.reshape(64, C).astype(jnp.bfloat16)
            lines = []
            for far in range(2):
                corner = 2 * far + side if axis else 2 * side + far
                entry = edge_ref[0, corner]
                slot = jnp.clip(entry, 0, SLOTS - 1)
                live = entry < SLOTS
                at_x, at_y = (7 * far, 7 * side) if axis else (7 * side, 7 * far)
                if axis == 0:
                    for f in range(2):
                        lines.append(jnp.where(live, full[f, slot, at_x, at_y], 0.0))
                    continue
                base = 18 * far + 6 * side
                low, mid, high = near[slot, base], near[slot, base + 1], near[slot, base + 2]
                up, same, down = shifts(
                    full[1, slot, at_x, at_y],
                    live & (mid < ZERO),
                    live & (high < ZERO),
                    live & (low < ZERO),
                )
                lines += [down, same, up]
            lines = jnp.concatenate(lines, axis=0).astype(jnp.bfloat16)
            outs[k][pl.ds(FACE_ROWS, lines.shape[0])] = lines


def pack(features, out_grad, mask, near, face_sends, edge_sends):
    sends = [jax.ShapeDtypeStruct((rows, C), jnp.bfloat16) for rows in 2 * (Y_ROWS + FACE_ROWS,) + 2 * (X_ROWS + FACE_ROWS,)]
    brick = jax.ShapeDtypeStruct((SLOTS, 512, C), jnp.bfloat16)
    return pl.pallas_call(
        pack_kernel,
        out_shape=[brick, brick] + sends,
        in_specs=[hbm()] * 6,
        out_specs=[vmem()] * 6,
        scratch_shapes=[
            pltpu.SMEM((FACE, 4), jnp.int32),
            pltpu.SMEM((1, 4), jnp.int32),
            pltpu.SMEM((SLOTS, 27), jnp.int32),
            pltpu.VMEM((2, SLOTS, 512, C), jnp.bfloat16),
            pltpu.VMEM((SLOTS, 512), jnp.int32),
            pltpu.VMEM((2, SLOTS, 8, 8, 8, C), jnp.float32),
            pltpu.SemaphoreType.DMA((6,)),
        ],
        compiler_params=pltpu.CompilerParams(vmem_limit_bytes=PACK_LIMIT),
        name="pack",
    )(face_sends.T, edge_sends.T, near, features, out_grad, mask)


def parts_of(ref):
    rows = ref.shape[0] // 2
    return ref.at[pl.ds(0, rows)], ref.at[pl.ds(rows, rows)]


def join_kernel(x0, x1, y0, y1, *outs):
    for axis, pair in enumerate(((x0, x1), (y0, y1))):
        rows = (X_ROWS, Y_ROWS)[axis]
        for k, src in enumerate(pair):
            outs[axis][pl.ds(k * rows, rows)] = src[pl.ds(0, rows)]
            outs[2 + axis][pl.ds(k * FACE_ROWS, FACE_ROWS)] = src[pl.ds(rows, FACE_ROWS)]


def join(x0, x1, y0, y1):
    outs = [
        jax.ShapeDtypeStruct((2 * rows, C), jnp.bfloat16) for rows in (X_ROWS, Y_ROWS, FACE_ROWS, FACE_ROWS)
    ]
    return pl.pallas_call(
        join_kernel,
        out_shape=outs,
        in_specs=[vmem()] * 4,
        out_specs=[vmem()] * 4,
        compiler_params=pltpu.CompilerParams(vmem_limit_bytes=VMEM_LIMIT),
        name="join_sides",
    )(x0, x1, y0, y1)


def forward_kernel(x_came, out0, out1):
    odd_x, odd_y = parity("gx"), parity("gy")
    for k, out in enumerate((out0, out1)):
        far = side_of(k, odd_y)
        for j, came in enumerate(parts_of(x_came)):
            source = side_of(j, odd_x)
            rows = came[pl.ds(pl.multiple_of(FACE_ROWS + 16 * far, 16), 16)]
            out[pl.ds(pl.multiple_of(16 * source, 16), 16)] = rows


def forward_corners(x_came):
    send = jax.ShapeDtypeStruct((32, C), jnp.bfloat16)
    return pl.pallas_call(
        forward_kernel,
        out_shape=[send] * 2,
        in_specs=[vmem()],
        out_specs=[vmem()] * 2,
        compiler_params=pltpu.CompilerParams(vmem_limit_bytes=VMEM_LIMIT),
        name="forward_corners",
    )(x_came)


def fill_own(bricks, lx, ly, corners):
    for s in range(SLOTS):
        whole = bricks[s].astype(jnp.float32).reshape(8, 8, 8, C)
        for side, at in ((0, 7), (1, 0)):
            lx[side, s] = whole[at]
            ly[side, s] = whole[:, at]
            for other, far in ((0, 7), (1, 0)):
                corners[2 * side + other, s] = whole[at, far]


def fill_zero(lx, ly, corners, first):
    for ref in (lx, ly, corners):
        count = ref.shape[1] - first
        ref[:, pl.ds(first, count)] = jnp.zeros((ref.shape[0], count) + ref.shape[2:], jnp.float32)


def fill_came(f, x_came, y_came, edges, lx, ly, corners):
    odd_x, odd_y = parity("gx"), parity("gy")
    for came, odd, dst in ((x_came, odd_x, lx), (y_came, odd_y, ly)):
        for k, part in enumerate(parts_of(came)):
            side = side_of(k, odd)
            for r in range(FACE):
                rows = part[pl.ds(r * 64, 64)]
                dst[side, SLOTS + r] = rows.astype(jnp.float32).reshape(8, 8, C)
            dst[k, SLOTS + FACE] = jnp.zeros((8, 8, C), jnp.float32)
    for k, came in enumerate(edges):
        side = side_of(k, odd_y)
        for j in range(2):
            rows = came[pl.ds(16 * j, 16)].astype(jnp.float32)
            corners[2 * j + side, SLOTS + 2 * FACE] = rows[8 * f : 8 * f + 8]
    for sx in range(2):
        for sy in range(2):
            c = 2 * sx + sy
            for r in range(FACE):
                corners[c, SLOTS + r] = lx[sx, SLOTS + r, 0 if sy else 7]
                corners[c, SLOTS + FACE + r] = ly[sy, SLOTS + r, 0 if sx else 7]
            corners[c, SLOTS + 2 * FACE + 1] = jnp.zeros((8, C), jnp.float32)


def build_columns(s, bricks, near, lx, ly, corners, wide, which):
    def spread(cells, at_x, at_y, depth):
        flat = cells.reshape(-1, 8, C)
        for k, moved in enumerate(shifts(flat, depth == 0, depth == -1, depth == 1)):
            wide[k, at_x, at_y] = moved.reshape(cells.shape)

    def column(nx, ny):
        base = 9 * (nx + 1) + 3 * (ny + 1)
        low, mid, high = near[s, base], near[s, base + 1], near[s, base + 2]
        entry = jnp.minimum(jnp.minimum(low, mid), high)
        depth = jnp.where(low < ZERO, -1, jnp.where(high < ZERO, 1, 0))
        if which == "own":
            depth = jnp.where(entry < SLOTS, depth, 2)
        if which == "rim":
            depth = jnp.where((entry >= SLOTS) & (entry < SLOTS + 4 * FACE), depth, 2)
        return entry, depth

    middle = pl.ds(1, 8)
    if which != "rim":
        spread(bricks[s].astype(jnp.float32).reshape(8, 8, 8, C), middle, middle, 0)
    for side, n in ((0, -1), (1, 1)):
        edge_at = pl.ds(0 if n < 0 else 9, 1)
        entry, depth = column(n, 0)
        place = jnp.where(entry < SLOTS, entry, jnp.clip(entry - FACE * side, 0, SLOTS + FACE))
        spread(lx[side, place].reshape(1, 8, 8, C), edge_at, middle, depth)
        entry, depth = column(0, n)
        place = jnp.where(entry < SLOTS, entry, jnp.clip(entry - FACE * (2 + side), 0, SLOTS + FACE))
        spread(ly[side, place].reshape(8, 1, 8, C), middle, edge_at, depth)
    for sx in range(2):
        for sy in range(2):
            entry, depth = column(2 * sx - 1, 2 * sy - 1)
            first_x = SLOTS + FACE * sx
            first_y = SLOTS + FACE * (2 + sy)
            own_edge = SLOTS + 4 * FACE + 2 * sx + sy
            in_x = (entry >= first_x) & (entry < first_x + FACE)
            in_y = (entry >= first_y) & (entry < first_y + FACE)
            place = jnp.where(entry == own_edge, SLOTS + 2 * FACE, SLOTS + 2 * FACE + 1)
            place = jnp.where(in_y, SLOTS + FACE + entry - first_y, place)
            place = jnp.where(in_x, SLOTS + entry - first_x, place)
            place = jnp.where(entry < SLOTS, entry, place)
            spread(corners[2 * sx + sy, place].reshape(1, 1, 8, C), pl.ds(9 * sx, 1), pl.ds(9 * sy, 1), depth)


def stack_columns(s, wide, v):
    for y in range(3):
        for z in range(3):
            cells = wide[z, :, pl.ds(y, 8)].reshape(10, 64, C).astype(jnp.bfloat16)
            v[s, :, :, pl.ds((3 * y + z) * C, C)] = cells


def columns_scratch():
    return [
        pltpu.VMEM((2, SLOTS + FACE + 1, 8, 8, C), jnp.float32),
        pltpu.VMEM((2, SLOTS + FACE + 1, 8, 8, C), jnp.float32),
        pltpu.VMEM((4, SLOTS + 2 * FACE + 2, 8, C), jnp.float32),
        pltpu.VMEM((3, 10, 10, 8, C), jnp.float32),
        pltpu.SMEM((SLOTS, 27), jnp.int32),
        pltpu.SemaphoreType.DMA(()),
    ]


def columns_kernel(near_hbm, act, v, lx, ly, corners, wide, near, sem):
    (table,) = fetching((near_hbm, near, sem))
    fill_own(act, lx, ly, corners)
    fill_zero(lx, ly, corners, SLOTS)
    table.wait()

    def per_slot(s, carry):
        build_columns(s, act, near, lx, ly, corners, wide, "own")
        stack_columns(s, wide, v)
        return carry

    lax.fori_loop(0, SLOTS, per_slot, 0)


def own_columns(near, act):
    return pl.pallas_call(
        columns_kernel,
        out_shape=jax.ShapeDtypeStruct((SLOTS, 10, 64, 9 * C), jnp.bfloat16),
        in_specs=[hbm(), vmem()],
        out_specs=vmem(),
        scratch_shapes=columns_scratch(),
        compiler_params=pltpu.CompilerParams(vmem_limit_bytes=VMEM_LIMIT),
        cost_estimate=pl.CostEstimate(flops=1 << 24, bytes_accessed=6 << 20, transcendentals=0),
        name="own_columns",
    )(near, act)


def inner_kernel(v, grd, out, turned):
    for s in range(SLOTS):
        for q in range(4):
            turned[:, pl.ds((4 * s + q) * C, C)] = grd[s, pl.ds(q * C, C)].T
    for x in range(3):
        cells = v[:, pl.ds(x, 8)].reshape(SLOTS * 512, 9 * C)
        terms = jnp.dot(turned[...], cells, preferred_element_type=jnp.float32)
        for j in range(9):
            out[pl.ds((9 * x + j) * C, C)] = terms[:, j * C : (j + 1) * C].T


def inner_terms(v, grd):
    return pl.pallas_call(
        inner_kernel,
        out_shape=jax.ShapeDtypeStruct((ROWS, C), jnp.float32),
        in_specs=[vmem()] * 2,
        out_specs=vmem(),
        scratch_shapes=[pltpu.VMEM((C, SLOTS * 512), jnp.bfloat16)],
        compiler_params=pltpu.CompilerParams(vmem_limit_bytes=VMEM_LIMIT),
        cost_estimate=pl.CostEstimate(flops=2 * 2048 * ROWS * C, bytes_accessed=6 << 20, transcendentals=0),
        name="inner_terms",
    )(v, grd)


def rim_kernel(near_hbm, inner, grd, x_ref, y_ref, keep, send, lx, ly, corners, wide, near, sem, *refs):
    vx, vy, ends_a, ends_g, side_x, side_y = refs
    (table,) = fetching((near_hbm, near, sem))
    fill_came(0, x_ref, y_ref, (), lx, ly, corners)
    for k, came in enumerate(parts_of(x_ref)):
        side = side_of(k, parity("gx"))
        for j in range(2):
            ends_a[side, j] = came[pl.ds(FACE_ROWS + 16 * j, 16)].astype(jnp.float32)[0:8]
    for k, came in enumerate(parts_of(y_ref)):
        side = side_of(k, parity("gy"))
        ends_g[side] = came[pl.ds(FACE_ROWS, 48)].astype(jnp.float32).reshape(2, 3, 8, C)
    table.wait()
    for s in range(SLOTS):
        build_columns(s, None, near, lx, ly, corners, wide, "rim")
        rows = pl.ds(64 * s, 64)
        for side in range(2):
            for j in range(9):
                cells = wide[j % 3, 9 * side, pl.ds(j // 3, 8)]
                vx[side, rows, pl.ds(j * C, C)] = cells.reshape(64, C).astype(jnp.bfloat16)
        for z in range(3):
            for sx in range(2):
                for sy in range(2):
                    wide[z, 9 * sx, 9 * sy] = jnp.zeros((8, C), jnp.float32)
        for side in range(2):
            for j in range(9):
                cells = wide[j % 3, pl.ds(j // 3, 8), 9 * side]
                vy[side, rows, pl.ds(j * C, C)] = cells.reshape(64, C).astype(jnp.bfloat16)
    grads = grd[...]
    lines = grads.astype(jnp.float32).reshape(SLOTS, 8, 8, 8, C)

    def term(cells, rows):
        return lax.dot_general(cells, rows, (((0,), (0,)), ((), ())), preferred_element_type=jnp.float32)

    def end(line):
        return jnp.concatenate([line, jnp.zeros((8, C), jnp.float32)], axis=0).astype(jnp.bfloat16)

    for side in range(2):
        rows = grads[:, 448 * side : 448 * side + 64].reshape(SLOTS * 64, C)
        side_x[side] = term(vx[side], rows)
        rows = lines[:, :, 7 * side].reshape(SLOTS * 64, C).astype(jnp.bfloat16)
        side_y[side] = term(vy[side], rows)
    def write(halves):
        for x in range(3):
            for y in range(3):
                for z in range(3):
                    first = (9 * x + 3 * y + z) * C
                    value = inner[pl.ds(first, C)]
                    if x != 1:
                        value += side_x[x // 2, pl.ds((3 * y + z) * C, C)]
                    if y != 1:
                        value += side_y[y // 2, pl.ds((3 * x + z) * C, C)]
                    if x != 1 and y != 1:
                        sx, sy = x // 2, 1 - y // 2
                        value += term(end(ends_a[sx, sy]), end(ends_g[sy, sx, z]))
                    for half in range(2):
                        low = max(first, half * HALF)
                        rows = min(first + C, (half + 1) * HALF) - low
                        if rows > 0:
                            halves[half][pl.ds(low - half * HALF, rows)] = value[low - first : low - first + rows]

    core = parity("gy")

    @pl.when(core == 0)
    def _():
        write((keep, send))

    @pl.when(core == 1)
    def _():
        write((send, keep))


def rim_terms(near, inner, grd, x_came, y_came):
    half = jax.ShapeDtypeStruct((HALF, C), jnp.float32)
    side = pltpu.VMEM((2, SLOTS * 64, 9 * C), jnp.bfloat16)
    return pl.pallas_call(
        rim_kernel,
        out_shape=[half, half],
        in_specs=[hbm()] + [vmem()] * 4,
        out_specs=[vmem()] * 2,
        scratch_shapes=columns_scratch()
        + [
            side,
            side,
            pltpu.VMEM((2, 2, 8, C), jnp.float32),
            pltpu.VMEM((2, 2, 3, 8, C), jnp.float32),
            pltpu.VMEM((2, 9 * C, C), jnp.float32),
            pltpu.VMEM((2, 9 * C, C), jnp.float32),
        ],
        compiler_params=pltpu.CompilerParams(vmem_limit_bytes=VMEM_LIMIT),
        cost_estimate=pl.CostEstimate(flops=2 * 256 * 36 * C * C, bytes_accessed=6 << 20, transcendentals=0),
        name="rim_terms",
    )(near, inner, grd, x_came, y_came)


def power_of(values):
    peak = jnp.max(jnp.abs(values))
    return jnp.clip(jnp.ceil(jnp.log2(jnp.full((8, C), peak))), -100.0, 100.0)[0:1]


def merge_kernel(groups, take, keep, came, out, total):
    held = out.shape[1]
    total[pl.ds(0, HALF)] = keep[...] + came[...]
    if groups * take > HALF:
        total[pl.ds(HALF, groups * take - HALF)] = jnp.zeros((groups * take - HALF, C), jnp.float32)
    power = power_of(total[...])
    scale = jnp.exp2(14.0 - power)
    for p in range(groups):
        out[p, pl.ds(0, take)] = total[pl.ds(p * take, take)] * scale
        out[p, pl.ds(take, held - take)] = jnp.broadcast_to(power, (held - take, C))


def merge(groups, take, held, keep, came):
    return pl.pallas_call(
        lambda *refs: merge_kernel(groups, take, *refs),
        out_shape=jax.ShapeDtypeStruct((groups, held, C), jnp.float32),
        in_specs=[vmem()] * 2,
        out_specs=vmem(),
        scratch_shapes=[pltpu.VMEM((groups * take, C), jnp.float32)],
        compiler_params=pltpu.CompilerParams(vmem_limit_bytes=VMEM_LIMIT),
        name="merge",
    )(keep, came)


def sum_kernel(take, blocks, out):
    groups, held, _ = blocks.shape
    total = jnp.zeros((take, C), jnp.float32)
    for p in range(groups):
        total += blocks[p, pl.ds(0, take)] * jnp.exp2(blocks[p, pl.ds(take, 1)] - 14.0)
    power = power_of(total)
    total = total * jnp.exp2(14.0 - power)
    for p in range(groups):
        out[p, pl.ds(0, take)] = total
        out[p, pl.ds(take, held - take)] = jnp.broadcast_to(power, (held - take, C))


def sum_blocks(take, blocks):
    return pl.pallas_call(
        lambda *refs: sum_kernel(take, *refs),
        out_shape=jax.ShapeDtypeStruct(blocks.shape, jnp.float32),
        in_specs=[vmem()],
        out_specs=vmem(),
        compiler_params=pltpu.CompilerParams(vmem_limit_bytes=VMEM_LIMIT),
        name="sum_blocks",
    )(blocks)


def decode_kernel(take, scale, own, blocks, *refs):
    out, half, sems = refs[-3:]
    groups = blocks.shape[0]
    core = parity("gy")
    target = out.at[core if own else 1 - core]
    copies = []
    done = 0
    for p in range(groups):
        rows = min(take, HALF - p * take)
        if rows > 0:
            factor = jnp.exp2(blocks[p, pl.ds(take, 1)] - 14.0) * scale
            half[pl.ds(p * take, rows)] = blocks[p, pl.ds(0, rows)] * factor
        ready = min((p + 1) * take, HALF)
        if ready - done >= HALF // 4 and ready % 8 == 0 or p == groups - 1:
            piece = pl.ds(done, ready - done)
            copies += fetching((half.at[piece], target.at[piece], sems.at[len(copies)]))
            done = ready
    for copy in copies:
        copy.wait()


def decode(take, scale, blocks, begun=None):
    rest = () if begun is None else (begun,)
    return pl.pallas_call(
        lambda *refs: decode_kernel(take, scale, not rest, *refs),
        out_shape=jax.ShapeDtypeStruct((2, HALF, C), jnp.float32),
        in_specs=[vmem()] + [hbm()] * len(rest),
        out_specs=hbm(),
        scratch_shapes=[pltpu.VMEM((HALF, C), jnp.float32), pltpu.SemaphoreType.DMA((5,))],
        input_output_aliases={1: 0} if rest else {},
        compiler_params=pltpu.CompilerParams(vmem_limit_bytes=VMEM_LIMIT),
        name="decode_other" if rest else "decode_own",
    )(blocks, *rest)


def product_kernel(f, near_hbm, mask_ref, kernel_ref, bricks, x_ref, y_ref, e0, e1, out, *refs):
    lx, ly, corners, wide, near, sem, v, *flipped = refs
    (table,) = fetching((near_hbm, near, sem))
    weights = kernel_ref
    if f == 1:
        weights = flipped[0]
        for o in range(27):
            weights[pl.ds((26 - o) * C, C)] = kernel_ref[pl.ds(o * C, C)].T
    fill_own(bricks, lx, ly, corners)
    fill_came(f, x_ref, y_ref, (e0, e1), lx, ly, corners)
    table.wait()

    def per_slot(s, carry):
        build_columns(s, bricks, near, lx, ly, corners, wide, "all")
        stack_columns(s, wide, v)
        total = jnp.zeros((512, C), jnp.float32)
        for x in range(3):
            cells = v[s, pl.ds(x, 8)].reshape(512, 9 * C)
            total += jnp.dot(cells, weights[pl.ds(x * 9 * C, 9 * C)], preferred_element_type=jnp.float32)
        out[s] = (total * mask_columns(mask_ref, s)).astype(jnp.bfloat16)
        return carry

    lax.fori_loop(0, SLOTS, per_slot, 0)


def product(f, near, mask, kernel, bricks, x_came, y_came, edges):
    return pl.pallas_call(
        lambda *refs: product_kernel(f, *refs),
        out_shape=jax.ShapeDtypeStruct((SLOTS, 512, C), jnp.bfloat16),
        in_specs=[hbm()] + [vmem()] * 7,
        out_specs=vmem(),
        scratch_shapes=columns_scratch()
        + [pltpu.VMEM((SLOTS, 10, 64, 9 * C), jnp.bfloat16)]
        + ([pltpu.VMEM((ROWS, C), jnp.bfloat16)] if f else []),
        compiler_params=pltpu.CompilerParams(vmem_limit_bytes=VMEM_LIMIT),
        cost_estimate=pl.CostEstimate(flops=2 * 2048 * ROWS * C, bytes_accessed=4 << 20, transcendentals=0),
        name=("output_product", "input_grad_product")[f],
    )(near, mask, kernel, bricks, x_came, y_came, *edges)


def swapped(value, axis, k):
    pairs = []
    for low in range(k, lax.axis_size(axis) - 1, 2):
        pairs += [(low, low + 1), (low + 1, low)]
    return lax.ppermute(value, axis, pairs)


def hopped(value, axis):
    size = lax.axis_size(axis)
    pairs = [(i, i + 2) for i in range(1, size - 2, 2)] + [(i, i - 2) for i in range(2, size, 2)]
    return lax.ppermute(value, axis, pairs)


def local(features, out_grad, kernel, voxel_mask, neighbours, face_sends, edge_sends):
    size_x, size_y = lax.axis_size("gx"), lax.axis_size("gy")
    parts = size_x * size_y
    groups = parts // 2
    take = -(-HALF // groups)
    held = -(-(take + 1) // 16) * 16
    same_core = [[i for i in range(parts) if i % size_y % 2 == core] for core in range(2)]

    def spread(blocks):
        return lax.all_to_all(blocks, ("gx", "gy"), 0, 0, axis_index_groups=same_core, tiled=True)

    act, grd, y0, y1, x0, x1 = pack(
        features.reshape(SLOTS, 512, C),
        out_grad.reshape(SLOTS, 512, C),
        voxel_mask,
        neighbours,
        face_sends,
        edge_sends,
    )
    x1, y1 = hopped(x1, "gx"), hopped(y1, "gy")
    v = own_columns(neighbours, act)
    x1, y1, v = lax.optimization_barrier((x1, y1, v))
    x_came, y_came, x_more, y_more = join(x0, x1, y0, y1)
    x_came, y_came = swapped(x_came, "gx", 0), swapped(y_came, "gy", 0)
    inner = inner_terms(v, grd)
    keep, send = rim_terms(neighbours, inner, grd, x_came, y_came)
    blocks = merge(groups, take, held, keep, swapped(send, "gy", 0)).astype(jnp.float16)
    rows = kernel.reshape(ROWS, C)
    blocks, act, x_came, x_more, y_more = lax.optimization_barrier((blocks, act, x_came, x_more, y_more))
    x_more, y_more = swapped(x_more, "gx", 0), swapped(y_more, "gy", 0)
    e0, e1 = forward_corners(x_came)
    edges = [swapped(e0, "gy", 0), swapped(e1, "gy", 1)]
    output = product(0, neighbours, voxel_mask, rows, act, x_came, y_came, edges)
    arrived, output = lax.optimization_barrier((spread(blocks), output))
    copies = sum_blocks(take, arrived.astype(jnp.float32)).astype(jnp.float16)
    copies, grd = lax.optimization_barrier((copies, grd))
    input_grad = product(1, neighbours, voxel_mask, rows, grd, x_more, y_more, edges)
    mine, input_grad = lax.optimization_barrier((spread(copies), input_grad))
    other = swapped(mine, "gy", 0)
    scale = 1.0 / math.sqrt(parts * SLOTS * 512)
    weight = decode(take, scale, mine.astype(jnp.float32))
    weight = decode(take, scale, other.astype(jnp.float32), weight)
    shape = (SLOTS, 8, 8, 8, C)
    return output.reshape(shape), input_grad.reshape(shape), weight.reshape(27, C, C)


def solution(mesh):
    spec = P(("gx", "gy"))
    return jax.shard_map(
        local,
        mesh=mesh,
        in_specs=(spec, spec, P(), spec, spec, spec, spec),
        out_specs=(spec, spec, P()),
        check_vma=False,
    )
```

```python
import math

import jax
import jax.numpy as jnp
from jax import lax
from jax.experimental import pallas as pl
from jax.experimental.pallas import tpu as pltpu
from jax.sharding import PartitionSpec as P

FACES = ((-1, 0), (1, 0), (0, -1), (0, 1))
EDGES = ((-1, -1), (-1, 1), (1, -1), (1, 1))
C = 128
SLOTS = 4
FACE = 2
ZERO = SLOTS + 4 * FACE + 4
ROWS = 27 * C
FACE_ROWS = FACE * 64
X_ROWS = FACE_ROWS + 32
Y_ROWS = FACE_ROWS + 48
HALF = ROWS // 2
VMEM_LIMIT = 32 * 1024 * 1024
PACK_LIMIT = 60 * 1024 * 1024


def vmem():
    return pl.BlockSpec(memory_space=pltpu.VMEM)


def hbm():
    return pl.BlockSpec(memory_space=pltpu.HBM)


def fetching(*pairs):
    copies = [pltpu.make_async_copy(src, dst, sem) for src, dst, sem in pairs]
    for copy in copies:
        copy.start()
    return copies


def fetched(*pairs):
    for copy in fetching(*pairs):
        copy.wait()


def mask_columns(mask_ref, s):
    m = mask_ref[...].astype(jnp.float32)
    pick = (lax.broadcasted_iota(jnp.int32, (SLOTS, C), 0) == s).astype(jnp.float32)
    return lax.dot_general(m, pick, (((0,), (0,)), ((), ())), preferred_element_type=jnp.float32)


def parity(axis):
    return lax.rem(lax.axis_index(axis), 2)


def side_of(k, odd):
    return 1 - odd if k == 0 else odd


def shifts(cells, same, below, above):
    line = lax.broadcasted_iota(jnp.int32, cells.shape, cells.ndim - 2)
    axis = cells.ndim - 2
    up = jnp.where((same & (line >= 1)) | (below & (line == 0)), pltpu.roll(cells, 1, axis), 0.0)
    down = jnp.where((same & (line <= 6)) | (above & (line == 7)), pltpu.roll(cells, 7, axis), 0.0)
    return up, jnp.where(same, cells, 0.0), down


def pack_kernel(face_hbm, edge_hbm, near_hbm, feat_hbm, grad_hbm, mask_hbm, act_ref, grd_ref, *refs):
    y_out, x_out = refs[0:2], refs[2:4]
    face_ref, edge_ref, near, raw, mask_ref, full, sems = refs[4:]
    fetched(
        (mask_hbm, mask_ref, sems.at[0]),
        (feat_hbm, raw.at[0], sems.at[1]),
        (grad_hbm, raw.at[1], sems.at[2]),
        (face_hbm, face_ref, sems.at[3]),
        (edge_hbm, edge_ref, sems.at[4]),
        (near_hbm, near, sems.at[5]),
    )
    for s in range(SLOTS):
        rows = mask_columns(mask_ref, s)
        for f, dst in enumerate((act_ref, grd_ref)):
            masked = raw[f, s].astype(jnp.float32) * rows
            full[f, s] = masked.reshape(8, 8, 8, C)
            dst[s] = masked.astype(jnp.bfloat16)
    for axis, outs in enumerate((x_out, y_out)):
        odd = parity("gy" if axis else "gx")
        for k in range(2):
            side = side_of(k, odd)
            for f in range(2):
                for r in range(FACE):
                    entry = face_ref[r, 2 * axis + side]
                    slot = jnp.clip(entry, 0, SLOTS - 1)
                    layer = full[f, slot, :, 7 * side] if axis else full[f, slot, 7 * side]
                    layer = jnp.where(entry < SLOTS, layer, 0.0)
                    first = f * (Y_ROWS if axis else X_ROWS) + r * 64
                    outs[k][pl.ds(first, 64)] = layer.reshape(64, C).astype(jnp.bfloat16)
            lines = []
            for far in range(2):
                corner = 2 * far + side if axis else 2 * side + far
                entry = edge_ref[0, corner]
                slot = jnp.clip(entry, 0, SLOTS - 1)
                live = entry < SLOTS
                at_x, at_y = (7 * far, 7 * side) if axis else (7 * side, 7 * far)
                if axis == 0:
                    for f in range(2):
                        lines.append(jnp.where(live, full[f, slot, at_x, at_y], 0.0))
                    continue
                base = 18 * far + 6 * side
                low, mid, high = near[slot, base], near[slot, base + 1], near[slot, base + 2]
                up, same, down = shifts(
                    full[1, slot, at_x, at_y],
                    live & (mid < ZERO),
                    live & (high < ZERO),
                    live & (low < ZERO),
                )
                lines += [down, same, up]
            lines = jnp.concatenate(lines, axis=0).astype(jnp.bfloat16)
            outs[k][pl.ds(FACE_ROWS, lines.shape[0])] = lines


def pack(features, out_grad, mask, near, face_sends, edge_sends):
    sends = [jax.ShapeDtypeStruct((rows, C), jnp.bfloat16) for rows in 2 * (Y_ROWS + FACE_ROWS,) + 2 * (X_ROWS + FACE_ROWS,)]
    brick = jax.ShapeDtypeStruct((SLOTS, 512, C), jnp.bfloat16)
    return pl.pallas_call(
        pack_kernel,
        out_shape=[brick, brick] + sends,
        in_specs=[hbm()] * 6,
        out_specs=[vmem()] * 6,
        scratch_shapes=[
            pltpu.SMEM((FACE, 4), jnp.int32),
            pltpu.SMEM((1, 4), jnp.int32),
            pltpu.SMEM((SLOTS, 27), jnp.int32),
            pltpu.VMEM((2, SLOTS, 512, C), jnp.bfloat16),
            pltpu.VMEM((SLOTS, 512), jnp.int32),
            pltpu.VMEM((2, SLOTS, 8, 8, 8, C), jnp.float32),
            pltpu.SemaphoreType.DMA((6,)),
        ],
        compiler_params=pltpu.CompilerParams(vmem_limit_bytes=PACK_LIMIT),
        name="pack",
    )(face_sends.T, edge_sends.T, near, features, out_grad, mask)


def parts_of(ref):
    rows = ref.shape[0] // 2
    return ref.at[pl.ds(0, rows)], ref.at[pl.ds(rows, rows)]


def join_kernel(x0, x1, y0, y1, *outs):
    for axis, pair in enumerate(((x0, x1), (y0, y1))):
        rows = (X_ROWS, Y_ROWS)[axis]
        for k, src in enumerate(pair):
            outs[axis][pl.ds(k * rows, rows)] = src[pl.ds(0, rows)]
            outs[2 + axis][pl.ds(k * FACE_ROWS, FACE_ROWS)] = src[pl.ds(rows, FACE_ROWS)]


def join(x0, x1, y0, y1):
    outs = [
        jax.ShapeDtypeStruct((2 * rows, C), jnp.bfloat16) for rows in (X_ROWS, Y_ROWS, FACE_ROWS, FACE_ROWS)
    ]
    return pl.pallas_call(
        join_kernel,
        out_shape=outs,
        in_specs=[vmem()] * 4,
        out_specs=[vmem()] * 4,
        compiler_params=pltpu.CompilerParams(vmem_limit_bytes=VMEM_LIMIT),
        name="join_sides",
    )(x0, x1, y0, y1)


def forward_kernel(x_came, out0, out1):
    odd_x, odd_y = parity("gx"), parity("gy")
    for k, out in enumerate((out0, out1)):
        far = side_of(k, odd_y)
        for j, came in enumerate(parts_of(x_came)):
            source = side_of(j, odd_x)
            rows = came[pl.ds(pl.multiple_of(FACE_ROWS + 16 * far, 16), 16)]
            out[pl.ds(pl.multiple_of(16 * source, 16), 16)] = rows


def forward_corners(x_came):
    send = jax.ShapeDtypeStruct((32, C), jnp.bfloat16)
    return pl.pallas_call(
        forward_kernel,
        out_shape=[send] * 2,
        in_specs=[vmem()],
        out_specs=[vmem()] * 2,
        compiler_params=pltpu.CompilerParams(vmem_limit_bytes=VMEM_LIMIT),
        name="forward_corners",
    )(x_came)


def fill_own(bricks, lx, ly, corners):
    for s in range(SLOTS):
        whole = bricks[s].astype(jnp.float32).reshape(8, 8, 8, C)
        for side, at in ((0, 7), (1, 0)):
            lx[side, s] = whole[at]
            ly[side, s] = whole[:, at]
            for other, far in ((0, 7), (1, 0)):
                corners[2 * side + other, s] = whole[at, far]


def fill_zero(lx, ly, corners, first):
    for ref in (lx, ly, corners):
        count = ref.shape[1] - first
        ref[:, pl.ds(first, count)] = jnp.zeros((ref.shape[0], count) + ref.shape[2:], jnp.float32)


def fill_came(f, x_came, y_came, edges, lx, ly, corners):
    odd_x, odd_y = parity("gx"), parity("gy")
    for came, odd, dst in ((x_came, odd_x, lx), (y_came, odd_y, ly)):
        for k, part in enumerate(parts_of(came)):
            side = side_of(k, odd)
            for r in range(FACE):
                rows = part[pl.ds(r * 64, 64)]
                dst[side, SLOTS + r] = rows.astype(jnp.float32).reshape(8, 8, C)
            dst[k, SLOTS + FACE] = jnp.zeros((8, 8, C), jnp.float32)
    for k, came in enumerate(edges):
        side = side_of(k, odd_y)
        for j in range(2):
            rows = came[pl.ds(16 * j, 16)].astype(jnp.float32)
            corners[2 * j + side, SLOTS + 2 * FACE] = rows[8 * f : 8 * f + 8]
    for sx in range(2):
        for sy in range(2):
            c = 2 * sx + sy
            for r in range(FACE):
                corners[c, SLOTS + r] = lx[sx, SLOTS + r, 0 if sy else 7]
                corners[c, SLOTS + FACE + r] = ly[sy, SLOTS + r, 0 if sx else 7]
            corners[c, SLOTS + 2 * FACE + 1] = jnp.zeros((8, C), jnp.float32)


def build_columns(s, bricks, near, lx, ly, corners, wide, which):
    def spread(cells, at_x, at_y, depth):
        flat = cells.reshape(-1, 8, C)
        for k, moved in enumerate(shifts(flat, depth == 0, depth == -1, depth == 1)):
            wide[k, at_x, at_y] = moved.reshape(cells.shape)

    def column(nx, ny):
        base = 9 * (nx + 1) + 3 * (ny + 1)
        low, mid, high = near[s, base], near[s, base + 1], near[s, base + 2]
        entry = jnp.minimum(jnp.minimum(low, mid), high)
        depth = jnp.where(low < ZERO, -1, jnp.where(high < ZERO, 1, 0))
        if which == "own":
            depth = jnp.where(entry < SLOTS, depth, 2)
        if which == "rim":
            depth = jnp.where((entry >= SLOTS) & (entry < SLOTS + 4 * FACE), depth, 2)
        return entry, depth

    middle = pl.ds(1, 8)
    if which != "rim":
        spread(bricks[s].astype(jnp.float32).reshape(8, 8, 8, C), middle, middle, 0)
    for side, n in ((0, -1), (1, 1)):
        edge_at = pl.ds(0 if n < 0 else 9, 1)
        entry, depth = column(n, 0)
        place = jnp.where(entry < SLOTS, entry, jnp.clip(entry - FACE * side, 0, SLOTS + FACE))
        spread(lx[side, place].reshape(1, 8, 8, C), edge_at, middle, depth)
        entry, depth = column(0, n)
        place = jnp.where(entry < SLOTS, entry, jnp.clip(entry - FACE * (2 + side), 0, SLOTS + FACE))
        spread(ly[side, place].reshape(8, 1, 8, C), middle, edge_at, depth)
    for sx in range(2):
        for sy in range(2):
            entry, depth = column(2 * sx - 1, 2 * sy - 1)
            first_x = SLOTS + FACE * sx
            first_y = SLOTS + FACE * (2 + sy)
            own_edge = SLOTS + 4 * FACE + 2 * sx + sy
            in_x = (entry >= first_x) & (entry < first_x + FACE)
            in_y = (entry >= first_y) & (entry < first_y + FACE)
            place = jnp.where(entry == own_edge, SLOTS + 2 * FACE, SLOTS + 2 * FACE + 1)
            place = jnp.where(in_y, SLOTS + FACE + entry - first_y, place)
            place = jnp.where(in_x, SLOTS + entry - first_x, place)
            place = jnp.where(entry < SLOTS, entry, place)
            spread(corners[2 * sx + sy, place].reshape(1, 1, 8, C), pl.ds(9 * sx, 1), pl.ds(9 * sy, 1), depth)


def stack_columns(s, wide, v):
    for y in range(3):
        for z in range(3):
            cells = wide[z, :, pl.ds(y, 8)].reshape(10, 64, C).astype(jnp.bfloat16)
            v[s, :, :, pl.ds((3 * y + z) * C, C)] = cells


def columns_scratch():
    return [
        pltpu.VMEM((2, SLOTS + FACE + 1, 8, 8, C), jnp.float32),
        pltpu.VMEM((2, SLOTS + FACE + 1, 8, 8, C), jnp.float32),
        pltpu.VMEM((4, SLOTS + 2 * FACE + 2, 8, C), jnp.float32),
        pltpu.VMEM((3, 10, 10, 8, C), jnp.float32),
        pltpu.SMEM((SLOTS, 27), jnp.int32),
        pltpu.SemaphoreType.DMA(()),
    ]


def columns_kernel(near_hbm, act, v, lx, ly, corners, wide, near, sem):
    (table,) = fetching((near_hbm, near, sem))
    fill_own(act, lx, ly, corners)
    fill_zero(lx, ly, corners, SLOTS)
    table.wait()

    def per_slot(s, carry):
        build_columns(s, act, near, lx, ly, corners, wide, "own")
        stack_columns(s, wide, v)
        return carry

    lax.fori_loop(0, SLOTS, per_slot, 0)


def own_columns(near, act):
    return pl.pallas_call(
        columns_kernel,
        out_shape=jax.ShapeDtypeStruct((SLOTS, 10, 64, 9 * C), jnp.bfloat16),
        in_specs=[hbm(), vmem()],
        out_specs=vmem(),
        scratch_shapes=columns_scratch(),
        compiler_params=pltpu.CompilerParams(vmem_limit_bytes=VMEM_LIMIT),
        cost_estimate=pl.CostEstimate(flops=1 << 24, bytes_accessed=6 << 20, transcendentals=0),
        name="own_columns",
    )(near, act)


def inner_kernel(v, grd, out, turned):
    for s in range(SLOTS):
        for q in range(4):
            turned[:, pl.ds((4 * s + q) * C, C)] = grd[s, pl.ds(q * C, C)].T
    for x in range(3):
        cells = v[:, pl.ds(x, 8)].reshape(SLOTS * 512, 9 * C)
        terms = jnp.dot(turned[...], cells, preferred_element_type=jnp.float32)
        for j in range(9):
            out[pl.ds((9 * x + j) * C, C)] = terms[:, j * C : (j + 1) * C].T


def inner_terms(v, grd):
    return pl.pallas_call(
        inner_kernel,
        out_shape=jax.ShapeDtypeStruct((ROWS, C), jnp.float32),
        in_specs=[vmem()] * 2,
        out_specs=vmem(),
        scratch_shapes=[pltpu.VMEM((C, SLOTS * 512), jnp.bfloat16)],
        compiler_params=pltpu.CompilerParams(vmem_limit_bytes=VMEM_LIMIT),
        cost_estimate=pl.CostEstimate(flops=2 * 2048 * ROWS * C, bytes_accessed=6 << 20, transcendentals=0),
        name="inner_terms",
    )(v, grd)


def rim_kernel(near_hbm, inner, grd, x_ref, y_ref, keep, send, lx, ly, corners, wide, near, sem, *refs):
    vx, vy, ends_a, ends_g, side_x, side_y = refs
    (table,) = fetching((near_hbm, near, sem))
    fill_came(0, x_ref, y_ref, (), lx, ly, corners)
    for k, came in enumerate(parts_of(x_ref)):
        side = side_of(k, parity("gx"))
        for j in range(2):
            ends_a[side, j] = came[pl.ds(FACE_ROWS + 16 * j, 16)].astype(jnp.float32)[0:8]
    for k, came in enumerate(parts_of(y_ref)):
        side = side_of(k, parity("gy"))
        ends_g[side] = came[pl.ds(FACE_ROWS, 48)].astype(jnp.float32).reshape(2, 3, 8, C)
    table.wait()
    for s in range(SLOTS):
        build_columns(s, None, near, lx, ly, corners, wide, "rim")
        rows = pl.ds(64 * s, 64)
        for side in range(2):
            for j in range(9):
                cells = wide[j % 3, 9 * side, pl.ds(j // 3, 8)]
                vx[side, rows, pl.ds(j * C, C)] = cells.reshape(64, C).astype(jnp.bfloat16)
        for z in range(3):
            for sx in range(2):
                for sy in range(2):
                    wide[z, 9 * sx, 9 * sy] = jnp.zeros((8, C), jnp.float32)
        for side in range(2):
            for j in range(9):
                cells = wide[j % 3, pl.ds(j // 3, 8), 9 * side]
                vy[side, rows, pl.ds(j * C, C)] = cells.reshape(64, C).astype(jnp.bfloat16)
    grads = grd[...]
    lines = grads.astype(jnp.float32).reshape(SLOTS, 8, 8, 8, C)

    def term(cells, rows):
        return lax.dot_general(cells, rows, (((0,), (0,)), ((), ())), preferred_element_type=jnp.float32)

    def end(line):
        return jnp.concatenate([line, jnp.zeros((8, C), jnp.float32)], axis=0).astype(jnp.bfloat16)

    for side in range(2):
        rows = grads[:, 448 * side : 448 * side + 64].reshape(SLOTS * 64, C)
        side_x[side] = term(vx[side], rows)
        rows = lines[:, :, 7 * side].reshape(SLOTS * 64, C).astype(jnp.bfloat16)
        side_y[side] = term(vy[side], rows)
    def write(halves):
        for x in range(3):
            for y in range(3):
                for z in range(3):
                    first = (9 * x + 3 * y + z) * C
                    value = inner[pl.ds(first, C)]
                    if x != 1:
                        value += side_x[x // 2, pl.ds((3 * y + z) * C, C)]
                    if y != 1:
                        value += side_y[y // 2, pl.ds((3 * x + z) * C, C)]
                    if x != 1 and y != 1:
                        sx, sy = x // 2, 1 - y // 2
                        value += term(end(ends_a[sx, sy]), end(ends_g[sy, sx, z]))
                    for half in range(2):
                        low = max(first, half * HALF)
                        rows = min(first + C, (half + 1) * HALF) - low
                        if rows > 0:
                            halves[half][pl.ds(low - half * HALF, rows)] = value[low - first : low - first + rows]

    core = parity("gy")

    @pl.when(core == 0)
    def _():
        write((keep, send))

    @pl.when(core == 1)
    def _():
        write((send, keep))


def rim_terms(near, inner, grd, x_came, y_came):
    half = jax.ShapeDtypeStruct((HALF, C), jnp.float32)
    side = pltpu.VMEM((2, SLOTS * 64, 9 * C), jnp.bfloat16)
    return pl.pallas_call(
        rim_kernel,
        out_shape=[half, half],
        in_specs=[hbm()] + [vmem()] * 4,
        out_specs=[vmem()] * 2,
        scratch_shapes=columns_scratch()
        + [
            side,
            side,
            pltpu.VMEM((2, 2, 8, C), jnp.float32),
            pltpu.VMEM((2, 2, 3, 8, C), jnp.float32),
            pltpu.VMEM((2, 9 * C, C), jnp.float32),
            pltpu.VMEM((2, 9 * C, C), jnp.float32),
        ],
        compiler_params=pltpu.CompilerParams(vmem_limit_bytes=VMEM_LIMIT),
        cost_estimate=pl.CostEstimate(flops=2 * 256 * 36 * C * C, bytes_accessed=6 << 20, transcendentals=0),
        name="rim_terms",
    )(near, inner, grd, x_came, y_came)


def power_of(values):
    peak = jnp.max(jnp.abs(values))
    return jnp.clip(jnp.ceil(jnp.log2(jnp.full((8, C), peak))), -100.0, 100.0)[0:1]


def merge_kernel(groups, take, keep, came, out, total):
    held = out.shape[1]
    total[pl.ds(0, HALF)] = keep[...] + came[...]
    if groups * take > HALF:
        total[pl.ds(HALF, groups * take - HALF)] = jnp.zeros((groups * take - HALF, C), jnp.float32)
    power = power_of(total[...])
    scale = jnp.exp2(14.0 - power)
    for p in range(groups):
        out[p, pl.ds(0, take)] = total[pl.ds(p * take, take)] * scale
        out[p, pl.ds(take, held - take)] = jnp.broadcast_to(power, (held - take, C))


def merge(groups, take, held, keep, came):
    return pl.pallas_call(
        lambda *refs: merge_kernel(groups, take, *refs),
        out_shape=jax.ShapeDtypeStruct((groups, held, C), jnp.float32),
        in_specs=[vmem()] * 2,
        out_specs=vmem(),
        scratch_shapes=[pltpu.VMEM((groups * take, C), jnp.float32)],
        compiler_params=pltpu.CompilerParams(vmem_limit_bytes=VMEM_LIMIT),
        name="merge",
    )(keep, came)


def sum_kernel(take, blocks, out):
    groups, held, _ = blocks.shape
    total = jnp.zeros((take, C), jnp.float32)
    for p in range(groups):
        total += blocks[p, pl.ds(0, take)] * jnp.exp2(blocks[p, pl.ds(take, 1)] - 14.0)
    power = power_of(total)
    total = total * jnp.exp2(14.0 - power)
    for p in range(groups):
        out[p, pl.ds(0, take)] = total
        out[p, pl.ds(take, held - take)] = jnp.broadcast_to(power, (held - take, C))


def sum_blocks(take, blocks):
    return pl.pallas_call(
        lambda *refs: sum_kernel(take, *refs),
        out_shape=jax.ShapeDtypeStruct(blocks.shape, jnp.float32),
        in_specs=[vmem()],
        out_specs=vmem(),
        compiler_params=pltpu.CompilerParams(vmem_limit_bytes=VMEM_LIMIT),
        name="sum_blocks",
    )(blocks)


def decode_kernel(take, scale, own, blocks, *refs):
    out, half, sems = refs[-3:]
    groups = blocks.shape[0]
    core = parity("gy")
    target = out.at[core if own else 1 - core]
    copies = []
    done = 0
    for p in range(groups):
        rows = min(take, HALF - p * take)
        if rows > 0:
            factor = jnp.exp2(blocks[p, pl.ds(take, 1)] - 14.0) * scale
            half[pl.ds(p * take, rows)] = blocks[p, pl.ds(0, rows)] * factor
        ready = min((p + 1) * take, HALF)
        if ready - done >= HALF // 4 and ready % 8 == 0 or p == groups - 1:
            piece = pl.ds(done, ready - done)
            copies += fetching((half.at[piece], target.at[piece], sems.at[len(copies)]))
            done = ready
    for copy in copies:
        copy.wait()


def decode(take, scale, blocks, begun=None):
    rest = () if begun is None else (begun,)
    return pl.pallas_call(
        lambda *refs: decode_kernel(take, scale, not rest, *refs),
        out_shape=jax.ShapeDtypeStruct((2, HALF, C), jnp.float32),
        in_specs=[vmem()] + [hbm()] * len(rest),
        out_specs=hbm(),
        scratch_shapes=[pltpu.VMEM((HALF, C), jnp.float32), pltpu.SemaphoreType.DMA((5,))],
        input_output_aliases={1: 0} if rest else {},
        compiler_params=pltpu.CompilerParams(vmem_limit_bytes=VMEM_LIMIT),
        name="decode_other" if rest else "decode_own",
    )(blocks, *rest)


def product_kernel(f, near_hbm, mask_ref, kernel_ref, bricks, x_ref, y_ref, e0, e1, out, *refs):
    lx, ly, corners, wide, near, sem, v, *flipped = refs
    (table,) = fetching((near_hbm, near, sem))
    weights = kernel_ref
    if f == 1:
        weights = flipped[0]
        for o in range(27):
            weights[pl.ds((26 - o) * C, C)] = kernel_ref[pl.ds(o * C, C)].T
    fill_own(bricks, lx, ly, corners)
    fill_came(f, x_ref, y_ref, (e0, e1), lx, ly, corners)
    table.wait()

    def per_slot(s, carry):
        build_columns(s, bricks, near, lx, ly, corners, wide, "all")
        stack_columns(s, wide, v)
        total = jnp.zeros((512, C), jnp.float32)
        for x in range(3):
            cells = v[s, pl.ds(x, 8)].reshape(512, 9 * C)
            total += jnp.dot(cells, weights[pl.ds(x * 9 * C, 9 * C)], preferred_element_type=jnp.float32)
        out[s] = (total * mask_columns(mask_ref, s)).astype(jnp.bfloat16)
        return carry

    lax.fori_loop(0, SLOTS, per_slot, 0)


def product(f, near, mask, kernel, bricks, x_came, y_came, edges):
    return pl.pallas_call(
        lambda *refs: product_kernel(f, *refs),
        out_shape=jax.ShapeDtypeStruct((SLOTS, 512, C), jnp.bfloat16),
        in_specs=[hbm()] + [vmem()] * 7,
        out_specs=vmem(),
        scratch_shapes=columns_scratch()
        + [pltpu.VMEM((SLOTS, 10, 64, 9 * C), jnp.bfloat16)]
        + ([pltpu.VMEM((ROWS, C), jnp.bfloat16)] if f else []),
        compiler_params=pltpu.CompilerParams(vmem_limit_bytes=VMEM_LIMIT),
        cost_estimate=pl.CostEstimate(flops=2 * 2048 * ROWS * C, bytes_accessed=4 << 20, transcendentals=0),
        name=("output_product", "input_grad_product")[f],
    )(near, mask, kernel, bricks, x_came, y_came, *edges)


def swapped(value, axis, k):
    pairs = []
    for low in range(k, lax.axis_size(axis) - 1, 2):
        pairs += [(low, low + 1), (low + 1, low)]
    return lax.ppermute(value, axis, pairs)


def hopped(value, axis):
    size = lax.axis_size(axis)
    pairs = [(i, i + 2) for i in range(1, size - 2, 2)] + [(i, i - 2) for i in range(2, size, 2)]
    return lax.ppermute(value, axis, pairs)


def local(features, out_grad, kernel, voxel_mask, neighbours, face_sends, edge_sends):
    size_x, size_y = lax.axis_size("gx"), lax.axis_size("gy")
    parts = size_x * size_y
    groups = parts // 2
    take = -(-HALF // groups)
    held = -(-(take + 1) // 16) * 16
    order = [(i + parts // 2) % parts for i in range(parts)]
    same_core = [[i for i in order if i % size_y % 2 == core] for core in range(2)]

    def spread(blocks):
        return lax.all_to_all(blocks, ("gx", "gy"), 0, 0, axis_index_groups=same_core, tiled=True)

    act, grd, y0, y1, x0, x1 = pack(
        features.reshape(SLOTS, 512, C),
        out_grad.reshape(SLOTS, 512, C),
        voxel_mask,
        neighbours,
        face_sends,
        edge_sends,
    )
    x1, y1 = hopped(x1, "gx"), hopped(y1, "gy")
    v = own_columns(neighbours, act)
    x1, y1, v = lax.optimization_barrier((x1, y1, v))
    x_came, y_came, x_more, y_more = join(x0, x1, y0, y1)
    x_came, y_came = swapped(x_came, "gx", 0), swapped(y_came, "gy", 0)
    inner = inner_terms(v, grd)
    keep, send = rim_terms(neighbours, inner, grd, x_came, y_came)
    blocks = merge(groups, take, held, keep, swapped(send, "gy", 0)).astype(jnp.float16)
    rows = kernel.reshape(ROWS, C)
    blocks, act, x_came, x_more, y_more = lax.optimization_barrier((blocks, act, x_came, x_more, y_more))
    x_more, y_more = swapped(x_more, "gx", 0), swapped(y_more, "gy", 0)
    e0, e1 = forward_corners(x_came)
    edges = [swapped(e0, "gy", 0), swapped(e1, "gy", 1)]
    output = product(0, neighbours, voxel_mask, rows, act, x_came, y_came, edges)
    arrived, output, x_more, y_more = lax.optimization_barrier((spread(blocks), output, x_more, y_more))
    copies = sum_blocks(take, arrived.astype(jnp.float32)).astype(jnp.float16)
    copies, grd = lax.optimization_barrier((copies, grd))
    input_grad = product(1, neighbours, voxel_mask, rows, grd, x_more, y_more, edges)
    mine, input_grad = lax.optimization_barrier((spread(copies), input_grad))
    other = swapped(mine, "gy", 0)
    scale = 1.0 / math.sqrt(parts * SLOTS * 512)
    weight = decode(take, scale, mine.astype(jnp.float32))
    weight = decode(take, scale, other.astype(jnp.float32), weight)
    shape = (SLOTS, 8, 8, 8, C)
    return output.reshape(shape), input_grad.reshape(shape), weight.reshape(27, C, C)


def solution(mesh):
    spec = P(("gx", "gy"))
    return jax.shard_map(
        local,
        mesh=mesh,
        in_specs=(spec, spec, P(), spec, spec, spec, spec),
        out_specs=(spec, spec, P()),
        check_vma=False,
    )
```

```python
import math

import jax
import jax.numpy as jnp
from jax import lax
from jax.experimental import pallas as pl
from jax.experimental.pallas import tpu as pltpu
from jax.sharding import PartitionSpec as P

FACES = ((-1, 0), (1, 0), (0, -1), (0, 1))
EDGES = ((-1, -1), (-1, 1), (1, -1), (1, 1))
C = 128
SLOTS = 4
FACE = 2
ZERO = SLOTS + 4 * FACE + 4
ROWS = 27 * C
FACE_ROWS = FACE * 64
X_ROWS = FACE_ROWS + 32
Y_ROWS = FACE_ROWS + 48
HALF = ROWS // 2
VMEM_LIMIT = 32 * 1024 * 1024
PACK_LIMIT = 60 * 1024 * 1024
ROOM_BRICKS = 48
ROOM_TABLES = 12 * 1024


def vmem():
    return pl.BlockSpec(memory_space=pltpu.VMEM)


def hbm():
    return pl.BlockSpec(memory_space=pltpu.HBM)


def fetching(*pairs):
    copies = [pltpu.make_async_copy(src, dst, sem) for src, dst, sem in pairs]
    for copy in copies:
        copy.start()
    return copies


def fetched(*pairs):
    for copy in fetching(*pairs):
        copy.wait()


def mask_columns(mask_ref, s):
    m = mask_ref[...].astype(jnp.float32)
    pick = (lax.broadcasted_iota(jnp.int32, (SLOTS, C), 0) == s).astype(jnp.float32)
    return lax.dot_general(m, pick, (((0,), (0,)), ((), ())), preferred_element_type=jnp.float32)


def parity(axis):
    return lax.rem(lax.axis_index(axis), 2)


def side_of(k, odd):
    return 1 - odd if k == 0 else odd


def shifts(cells, same, below, above):
    line = lax.broadcasted_iota(jnp.int32, cells.shape, cells.ndim - 2)
    axis = cells.ndim - 2
    up = jnp.where((same & (line >= 1)) | (below & (line == 0)), pltpu.roll(cells, 1, axis), 0.0)
    down = jnp.where((same & (line <= 6)) | (above & (line == 7)), pltpu.roll(cells, 7, axis), 0.0)
    return up, jnp.where(same, cells, 0.0), down


def pack_kernel(face_hbm, edge_hbm, near_hbm, feat_hbm, grad_hbm, mask_hbm, act_out, grd_out, near_out, *refs):
    y_out, x_out = refs[0:2], refs[2:4]
    face_ref, edge_ref, near, raw, mask_ref, full, sems = refs[4:]
    got_mask, got_feat, got_grad, *tables = fetching(
        (mask_hbm, mask_ref, sems.at[0]),
        (feat_hbm, raw.at[0], sems.at[1]),
        (grad_hbm, raw.at[1], sems.at[2]),
        (face_hbm, face_ref, sems.at[3]),
        (edge_hbm, edge_ref, sems.at[4]),
        (near_hbm, near, sems.at[5]),
        (near_hbm, near_out.at[0], sems.at[6]),
    )
    got_mask.wait()
    results = []
    for f, got in enumerate((got_feat, got_grad)):
        got.wait()
        for s in range(SLOTS):
            masked = raw[f, s].astype(jnp.float32) * mask_columns(mask_ref, s)
            full[f, s] = masked.reshape(8, 8, 8, C)
            raw[f, s] = masked.astype(jnp.bfloat16)
        results += fetching((raw.at[f], (act_out.at[0], grd_out)[f], sems.at[7 + f]))
    for table in tables:
        table.wait()
    for axis, outs in enumerate((x_out, y_out)):
        odd = parity("gy" if axis else "gx")
        for k in range(2):
            side = side_of(k, odd)
            for f in range(2):
                for r in range(FACE):
                    entry = face_ref[r, 2 * axis + side]
                    slot = jnp.clip(entry, 0, SLOTS - 1)
                    layer = full[f, slot, :, 7 * side] if axis else full[f, slot, 7 * side]
                    layer = jnp.where(entry < SLOTS, layer, 0.0)
                    first = f * (Y_ROWS if axis else X_ROWS) + r * 64
                    outs[k][pl.ds(first, 64)] = layer.reshape(64, C).astype(jnp.bfloat16)
            lines = []
            for far in range(2):
                corner = 2 * far + side if axis else 2 * side + far
                entry = edge_ref[0, corner]
                slot = jnp.clip(entry, 0, SLOTS - 1)
                live = entry < SLOTS
                at_x, at_y = (7 * far, 7 * side) if axis else (7 * side, 7 * far)
                if axis == 0:
                    for f in range(2):
                        lines.append(jnp.where(live, full[f, slot, at_x, at_y], 0.0))
                    continue
                base = 18 * far + 6 * side
                low, mid, high = near[slot, base], near[slot, base + 1], near[slot, base + 2]
                up, same, down = shifts(
                    full[1, slot, at_x, at_y],
                    live & (mid < ZERO),
                    live & (high < ZERO),
                    live & (low < ZERO),
                )
                lines += [down, same, up]
            lines = jnp.concatenate(lines, axis=0).astype(jnp.bfloat16)
            outs[k][pl.ds(FACE_ROWS, lines.shape[0])] = lines
    for result in results:
        result.wait()


def pack(features, out_grad, mask, near, face_sends, edge_sends):
    sends = [
        jax.ShapeDtypeStruct((rows + FACE_ROWS, C), jnp.bfloat16) for rows in (Y_ROWS, Y_ROWS, X_ROWS, X_ROWS)
    ]
    return pl.pallas_call(
        pack_kernel,
        out_shape=[
            jax.ShapeDtypeStruct((ROOM_BRICKS, SLOTS, 512, C), jnp.bfloat16),
            jax.ShapeDtypeStruct((SLOTS, 512, C), jnp.bfloat16),
            jax.ShapeDtypeStruct((ROOM_TABLES, SLOTS, 27), jnp.int32),
        ]
        + sends,
        in_specs=[hbm()] * 6,
        out_specs=[hbm()] * 3 + [vmem()] * 4,
        scratch_shapes=[
            pltpu.SMEM((FACE, 4), jnp.int32),
            pltpu.SMEM((1, 4), jnp.int32),
            pltpu.SMEM((SLOTS, 27), jnp.int32),
            pltpu.VMEM((2, SLOTS, 512, C), jnp.bfloat16),
            pltpu.VMEM((SLOTS, 512), jnp.int32),
            pltpu.VMEM((2, SLOTS, 8, 8, 8, C), jnp.float32),
            pltpu.SemaphoreType.DMA((9,)),
        ],
        compiler_params=pltpu.CompilerParams(vmem_limit_bytes=PACK_LIMIT),
        name="pack",
    )(face_sends.T, edge_sends.T, near, features, out_grad, mask)


def parts_of(ref):
    rows = ref.shape[0] // 2
    return ref.at[pl.ds(0, rows)], ref.at[pl.ds(rows, rows)]


def join_kernel(x0, x1, y0, y1, *outs):
    for axis, pair in enumerate(((x0, x1), (y0, y1))):
        rows = (X_ROWS, Y_ROWS)[axis]
        for k, src in enumerate(pair):
            outs[axis][pl.ds(k * rows, rows)] = src[pl.ds(0, rows)]
            outs[2 + axis][pl.ds(k * FACE_ROWS, FACE_ROWS)] = src[pl.ds(rows, FACE_ROWS)]


def join(x0, x1, y0, y1):
    outs = [
        jax.ShapeDtypeStruct((2 * rows, C), jnp.bfloat16) for rows in (X_ROWS, Y_ROWS, FACE_ROWS, FACE_ROWS)
    ]
    return pl.pallas_call(
        join_kernel,
        out_shape=outs,
        in_specs=[vmem()] * 4,
        out_specs=[vmem()] * 4,
        compiler_params=pltpu.CompilerParams(vmem_limit_bytes=VMEM_LIMIT),
        name="join_sides",
    )(x0, x1, y0, y1)


def forward_kernel(x_came, out0, out1):
    odd_x, odd_y = parity("gx"), parity("gy")
    for k, out in enumerate((out0, out1)):
        far = side_of(k, odd_y)
        for j, came in enumerate(parts_of(x_came)):
            source = side_of(j, odd_x)
            rows = came[pl.ds(pl.multiple_of(FACE_ROWS + 16 * far, 16), 16)]
            out[pl.ds(pl.multiple_of(16 * source, 16), 16)] = rows


def forward_corners(x_came):
    send = jax.ShapeDtypeStruct((32, C), jnp.bfloat16)
    return pl.pallas_call(
        forward_kernel,
        out_shape=[send] * 2,
        in_specs=[vmem()],
        out_specs=[vmem()] * 2,
        compiler_params=pltpu.CompilerParams(vmem_limit_bytes=VMEM_LIMIT),
        name="forward_corners",
    )(x_came)


def fill_own(bricks, lx, ly, corners):
    for s in range(SLOTS):
        whole = bricks[s].astype(jnp.float32).reshape(8, 8, 8, C)
        for side, at in ((0, 7), (1, 0)):
            lx[side, s] = whole[at]
            ly[side, s] = whole[:, at]
            for other, far in ((0, 7), (1, 0)):
                corners[2 * side + other, s] = whole[at, far]


def fill_zero(lx, ly, corners, first):
    for ref in (lx, ly, corners):
        count = ref.shape[1] - first
        ref[:, pl.ds(first, count)] = jnp.zeros((ref.shape[0], count) + ref.shape[2:], jnp.float32)


def fill_came(f, x_came, y_came, edges, lx, ly, corners):
    odd_x, odd_y = parity("gx"), parity("gy")
    for came, odd, dst in ((x_came, odd_x, lx), (y_came, odd_y, ly)):
        for k, part in enumerate(parts_of(came)):
            side = side_of(k, odd)
            for r in range(FACE):
                rows = part[pl.ds(r * 64, 64)]
                dst[side, SLOTS + r] = rows.astype(jnp.float32).reshape(8, 8, C)
            dst[k, SLOTS + FACE] = jnp.zeros((8, 8, C), jnp.float32)
    for k, came in enumerate(edges):
        side = side_of(k, odd_y)
        for j in range(2):
            rows = came[pl.ds(16 * j, 16)].astype(jnp.float32)
            corners[2 * j + side, SLOTS + 2 * FACE] = rows[8 * f : 8 * f + 8]
    for sx in range(2):
        for sy in range(2):
            c = 2 * sx + sy
            for r in range(FACE):
                corners[c, SLOTS + r] = lx[sx, SLOTS + r, 0 if sy else 7]
                corners[c, SLOTS + FACE + r] = ly[sy, SLOTS + r, 0 if sx else 7]
            corners[c, SLOTS + 2 * FACE + 1] = jnp.zeros((8, C), jnp.float32)


def build_columns(s, bricks, near, lx, ly, corners, wide, which):
    def spread(cells, at_x, at_y, depth):
        flat = cells.reshape(-1, 8, C)
        for k, moved in enumerate(shifts(flat, depth == 0, depth == -1, depth == 1)):
            wide[k, at_x, at_y] = moved.reshape(cells.shape)

    def column(nx, ny):
        base = 9 * (nx + 1) + 3 * (ny + 1)
        low, mid, high = near[s, base], near[s, base + 1], near[s, base + 2]
        entry = jnp.minimum(jnp.minimum(low, mid), high)
        depth = jnp.where(low < ZERO, -1, jnp.where(high < ZERO, 1, 0))
        if which == "own":
            depth = jnp.where(entry < SLOTS, depth, 2)
        if which == "rim":
            depth = jnp.where((entry >= SLOTS) & (entry < SLOTS + 4 * FACE), depth, 2)
        return entry, depth

    middle = pl.ds(1, 8)
    if which != "rim":
        spread(bricks[s].astype(jnp.float32).reshape(8, 8, 8, C), middle, middle, 0)
    for side, n in ((0, -1), (1, 1)):
        edge_at = pl.ds(0 if n < 0 else 9, 1)
        entry, depth = column(n, 0)
        place = jnp.where(entry < SLOTS, entry, jnp.clip(entry - FACE * side, 0, SLOTS + FACE))
        spread(lx[side, place].reshape(1, 8, 8, C), edge_at, middle, depth)
        entry, depth = column(0, n)
        place = jnp.where(entry < SLOTS, entry, jnp.clip(entry - FACE * (2 + side), 0, SLOTS + FACE))
        spread(ly[side, place].reshape(8, 1, 8, C), middle, edge_at, depth)
    for sx in range(2):
        for sy in range(2):
            entry, depth = column(2 * sx - 1, 2 * sy - 1)
            first_x = SLOTS + FACE * sx
            first_y = SLOTS + FACE * (2 + sy)
            own_edge = SLOTS + 4 * FACE + 2 * sx + sy
            in_x = (entry >= first_x) & (entry < first_x + FACE)
            in_y = (entry >= first_y) & (entry < first_y + FACE)
            place = jnp.where(entry == own_edge, SLOTS + 2 * FACE, SLOTS + 2 * FACE + 1)
            place = jnp.where(in_y, SLOTS + FACE + entry - first_y, place)
            place = jnp.where(in_x, SLOTS + entry - first_x, place)
            place = jnp.where(entry < SLOTS, entry, place)
            spread(corners[2 * sx + sy, place].reshape(1, 1, 8, C), pl.ds(9 * sx, 1), pl.ds(9 * sy, 1), depth)


def stack_columns(s, wide, v):
    for y in range(3):
        for z in range(3):
            cells = wide[z, :, pl.ds(y, 8)].reshape(10, 64, C).astype(jnp.bfloat16)
            v[s, :, :, pl.ds((3 * y + z) * C, C)] = cells


def columns_scratch():
    return [
        pltpu.VMEM((2, SLOTS + FACE + 1, 8, 8, C), jnp.float32),
        pltpu.VMEM((2, SLOTS + FACE + 1, 8, 8, C), jnp.float32),
        pltpu.VMEM((4, SLOTS + 2 * FACE + 2, 8, C), jnp.float32),
        pltpu.VMEM((3, 10, 10, 8, C), jnp.float32),
        pltpu.SMEM((SLOTS, 27), jnp.int32),
        pltpu.SemaphoreType.DMA(()),
    ]


def columns_kernel(near_hbm, act_hbm, v, lx, ly, corners, wide, near, sem, act, act_sem):
    table, bricks = fetching((near_hbm.at[0], near, sem), (act_hbm.at[0], act, act_sem))
    fill_zero(lx, ly, corners, SLOTS)
    bricks.wait()
    fill_own(act, lx, ly, corners)
    table.wait()

    def per_slot(s, carry):
        build_columns(s, act, near, lx, ly, corners, wide, "own")
        stack_columns(s, wide, v)
        return carry

    lax.fori_loop(0, SLOTS, per_slot, 0)


def own_columns(near, act):
    return pl.pallas_call(
        columns_kernel,
        out_shape=jax.ShapeDtypeStruct((SLOTS, 10, 64, 9 * C), jnp.bfloat16),
        in_specs=[hbm()] * 2,
        out_specs=vmem(),
        scratch_shapes=columns_scratch()
        + [pltpu.VMEM((SLOTS, 512, C), jnp.bfloat16), pltpu.SemaphoreType.DMA(())],
        compiler_params=pltpu.CompilerParams(vmem_limit_bytes=VMEM_LIMIT),
        cost_estimate=pl.CostEstimate(flops=1 << 24, bytes_accessed=6 << 20, transcendentals=0),
        name="own_columns",
    )(near, act)


def inner_kernel(v, grd, out, turned):
    for s in range(SLOTS):
        for q in range(4):
            turned[:, pl.ds((4 * s + q) * C, C)] = grd[s, pl.ds(q * C, C)].T
    for x in range(3):
        cells = v[:, pl.ds(x, 8)].reshape(SLOTS * 512, 9 * C)
        out[x] = jnp.dot(turned[...], cells, preferred_element_type=jnp.float32)


def inner_terms(v, grd):
    return pl.pallas_call(
        inner_kernel,
        out_shape=jax.ShapeDtypeStruct((3, C, 9 * C), jnp.float32),
        in_specs=[vmem()] * 2,
        out_specs=vmem(),
        scratch_shapes=[pltpu.VMEM((C, SLOTS * 512), jnp.bfloat16)],
        compiler_params=pltpu.CompilerParams(vmem_limit_bytes=VMEM_LIMIT),
        cost_estimate=pl.CostEstimate(flops=2 * 2048 * ROWS * C, bytes_accessed=6 << 20, transcendentals=0),
        name="inner_terms",
    )(v, grd)


def rim_kernel(near_hbm, inner, grd, x_ref, y_ref, keep, send, lx, ly, corners, wide, near, sem, *refs):
    vx, vy, ends_a, ends_g, side_x, side_y = refs
    (table,) = fetching((near_hbm, near, sem))
    fill_came(0, x_ref, y_ref, (), lx, ly, corners)
    for k, came in enumerate(parts_of(x_ref)):
        side = side_of(k, parity("gx"))
        for j in range(2):
            ends_a[side, j] = came[pl.ds(FACE_ROWS + 16 * j, 16)].astype(jnp.float32)[0:8]
    for k, came in enumerate(parts_of(y_ref)):
        side = side_of(k, parity("gy"))
        ends_g[side] = came[pl.ds(FACE_ROWS, 48)].astype(jnp.float32).reshape(2, 3, 8, C)
    table.wait()
    for s in range(SLOTS):
        build_columns(s, None, near, lx, ly, corners, wide, "rim")
        rows = pl.ds(64 * s, 64)
        for side in range(2):
            for j in range(9):
                cells = wide[j % 3, 9 * side, pl.ds(j // 3, 8)]
                vx[side, rows, pl.ds(j * C, C)] = cells.reshape(64, C).astype(jnp.bfloat16)
        for z in range(3):
            for sx in range(2):
                for sy in range(2):
                    wide[z, 9 * sx, 9 * sy] = jnp.zeros((8, C), jnp.float32)
        for side in range(2):
            for j in range(9):
                cells = wide[j % 3, pl.ds(j // 3, 8), 9 * side]
                vy[side, rows, pl.ds(j * C, C)] = cells.reshape(64, C).astype(jnp.bfloat16)
    grads = grd[...]
    lines = grads.astype(jnp.float32).reshape(SLOTS, 8, 8, 8, C)

    def term(rows, cells):
        return lax.dot_general(rows, cells, (((0,), (0,)), ((), ())), preferred_element_type=jnp.float32)

    def end(line):
        return jnp.concatenate([line, jnp.zeros((8, C), jnp.float32)], axis=0).astype(jnp.bfloat16)

    for side in range(2):
        rows = grads[:, 448 * side : 448 * side + 64].reshape(SLOTS * 64, C)
        side_x[side] = term(rows, vx[side])
        rows = lines[:, :, 7 * side].reshape(SLOTS * 64, C).astype(jnp.bfloat16)
        side_y[side] = term(rows, vy[side])
    def write(halves):
        for x in range(3):
            for y in range(3):
                for z in range(3):
                    first = (9 * x + 3 * y + z) * C
                    value = inner[x, :, pl.ds((3 * y + z) * C, C)]
                    if x != 1:
                        value += side_x[x // 2, :, pl.ds((3 * y + z) * C, C)]
                    if y != 1:
                        value += side_y[y // 2, :, pl.ds((3 * x + z) * C, C)]
                    if x != 1 and y != 1:
                        sx, sy = x // 2, 1 - y // 2
                        value += term(end(ends_g[sy, sx, z]), end(ends_a[sx, sy]))
                    value = value.T
                    for half in range(2):
                        low = max(first, half * HALF)
                        rows = min(first + C, (half + 1) * HALF) - low
                        if rows > 0:
                            halves[half][pl.ds(low - half * HALF, rows)] = value[low - first : low - first + rows]

    core = parity("gy")

    @pl.when(core == 0)
    def _():
        write((keep, send))

    @pl.when(core == 1)
    def _():
        write((send, keep))


def rim_terms(near, inner, grd, x_came, y_came):
    half = jax.ShapeDtypeStruct((HALF, C), jnp.float32)
    side = pltpu.VMEM((2, SLOTS * 64, 9 * C), jnp.bfloat16)
    return pl.pallas_call(
        rim_kernel,
        out_shape=[half, half],
        in_specs=[hbm()] + [vmem()] * 4,
        out_specs=[vmem()] * 2,
        scratch_shapes=columns_scratch()
        + [
            side,
            side,
            pltpu.VMEM((2, 2, 8, C), jnp.float32),
            pltpu.VMEM((2, 2, 3, 8, C), jnp.float32),
            pltpu.VMEM((2, C, 9 * C), jnp.float32),
            pltpu.VMEM((2, C, 9 * C), jnp.float32),
        ],
        compiler_params=pltpu.CompilerParams(vmem_limit_bytes=VMEM_LIMIT),
        cost_estimate=pl.CostEstimate(flops=2 * 256 * 36 * C * C, bytes_accessed=6 << 20, transcendentals=0),
        name="rim_terms",
    )(near, inner, grd, x_came, y_came)


def power_of(values):
    peak = jnp.max(jnp.abs(values))
    return jnp.clip(jnp.ceil(jnp.log2(jnp.full((8, C), peak))), -100.0, 100.0)[0:1]


def merge_kernel(groups, take, keep, came, out, total):
    held = out.shape[1]
    total[pl.ds(0, HALF)] = keep[...] + came[...]
    if groups * take > HALF:
        total[pl.ds(HALF, groups * take - HALF)] = jnp.zeros((groups * take - HALF, C), jnp.float32)
    power = power_of(total[...])
    scale = jnp.exp2(14.0 - power)
    for p in range(groups):
        out[p, pl.ds(0, take)] = total[pl.ds(p * take, take)] * scale
        out[p, pl.ds(take, held - take)] = jnp.broadcast_to(power, (held - take, C))


def merge(groups, take, held, keep, came):
    return pl.pallas_call(
        lambda *refs: merge_kernel(groups, take, *refs),
        out_shape=jax.ShapeDtypeStruct((groups, held, C), jnp.float32),
        in_specs=[vmem()] * 2,
        out_specs=vmem(),
        scratch_shapes=[pltpu.VMEM((groups * take, C), jnp.float32)],
        compiler_params=pltpu.CompilerParams(vmem_limit_bytes=VMEM_LIMIT),
        name="merge",
    )(keep, came)


def sum_kernel(take, blocks, out):
    groups, held, _ = blocks.shape
    total = jnp.zeros((take, C), jnp.float32)
    for p in range(groups):
        total += blocks[p, pl.ds(0, take)] * jnp.exp2(blocks[p, pl.ds(take, 1)] - 14.0)
    power = power_of(total)
    total = total * jnp.exp2(14.0 - power)
    for p in range(groups):
        out[p, pl.ds(0, take)] = total
        out[p, pl.ds(take, held - take)] = jnp.broadcast_to(power, (held - take, C))


def sum_blocks(take, blocks):
    return pl.pallas_call(
        lambda *refs: sum_kernel(take, *refs),
        out_shape=jax.ShapeDtypeStruct(blocks.shape, jnp.float32),
        in_specs=[vmem()],
        out_specs=vmem(),
        compiler_params=pltpu.CompilerParams(vmem_limit_bytes=VMEM_LIMIT),
        name="sum_blocks",
    )(blocks)


def decode_kernel(take, scale, own, blocks, *refs):
    out, half, sems = refs[-3:]
    groups = blocks.shape[0]
    core = parity("gy")
    target = out.at[core if own else 1 - core]
    copies = []
    done = 0
    for p in range(groups):
        rows = min(take, HALF - p * take)
        if rows > 0:
            factor = jnp.exp2(blocks[p, pl.ds(take, 1)] - 14.0) * scale
            half[pl.ds(p * take, rows)] = blocks[p, pl.ds(0, rows)] * factor
        ready = min((p + 1) * take, HALF)
        if ready - done >= HALF // 4 and ready % 8 == 0 or p == groups - 1:
            piece = pl.ds(done, ready - done)
            copies += fetching((half.at[piece], target.at[piece], sems.at[len(copies)]))
            done = ready
    for copy in copies:
        copy.wait()


def decode(take, scale, blocks, begun=None):
    rest = () if begun is None else (begun,)
    return pl.pallas_call(
        lambda *refs: decode_kernel(take, scale, not rest, *refs),
        out_shape=jax.ShapeDtypeStruct((2, HALF, C), jnp.float32),
        in_specs=[vmem()] + [hbm()] * len(rest),
        out_specs=hbm(),
        scratch_shapes=[pltpu.VMEM((HALF, C), jnp.float32), pltpu.SemaphoreType.DMA((5,))],
        input_output_aliases={1: 0} if rest else {},
        compiler_params=pltpu.CompilerParams(vmem_limit_bytes=VMEM_LIMIT),
        name="decode_other" if rest else "decode_own",
    )(blocks, *rest)


def product_kernel(f, near_hbm, mask_ref, kernel_ref, bricks, x_ref, y_ref, e0, e1, out, *refs):
    lx, ly, corners, wide, near, sem, v, *more = refs
    (table,) = fetching((near_hbm, near, sem))
    weights = kernel_ref
    if f == 0:
        fetched((bricks.at[0], more[0], more[1]))
        bricks = more[0]
    else:
        weights = more[0]
        for o in range(27):
            weights[pl.ds((26 - o) * C, C)] = kernel_ref[pl.ds(o * C, C)].T
    fill_own(bricks, lx, ly, corners)
    fill_came(f, x_ref, y_ref, (e0, e1), lx, ly, corners)
    table.wait()

    def per_slot(s, carry):
        build_columns(s, bricks, near, lx, ly, corners, wide, "all")
        stack_columns(s, wide, v)
        total = jnp.zeros((512, C), jnp.float32)
        for x in range(3):
            cells = v[s, pl.ds(x, 8)].reshape(512, 9 * C)
            total += jnp.dot(cells, weights[pl.ds(x * 9 * C, 9 * C)], preferred_element_type=jnp.float32)
        out[s] = (total * mask_columns(mask_ref, s)).astype(jnp.bfloat16)
        return carry

    lax.fori_loop(0, SLOTS, per_slot, 0)


def product(f, near, mask, kernel, bricks, x_came, y_came, edges):
    return pl.pallas_call(
        lambda *refs: product_kernel(f, *refs),
        out_shape=jax.ShapeDtypeStruct((SLOTS, 512, C), jnp.bfloat16),
        in_specs=[hbm()] + [vmem()] * 2 + [vmem() if f else hbm()] + [vmem()] * 4,
        out_specs=vmem(),
        scratch_shapes=columns_scratch()
        + [pltpu.VMEM((SLOTS, 10, 64, 9 * C), jnp.bfloat16)]
        + (
            [pltpu.VMEM((ROWS, C), jnp.bfloat16)]
            if f
            else [pltpu.VMEM((SLOTS, 512, C), jnp.bfloat16), pltpu.SemaphoreType.DMA(())]
        ),
        compiler_params=pltpu.CompilerParams(vmem_limit_bytes=VMEM_LIMIT),
        cost_estimate=pl.CostEstimate(flops=2 * 2048 * ROWS * C, bytes_accessed=4 << 20, transcendentals=0),
        name=("output_product", "input_grad_product")[f],
    )(near, mask, kernel, bricks, x_came, y_came, *edges)


def swapped(value, axis, k):
    pairs = []
    for low in range(k, lax.axis_size(axis) - 1, 2):
        pairs += [(low, low + 1), (low + 1, low)]
    return lax.ppermute(value, axis, pairs)


def hopped(value, axis):
    size = lax.axis_size(axis)
    pairs = [(i, i + 2) for i in range(1, size - 2, 2)] + [(i, i - 2) for i in range(2, size, 2)]
    return lax.ppermute(value, axis, pairs)


def local(features, out_grad, kernel, voxel_mask, neighbours, face_sends, edge_sends):
    size_x, size_y = lax.axis_size("gx"), lax.axis_size("gy")
    parts = size_x * size_y
    groups = parts // 2
    take = -(-HALF // groups)
    held = -(-(take + 1) // 16) * 16
    order = [(i + parts // 2) % parts for i in range(parts)]
    same_core = [[i for i in order if i % size_y % 2 == core] for core in range(2)]

    def spread(blocks):
        return lax.all_to_all(blocks, ("gx", "gy"), 0, 0, axis_index_groups=same_core, tiled=True)

    act, grd, table, y0, y1, x0, x1 = pack(
        features.reshape(SLOTS, 512, C),
        out_grad.reshape(SLOTS, 512, C),
        voxel_mask,
        neighbours,
        face_sends,
        edge_sends,
    )
    x1, y1 = hopped(x1, "gx"), hopped(y1, "gy")
    v = own_columns(table, act)
    x1, y1, v = lax.optimization_barrier((x1, y1, v))
    x_came, y_came, x_more, y_more = join(x0, x1, y0, y1)
    x_came, y_came = swapped(x_came, "gx", 0), swapped(y_came, "gy", 0)
    inner = inner_terms(v, grd)
    keep, send = rim_terms(neighbours, inner, grd, x_came, y_came)
    blocks = merge(groups, take, held, keep, swapped(send, "gy", 0)).astype(jnp.float16)
    rows = kernel.reshape(ROWS, C)
    blocks, act, x_came, x_more, y_more = lax.optimization_barrier((blocks, act, x_came, x_more, y_more))
    x_more, y_more = swapped(x_more, "gx", 0), swapped(y_more, "gy", 0)
    e0, e1 = forward_corners(x_came)
    edges = [swapped(e0, "gy", 0), swapped(e1, "gy", 1)]
    output = product(0, neighbours, voxel_mask, rows, act, x_came, y_came, edges)
    arrived, output, x_more, y_more = lax.optimization_barrier((spread(blocks), output, x_more, y_more))
    copies = sum_blocks(take, arrived.astype(jnp.float32)).astype(jnp.float16)
    copies, grd = lax.optimization_barrier((copies, grd))
    input_grad = product(1, neighbours, voxel_mask, rows, grd, x_more, y_more, edges)
    mine, input_grad = lax.optimization_barrier((spread(copies), input_grad))
    other = swapped(mine, "gy", 0)
    scale = 1.0 / math.sqrt(parts * SLOTS * 512)
    weight = decode(take, scale, mine.astype(jnp.float32))
    weight = decode(take, scale, other.astype(jnp.float32), weight)
    shape = (SLOTS, 8, 8, 8, C)
    return output.reshape(shape), input_grad.reshape(shape), weight.reshape(27, C, C)


def solution(mesh):
    spec = P(("gx", "gy"))
    return jax.shard_map(
        local,
        mesh=mesh,
        in_specs=(spec, spec, P(), spec, spec, spec, spec),
        out_specs=(spec, spec, P()),
        check_vma=False,
    )
```

```python
import math

import jax
import jax.numpy as jnp
from jax import lax
from jax.experimental import pallas as pl
from jax.experimental.pallas import tpu as pltpu
from jax.sharding import PartitionSpec as P

FACES = ((-1, 0), (1, 0), (0, -1), (0, 1))
EDGES = ((-1, -1), (-1, 1), (1, -1), (1, 1))
C = 128
SLOTS = 4
FACE = 2
ZERO = SLOTS + 4 * FACE + 4
ROWS = 27 * C
FACE_ROWS = FACE * 64
X_ROWS = FACE_ROWS + 32
Y_ROWS = FACE_ROWS + 48
HALF = ROWS // 2
SPARE_ROWS = 32
VMEM_LIMIT = 32 * 1024 * 1024
PACK_LIMIT = 60 * 1024 * 1024
ROOM_BRICKS = 48
ROOM_TABLES = 12 * 1024


def vmem():
    return pl.BlockSpec(memory_space=pltpu.VMEM)


def hbm():
    return pl.BlockSpec(memory_space=pltpu.HBM)


def fetching(*pairs):
    copies = [pltpu.make_async_copy(src, dst, sem) for src, dst, sem in pairs]
    for copy in copies:
        copy.start()
    return copies


def fetched(*pairs):
    for copy in fetching(*pairs):
        copy.wait()


def mask_columns(mask_ref, s):
    m = mask_ref[...].astype(jnp.float32).astype(jnp.bfloat16)
    pick = (lax.broadcasted_iota(jnp.int32, (SLOTS, C), 0) == s).astype(jnp.float32).astype(jnp.bfloat16)
    return lax.dot_general(m, pick, (((0,), (0,)), ((), ())), preferred_element_type=jnp.float32)


def parity(axis):
    return lax.rem(lax.axis_index(axis), 2)


def side_of(k, odd):
    return 1 - odd if k == 0 else odd


def shifts(cells, same, below, above):
    line = lax.broadcasted_iota(jnp.int32, cells.shape, cells.ndim - 2)
    axis = cells.ndim - 2
    up = jnp.where((same & (line >= 1)) | (below & (line == 0)), pltpu.roll(cells, 1, axis), 0.0)
    down = jnp.where((same & (line <= 6)) | (above & (line == 7)), pltpu.roll(cells, 7, axis), 0.0)
    return up, jnp.where(same, cells, 0.0), down


def pack_kernel(face_hbm, edge_hbm, near_hbm, feat_hbm, grad_hbm, mask_hbm, held_out, act_out, grd_out, near_out, *refs):
    y_out, x_out = refs[0:2], refs[2:4]
    face_ref, edge_ref, near, raw, mask_ref, full, sems = refs[4:]
    got_mask, got_feat, got_grad, *tables = fetching(
        (mask_hbm, mask_ref, sems.at[0]),
        (feat_hbm, raw.at[0], sems.at[1]),
        (grad_hbm, raw.at[1], sems.at[2]),
        (face_hbm, face_ref, sems.at[3]),
        (edge_hbm, edge_ref, sems.at[4]),
        (near_hbm, near, sems.at[5]),
        (near_hbm, near_out.at[0], sems.at[6]),
    )
    got_mask.wait()
    got_feat.wait()
    got_grad.wait()
    for s in range(SLOTS):
        rows = mask_columns(mask_ref, s)
        for f in range(2):
            masked = raw[f, s].astype(jnp.float32) * rows
            full[f, s] = masked.reshape(8, 8, 8, C)
            raw[f, s] = masked.astype(jnp.bfloat16)
    results = fetching(
        (raw.at[0], held_out.at[0], sems.at[7]),
        (raw.at[0], act_out, sems.at[8]),
        (raw.at[1], grd_out, sems.at[9]),
    )
    for table in tables:
        table.wait()
    for axis, outs in enumerate((x_out, y_out)):
        odd = parity("gy" if axis else "gx")
        for k in range(2):
            side = side_of(k, odd)
            for f in range(2):
                for r in range(FACE):
                    entry = face_ref[r, 2 * axis + side]
                    slot = jnp.clip(entry, 0, SLOTS - 1)
                    layer = full[f, slot, :, 7 * side] if axis else full[f, slot, 7 * side]
                    layer = jnp.where(entry < SLOTS, layer, 0.0)
                    first = f * (Y_ROWS if axis else X_ROWS) + r * 64
                    outs[k][pl.ds(first, 64)] = layer.reshape(64, C).astype(jnp.bfloat16)
            lines = []
            for far in range(2):
                corner = 2 * far + side if axis else 2 * side + far
                entry = edge_ref[0, corner]
                slot = jnp.clip(entry, 0, SLOTS - 1)
                live = entry < SLOTS
                at_x, at_y = (7 * far, 7 * side) if axis else (7 * side, 7 * far)
                if axis == 0:
                    for f in range(2):
                        lines.append(jnp.where(live, full[f, slot, at_x, at_y], 0.0))
                    continue
                base = 18 * far + 6 * side
                low, mid, high = near[slot, base], near[slot, base + 1], near[slot, base + 2]
                up, same, down = shifts(
                    full[1, slot, at_x, at_y],
                    live & (mid < ZERO),
                    live & (high < ZERO),
                    live & (low < ZERO),
                )
                lines += [down, same, up]
            lines = jnp.concatenate(lines, axis=0).astype(jnp.bfloat16)
            outs[k][pl.ds(FACE_ROWS, lines.shape[0])] = lines
    x_out[1][pl.ds(X_ROWS + FACE_ROWS, SPARE_ROWS)] = jnp.zeros((SPARE_ROWS, C), jnp.bfloat16)
    for result in results:
        result.wait()


def pack(features, out_grad, mask, near, face_sends, edge_sends):
    sends = [
        jax.ShapeDtypeStruct((rows + FACE_ROWS, C), jnp.bfloat16)
        for rows in (Y_ROWS, Y_ROWS, X_ROWS, X_ROWS + SPARE_ROWS)
    ]
    return pl.pallas_call(
        pack_kernel,
        out_shape=[
            jax.ShapeDtypeStruct((ROOM_BRICKS, SLOTS, 512, C), jnp.bfloat16),
            jax.ShapeDtypeStruct((SLOTS, 512, C), jnp.bfloat16),
            jax.ShapeDtypeStruct((SLOTS, 512, C), jnp.bfloat16),
            jax.ShapeDtypeStruct((ROOM_TABLES, SLOTS, 27), jnp.int32),
        ]
        + sends,
        in_specs=[hbm()] * 6,
        out_specs=[hbm()] * 4 + [vmem()] * 4,
        scratch_shapes=[
            pltpu.SMEM((FACE, 4), jnp.int32),
            pltpu.SMEM((1, 4), jnp.int32),
            pltpu.SMEM((SLOTS, 27), jnp.int32),
            pltpu.VMEM((2, SLOTS, 512, C), jnp.bfloat16),
            pltpu.VMEM((SLOTS, 512), jnp.int32),
            pltpu.VMEM((2, SLOTS, 8, 8, 8, C), jnp.float32),
            pltpu.SemaphoreType.DMA((10,)),
        ],
        compiler_params=pltpu.CompilerParams(vmem_limit_bytes=PACK_LIMIT),
        name="pack",
    )(face_sends.T, edge_sends.T, near, features, out_grad, mask)


def parts_of(ref):
    rows = ref.shape[0] // 2
    return ref.at[pl.ds(0, rows)], ref.at[pl.ds(rows, rows)]


def join_kernel(first, second, out, more):
    rows = first.shape[0] - FACE_ROWS
    for k, src in enumerate((first, second)):
        out[pl.ds(k * rows, rows)] = src[pl.ds(0, rows)]
        more[pl.ds(k * FACE_ROWS, FACE_ROWS)] = src[pl.ds(rows, FACE_ROWS)]


def join(first, second):
    outs = [
        jax.ShapeDtypeStruct((2 * rows, C), jnp.bfloat16) for rows in (first.shape[0] - FACE_ROWS, FACE_ROWS)
    ]
    return pl.pallas_call(
        join_kernel,
        out_shape=outs,
        in_specs=[vmem()] * 2,
        out_specs=[vmem()] * 2,
        compiler_params=pltpu.CompilerParams(vmem_limit_bytes=VMEM_LIMIT),
        name="join_sides",
    )(first, second)


def forward_kernel(x_came, out0, out1):
    odd_x, odd_y = parity("gx"), parity("gy")
    for k, out in enumerate((out0, out1)):
        far = side_of(k, odd_y)
        for j, came in enumerate(parts_of(x_came)):
            source = side_of(j, odd_x)
            rows = came[pl.ds(pl.multiple_of(FACE_ROWS + 16 * far, 16), 16)]
            out[pl.ds(pl.multiple_of(16 * source, 16), 16)] = rows


def forward_corners(x_came):
    send = jax.ShapeDtypeStruct((32, C), jnp.bfloat16)
    return pl.pallas_call(
        forward_kernel,
        out_shape=[send] * 2,
        in_specs=[vmem()],
        out_specs=[vmem()] * 2,
        compiler_params=pltpu.CompilerParams(vmem_limit_bytes=VMEM_LIMIT),
        name="forward_corners",
    )(x_came)


def fill_own(bricks, lx, ly, corners):
    for s in range(SLOTS):
        whole = bricks[s].astype(jnp.float32).reshape(8, 8, 8, C)
        for side, at in ((0, 7), (1, 0)):
            lx[side, s] = whole[at]
            ly[side, s] = whole[:, at]
            for other, far in ((0, 7), (1, 0)):
                corners[2 * side + other, s] = whole[at, far]


def fill_zero(lx, ly, corners, first):
    for ref in (lx, ly, corners):
        count = ref.shape[1] - first
        ref[:, pl.ds(first, count)] = jnp.zeros((ref.shape[0], count) + ref.shape[2:], jnp.float32)


def fill_came(f, x_came, y_came, edges, lx, ly, corners):
    odd_x, odd_y = parity("gx"), parity("gy")
    for came, odd, dst in ((x_came, odd_x, lx), (y_came, odd_y, ly)):
        for k, part in enumerate(parts_of(came)):
            side = side_of(k, odd)
            for r in range(FACE):
                rows = part[pl.ds(r * 64, 64)]
                dst[side, SLOTS + r] = rows.astype(jnp.float32).reshape(8, 8, C)
            dst[k, SLOTS + FACE] = jnp.zeros((8, 8, C), jnp.float32)
    for k, came in enumerate(edges):
        side = side_of(k, odd_y)
        for j in range(2):
            rows = came[pl.ds(16 * j, 16)].astype(jnp.float32)
            corners[2 * j + side, SLOTS + 2 * FACE] = rows[8 * f : 8 * f + 8]
    for sx in range(2):
        for sy in range(2):
            c = 2 * sx + sy
            for r in range(FACE):
                corners[c, SLOTS + r] = lx[sx, SLOTS + r, 0 if sy else 7]
                corners[c, SLOTS + FACE + r] = ly[sy, SLOTS + r, 0 if sx else 7]
            corners[c, SLOTS + 2 * FACE + 1] = jnp.zeros((8, C), jnp.float32)


def build_columns(s, bricks, near, lx, ly, corners, wide, which):
    def spread(cells, at_x, at_y, depth):
        flat = cells.reshape(-1, 8, C)
        for k, moved in enumerate(shifts(flat, depth == 0, depth == -1, depth == 1)):
            wide[k, at_x, at_y] = moved.reshape(cells.shape)

    def column(nx, ny):
        base = 9 * (nx + 1) + 3 * (ny + 1)
        low, mid, high = near[s, base], near[s, base + 1], near[s, base + 2]
        entry = jnp.minimum(jnp.minimum(low, mid), high)
        depth = jnp.where(low < ZERO, -1, jnp.where(high < ZERO, 1, 0))
        if which == "own":
            depth = jnp.where(entry < SLOTS, depth, 2)
        if which == "rim":
            depth = jnp.where((entry >= SLOTS) & (entry < SLOTS + 4 * FACE), depth, 2)
        return entry, depth

    middle = pl.ds(1, 8)
    if which != "rim":
        spread(bricks[s].astype(jnp.float32).reshape(8, 8, 8, C), middle, middle, 0)
    for side, n in ((0, -1), (1, 1)):
        edge_at = pl.ds(0 if n < 0 else 9, 1)
        entry, depth = column(n, 0)
        place = jnp.where(entry < SLOTS, entry, jnp.clip(entry - FACE * side, 0, SLOTS + FACE))
        spread(lx[side, place].reshape(1, 8, 8, C), edge_at, middle, depth)
        entry, depth = column(0, n)
        place = jnp.where(entry < SLOTS, entry, jnp.clip(entry - FACE * (2 + side), 0, SLOTS + FACE))
        spread(ly[side, place].reshape(8, 1, 8, C), middle, edge_at, depth)
    for sx in range(2):
        for sy in range(2):
            entry, depth = column(2 * sx - 1, 2 * sy - 1)
            first_x = SLOTS + FACE * sx
            first_y = SLOTS + FACE * (2 + sy)
            own_edge = SLOTS + 4 * FACE + 2 * sx + sy
            in_x = (entry >= first_x) & (entry < first_x + FACE)
            in_y = (entry >= first_y) & (entry < first_y + FACE)
            place = jnp.where(entry == own_edge, SLOTS + 2 * FACE, SLOTS + 2 * FACE + 1)
            place = jnp.where(in_y, SLOTS + FACE + entry - first_y, place)
            place = jnp.where(in_x, SLOTS + entry - first_x, place)
            place = jnp.where(entry < SLOTS, entry, place)
            spread(corners[2 * sx + sy, place].reshape(1, 1, 8, C), pl.ds(9 * sx, 1), pl.ds(9 * sy, 1), depth)


def stack_columns(s, wide, v):
    for y in range(3):
        for z in range(3):
            cells = wide[z, :, pl.ds(y, 8)].reshape(10, 64, C).astype(jnp.bfloat16)
            v[s, :, :, pl.ds((3 * y + z) * C, C)] = cells


def columns_scratch():
    return [
        pltpu.VMEM((2, SLOTS + FACE + 1, 8, 8, C), jnp.float32),
        pltpu.VMEM((2, SLOTS + FACE + 1, 8, 8, C), jnp.float32),
        pltpu.VMEM((4, SLOTS + 2 * FACE + 2, 8, C), jnp.float32),
        pltpu.VMEM((3, 10, 10, 8, C), jnp.float32),
        pltpu.SMEM((SLOTS, 27), jnp.int32),
        pltpu.SemaphoreType.DMA(()),
    ]


def columns_kernel(near_hbm, act_hbm, v, lx, ly, corners, wide, near, sem, act, act_sem):
    table, bricks = fetching((near_hbm.at[0], near, sem), (act_hbm.at[0], act, act_sem))
    fill_zero(lx, ly, corners, SLOTS)
    bricks.wait()
    fill_own(act, lx, ly, corners)
    table.wait()

    def per_slot(s, carry):
        build_columns(s, act, near, lx, ly, corners, wide, "own")
        stack_columns(s, wide, v)
        return carry

    lax.fori_loop(0, SLOTS, per_slot, 0)


def own_columns(near, act):
    return pl.pallas_call(
        columns_kernel,
        out_shape=jax.ShapeDtypeStruct((SLOTS, 10, 64, 9 * C), jnp.bfloat16),
        in_specs=[hbm()] * 2,
        out_specs=vmem(),
        scratch_shapes=columns_scratch()
        + [pltpu.VMEM((SLOTS, 512, C), jnp.bfloat16), pltpu.SemaphoreType.DMA(())],
        compiler_params=pltpu.CompilerParams(vmem_limit_bytes=VMEM_LIMIT),
        cost_estimate=pl.CostEstimate(flops=1 << 24, bytes_accessed=6 << 20, transcendentals=0),
        name="own_columns",
    )(near, act)


def inner_kernel(v, grd, out, turned):
    for s in range(SLOTS):
        for q in range(4):
            turned[:, pl.ds((4 * s + q) * C, C)] = grd[s, pl.ds(q * C, C)].T
    for x in range(3):
        cells = v[:, pl.ds(x, 8)].reshape(SLOTS * 512, 9 * C)
        terms = jnp.dot(turned[...], cells, preferred_element_type=jnp.float32)
        for j in range(9):
            out[pl.ds((9 * x + j) * C, C)] = terms[:, j * C : (j + 1) * C].T


def inner_terms(v, grd):
    return pl.pallas_call(
        inner_kernel,
        out_shape=jax.ShapeDtypeStruct((ROWS, C), jnp.float32),
        in_specs=[vmem()] * 2,
        out_specs=vmem(),
        scratch_shapes=[pltpu.VMEM((C, SLOTS * 512), jnp.bfloat16)],
        compiler_params=pltpu.CompilerParams(vmem_limit_bytes=VMEM_LIMIT),
        cost_estimate=pl.CostEstimate(flops=2 * 2048 * ROWS * C, bytes_accessed=6 << 20, transcendentals=0),
        name="inner_terms",
    )(v, grd)


def rim_kernel(near_hbm, inner, grd, x_ref, y_ref, keep, send, lx, ly, corners, wide, near, sem, *refs):
    vx, vy, ends_a, ends_g, side_x, side_y = refs
    (table,) = fetching((near_hbm, near, sem))
    fill_came(0, x_ref, y_ref, (), lx, ly, corners)
    for k, came in enumerate(parts_of(x_ref)):
        side = side_of(k, parity("gx"))
        for j in range(2):
            ends_a[side, j] = came[pl.ds(FACE_ROWS + 16 * j, 16)].astype(jnp.float32)[0:8]
    for k, came in enumerate(parts_of(y_ref)):
        side = side_of(k, parity("gy"))
        ends_g[side] = came[pl.ds(FACE_ROWS, 48)].astype(jnp.float32).reshape(2, 3, 8, C)
    table.wait()
    for s in range(SLOTS):
        build_columns(s, None, near, lx, ly, corners, wide, "rim")
        rows = pl.ds(64 * s, 64)
        for side in range(2):
            for j in range(9):
                cells = wide[j % 3, 9 * side, pl.ds(j // 3, 8)]
                vx[side, rows, pl.ds(j * C, C)] = cells.reshape(64, C).astype(jnp.bfloat16)
        for z in range(3):
            for sx in range(2):
                for sy in range(2):
                    wide[z, 9 * sx, 9 * sy] = jnp.zeros((8, C), jnp.float32)
        for side in range(2):
            for j in range(9):
                cells = wide[j % 3, pl.ds(j // 3, 8), 9 * side]
                vy[side, rows, pl.ds(j * C, C)] = cells.reshape(64, C).astype(jnp.bfloat16)
    grads = grd[...]
    lines = grads.astype(jnp.float32).reshape(SLOTS, 8, 8, 8, C)

    def term(cells, rows):
        return lax.dot_general(cells, rows, (((0,), (0,)), ((), ())), preferred_element_type=jnp.float32)

    def end(line):
        return jnp.concatenate([line, jnp.zeros((8, C), jnp.float32)], axis=0).astype(jnp.bfloat16)

    for side in range(2):
        rows = grads[:, 448 * side : 448 * side + 64].reshape(SLOTS * 64, C)
        side_x[side] = term(vx[side], rows)
        rows = lines[:, :, 7 * side].reshape(SLOTS * 64, C).astype(jnp.bfloat16)
        side_y[side] = term(vy[side], rows)
    def write(halves):
        for x in range(3):
            for y in range(3):
                for z in range(3):
                    first = (9 * x + 3 * y + z) * C
                    value = inner[pl.ds(first, C)]
                    if x != 1:
                        value += side_x[x // 2, pl.ds((3 * y + z) * C, C)]
                    if y != 1:
                        value += side_y[y // 2, pl.ds((3 * x + z) * C, C)]
                    if x != 1 and y != 1:
                        sx, sy = x // 2, 1 - y // 2
                        value += term(end(ends_a[sx, sy]), end(ends_g[sy, sx, z]))
                    for half in range(2):
                        low = max(first, half * HALF)
                        rows = min(first + C, (half + 1) * HALF) - low
                        if rows > 0:
                            halves[half][pl.ds(low - half * HALF, rows)] = value[low - first : low - first + rows]

    core = parity("gy")

    @pl.when(core == 0)
    def _():
        write((keep, send))

    @pl.when(core == 1)
    def _():
        write((send, keep))


def rim_terms(near, inner, grd, x_came, y_came):
    half = jax.ShapeDtypeStruct((HALF, C), jnp.float32)
    side = pltpu.VMEM((2, SLOTS * 64, 9 * C), jnp.bfloat16)
    return pl.pallas_call(
        rim_kernel,
        out_shape=[half, half],
        in_specs=[hbm()] + [vmem()] * 4,
        out_specs=[vmem()] * 2,
        scratch_shapes=columns_scratch()
        + [
            side,
            side,
            pltpu.VMEM((2, 2, 8, C), jnp.float32),
            pltpu.VMEM((2, 2, 3, 8, C), jnp.float32),
            pltpu.VMEM((2, 9 * C, C), jnp.float32),
            pltpu.VMEM((2, 9 * C, C), jnp.float32),
        ],
        compiler_params=pltpu.CompilerParams(vmem_limit_bytes=VMEM_LIMIT),
        cost_estimate=pl.CostEstimate(flops=2 * 256 * 36 * C * C, bytes_accessed=6 << 20, transcendentals=0),
        name="rim_terms",
    )(near, inner, grd, x_came, y_came)


def power_of(values):
    peak = jnp.max(jnp.abs(values))
    return jnp.clip(jnp.ceil(jnp.log2(jnp.full((8, C), peak))), -100.0, 100.0)[0:1]


def merge_kernel(groups, take, keep, came, out, total):
    held = out.shape[1]
    total[pl.ds(0, HALF)] = keep[...] + came[...]
    if groups * take > HALF:
        total[pl.ds(HALF, groups * take - HALF)] = jnp.zeros((groups * take - HALF, C), jnp.float32)
    power = power_of(total[...])
    scale = jnp.exp2(14.0 - power)
    for p in range(groups):
        out[p, pl.ds(0, take)] = total[pl.ds(p * take, take)] * scale
        out[p, pl.ds(take, held - take)] = jnp.broadcast_to(power, (held - take, C))


def merge(groups, take, held, keep, came):
    return pl.pallas_call(
        lambda *refs: merge_kernel(groups, take, *refs),
        out_shape=jax.ShapeDtypeStruct((groups, held, C), jnp.float32),
        in_specs=[vmem()] * 2,
        out_specs=vmem(),
        scratch_shapes=[pltpu.VMEM((groups * take, C), jnp.float32)],
        compiler_params=pltpu.CompilerParams(vmem_limit_bytes=VMEM_LIMIT),
        name="merge",
    )(keep, came)


def sum_kernel(take, blocks, out):
    groups, held, _ = blocks.shape
    total = jnp.zeros((take, C), jnp.float32)
    for p in range(groups):
        total += blocks[p, pl.ds(0, take)] * jnp.exp2(blocks[p, pl.ds(take, 1)] - 14.0)
    power = power_of(total)
    total = total * jnp.exp2(14.0 - power)
    for p in range(groups):
        out[p, pl.ds(0, take)] = total
        out[p, pl.ds(take, held - take)] = jnp.broadcast_to(power, (held - take, C))


def sum_blocks(take, blocks):
    return pl.pallas_call(
        lambda *refs: sum_kernel(take, *refs),
        out_shape=jax.ShapeDtypeStruct(blocks.shape, jnp.float32),
        in_specs=[vmem()],
        out_specs=vmem(),
        compiler_params=pltpu.CompilerParams(vmem_limit_bytes=VMEM_LIMIT),
        name="sum_blocks",
    )(blocks)


def decode_kernel(take, scale, own, blocks, *refs):
    out, half, sems = refs[-3:]
    groups = blocks.shape[0]
    core = parity("gy")
    target = out.at[core if own else 1 - core]
    copies = []
    done = 0
    for p in range(groups):
        rows = min(take, HALF - p * take)
        if rows > 0:
            factor = jnp.exp2(blocks[p, pl.ds(take, 1)] - 14.0) * scale
            half[pl.ds(p * take, rows)] = blocks[p, pl.ds(0, rows)] * factor
        ready = min((p + 1) * take, HALF)
        if ready - done >= HALF // 4 and ready % 8 == 0 or p == groups - 1:
            piece = pl.ds(done, ready - done)
            copies += fetching((half.at[piece], target.at[piece], sems.at[len(copies)]))
            done = ready
    for copy in copies:
        copy.wait()


def decode(take, scale, blocks, begun=None):
    rest = () if begun is None else (begun,)
    return pl.pallas_call(
        lambda *refs: decode_kernel(take, scale, not rest, *refs),
        out_shape=jax.ShapeDtypeStruct((2, HALF, C), jnp.float32),
        in_specs=[vmem()] + [hbm()] * len(rest),
        out_specs=hbm(),
        scratch_shapes=[pltpu.VMEM((HALF, C), jnp.float32), pltpu.SemaphoreType.DMA((5,))],
        input_output_aliases={1: 0} if rest else {},
        compiler_params=pltpu.CompilerParams(vmem_limit_bytes=VMEM_LIMIT),
        name="decode_other" if rest else "decode_own",
    )(blocks, *rest)


def product_kernel(f, near_hbm, mask_ref, kernel_ref, bricks, x_ref, y_ref, e0, e1, out, *refs):
    lx, ly, corners, wide, near, sem, v, *flipped = refs
    (table,) = fetching((near_hbm, near, sem))
    weights = kernel_ref
    if f == 1:
        weights = flipped[0]
        for o in range(27):
            weights[pl.ds((26 - o) * C, C)] = kernel_ref[pl.ds(o * C, C)].T
    fill_own(bricks, lx, ly, corners)
    fill_came(f, x_ref, y_ref, (e0, e1), lx, ly, corners)
    table.wait()

    def per_slot(s, carry):
        build_columns(s, bricks, near, lx, ly, corners, wide, "all")
        stack_columns(s, wide, v)
        total = jnp.zeros((512, C), jnp.float32)
        for x in range(3):
            cells = v[s, pl.ds(x, 8)].reshape(512, 9 * C)
            total += jnp.dot(cells, weights[pl.ds(x * 9 * C, 9 * C)], preferred_element_type=jnp.float32)
        out[s] = (total * mask_columns(mask_ref, s)).astype(jnp.bfloat16)
        return carry

    lax.fori_loop(0, SLOTS, per_slot, 0)


def product(f, near, mask, kernel, bricks, x_came, y_came, edges):
    return pl.pallas_call(
        lambda *refs: product_kernel(f, *refs),
        out_shape=jax.ShapeDtypeStruct((SLOTS, 512, C), jnp.bfloat16),
        in_specs=[hbm()] + [vmem()] * 7,
        out_specs=vmem(),
        scratch_shapes=columns_scratch()
        + [pltpu.VMEM((SLOTS, 10, 64, 9 * C), jnp.bfloat16)]
        + ([pltpu.VMEM((ROWS, C), jnp.bfloat16)] if f else []),
        compiler_params=pltpu.CompilerParams(vmem_limit_bytes=VMEM_LIMIT),
        cost_estimate=pl.CostEstimate(flops=2 * 2048 * ROWS * C, bytes_accessed=4 << 20, transcendentals=0),
        name=("output_product", "input_grad_product")[f],
    )(near, mask, kernel, bricks, x_came, y_came, *edges)


def swapped(value, axis, k):
    pairs = []
    for low in range(k, lax.axis_size(axis) - 1, 2):
        pairs += [(low, low + 1), (low + 1, low)]
    return lax.ppermute(value, axis, pairs)


def hopped(value, axis):
    size = lax.axis_size(axis)
    pairs = [(i, i + 2) for i in range(1, size - 2, 2)] + [(i, i - 2) for i in range(2, size, 2)]
    return lax.ppermute(value, axis, pairs)


def local(features, out_grad, kernel, voxel_mask, neighbours, face_sends, edge_sends):
    size_x, size_y = lax.axis_size("gx"), lax.axis_size("gy")
    parts = size_x * size_y
    groups = parts // 2
    take = -(-HALF // groups)
    held = -(-(take + 1) // 16) * 16
    order = [(i + parts // 2) % parts for i in range(parts)]
    same_core = [[i for i in order if i % size_y % 2 == core] for core in range(2)]

    def spread(blocks):
        return lax.all_to_all(blocks, ("gx", "gy"), 0, 0, axis_index_groups=same_core, tiled=True)

    held_act, act, grd, table, y0, y1, x0, x1 = pack(
        features.reshape(SLOTS, 512, C),
        out_grad.reshape(SLOTS, 512, C),
        voxel_mask,
        neighbours,
        face_sends,
        edge_sends,
    )
    y1 = hopped(y1, "gy")
    x1 = hopped(x1, "gx")
    v = own_columns(table, held_act)
    x1, v = lax.optimization_barrier((x1, v))
    x_came, x_more = join(x0, x1)
    x_more, y1 = lax.optimization_barrier((x_more, y1))
    x_came = swapped(x_came, "gx", 0)
    y_came, y_more = join(y0, y1)
    y_came = swapped(y_came, "gy", 0)
    inner = inner_terms(v, grd)
    keep, send = rim_terms(neighbours, inner, grd, x_came, y_came)
    blocks = merge(groups, take, held, keep, swapped(send, "gy", 0)).astype(jnp.float16)
    rows = kernel.reshape(ROWS, C)
    blocks, act, x_came, x_more, y_more = lax.optimization_barrier((blocks, act, x_came, x_more, y_more))
    x_more, y_more = swapped(x_more, "gx", 0), swapped(y_more, "gy", 0)
    e0, e1 = forward_corners(x_came)
    edges = [swapped(e0, "gy", 0), swapped(e1, "gy", 1)]
    output = product(0, neighbours, voxel_mask, rows, act, x_came, y_came, edges)
    arrived, output, x_more, y_more = lax.optimization_barrier((spread(blocks), output, x_more, y_more))
    copies = sum_blocks(take, arrived.astype(jnp.float32)).astype(jnp.float16)
    copies, grd = lax.optimization_barrier((copies, grd))
    input_grad = product(1, neighbours, voxel_mask, rows, grd, x_more, y_more, edges)
    mine, input_grad = lax.optimization_barrier((spread(copies), input_grad))
    other = swapped(mine, "gy", 0)
    scale = 1.0 / math.sqrt(parts * SLOTS * 512)
    weight = decode(take, scale, mine.astype(jnp.float32))
    weight = decode(take, scale, other.astype(jnp.float32), weight)
    shape = (SLOTS, 8, 8, 8, C)
    return output.reshape(shape), input_grad.reshape(shape), weight.reshape(27, C, C)


def solution(mesh):
    spec = P(("gx", "gy"))
    return jax.shard_map(
        local,
        mesh=mesh,
        in_specs=(spec, spec, P(), spec, spec, spec, spec),
        out_specs=(spec, spec, P()),
        check_vma=False,
    )
```

```python
import math

import jax
import jax.numpy as jnp
from jax import lax
from jax.experimental import pallas as pl
from jax.experimental.pallas import tpu as pltpu
from jax.sharding import PartitionSpec as P

FACES = ((-1, 0), (1, 0), (0, -1), (0, 1))
EDGES = ((-1, -1), (-1, 1), (1, -1), (1, 1))
C = 128
SLOTS = 4
FACE = 2
ZERO = SLOTS + 4 * FACE + 4
ROWS = 27 * C
FACE_ROWS = FACE * 64
X_ROWS = FACE_ROWS + 64
Y_ROWS = FACE_ROWS + 48
HALF = ROWS // 2
VMEM_LIMIT = 32 * 1024 * 1024
PACK_LIMIT = 60 * 1024 * 1024
ROOM_BRICKS = 48
ROOM_TABLES = 12 * 1024


def vmem():
    return pl.BlockSpec(memory_space=pltpu.VMEM)


def hbm():
    return pl.BlockSpec(memory_space=pltpu.HBM)


def fetching(*pairs):
    copies = [pltpu.make_async_copy(src, dst, sem) for src, dst, sem in pairs]
    for copy in copies:
        copy.start()
    return copies


def fetched(*pairs):
    for copy in fetching(*pairs):
        copy.wait()


def mask_columns(mask_ref, s):
    m = mask_ref[...].astype(jnp.float32).astype(jnp.bfloat16)
    pick = (lax.broadcasted_iota(jnp.int32, (SLOTS, C), 0) == s).astype(jnp.float32).astype(jnp.bfloat16)
    return lax.dot_general(m, pick, (((0,), (0,)), ((), ())), preferred_element_type=jnp.float32)


def parity(axis):
    return lax.rem(lax.axis_index(axis), 2)


def side_of(k, odd):
    return 1 - odd if k == 0 else odd


def shifts(cells, same, below, above):
    line = lax.broadcasted_iota(jnp.int32, cells.shape, cells.ndim - 2)
    axis = cells.ndim - 2
    up = jnp.where((same & (line >= 1)) | (below & (line == 0)), pltpu.roll(cells, 1, axis), 0.0)
    down = jnp.where((same & (line <= 6)) | (above & (line == 7)), pltpu.roll(cells, 7, axis), 0.0)
    return up, jnp.where(same, cells, 0.0), down


def pack_kernel(face_hbm, edge_hbm, near_hbm, feat_hbm, grad_hbm, mask_hbm, held_out, act_out, grd_out, near_out, *refs):
    y_out, x_out = refs[0:2], refs[2:4]
    face_ref, edge_ref, near, raw, mask_ref, full, sems = refs[4:]
    got_mask, got_feat, got_grad, *tables = fetching(
        (mask_hbm, mask_ref, sems.at[0]),
        (feat_hbm, raw.at[0], sems.at[1]),
        (grad_hbm, raw.at[1], sems.at[2]),
        (face_hbm, face_ref, sems.at[3]),
        (edge_hbm, edge_ref, sems.at[4]),
        (near_hbm, near, sems.at[5]),
    )
    got_mask.wait()
    got_feat.wait()
    got_grad.wait()
    for s in range(SLOTS):
        rows = mask_columns(mask_ref, s)
        for f in range(2):
            masked = raw[f, s].astype(jnp.float32) * rows
            full[f, s] = masked.reshape(8, 8, 8, C)
            raw[f, s] = masked.astype(jnp.bfloat16)
    results = fetching(
        (raw.at[0], held_out.at[0], sems.at[7]),
        (raw.at[0], act_out, sems.at[8]),
        (raw.at[1], grd_out, sems.at[9]),
    )
    for table in tables:
        table.wait()
    results += fetching((near, near_out.at[0], sems.at[6]))
    for axis, outs in enumerate((x_out, y_out)):
        odd = parity("gy" if axis else "gx")
        for k in range(2):
            side = side_of(k, odd)
            for f in range(2):
                for r in range(FACE):
                    entry = face_ref[r, 2 * axis + side]
                    slot = jnp.clip(entry, 0, SLOTS - 1)
                    layer = full[f, slot, :, 7 * side] if axis else full[f, slot, 7 * side]
                    layer = jnp.where(entry < SLOTS, layer, 0.0)
                    first = f * (Y_ROWS if axis else X_ROWS) + r * 64
                    outs[k][pl.ds(first, 64)] = layer.reshape(64, C).astype(jnp.bfloat16)
            lines = []
            for far in range(2):
                corner = 2 * far + side if axis else 2 * side + far
                entry = edge_ref[0, corner]
                slot = jnp.clip(entry, 0, SLOTS - 1)
                live = entry < SLOTS
                at_x, at_y = (7 * far, 7 * side) if axis else (7 * side, 7 * far)
                if axis == 0:
                    for f in range(2):
                        lines.append(jnp.where(live, full[f, slot, at_x, at_y], 0.0))
                    continue
                base = 18 * far + 6 * side
                low, mid, high = near[slot, base], near[slot, base + 1], near[slot, base + 2]
                up, same, down = shifts(
                    full[1, slot, at_x, at_y],
                    live & (mid < ZERO),
                    live & (high < ZERO),
                    live & (low < ZERO),
                )
                lines += [down, same, up]
            if axis == 0:
                lines.append(jnp.zeros((32, C), jnp.float32))
            lines = jnp.concatenate(lines, axis=0).astype(jnp.bfloat16)
            outs[k][pl.ds(FACE_ROWS, lines.shape[0])] = lines
    for result in results:
        result.wait()


def pack(features, out_grad, mask, near, face_sends, edge_sends):
    sends = [
        jax.ShapeDtypeStruct((rows + FACE_ROWS, C), jnp.bfloat16) for rows in (Y_ROWS, Y_ROWS, X_ROWS, X_ROWS)
    ]
    return pl.pallas_call(
        pack_kernel,
        out_shape=[
            jax.ShapeDtypeStruct((ROOM_BRICKS, SLOTS, 512, C), jnp.bfloat16),
            jax.ShapeDtypeStruct((SLOTS, 512, C), jnp.bfloat16),
            jax.ShapeDtypeStruct((SLOTS, 512, C), jnp.bfloat16),
            jax.ShapeDtypeStruct((ROOM_TABLES, SLOTS, 27), jnp.int32),
        ]
        + sends,
        in_specs=[hbm()] * 6,
        out_specs=[hbm()] * 4 + [vmem()] * 4,
        scratch_shapes=[
            pltpu.SMEM((FACE, 4), jnp.int32),
            pltpu.SMEM((1, 4), jnp.int32),
            pltpu.SMEM((SLOTS, 27), jnp.int32),
            pltpu.VMEM((2, SLOTS, 512, C), jnp.bfloat16),
            pltpu.VMEM((SLOTS, 512), jnp.int32),
            pltpu.VMEM((2, SLOTS, 8, 8, 8, C), jnp.float32),
            pltpu.SemaphoreType.DMA((10,)),
        ],
        compiler_params=pltpu.CompilerParams(vmem_limit_bytes=PACK_LIMIT),
        name="pack",
    )(face_sends.T, edge_sends.T, near, features, out_grad, mask)


def parts_of(ref):
    rows = ref.shape[0] // 2
    return ref.at[pl.ds(0, rows)], ref.at[pl.ds(rows, rows)]


def join_kernel(first, second, out, more):
    rows = first.shape[0] - FACE_ROWS
    for k, src in enumerate((first, second)):
        out[pl.ds(k * rows, rows)] = src[pl.ds(0, rows)]
        more[pl.ds(k * FACE_ROWS, FACE_ROWS)] = src[pl.ds(rows, FACE_ROWS)]


def join(first, second):
    outs = [
        jax.ShapeDtypeStruct((2 * rows, C), jnp.bfloat16) for rows in (first.shape[0] - FACE_ROWS, FACE_ROWS)
    ]
    return pl.pallas_call(
        join_kernel,
        out_shape=outs,
        in_specs=[vmem()] * 2,
        out_specs=[vmem()] * 2,
        compiler_params=pltpu.CompilerParams(vmem_limit_bytes=VMEM_LIMIT),
        name="join_sides",
    )(first, second)


def forward_kernel(x_came, out0, out1):
    odd_x, odd_y = parity("gx"), parity("gy")
    for k, out in enumerate((out0, out1)):
        far = side_of(k, odd_y)
        for j, came in enumerate(parts_of(x_came)):
            source = side_of(j, odd_x)
            rows = came[pl.ds(pl.multiple_of(FACE_ROWS + 16 * far, 16), 16)]
            out[pl.ds(pl.multiple_of(16 * source, 16), 16)] = rows


def forward_corners(x_came):
    send = jax.ShapeDtypeStruct((32, C), jnp.bfloat16)
    return pl.pallas_call(
        forward_kernel,
        out_shape=[send] * 2,
        in_specs=[vmem()],
        out_specs=[vmem()] * 2,
        compiler_params=pltpu.CompilerParams(vmem_limit_bytes=VMEM_LIMIT),
        name="forward_corners",
    )(x_came)


def fill_own(bricks, lx, ly, corners):
    for s in range(SLOTS):
        whole = bricks[s].astype(jnp.float32).reshape(8, 8, 8, C)
        for side, at in ((0, 7), (1, 0)):
            lx[side, s] = whole[at]
            ly[side, s] = whole[:, at]
            for other, far in ((0, 7), (1, 0)):
                corners[2 * side + other, s] = whole[at, far]


def fill_zero(lx, ly, corners, first):
    for ref in (lx, ly, corners):
        count = ref.shape[1] - first
        ref[:, pl.ds(first, count)] = jnp.zeros((ref.shape[0], count) + ref.shape[2:], jnp.float32)


def fill_came(f, x_came, y_came, edges, lx, ly, corners):
    odd_x, odd_y = parity("gx"), parity("gy")
    for came, odd, dst in ((x_came, odd_x, lx), (y_came, odd_y, ly)):
        for k, part in enumerate(parts_of(came)):
            side = side_of(k, odd)
            for r in range(FACE):
                rows = part[pl.ds(r * 64, 64)]
                dst[side, SLOTS + r] = rows.astype(jnp.float32).reshape(8, 8, C)
            dst[k, SLOTS + FACE] = jnp.zeros((8, 8, C), jnp.float32)
    for k, came in enumerate(edges):
        side = side_of(k, odd_y)
        for j in range(2):
            rows = came[pl.ds(16 * j, 16)].astype(jnp.float32)
            corners[2 * j + side, SLOTS + 2 * FACE] = rows[8 * f : 8 * f + 8]
    for sx in range(2):
        for sy in range(2):
            c = 2 * sx + sy
            for r in range(FACE):
                corners[c, SLOTS + r] = lx[sx, SLOTS + r, 0 if sy else 7]
                corners[c, SLOTS + FACE + r] = ly[sy, SLOTS + r, 0 if sx else 7]
            corners[c, SLOTS + 2 * FACE + 1] = jnp.zeros((8, C), jnp.float32)


def build_columns(s, bricks, near, lx, ly, corners, wide, which):
    def spread(cells, at_x, at_y, depth):
        flat = cells.reshape(-1, 8, C)
        for k, moved in enumerate(shifts(flat, depth == 0, depth == -1, depth == 1)):
            wide[k, at_x, at_y] = moved.reshape(cells.shape)

    def column(nx, ny):
        base = 9 * (nx + 1) + 3 * (ny + 1)
        low, mid, high = near[s, base], near[s, base + 1], near[s, base + 2]
        entry = jnp.minimum(jnp.minimum(low, mid), high)
        depth = jnp.where(low < ZERO, -1, jnp.where(high < ZERO, 1, 0))
        if which == "own":
            depth = jnp.where(entry < SLOTS, depth, 2)
        if which == "rim":
            depth = jnp.where((entry >= SLOTS) & (entry < SLOTS + 4 * FACE), depth, 2)
        return entry, depth

    middle = pl.ds(1, 8)
    if which != "rim":
        spread(bricks[s].astype(jnp.float32).reshape(8, 8, 8, C), middle, middle, 0)
    for side, n in ((0, -1), (1, 1)):
        edge_at = pl.ds(0 if n < 0 else 9, 1)
        entry, depth = column(n, 0)
        place = jnp.where(entry < SLOTS, entry, jnp.clip(entry - FACE * side, 0, SLOTS + FACE))
        spread(lx[side, place].reshape(1, 8, 8, C), edge_at, middle, depth)
        entry, depth = column(0, n)
        place = jnp.where(entry < SLOTS, entry, jnp.clip(entry - FACE * (2 + side), 0, SLOTS + FACE))
        spread(ly[side, place].reshape(8, 1, 8, C), middle, edge_at, depth)
    for sx in range(2):
        for sy in range(2):
            entry, depth = column(2 * sx - 1, 2 * sy - 1)
            first_x = SLOTS + FACE * sx
            first_y = SLOTS + FACE * (2 + sy)
            own_edge = SLOTS + 4 * FACE + 2 * sx + sy
            in_x = (entry >= first_x) & (entry < first_x + FACE)
            in_y = (entry >= first_y) & (entry < first_y + FACE)
            place = jnp.where(entry == own_edge, SLOTS + 2 * FACE, SLOTS + 2 * FACE + 1)
            place = jnp.where(in_y, SLOTS + FACE + entry - first_y, place)
            place = jnp.where(in_x, SLOTS + entry - first_x, place)
            place = jnp.where(entry < SLOTS, entry, place)
            spread(corners[2 * sx + sy, place].reshape(1, 1, 8, C), pl.ds(9 * sx, 1), pl.ds(9 * sy, 1), depth)


def stack_columns(s, wide, v):
    for y in range(3):
        for z in range(3):
            cells = wide[z, :, pl.ds(y, 8)].reshape(10, 64, C).astype(jnp.bfloat16)
            v[s, :, :, pl.ds((3 * y + z) * C, C)] = cells


def columns_scratch():
    return [
        pltpu.VMEM((2, SLOTS + FACE + 1, 8, 8, C), jnp.float32),
        pltpu.VMEM((2, SLOTS + FACE + 1, 8, 8, C), jnp.float32),
        pltpu.VMEM((4, SLOTS + 2 * FACE + 2, 8, C), jnp.float32),
        pltpu.VMEM((3, 10, 10, 8, C), jnp.float32),
        pltpu.SMEM((SLOTS, 27), jnp.int32),
        pltpu.SemaphoreType.DMA(()),
    ]


def columns_kernel(near_hbm, act_hbm, v, lx, ly, corners, wide, near, sem, act, act_sem):
    table, bricks = fetching((near_hbm.at[0], near, sem), (act_hbm.at[0], act, act_sem))
    fill_zero(lx, ly, corners, SLOTS)
    bricks.wait()
    fill_own(act, lx, ly, corners)
    table.wait()

    def per_slot(s, carry):
        build_columns(s, act, near, lx, ly, corners, wide, "own")
        stack_columns(s, wide, v)
        return carry

    lax.fori_loop(0, SLOTS, per_slot, 0)


def own_columns(near, act):
    return pl.pallas_call(
        columns_kernel,
        out_shape=jax.ShapeDtypeStruct((SLOTS, 10, 64, 9 * C), jnp.bfloat16),
        in_specs=[hbm()] * 2,
        out_specs=vmem(),
        scratch_shapes=columns_scratch()
        + [pltpu.VMEM((SLOTS, 512, C), jnp.bfloat16), pltpu.SemaphoreType.DMA(())],
        compiler_params=pltpu.CompilerParams(vmem_limit_bytes=VMEM_LIMIT),
        cost_estimate=pl.CostEstimate(flops=1 << 24, bytes_accessed=6 << 20, transcendentals=0),
        name="own_columns",
    )(near, act)


def inner_kernel(v, grd, out, turned):
    for s in range(SLOTS):
        for q in range(4):
            turned[:, pl.ds((4 * s + q) * C, C)] = grd[s, pl.ds(q * C, C)].T
    for x in range(3):
        cells = v[:, pl.ds(x, 8)].reshape(SLOTS * 512, 9 * C)
        terms = jnp.dot(turned[...], cells, preferred_element_type=jnp.float32)
        for j in range(9):
            out[pl.ds((9 * x + j) * C, C)] = terms[:, j * C : (j + 1) * C].T


def inner_terms(v, grd):
    return pl.pallas_call(
        inner_kernel,
        out_shape=jax.ShapeDtypeStruct((ROWS, C), jnp.float32),
        in_specs=[vmem()] * 2,
        out_specs=vmem(),
        scratch_shapes=[pltpu.VMEM((C, SLOTS * 512), jnp.bfloat16)],
        compiler_params=pltpu.CompilerParams(vmem_limit_bytes=VMEM_LIMIT),
        cost_estimate=pl.CostEstimate(flops=2 * 2048 * ROWS * C, bytes_accessed=6 << 20, transcendentals=0),
        name="inner_terms",
    )(v, grd)


def rim_kernel(near_hbm, inner, grd, x_ref, y_ref, keep, send, lx, ly, corners, wide, near, sem, *refs):
    vx, vy, ends_a, ends_g, side_x, side_y = refs
    (table,) = fetching((near_hbm, near, sem))
    fill_came(0, x_ref, y_ref, (), lx, ly, corners)
    for k, came in enumerate(parts_of(x_ref)):
        side = side_of(k, parity("gx"))
        for j in range(2):
            ends_a[side, j] = came[pl.ds(FACE_ROWS + 16 * j, 16)].astype(jnp.float32)[0:8]
    for k, came in enumerate(parts_of(y_ref)):
        side = side_of(k, parity("gy"))
        ends_g[side] = came[pl.ds(FACE_ROWS, 48)].astype(jnp.float32).reshape(2, 3, 8, C)
    table.wait()
    for s in range(SLOTS):
        build_columns(s, None, near, lx, ly, corners, wide, "rim")
        rows = pl.ds(64 * s, 64)
        for side in range(2):
            for j in range(9):
                cells = wide[j % 3, 9 * side, pl.ds(j // 3, 8)]
                vx[side, rows, pl.ds(j * C, C)] = cells.reshape(64, C).astype(jnp.bfloat16)
        for z in range(3):
            for sx in range(2):
                for sy in range(2):
                    wide[z, 9 * sx, 9 * sy] = jnp.zeros((8, C), jnp.float32)
        for side in range(2):
            for j in range(9):
                cells = wide[j % 3, pl.ds(j // 3, 8), 9 * side]
                vy[side, rows, pl.ds(j * C, C)] = cells.reshape(64, C).astype(jnp.bfloat16)
    grads = grd[...]
    lines = grads.astype(jnp.float32).reshape(SLOTS, 8, 8, 8, C)

    def term(cells, rows):
        return lax.dot_general(cells, rows, (((0,), (0,)), ((), ())), preferred_element_type=jnp.float32)

    def end(line):
        return jnp.concatenate([line, jnp.zeros((8, C), jnp.float32)], axis=0).astype(jnp.bfloat16)

    for side in range(2):
        rows = grads[:, 448 * side : 448 * side + 64].reshape(SLOTS * 64, C)
        side_x[side] = term(vx[side], rows)
        rows = lines[:, :, 7 * side].reshape(SLOTS * 64, C).astype(jnp.bfloat16)
        side_y[side] = term(vy[side], rows)
    def write(halves):
        for x in range(3):
            for y in range(3):
                for z in range(3):
                    first = (9 * x + 3 * y + z) * C
                    value = inner[pl.ds(first, C)]
                    if x != 1:
                        value += side_x[x // 2, pl.ds((3 * y + z) * C, C)]
                    if y != 1:
                        value += side_y[y // 2, pl.ds((3 * x + z) * C, C)]
                    if x != 1 and y != 1:
                        sx, sy = x // 2, 1 - y // 2
                        value += term(end(ends_a[sx, sy]), end(ends_g[sy, sx, z]))
                    for half in range(2):
                        low = max(first, half * HALF)
                        rows = min(first + C, (half + 1) * HALF) - low
                        if rows > 0:
                            halves[half][pl.ds(low - half * HALF, rows)] = value[low - first : low - first + rows]

    core = parity("gy")

    @pl.when(core == 0)
    def _():
        write((keep, send))

    @pl.when(core == 1)
    def _():
        write((send, keep))


def rim_terms(near, inner, grd, x_came, y_came):
    half = jax.ShapeDtypeStruct((HALF, C), jnp.float32)
    side = pltpu.VMEM((2, SLOTS * 64, 9 * C), jnp.bfloat16)
    return pl.pallas_call(
        rim_kernel,
        out_shape=[half, half],
        in_specs=[hbm()] + [vmem()] * 4,
        out_specs=[vmem()] * 2,
        scratch_shapes=columns_scratch()
        + [
            side,
            side,
            pltpu.VMEM((2, 2, 8, C), jnp.float32),
            pltpu.VMEM((2, 2, 3, 8, C), jnp.float32),
            pltpu.VMEM((2, 9 * C, C), jnp.float32),
            pltpu.VMEM((2, 9 * C, C), jnp.float32),
        ],
        compiler_params=pltpu.CompilerParams(vmem_limit_bytes=VMEM_LIMIT),
        cost_estimate=pl.CostEstimate(flops=2 * 256 * 36 * C * C, bytes_accessed=6 << 20, transcendentals=0),
        name="rim_terms",
    )(near, inner, grd, x_came, y_came)


def power_of(values):
    peak = jnp.max(jnp.abs(values))
    return jnp.clip(jnp.ceil(jnp.log2(jnp.full((8, C), peak))), -100.0, 100.0)[0:1]


def merge_kernel(groups, take, keep, came, out, total):
    held = out.shape[1]
    total[pl.ds(0, HALF)] = keep[...] + came[...]
    if groups * take > HALF:
        total[pl.ds(HALF, groups * take - HALF)] = jnp.zeros((groups * take - HALF, C), jnp.float32)
    power = power_of(total[...])
    scale = jnp.exp2(14.0 - power)
    for p in range(groups):
        out[p, pl.ds(0, take)] = total[pl.ds(p * take, take)] * scale
        out[p, pl.ds(take, held - take)] = jnp.broadcast_to(power, (held - take, C))


def merge(groups, take, held, keep, came):
    return pl.pallas_call(
        lambda *refs: merge_kernel(groups, take, *refs),
        out_shape=jax.ShapeDtypeStruct((groups, held, C), jnp.float32),
        in_specs=[vmem()] * 2,
        out_specs=vmem(),
        scratch_shapes=[pltpu.VMEM((groups * take, C), jnp.float32)],
        compiler_params=pltpu.CompilerParams(vmem_limit_bytes=VMEM_LIMIT),
        name="merge",
    )(keep, came)


def sum_kernel(take, blocks, out):
    groups, held, _ = blocks.shape
    total = jnp.zeros((take, C), jnp.float32)
    for p in range(groups):
        total += blocks[p, pl.ds(0, take)] * jnp.exp2(blocks[p, pl.ds(take, 1)] - 14.0)
    power = power_of(total)
    total = total * jnp.exp2(14.0 - power)
    for p in range(groups):
        out[p, pl.ds(0, take)] = total
        out[p, pl.ds(take, held - take)] = jnp.broadcast_to(power, (held - take, C))


def sum_blocks(take, blocks):
    return pl.pallas_call(
        lambda *refs: sum_kernel(take, *refs),
        out_shape=jax.ShapeDtypeStruct(blocks.shape, jnp.float32),
        in_specs=[vmem()],
        out_specs=vmem(),
        compiler_params=pltpu.CompilerParams(vmem_limit_bytes=VMEM_LIMIT),
        name="sum_blocks",
    )(blocks)


def decode_kernel(take, scale, own, blocks, *refs):
    out, half, sems = refs[-3:]
    groups = blocks.shape[0]
    core = parity("gy")
    target = out.at[core if own else 1 - core]
    copies = []
    done = 0
    for p in range(groups):
        rows = min(take, HALF - p * take)
        if rows > 0:
            factor = jnp.exp2(blocks[p, pl.ds(take, 1)] - 14.0) * scale
            half[pl.ds(p * take, rows)] = blocks[p, pl.ds(0, rows)] * factor
        ready = min((p + 1) * take, HALF)
        if ready - done >= HALF // 4 and ready % 8 == 0 or p == groups - 1:
            piece = pl.ds(done, ready - done)
            copies += fetching((half.at[piece], target.at[piece], sems.at[len(copies)]))
            done = ready
    for copy in copies:
        copy.wait()


def decode(take, scale, blocks, begun=None):
    rest = () if begun is None else (begun,)
    return pl.pallas_call(
        lambda *refs: decode_kernel(take, scale, not rest, *refs),
        out_shape=jax.ShapeDtypeStruct((2, HALF, C), jnp.float32),
        in_specs=[vmem()] + [hbm()] * len(rest),
        out_specs=hbm(),
        scratch_shapes=[pltpu.VMEM((HALF, C), jnp.float32), pltpu.SemaphoreType.DMA((5,))],
        input_output_aliases={1: 0} if rest else {},
        compiler_params=pltpu.CompilerParams(vmem_limit_bytes=VMEM_LIMIT),
        name="decode_other" if rest else "decode_own",
    )(blocks, *rest)


def product_kernel(f, near_hbm, mask_ref, kernel_ref, bricks, x_ref, y_ref, e0, e1, out, *refs):
    lx, ly, corners, wide, near, sem, v, *flipped = refs
    (table,) = fetching((near_hbm, near, sem))
    weights = kernel_ref
    if f == 1:
        weights = flipped[0]
        for o in range(27):
            weights[pl.ds((26 - o) * C, C)] = kernel_ref[pl.ds(o * C, C)].T
    fill_own(bricks, lx, ly, corners)
    fill_came(f, x_ref, y_ref, (e0, e1), lx, ly, corners)
    table.wait()

    def per_slot(s, carry):
        build_columns(s, bricks, near, lx, ly, corners, wide, "all")
        stack_columns(s, wide, v)
        total = jnp.zeros((512, C), jnp.float32)
        for x in range(3):
            cells = v[s, pl.ds(x, 8)].reshape(512, 9 * C)
            total += jnp.dot(cells, weights[pl.ds(x * 9 * C, 9 * C)], preferred_element_type=jnp.float32)
        out[s] = (total * mask_columns(mask_ref, s)).astype(jnp.bfloat16)
        return carry

    lax.fori_loop(0, SLOTS, per_slot, 0)


def product(f, near, mask, kernel, bricks, x_came, y_came, edges):
    return pl.pallas_call(
        lambda *refs: product_kernel(f, *refs),
        out_shape=jax.ShapeDtypeStruct((SLOTS, 512, C), jnp.bfloat16),
        in_specs=[hbm()] + [vmem()] * 7,
        out_specs=vmem(),
        scratch_shapes=columns_scratch()
        + [pltpu.VMEM((SLOTS, 10, 64, 9 * C), jnp.bfloat16)]
        + ([pltpu.VMEM((ROWS, C), jnp.bfloat16)] if f else []),
        compiler_params=pltpu.CompilerParams(vmem_limit_bytes=VMEM_LIMIT),
        cost_estimate=pl.CostEstimate(flops=2 * 2048 * ROWS * C, bytes_accessed=4 << 20, transcendentals=0),
        name=("output_product", "input_grad_product")[f],
    )(near, mask, kernel, bricks, x_came, y_came, *edges)


def swapped(value, axis, k):
    pairs = []
    for low in range(k, lax.axis_size(axis) - 1, 2):
        pairs += [(low, low + 1), (low + 1, low)]
    return lax.ppermute(value, axis, pairs)


def hopped(value, axis):
    size = lax.axis_size(axis)
    pairs = [(i, i + 2) for i in range(1, size - 2, 2)] + [(i, i - 2) for i in range(2, size, 2)]
    return lax.ppermute(value, axis, pairs)


def local(features, out_grad, kernel, voxel_mask, neighbours, face_sends, edge_sends):
    size_x, size_y = lax.axis_size("gx"), lax.axis_size("gy")
    parts = size_x * size_y
    groups = parts // 2
    take = -(-HALF // groups)
    held = -(-(take + 1) // 16) * 16
    order = [(i + parts // 2) % parts for i in range(parts)]
    same_core = [[i for i in order if i % size_y % 2 == core] for core in range(2)]

    def spread(blocks):
        return lax.all_to_all(blocks, ("gx", "gy"), 0, 0, axis_index_groups=same_core, tiled=True)

    held_act, act, grd, table, y0, y1, x0, x1 = pack(
        features.reshape(SLOTS, 512, C),
        out_grad.reshape(SLOTS, 512, C),
        voxel_mask,
        neighbours,
        face_sends,
        edge_sends,
    )
    y1 = hopped(y1, "gy")
    x1 = hopped(x1, "gx")
    v = own_columns(table, held_act)
    x1, v = lax.optimization_barrier((x1, v))
    x_came, x_more = join(x0, x1)
    x_more, v = lax.optimization_barrier((x_more, v))
    x_came = swapped(x_came, "gx", 0)
    inner = inner_terms(v, grd)
    inner, y1 = lax.optimization_barrier((inner, y1))
    y_came, y_more = join(y0, y1)
    y_came = swapped(y_came, "gy", 0)
    keep, send = rim_terms(neighbours, inner, grd, x_came, y_came)
    blocks = merge(groups, take, held, keep, swapped(send, "gy", 0)).astype(jnp.float16)
    rows = kernel.reshape(ROWS, C)
    blocks, act, x_came, x_more, y_more = lax.optimization_barrier((blocks, act, x_came, x_more, y_more))
    x_more, y_more = swapped(x_more, "gx", 0), swapped(y_more, "gy", 0)
    e0, e1 = forward_corners(x_came)
    edges = [swapped(e0, "gy", 0), swapped(e1, "gy", 1)]
    output = product(0, neighbours, voxel_mask, rows, act, x_came, y_came, edges)
    arrived, output, x_more, y_more = lax.optimization_barrier((spread(blocks), output, x_more, y_more))
    copies = sum_blocks(take, arrived.astype(jnp.float32)).astype(jnp.float16)
    copies, grd = lax.optimization_barrier((copies, grd))
    input_grad = product(1, neighbours, voxel_mask, rows, grd, x_more, y_more, edges)
    mine, input_grad = lax.optimization_barrier((spread(copies), input_grad))
    other = swapped(mine, "gy", 0)
    scale = 1.0 / math.sqrt(parts * SLOTS * 512)
    weight = decode(take, scale, mine.astype(jnp.float32))
    weight = decode(take, scale, other.astype(jnp.float32), weight)
    shape = (SLOTS, 8, 8, 8, C)
    return output.reshape(shape), input_grad.reshape(shape), weight.reshape(27, C, C)


def solution(mesh):
    spec = P(("gx", "gy"))
    return jax.shard_map(
        local,
        mesh=mesh,
        in_specs=(spec, spec, P(), spec, spec, spec, spec),
        out_specs=(spec, spec, P()),
        check_vma=False,
    )
```

```python
import math

import jax
import jax.numpy as jnp
from jax import lax
from jax.experimental import pallas as pl
from jax.experimental.pallas import tpu as pltpu
from jax.sharding import PartitionSpec as P

FACES = ((-1, 0), (1, 0), (0, -1), (0, 1))
EDGES = ((-1, -1), (-1, 1), (1, -1), (1, 1))
C = 128
SLOTS = 4
FACE = 2
ZERO = SLOTS + 4 * FACE + 4
ROWS = 27 * C
FACE_ROWS = FACE * 64
X_ROWS = FACE_ROWS + 64
Y_ROWS = FACE_ROWS + 48
HALF = ROWS // 2
VMEM_LIMIT = 32 * 1024 * 1024
PACK_LIMIT = 60 * 1024 * 1024
ROOM_BRICKS = 48
ROOM_TABLES = 12 * 1024


def vmem():
    return pl.BlockSpec(memory_space=pltpu.VMEM)


def hbm():
    return pl.BlockSpec(memory_space=pltpu.HBM)


def fetching(*pairs):
    copies = [pltpu.make_async_copy(src, dst, sem) for src, dst, sem in pairs]
    for copy in copies:
        copy.start()
    return copies


def fetched(*pairs):
    for copy in fetching(*pairs):
        copy.wait()


def mask_columns(mask_ref, s):
    m = mask_ref[...].astype(jnp.float32).astype(jnp.bfloat16)
    pick = (lax.broadcasted_iota(jnp.int32, (SLOTS, C), 0) == s).astype(jnp.float32).astype(jnp.bfloat16)
    return lax.dot_general(m, pick, (((0,), (0,)), ((), ())), preferred_element_type=jnp.float32)


def parity(axis):
    return lax.rem(lax.axis_index(axis), 2)


def side_of(k, odd):
    return 1 - odd if k == 0 else odd


def shifts(cells, same, below, above):
    line = lax.broadcasted_iota(jnp.int32, cells.shape, cells.ndim - 2)
    axis = cells.ndim - 2
    up = jnp.where((same & (line >= 1)) | (below & (line == 0)), pltpu.roll(cells, 1, axis), 0.0)
    down = jnp.where((same & (line <= 6)) | (above & (line == 7)), pltpu.roll(cells, 7, axis), 0.0)
    return up, jnp.where(same, cells, 0.0), down


def pack_kernel(face_hbm, edge_hbm, near_hbm, feat_hbm, grad_hbm, mask_hbm, held_out, act_out, grd_out, near_out, *refs):
    sends = refs[0:4]
    y_out, x_out = refs[4:6], refs[6:8]
    face_ref, edge_ref, near, raw, mask_ref, full, sems = refs[8:]
    got_mask, got_feat, got_grad, *tables = fetching(
        (mask_hbm, mask_ref, sems.at[0]),
        (feat_hbm, raw.at[0], sems.at[1]),
        (grad_hbm, raw.at[1], sems.at[2]),
        (face_hbm, face_ref, sems.at[3]),
        (edge_hbm, edge_ref, sems.at[4]),
        (near_hbm, near, sems.at[5]),
    )
    got_mask.wait()
    got_feat.wait()
    got_grad.wait()
    for s in range(SLOTS):
        rows = mask_columns(mask_ref, s)
        for f in range(2):
            masked = raw[f, s].astype(jnp.float32) * rows
            full[f, s] = masked.reshape(8, 8, 8, C)
            raw[f, s] = masked.astype(jnp.bfloat16)
    results = fetching(
        (raw.at[0], held_out.at[0], sems.at[7]),
        (raw.at[0], act_out, sems.at[8]),
        (raw.at[1], grd_out, sems.at[9]),
    )
    for table in tables:
        table.wait()
    results += fetching((near, near_out.at[0], sems.at[6]))
    for axis, outs in enumerate((x_out, y_out)):
        odd = parity("gy" if axis else "gx")
        for k in range(2):
            side = side_of(k, odd)
            for f in range(2):
                for r in range(FACE):
                    entry = face_ref[r, 2 * axis + side]
                    slot = jnp.clip(entry, 0, SLOTS - 1)
                    layer = full[f, slot, :, 7 * side] if axis else full[f, slot, 7 * side]
                    layer = jnp.where(entry < SLOTS, layer, 0.0)
                    first = f * (Y_ROWS if axis else X_ROWS) + r * 64
                    outs[k][pl.ds(first, 64)] = layer.reshape(64, C).astype(jnp.bfloat16)
            lines = []
            for far in range(2):
                corner = 2 * far + side if axis else 2 * side + far
                entry = edge_ref[0, corner]
                slot = jnp.clip(entry, 0, SLOTS - 1)
                live = entry < SLOTS
                at_x, at_y = (7 * far, 7 * side) if axis else (7 * side, 7 * far)
                if axis == 0:
                    for f in range(2):
                        lines.append(jnp.where(live, full[f, slot, at_x, at_y], 0.0))
                    continue
                base = 18 * far + 6 * side
                low, mid, high = near[slot, base], near[slot, base + 1], near[slot, base + 2]
                up, same, down = shifts(
                    full[1, slot, at_x, at_y],
                    live & (mid < ZERO),
                    live & (high < ZERO),
                    live & (low < ZERO),
                )
                lines += [down, same, up]
            if axis == 0:
                lines.append(jnp.zeros((32, C), jnp.float32))
            lines = jnp.concatenate(lines, axis=0).astype(jnp.bfloat16)
            outs[k][pl.ds(FACE_ROWS, lines.shape[0])] = lines
    for i, (built, send) in enumerate(zip(refs[4:8], sends)):
        results += fetching((built, send, sems.at[10 + i]))
    for result in results:
        result.wait()


def pack(features, out_grad, mask, near, face_sends, edge_sends):
    sends = [
        jax.ShapeDtypeStruct((rows + FACE_ROWS, C), jnp.bfloat16) for rows in (Y_ROWS, Y_ROWS, X_ROWS, X_ROWS)
    ]
    return pl.pallas_call(
        pack_kernel,
        out_shape=[
            jax.ShapeDtypeStruct((ROOM_BRICKS, SLOTS, 512, C), jnp.bfloat16),
            jax.ShapeDtypeStruct((SLOTS, 512, C), jnp.bfloat16),
            jax.ShapeDtypeStruct((SLOTS, 512, C), jnp.bfloat16),
            jax.ShapeDtypeStruct((ROOM_TABLES, SLOTS, 27), jnp.int32),
        ]
        + sends,
        in_specs=[hbm()] * 6,
        out_specs=[hbm()] * 8,
        scratch_shapes=[pltpu.VMEM(send.shape, send.dtype) for send in sends]
        + [
            pltpu.SMEM((FACE, 4), jnp.int32),
            pltpu.SMEM((1, 4), jnp.int32),
            pltpu.SMEM((SLOTS, 27), jnp.int32),
            pltpu.VMEM((2, SLOTS, 512, C), jnp.bfloat16),
            pltpu.VMEM((SLOTS, 512), jnp.int32),
            pltpu.VMEM((2, SLOTS, 8, 8, 8, C), jnp.float32),
            pltpu.SemaphoreType.DMA((14,)),
        ],
        compiler_params=pltpu.CompilerParams(vmem_limit_bytes=PACK_LIMIT),
        name="pack",
    )(face_sends.T, edge_sends.T, near, features, out_grad, mask)


def parts_of(ref):
    rows = ref.shape[0] // 2
    return ref.at[pl.ds(0, rows)], ref.at[pl.ds(rows, rows)]


def join_kernel(first, second, out, more):
    rows = first.shape[0] - FACE_ROWS
    for k, src in enumerate((first, second)):
        out[pl.ds(k * rows, rows)] = src[pl.ds(0, rows)]
        more[pl.ds(k * FACE_ROWS, FACE_ROWS)] = src[pl.ds(rows, FACE_ROWS)]


def join(first, second):
    outs = [
        jax.ShapeDtypeStruct((2 * rows, C), jnp.bfloat16) for rows in (first.shape[0] - FACE_ROWS, FACE_ROWS)
    ]
    return pl.pallas_call(
        join_kernel,
        out_shape=outs,
        in_specs=[vmem()] * 2,
        out_specs=[vmem()] * 2,
        compiler_params=pltpu.CompilerParams(vmem_limit_bytes=VMEM_LIMIT),
        name="join_sides",
    )(first, second)


def forward_kernel(x_came, out0, out1):
    odd_x, odd_y = parity("gx"), parity("gy")
    for k, out in enumerate((out0, out1)):
        far = side_of(k, odd_y)
        for j, came in enumerate(parts_of(x_came)):
            source = side_of(j, odd_x)
            rows = came[pl.ds(pl.multiple_of(FACE_ROWS + 16 * far, 16), 16)]
            out[pl.ds(pl.multiple_of(16 * source, 16), 16)] = rows


def forward_corners(x_came):
    send = jax.ShapeDtypeStruct((32, C), jnp.bfloat16)
    return pl.pallas_call(
        forward_kernel,
        out_shape=[send] * 2,
        in_specs=[vmem()],
        out_specs=[vmem()] * 2,
        compiler_params=pltpu.CompilerParams(vmem_limit_bytes=VMEM_LIMIT),
        name="forward_corners",
    )(x_came)


def fill_own(bricks, lx, ly, corners):
    for s in range(SLOTS):
        whole = bricks[s].astype(jnp.float32).reshape(8, 8, 8, C)
        for side, at in ((0, 7), (1, 0)):
            lx[side, s] = whole[at]
            ly[side, s] = whole[:, at]
            for other, far in ((0, 7), (1, 0)):
                corners[2 * side + other, s] = whole[at, far]


def fill_zero(lx, ly, corners, first):
    for ref in (lx, ly, corners):
        count = ref.shape[1] - first
        ref[:, pl.ds(first, count)] = jnp.zeros((ref.shape[0], count) + ref.shape[2:], jnp.float32)


def fill_came(f, x_came, y_came, edges, lx, ly, corners):
    odd_x, odd_y = parity("gx"), parity("gy")
    for came, odd, dst in ((x_came, odd_x, lx), (y_came, odd_y, ly)):
        for k, part in enumerate(parts_of(came)):
            side = side_of(k, odd)
            for r in range(FACE):
                rows = part[pl.ds(r * 64, 64)]
                dst[side, SLOTS + r] = rows.astype(jnp.float32).reshape(8, 8, C)
            dst[k, SLOTS + FACE] = jnp.zeros((8, 8, C), jnp.float32)
    for k, came in enumerate(edges):
        side = side_of(k, odd_y)
        for j in range(2):
            rows = came[pl.ds(16 * j, 16)].astype(jnp.float32)
            corners[2 * j + side, SLOTS + 2 * FACE] = rows[8 * f : 8 * f + 8]
    for sx in range(2):
        for sy in range(2):
            c = 2 * sx + sy
            for r in range(FACE):
                corners[c, SLOTS + r] = lx[sx, SLOTS + r, 0 if sy else 7]
                corners[c, SLOTS + FACE + r] = ly[sy, SLOTS + r, 0 if sx else 7]
            corners[c, SLOTS + 2 * FACE + 1] = jnp.zeros((8, C), jnp.float32)


def build_columns(s, bricks, near, lx, ly, corners, wide, which):
    def spread(cells, at_x, at_y, depth):
        flat = cells.reshape(-1, 8, C)
        for k, moved in enumerate(shifts(flat, depth == 0, depth == -1, depth == 1)):
            wide[k, at_x, at_y] = moved.reshape(cells.shape)

    def column(nx, ny):
        base = 9 * (nx + 1) + 3 * (ny + 1)
        low, mid, high = near[s, base], near[s, base + 1], near[s, base + 2]
        entry = jnp.minimum(jnp.minimum(low, mid), high)
        depth = jnp.where(low < ZERO, -1, jnp.where(high < ZERO, 1, 0))
        if which == "own":
            depth = jnp.where(entry < SLOTS, depth, 2)
        if which == "rim":
            depth = jnp.where((entry >= SLOTS) & (entry < SLOTS + 4 * FACE), depth, 2)
        return entry, depth

    middle = pl.ds(1, 8)
    if which != "rim":
        spread(bricks[s].astype(jnp.float32).reshape(8, 8, 8, C), middle, middle, 0)
    for side, n in ((0, -1), (1, 1)):
        edge_at = pl.ds(0 if n < 0 else 9, 1)
        entry, depth = column(n, 0)
        place = jnp.where(entry < SLOTS, entry, jnp.clip(entry - FACE * side, 0, SLOTS + FACE))
        spread(lx[side, place].reshape(1, 8, 8, C), edge_at, middle, depth)
        entry, depth = column(0, n)
        place = jnp.where(entry < SLOTS, entry, jnp.clip(entry - FACE * (2 + side), 0, SLOTS + FACE))
        spread(ly[side, place].reshape(8, 1, 8, C), middle, edge_at, depth)
    for sx in range(2):
        for sy in range(2):
            entry, depth = column(2 * sx - 1, 2 * sy - 1)
            first_x = SLOTS + FACE * sx
            first_y = SLOTS + FACE * (2 + sy)
            own_edge = SLOTS + 4 * FACE + 2 * sx + sy
            in_x = (entry >= first_x) & (entry < first_x + FACE)
            in_y = (entry >= first_y) & (entry < first_y + FACE)
            place = jnp.where(entry == own_edge, SLOTS + 2 * FACE, SLOTS + 2 * FACE + 1)
            place = jnp.where(in_y, SLOTS + FACE + entry - first_y, place)
            place = jnp.where(in_x, SLOTS + entry - first_x, place)
            place = jnp.where(entry < SLOTS, entry, place)
            spread(corners[2 * sx + sy, place].reshape(1, 1, 8, C), pl.ds(9 * sx, 1), pl.ds(9 * sy, 1), depth)


def stack_columns(s, wide, v):
    for y in range(3):
        for z in range(3):
            cells = wide[z, :, pl.ds(y, 8)].reshape(10, 64, C).astype(jnp.bfloat16)
            v[s, :, :, pl.ds((3 * y + z) * C, C)] = cells


def columns_scratch():
    return [
        pltpu.VMEM((2, SLOTS + FACE + 1, 8, 8, C), jnp.float32),
        pltpu.VMEM((2, SLOTS + FACE + 1, 8, 8, C), jnp.float32),
        pltpu.VMEM((4, SLOTS + 2 * FACE + 2, 8, C), jnp.float32),
        pltpu.VMEM((3, 10, 10, 8, C), jnp.float32),
        pltpu.SMEM((SLOTS, 27), jnp.int32),
        pltpu.SemaphoreType.DMA(()),
    ]


def columns_kernel(near_hbm, act_hbm, v, lx, ly, corners, wide, near, sem, act, act_sem):
    table, bricks = fetching((near_hbm.at[0], near, sem), (act_hbm.at[0], act, act_sem))
    fill_zero(lx, ly, corners, SLOTS)
    bricks.wait()
    fill_own(act, lx, ly, corners)
    table.wait()

    def per_slot(s, carry):
        build_columns(s, act, near, lx, ly, corners, wide, "own")
        stack_columns(s, wide, v)
        return carry

    lax.fori_loop(0, SLOTS, per_slot, 0)


def own_columns(near, act):
    return pl.pallas_call(
        columns_kernel,
        out_shape=jax.ShapeDtypeStruct((SLOTS, 10, 64, 9 * C), jnp.bfloat16),
        in_specs=[hbm()] * 2,
        out_specs=vmem(),
        scratch_shapes=columns_scratch()
        + [pltpu.VMEM((SLOTS, 512, C), jnp.bfloat16), pltpu.SemaphoreType.DMA(())],
        compiler_params=pltpu.CompilerParams(vmem_limit_bytes=VMEM_LIMIT),
        cost_estimate=pl.CostEstimate(flops=1 << 24, bytes_accessed=6 << 20, transcendentals=0),
        name="own_columns",
    )(near, act)


def inner_kernel(v, grd, out, turned):
    for s in range(SLOTS):
        for q in range(4):
            turned[:, pl.ds((4 * s + q) * C, C)] = grd[s, pl.ds(q * C, C)].T
    for x in range(3):
        cells = v[:, pl.ds(x, 8)].reshape(SLOTS * 512, 9 * C)
        terms = jnp.dot(turned[...], cells, preferred_element_type=jnp.float32)
        for j in range(9):
            out[pl.ds((9 * x + j) * C, C)] = terms[:, j * C : (j + 1) * C].T


def inner_terms(v, grd):
    return pl.pallas_call(
        inner_kernel,
        out_shape=jax.ShapeDtypeStruct((ROWS, C), jnp.float32),
        in_specs=[vmem()] * 2,
        out_specs=vmem(),
        scratch_shapes=[pltpu.VMEM((C, SLOTS * 512), jnp.bfloat16)],
        compiler_params=pltpu.CompilerParams(vmem_limit_bytes=VMEM_LIMIT),
        cost_estimate=pl.CostEstimate(flops=2 * 2048 * ROWS * C, bytes_accessed=6 << 20, transcendentals=0),
        name="inner_terms",
    )(v, grd)


def rim_kernel(near_hbm, inner, grd, x_ref, y_ref, keep, send, lx, ly, corners, wide, near, sem, *refs):
    vx, vy, ends_a, ends_g, side_x, side_y = refs
    (table,) = fetching((near_hbm, near, sem))
    fill_came(0, x_ref, y_ref, (), lx, ly, corners)
    for k, came in enumerate(parts_of(x_ref)):
        side = side_of(k, parity("gx"))
        for j in range(2):
            ends_a[side, j] = came[pl.ds(FACE_ROWS + 16 * j, 16)].astype(jnp.float32)[0:8]
    for k, came in enumerate(parts_of(y_ref)):
        side = side_of(k, parity("gy"))
        ends_g[side] = came[pl.ds(FACE_ROWS, 48)].astype(jnp.float32).reshape(2, 3, 8, C)
    table.wait()
    for s in range(SLOTS):
        build_columns(s, None, near, lx, ly, corners, wide, "rim")
        rows = pl.ds(64 * s, 64)
        for side in range(2):
            for j in range(9):
                cells = wide[j % 3, 9 * side, pl.ds(j // 3, 8)]
                vx[side, rows, pl.ds(j * C, C)] = cells.reshape(64, C).astype(jnp.bfloat16)
        for z in range(3):
            for sx in range(2):
                for sy in range(2):
                    wide[z, 9 * sx, 9 * sy] = jnp.zeros((8, C), jnp.float32)
        for side in range(2):
            for j in range(9):
                cells = wide[j % 3, pl.ds(j // 3, 8), 9 * side]
                vy[side, rows, pl.ds(j * C, C)] = cells.reshape(64, C).astype(jnp.bfloat16)
    grads = grd[...]
    lines = grads.astype(jnp.float32).reshape(SLOTS, 8, 8, 8, C)

    def term(cells, rows):
        return lax.dot_general(cells, rows, (((0,), (0,)), ((), ())), preferred_element_type=jnp.float32)

    def end(line):
        return jnp.concatenate([line, jnp.zeros((8, C), jnp.float32)], axis=0).astype(jnp.bfloat16)

    for side in range(2):
        rows = grads[:, 448 * side : 448 * side + 64].reshape(SLOTS * 64, C)
        side_x[side] = term(vx[side], rows)
        rows = lines[:, :, 7 * side].reshape(SLOTS * 64, C).astype(jnp.bfloat16)
        side_y[side] = term(vy[side], rows)
    def write(halves):
        for x in range(3):
            for y in range(3):
                for z in range(3):
                    first = (9 * x + 3 * y + z) * C
                    value = inner[pl.ds(first, C)]
                    if x != 1:
                        value += side_x[x // 2, pl.ds((3 * y + z) * C, C)]
                    if y != 1:
                        value += side_y[y // 2, pl.ds((3 * x + z) * C, C)]
                    if x != 1 and y != 1:
                        sx, sy = x // 2, 1 - y // 2
                        value += term(end(ends_a[sx, sy]), end(ends_g[sy, sx, z]))
                    for half in range(2):
                        low = max(first, half * HALF)
                        rows = min(first + C, (half + 1) * HALF) - low
                        if rows > 0:
                            halves[half][pl.ds(low - half * HALF, rows)] = value[low - first : low - first + rows]

    core = parity("gy")

    @pl.when(core == 0)
    def _():
        write((keep, send))

    @pl.when(core == 1)
    def _():
        write((send, keep))


def rim_terms(near, inner, grd, x_came, y_came):
    half = jax.ShapeDtypeStruct((HALF, C), jnp.float32)
    side = pltpu.VMEM((2, SLOTS * 64, 9 * C), jnp.bfloat16)
    return pl.pallas_call(
        rim_kernel,
        out_shape=[half, half],
        in_specs=[hbm()] + [vmem()] * 4,
        out_specs=[vmem()] * 2,
        scratch_shapes=columns_scratch()
        + [
            side,
            side,
            pltpu.VMEM((2, 2, 8, C), jnp.float32),
            pltpu.VMEM((2, 2, 3, 8, C), jnp.float32),
            pltpu.VMEM((2, 9 * C, C), jnp.float32),
            pltpu.VMEM((2, 9 * C, C), jnp.float32),
        ],
        compiler_params=pltpu.CompilerParams(vmem_limit_bytes=VMEM_LIMIT),
        cost_estimate=pl.CostEstimate(flops=2 * 256 * 36 * C * C, bytes_accessed=6 << 20, transcendentals=0),
        name="rim_terms",
    )(near, inner, grd, x_came, y_came)


def power_of(values):
    peak = jnp.max(jnp.abs(values))
    return jnp.clip(jnp.ceil(jnp.log2(jnp.full((8, C), peak))), -100.0, 100.0)[0:1]


def merge_kernel(groups, take, keep, came, out, total):
    held = out.shape[1]
    total[pl.ds(0, HALF)] = keep[...] + came[...]
    if groups * take > HALF:
        total[pl.ds(HALF, groups * take - HALF)] = jnp.zeros((groups * take - HALF, C), jnp.float32)
    power = power_of(total[...])
    scale = jnp.exp2(14.0 - power)
    for p in range(groups):
        out[p, pl.ds(0, take)] = total[pl.ds(p * take, take)] * scale
        out[p, pl.ds(take, held - take)] = jnp.broadcast_to(power, (held - take, C))


def merge(groups, take, held, keep, came):
    return pl.pallas_call(
        lambda *refs: merge_kernel(groups, take, *refs),
        out_shape=jax.ShapeDtypeStruct((groups, held, C), jnp.float32),
        in_specs=[vmem()] * 2,
        out_specs=vmem(),
        scratch_shapes=[pltpu.VMEM((groups * take, C), jnp.float32)],
        compiler_params=pltpu.CompilerParams(vmem_limit_bytes=VMEM_LIMIT),
        name="merge",
    )(keep, came)


def sum_kernel(take, blocks, out):
    groups, held, _ = blocks.shape
    total = jnp.zeros((take, C), jnp.float32)
    for p in range(groups):
        total += blocks[p, pl.ds(0, take)] * jnp.exp2(blocks[p, pl.ds(take, 1)] - 14.0)
    power = power_of(total)
    total = total * jnp.exp2(14.0 - power)
    for p in range(groups):
        out[p, pl.ds(0, take)] = total
        out[p, pl.ds(take, held - take)] = jnp.broadcast_to(power, (held - take, C))


def sum_blocks(take, blocks):
    return pl.pallas_call(
        lambda *refs: sum_kernel(take, *refs),
        out_shape=jax.ShapeDtypeStruct(blocks.shape, jnp.float32),
        in_specs=[vmem()],
        out_specs=vmem(),
        compiler_params=pltpu.CompilerParams(vmem_limit_bytes=VMEM_LIMIT),
        name="sum_blocks",
    )(blocks)


def decode_kernel(take, scale, own, blocks, *refs):
    out, half, sems = refs[-3:]
    groups = blocks.shape[0]
    core = parity("gy")
    target = out.at[core if own else 1 - core]
    copies = []
    done = 0
    for p in range(groups):
        rows = min(take, HALF - p * take)
        if rows > 0:
            factor = jnp.exp2(blocks[p, pl.ds(take, 1)] - 14.0) * scale
            half[pl.ds(p * take, rows)] = blocks[p, pl.ds(0, rows)] * factor
        ready = min((p + 1) * take, HALF)
        if ready - done >= HALF // 4 and ready % 8 == 0 or p == groups - 1:
            piece = pl.ds(done, ready - done)
            copies += fetching((half.at[piece], target.at[piece], sems.at[len(copies)]))
            done = ready
    for copy in copies:
        copy.wait()


def decode(take, scale, blocks, begun=None):
    rest = () if begun is None else (begun,)
    return pl.pallas_call(
        lambda *refs: decode_kernel(take, scale, not rest, *refs),
        out_shape=jax.ShapeDtypeStruct((2, HALF, C), jnp.float32),
        in_specs=[vmem()] + [hbm()] * len(rest),
        out_specs=hbm(),
        scratch_shapes=[pltpu.VMEM((HALF, C), jnp.float32), pltpu.SemaphoreType.DMA((5,))],
        input_output_aliases={1: 0} if rest else {},
        compiler_params=pltpu.CompilerParams(vmem_limit_bytes=VMEM_LIMIT),
        name="decode_other" if rest else "decode_own",
    )(blocks, *rest)


def product_kernel(f, near_hbm, mask_ref, kernel_ref, bricks, x_ref, y_ref, e0, e1, out, *refs):
    lx, ly, corners, wide, near, sem, v, *flipped = refs
    (table,) = fetching((near_hbm, near, sem))
    weights = kernel_ref
    if f == 1:
        weights = flipped[0]
        for o in range(27):
            weights[pl.ds((26 - o) * C, C)] = kernel_ref[pl.ds(o * C, C)].T
    fill_own(bricks, lx, ly, corners)
    fill_came(f, x_ref, y_ref, (e0, e1), lx, ly, corners)
    table.wait()

    def per_slot(s, carry):
        build_columns(s, bricks, near, lx, ly, corners, wide, "all")
        stack_columns(s, wide, v)
        total = jnp.zeros((512, C), jnp.float32)
        for x in range(3):
            cells = v[s, pl.ds(x, 8)].reshape(512, 9 * C)
            total += jnp.dot(cells, weights[pl.ds(x * 9 * C, 9 * C)], preferred_element_type=jnp.float32)
        out[s] = (total * mask_columns(mask_ref, s)).astype(jnp.bfloat16)
        return carry

    lax.fori_loop(0, SLOTS, per_slot, 0)


def product(f, near, mask, kernel, bricks, x_came, y_came, edges):
    return pl.pallas_call(
        lambda *refs: product_kernel(f, *refs),
        out_shape=jax.ShapeDtypeStruct((SLOTS, 512, C), jnp.bfloat16),
        in_specs=[hbm()] + [vmem()] * 7,
        out_specs=vmem(),
        scratch_shapes=columns_scratch()
        + [pltpu.VMEM((SLOTS, 10, 64, 9 * C), jnp.bfloat16)]
        + ([pltpu.VMEM((ROWS, C), jnp.bfloat16)] if f else []),
        compiler_params=pltpu.CompilerParams(vmem_limit_bytes=VMEM_LIMIT),
        cost_estimate=pl.CostEstimate(flops=2 * 2048 * ROWS * C, bytes_accessed=4 << 20, transcendentals=0),
        name=("output_product", "input_grad_product")[f],
    )(near, mask, kernel, bricks, x_came, y_came, *edges)


def swapped(value, axis, k):
    pairs = []
    for low in range(k, lax.axis_size(axis) - 1, 2):
        pairs += [(low, low + 1), (low + 1, low)]
    return lax.ppermute(value, axis, pairs)


def hopped(value, axis):
    size = lax.axis_size(axis)
    pairs = [(i, i + 2) for i in range(1, size - 2, 2)] + [(i, i - 2) for i in range(2, size, 2)]
    return lax.ppermute(value, axis, pairs)


def local(features, out_grad, kernel, voxel_mask, neighbours, face_sends, edge_sends):
    size_x, size_y = lax.axis_size("gx"), lax.axis_size("gy")
    parts = size_x * size_y
    groups = parts // 2
    take = -(-HALF // groups)
    held = -(-(take + 1) // 16) * 16
    order = [(i + parts // 2) % parts for i in range(parts)]
    same_core = [[i for i in order if i % size_y % 2 == core] for core in range(2)]

    def spread(blocks):
        return lax.all_to_all(blocks, ("gx", "gy"), 0, 0, axis_index_groups=same_core, tiled=True)

    held_act, act, grd, table, y0, y1, x0, x1 = pack(
        features.reshape(SLOTS, 512, C),
        out_grad.reshape(SLOTS, 512, C),
        voxel_mask,
        neighbours,
        face_sends,
        edge_sends,
    )
    y1 = hopped(y1, "gy")
    x1 = hopped(x1, "gx")
    v = own_columns(table, held_act)
    x1, v = lax.optimization_barrier((x1, v))
    x_came, x_more = join(x0, x1)
    x_more, v = lax.optimization_barrier((x_more, v))
    x_came = swapped(x_came, "gx", 0)
    inner = inner_terms(v, grd)
    inner, y1 = lax.optimization_barrier((inner, y1))
    y_came, y_more = join(y0, y1)
    y_came = swapped(y_came, "gy", 0)
    keep, send = rim_terms(neighbours, inner, grd, x_came, y_came)
    blocks = merge(groups, take, held, keep, swapped(send, "gy", 0)).astype(jnp.float16)
    rows = kernel.reshape(ROWS, C)
    blocks, act, x_came, x_more, y_more = lax.optimization_barrier((blocks, act, x_came, x_more, y_more))
    x_more, y_more = swapped(x_more, "gx", 0), swapped(y_more, "gy", 0)
    e0, e1 = forward_corners(x_came)
    edges = [swapped(e0, "gy", 0), swapped(e1, "gy", 1)]
    output = product(0, neighbours, voxel_mask, rows, act, x_came, y_came, edges)
    arrived, output, x_more, y_more = lax.optimization_barrier((spread(blocks), output, x_more, y_more))
    copies = sum_blocks(take, arrived.astype(jnp.float32)).astype(jnp.float16)
    copies, grd = lax.optimization_barrier((copies, grd))
    input_grad = product(1, neighbours, voxel_mask, rows, grd, x_more, y_more, edges)
    mine, input_grad = lax.optimization_barrier((spread(copies), input_grad))
    other = swapped(mine, "gy", 0)
    scale = 1.0 / math.sqrt(parts * SLOTS * 512)
    weight = decode(take, scale, mine.astype(jnp.float32))
    weight = decode(take, scale, other.astype(jnp.float32), weight)
    shape = (SLOTS, 8, 8, 8, C)
    return output.reshape(shape), input_grad.reshape(shape), weight.reshape(27, C, C)


def solution(mesh):
    spec = P(("gx", "gy"))
    return jax.shard_map(
        local,
        mesh=mesh,
        in_specs=(spec, spec, P(), spec, spec, spec, spec),
        out_specs=(spec, spec, P()),
        check_vma=False,
    )
```

```python
import math

import jax
import jax.numpy as jnp
from jax import lax
from jax.experimental import pallas as pl
from jax.experimental.pallas import tpu as pltpu
from jax.sharding import PartitionSpec as P

FACES = ((-1, 0), (1, 0), (0, -1), (0, 1))
EDGES = ((-1, -1), (-1, 1), (1, -1), (1, 1))
C = 128
SLOTS = 4
FACE = 2
ZERO = SLOTS + 4 * FACE + 4
ROWS = 27 * C
FACE_ROWS = FACE * 64
X_ROWS = FACE_ROWS + 64
Y_ROWS = FACE_ROWS + 48
HALF = ROWS // 2
VMEM_LIMIT = 32 * 1024 * 1024
PACK_LIMIT = 60 * 1024 * 1024
ROOM_BRICKS = 48
ROOM_TABLES = 12 * 1024


def vmem():
    return pl.BlockSpec(memory_space=pltpu.VMEM)


def hbm():
    return pl.BlockSpec(memory_space=pltpu.HBM)


def fetching(*pairs):
    copies = [pltpu.make_async_copy(src, dst, sem) for src, dst, sem in pairs]
    for copy in copies:
        copy.start()
    return copies


def fetched(*pairs):
    for copy in fetching(*pairs):
        copy.wait()


def mask_columns(mask_ref, s):
    m = mask_ref[...].astype(jnp.float32).astype(jnp.bfloat16)
    pick = (lax.broadcasted_iota(jnp.int32, (SLOTS, C), 0) == s).astype(jnp.float32).astype(jnp.bfloat16)
    return lax.dot_general(m, pick, (((0,), (0,)), ((), ())), preferred_element_type=jnp.float32)


def parity(axis):
    return lax.rem(lax.axis_index(axis), 2)


def side_of(k, odd):
    return 1 - odd if k == 0 else odd


def shifts(cells, same, below, above):
    line = lax.broadcasted_iota(jnp.int32, cells.shape, cells.ndim - 2)
    axis = cells.ndim - 2
    up = jnp.where((same & (line >= 1)) | (below & (line == 0)), pltpu.roll(cells, 1, axis), 0.0)
    down = jnp.where((same & (line <= 6)) | (above & (line == 7)), pltpu.roll(cells, 7, axis), 0.0)
    return up, jnp.where(same, cells, 0.0), down


def pack_kernel(face_hbm, edge_hbm, near_hbm, feat_hbm, grad_hbm, mask_hbm, act_out, grd_out, near_out, *refs):
    sends = refs[0:4]
    y_out, x_out = refs[4:6], refs[6:8]
    face_ref, edge_ref, near, raw, mask_ref, full, sems = refs[8:]
    got_mask, got_feat, got_grad, *tables = fetching(
        (mask_hbm, mask_ref, sems.at[0]),
        (feat_hbm, raw.at[0], sems.at[1]),
        (grad_hbm, raw.at[1], sems.at[2]),
        (face_hbm, face_ref, sems.at[3]),
        (edge_hbm, edge_ref, sems.at[4]),
        (near_hbm, near, sems.at[5]),
    )
    got_mask.wait()
    got_feat.wait()
    got_grad.wait()
    for s in range(SLOTS):
        rows = mask_columns(mask_ref, s)
        for f in range(2):
            masked = raw[f, s].astype(jnp.float32) * rows
            full[f, s] = masked.reshape(8, 8, 8, C)
            raw[f, s] = masked.astype(jnp.bfloat16)
    results = fetching(
        (raw.at[0], act_out.at[0], sems.at[7]),
        (raw.at[1], grd_out, sems.at[9]),
    )
    for table in tables:
        table.wait()
    results += fetching((near, near_out.at[0], sems.at[6]))
    for axis, outs in enumerate((x_out, y_out)):
        odd = parity("gy" if axis else "gx")
        for k in range(2):
            side = side_of(k, odd)
            for f in range(2):
                for r in range(FACE):
                    entry = face_ref[r, 2 * axis + side]
                    slot = jnp.clip(entry, 0, SLOTS - 1)
                    layer = full[f, slot, :, 7 * side] if axis else full[f, slot, 7 * side]
                    layer = jnp.where(entry < SLOTS, layer, 0.0)
                    first = f * (Y_ROWS if axis else X_ROWS) + r * 64
                    outs[k][pl.ds(first, 64)] = layer.reshape(64, C).astype(jnp.bfloat16)
            lines = []
            for far in range(2):
                corner = 2 * far + side if axis else 2 * side + far
                entry = edge_ref[0, corner]
                slot = jnp.clip(entry, 0, SLOTS - 1)
                live = entry < SLOTS
                at_x, at_y = (7 * far, 7 * side) if axis else (7 * side, 7 * far)
                if axis == 0:
                    for f in range(2):
                        lines.append(jnp.where(live, full[f, slot, at_x, at_y], 0.0))
                    continue
                base = 18 * far + 6 * side
                low, mid, high = near[slot, base], near[slot, base + 1], near[slot, base + 2]
                up, same, down = shifts(
                    full[1, slot, at_x, at_y],
                    live & (mid < ZERO),
                    live & (high < ZERO),
                    live & (low < ZERO),
                )
                lines += [down, same, up]
            if axis == 0:
                lines.append(jnp.zeros((32, C), jnp.float32))
            lines = jnp.concatenate(lines, axis=0).astype(jnp.bfloat16)
            outs[k][pl.ds(FACE_ROWS, lines.shape[0])] = lines
    for i, (built, send) in enumerate(zip(refs[4:8], sends)):
        results += fetching((built, send, sems.at[10 + i]))
    for result in results:
        result.wait()


def pack(features, out_grad, mask, near, face_sends, edge_sends):
    sends = [
        jax.ShapeDtypeStruct((rows + FACE_ROWS, C), jnp.bfloat16) for rows in (Y_ROWS, Y_ROWS, X_ROWS, X_ROWS)
    ]
    return pl.pallas_call(
        pack_kernel,
        out_shape=[
            jax.ShapeDtypeStruct((ROOM_BRICKS, SLOTS, 512, C), jnp.bfloat16),
            jax.ShapeDtypeStruct((SLOTS, 512, C), jnp.bfloat16),
            jax.ShapeDtypeStruct((ROOM_TABLES, SLOTS, 27), jnp.int32),
        ]
        + sends,
        in_specs=[hbm()] * 6,
        out_specs=[hbm()] * 7,
        scratch_shapes=[pltpu.VMEM(send.shape, send.dtype) for send in sends]
        + [
            pltpu.SMEM((FACE, 4), jnp.int32),
            pltpu.SMEM((1, 4), jnp.int32),
            pltpu.SMEM((SLOTS, 27), jnp.int32),
            pltpu.VMEM((2, SLOTS, 512, C), jnp.bfloat16),
            pltpu.VMEM((SLOTS, 512), jnp.int32),
            pltpu.VMEM((2, SLOTS, 8, 8, 8, C), jnp.float32),
            pltpu.SemaphoreType.DMA((14,)),
        ],
        compiler_params=pltpu.CompilerParams(vmem_limit_bytes=PACK_LIMIT),
        name="pack",
    )(face_sends.T, edge_sends.T, near, features, out_grad, mask)


def parts_of(ref):
    rows = ref.shape[0] // 2
    return ref.at[pl.ds(0, rows)], ref.at[pl.ds(rows, rows)]


def join_kernel(first, second, out, more):
    rows = first.shape[0] - FACE_ROWS
    for k, src in enumerate((first, second)):
        out[pl.ds(k * rows, rows)] = src[pl.ds(0, rows)]
        more[pl.ds(k * FACE_ROWS, FACE_ROWS)] = src[pl.ds(rows, FACE_ROWS)]


def join(first, second):
    outs = [
        jax.ShapeDtypeStruct((2 * rows, C), jnp.bfloat16) for rows in (first.shape[0] - FACE_ROWS, FACE_ROWS)
    ]
    return pl.pallas_call(
        join_kernel,
        out_shape=outs,
        in_specs=[vmem()] * 2,
        out_specs=[vmem()] * 2,
        compiler_params=pltpu.CompilerParams(vmem_limit_bytes=VMEM_LIMIT),
        name="join_sides",
    )(first, second)


def forward_kernel(x_came, out0, out1):
    odd_x, odd_y = parity("gx"), parity("gy")
    for k, out in enumerate((out0, out1)):
        far = side_of(k, odd_y)
        for j, came in enumerate(parts_of(x_came)):
            source = side_of(j, odd_x)
            rows = came[pl.ds(pl.multiple_of(FACE_ROWS + 16 * far, 16), 16)]
            out[pl.ds(pl.multiple_of(16 * source, 16), 16)] = rows


def forward_corners(x_came):
    send = jax.ShapeDtypeStruct((32, C), jnp.bfloat16)
    return pl.pallas_call(
        forward_kernel,
        out_shape=[send] * 2,
        in_specs=[vmem()],
        out_specs=[vmem()] * 2,
        compiler_params=pltpu.CompilerParams(vmem_limit_bytes=VMEM_LIMIT),
        name="forward_corners",
    )(x_came)


def fill_own(bricks, lx, ly, corners):
    for s in range(SLOTS):
        whole = bricks[s].astype(jnp.float32).reshape(8, 8, 8, C)
        for side, at in ((0, 7), (1, 0)):
            lx[side, s] = whole[at]
            ly[side, s] = whole[:, at]
            for other, far in ((0, 7), (1, 0)):
                corners[2 * side + other, s] = whole[at, far]


def fill_zero(lx, ly, corners, first):
    for ref in (lx, ly, corners):
        count = ref.shape[1] - first
        ref[:, pl.ds(first, count)] = jnp.zeros((ref.shape[0], count) + ref.shape[2:], jnp.float32)


def fill_came(f, x_came, y_came, edges, lx, ly, corners):
    odd_x, odd_y = parity("gx"), parity("gy")
    for came, odd, dst in ((x_came, odd_x, lx), (y_came, odd_y, ly)):
        for k, part in enumerate(parts_of(came)):
            side = side_of(k, odd)
            for r in range(FACE):
                rows = part[pl.ds(r * 64, 64)]
                dst[side, SLOTS + r] = rows.astype(jnp.float32).reshape(8, 8, C)
            dst[k, SLOTS + FACE] = jnp.zeros((8, 8, C), jnp.float32)
    for k, came in enumerate(edges):
        side = side_of(k, odd_y)
        for j in range(2):
            rows = came[pl.ds(16 * j, 16)].astype(jnp.float32)
            corners[2 * j + side, SLOTS + 2 * FACE] = rows[8 * f : 8 * f + 8]
    for sx in range(2):
        for sy in range(2):
            c = 2 * sx + sy
            for r in range(FACE):
                corners[c, SLOTS + r] = lx[sx, SLOTS + r, 0 if sy else 7]
                corners[c, SLOTS + FACE + r] = ly[sy, SLOTS + r, 0 if sx else 7]
            corners[c, SLOTS + 2 * FACE + 1] = jnp.zeros((8, C), jnp.float32)


def build_columns(s, bricks, near, lx, ly, corners, wide, which):
    def spread(cells, at_x, at_y, depth):
        flat = cells.reshape(-1, 8, C)
        for k, moved in enumerate(shifts(flat, depth == 0, depth == -1, depth == 1)):
            wide[k, at_x, at_y] = moved.reshape(cells.shape)

    def column(nx, ny):
        base = 9 * (nx + 1) + 3 * (ny + 1)
        low, mid, high = near[s, base], near[s, base + 1], near[s, base + 2]
        entry = jnp.minimum(jnp.minimum(low, mid), high)
        depth = jnp.where(low < ZERO, -1, jnp.where(high < ZERO, 1, 0))
        if which == "own":
            depth = jnp.where(entry < SLOTS, depth, 2)
        if which == "rim":
            depth = jnp.where((entry >= SLOTS) & (entry < SLOTS + 4 * FACE), depth, 2)
        return entry, depth

    middle = pl.ds(1, 8)
    if which != "rim":
        spread(bricks[s].astype(jnp.float32).reshape(8, 8, 8, C), middle, middle, 0)
    for side, n in ((0, -1), (1, 1)):
        edge_at = pl.ds(0 if n < 0 else 9, 1)
        entry, depth = column(n, 0)
        place = jnp.where(entry < SLOTS, entry, jnp.clip(entry - FACE * side, 0, SLOTS + FACE))
        spread(lx[side, place].reshape(1, 8, 8, C), edge_at, middle, depth)
        entry, depth = column(0, n)
        place = jnp.where(entry < SLOTS, entry, jnp.clip(entry - FACE * (2 + side), 0, SLOTS + FACE))
        spread(ly[side, place].reshape(8, 1, 8, C), middle, edge_at, depth)
    for sx in range(2):
        for sy in range(2):
            entry, depth = column(2 * sx - 1, 2 * sy - 1)
            first_x = SLOTS + FACE * sx
            first_y = SLOTS + FACE * (2 + sy)
            own_edge = SLOTS + 4 * FACE + 2 * sx + sy
            in_x = (entry >= first_x) & (entry < first_x + FACE)
            in_y = (entry >= first_y) & (entry < first_y + FACE)
            place = jnp.where(entry == own_edge, SLOTS + 2 * FACE, SLOTS + 2 * FACE + 1)
            place = jnp.where(in_y, SLOTS + FACE + entry - first_y, place)
            place = jnp.where(in_x, SLOTS + entry - first_x, place)
            place = jnp.where(entry < SLOTS, entry, place)
            spread(corners[2 * sx + sy, place].reshape(1, 1, 8, C), pl.ds(9 * sx, 1), pl.ds(9 * sy, 1), depth)


def stack_columns(s, wide, v):
    for y in range(3):
        for z in range(3):
            cells = wide[z, :, pl.ds(y, 8)].reshape(10, 64, C).astype(jnp.bfloat16)
            v[s, :, :, pl.ds((3 * y + z) * C, C)] = cells


def columns_scratch():
    return [
        pltpu.VMEM((2, SLOTS + FACE + 1, 8, 8, C), jnp.float32),
        pltpu.VMEM((2, SLOTS + FACE + 1, 8, 8, C), jnp.float32),
        pltpu.VMEM((4, SLOTS + 2 * FACE + 2, 8, C), jnp.float32),
        pltpu.VMEM((3, 10, 10, 8, C), jnp.float32),
        pltpu.SMEM((SLOTS, 27), jnp.int32),
        pltpu.SemaphoreType.DMA(()),
    ]


def columns_kernel(near_hbm, act_hbm, v, lx, ly, corners, wide, near, sem, act, act_sem):
    table, bricks = fetching((near_hbm.at[0], near, sem), (act_hbm.at[0], act, act_sem))
    fill_zero(lx, ly, corners, SLOTS)
    bricks.wait()
    fill_own(act, lx, ly, corners)
    table.wait()

    def per_slot(s, carry):
        build_columns(s, act, near, lx, ly, corners, wide, "own")
        stack_columns(s, wide, v)
        return carry

    lax.fori_loop(0, SLOTS, per_slot, 0)


def own_columns(near, act):
    return pl.pallas_call(
        columns_kernel,
        out_shape=jax.ShapeDtypeStruct((SLOTS, 10, 64, 9 * C), jnp.bfloat16),
        in_specs=[hbm()] * 2,
        out_specs=vmem(),
        scratch_shapes=columns_scratch()
        + [pltpu.VMEM((SLOTS, 512, C), jnp.bfloat16), pltpu.SemaphoreType.DMA(())],
        compiler_params=pltpu.CompilerParams(vmem_limit_bytes=VMEM_LIMIT),
        cost_estimate=pl.CostEstimate(flops=1 << 24, bytes_accessed=6 << 20, transcendentals=0),
        name="own_columns",
    )(near, act)


def inner_kernel(v, grd, out, turned):
    for s in range(SLOTS):
        for q in range(4):
            turned[:, pl.ds((4 * s + q) * C, C)] = grd[s, pl.ds(q * C, C)].T
    for x in range(3):
        cells = v[:, pl.ds(x, 8)].reshape(SLOTS * 512, 9 * C)
        terms = jnp.dot(turned[...], cells, preferred_element_type=jnp.float32)
        for j in range(9):
            out[pl.ds((9 * x + j) * C, C)] = terms[:, j * C : (j + 1) * C].T


def inner_terms(v, grd):
    return pl.pallas_call(
        inner_kernel,
        out_shape=jax.ShapeDtypeStruct((ROWS, C), jnp.float32),
        in_specs=[vmem()] * 2,
        out_specs=vmem(),
        scratch_shapes=[pltpu.VMEM((C, SLOTS * 512), jnp.bfloat16)],
        compiler_params=pltpu.CompilerParams(vmem_limit_bytes=VMEM_LIMIT),
        cost_estimate=pl.CostEstimate(flops=2 * 2048 * ROWS * C, bytes_accessed=6 << 20, transcendentals=0),
        name="inner_terms",
    )(v, grd)


def rim_kernel(near_hbm, inner, grd, x_ref, y_ref, keep, send, lx, ly, corners, wide, near, sem, *refs):
    vx, vy, ends_a, ends_g, side_x, side_y = refs
    (table,) = fetching((near_hbm, near, sem))
    fill_came(0, x_ref, y_ref, (), lx, ly, corners)
    for k, came in enumerate(parts_of(x_ref)):
        side = side_of(k, parity("gx"))
        for j in range(2):
            ends_a[side, j] = came[pl.ds(FACE_ROWS + 16 * j, 16)].astype(jnp.float32)[0:8]
    for k, came in enumerate(parts_of(y_ref)):
        side = side_of(k, parity("gy"))
        ends_g[side] = came[pl.ds(FACE_ROWS, 48)].astype(jnp.float32).reshape(2, 3, 8, C)
    table.wait()
    for s in range(SLOTS):
        build_columns(s, None, near, lx, ly, corners, wide, "rim")
        rows = pl.ds(64 * s, 64)
        for side in range(2):
            for j in range(9):
                cells = wide[j % 3, 9 * side, pl.ds(j // 3, 8)]
                vx[side, rows, pl.ds(j * C, C)] = cells.reshape(64, C).astype(jnp.bfloat16)
        for z in range(3):
            for sx in range(2):
                for sy in range(2):
                    wide[z, 9 * sx, 9 * sy] = jnp.zeros((8, C), jnp.float32)
        for side in range(2):
            for j in range(9):
                cells = wide[j % 3, pl.ds(j // 3, 8), 9 * side]
                vy[side, rows, pl.ds(j * C, C)] = cells.reshape(64, C).astype(jnp.bfloat16)
    grads = grd[...]
    lines = grads.astype(jnp.float32).reshape(SLOTS, 8, 8, 8, C)

    def term(cells, rows):
        return lax.dot_general(cells, rows, (((0,), (0,)), ((), ())), preferred_element_type=jnp.float32)

    def end(line):
        return jnp.concatenate([line, jnp.zeros((8, C), jnp.float32)], axis=0).astype(jnp.bfloat16)

    for side in range(2):
        rows = grads[:, 448 * side : 448 * side + 64].reshape(SLOTS * 64, C)
        side_x[side] = term(vx[side], rows)
        rows = lines[:, :, 7 * side].reshape(SLOTS * 64, C).astype(jnp.bfloat16)
        side_y[side] = term(vy[side], rows)
    def write(halves):
        for x in range(3):
            for y in range(3):
                for z in range(3):
                    first = (9 * x + 3 * y + z) * C
                    value = inner[pl.ds(first, C)]
                    if x != 1:
                        value += side_x[x // 2, pl.ds((3 * y + z) * C, C)]
                    if y != 1:
                        value += side_y[y // 2, pl.ds((3 * x + z) * C, C)]
                    if x != 1 and y != 1:
                        sx, sy = x // 2, 1 - y // 2
                        value += term(end(ends_a[sx, sy]), end(ends_g[sy, sx, z]))
                    for half in range(2):
                        low = max(first, half * HALF)
                        rows = min(first + C, (half + 1) * HALF) - low
                        if rows > 0:
                            halves[half][pl.ds(low - half * HALF, rows)] = value[low - first : low - first + rows]

    core = parity("gy")

    @pl.when(core == 0)
    def _():
        write((keep, send))

    @pl.when(core == 1)
    def _():
        write((send, keep))


def rim_terms(near, inner, grd, x_came, y_came):
    half = jax.ShapeDtypeStruct((HALF, C), jnp.float32)
    side = pltpu.VMEM((2, SLOTS * 64, 9 * C), jnp.bfloat16)
    return pl.pallas_call(
        rim_kernel,
        out_shape=[half, half],
        in_specs=[hbm()] + [vmem()] * 4,
        out_specs=[vmem()] * 2,
        scratch_shapes=columns_scratch()
        + [
            side,
            side,
            pltpu.VMEM((2, 2, 8, C), jnp.float32),
            pltpu.VMEM((2, 2, 3, 8, C), jnp.float32),
            pltpu.VMEM((2, 9 * C, C), jnp.float32),
            pltpu.VMEM((2, 9 * C, C), jnp.float32),
        ],
        compiler_params=pltpu.CompilerParams(vmem_limit_bytes=VMEM_LIMIT),
        cost_estimate=pl.CostEstimate(flops=2 * 256 * 36 * C * C, bytes_accessed=6 << 20, transcendentals=0),
        name="rim_terms",
    )(near, inner, grd, x_came, y_came)


def power_of(values):
    peak = jnp.max(jnp.abs(values))
    return jnp.clip(jnp.ceil(jnp.log2(jnp.full((8, C), peak))), -100.0, 100.0)[0:1]


def merge_kernel(groups, take, keep, came, out, total):
    held = out.shape[1]
    total[pl.ds(0, HALF)] = keep[...] + came[...]
    if groups * take > HALF:
        total[pl.ds(HALF, groups * take - HALF)] = jnp.zeros((groups * take - HALF, C), jnp.float32)
    power = power_of(total[...])
    scale = jnp.exp2(14.0 - power)
    for p in range(groups):
        out[p, pl.ds(0, take)] = total[pl.ds(p * take, take)] * scale
        out[p, pl.ds(take, held - take)] = jnp.broadcast_to(power, (held - take, C))


def merge(groups, take, held, keep, came):
    return pl.pallas_call(
        lambda *refs: merge_kernel(groups, take, *refs),
        out_shape=jax.ShapeDtypeStruct((groups, held, C), jnp.float32),
        in_specs=[vmem()] * 2,
        out_specs=vmem(),
        scratch_shapes=[pltpu.VMEM((groups * take, C), jnp.float32)],
        compiler_params=pltpu.CompilerParams(vmem_limit_bytes=VMEM_LIMIT),
        name="merge",
    )(keep, came)


def sum_kernel(take, blocks, out):
    groups, held, _ = blocks.shape
    total = jnp.zeros((take, C), jnp.float32)
    for p in range(groups):
        total += blocks[p, pl.ds(0, take)] * jnp.exp2(blocks[p, pl.ds(take, 1)] - 14.0)
    power = power_of(total)
    total = total * jnp.exp2(14.0 - power)
    for p in range(groups):
        out[p, pl.ds(0, take)] = total
        out[p, pl.ds(take, held - take)] = jnp.broadcast_to(power, (held - take, C))


def sum_blocks(take, blocks):
    return pl.pallas_call(
        lambda *refs: sum_kernel(take, *refs),
        out_shape=jax.ShapeDtypeStruct(blocks.shape, jnp.float32),
        in_specs=[vmem()],
        out_specs=vmem(),
        compiler_params=pltpu.CompilerParams(vmem_limit_bytes=VMEM_LIMIT),
        name="sum_blocks",
    )(blocks)


def decode_kernel(take, scale, own, blocks, *refs):
    out, half, sems = refs[-3:]
    groups = blocks.shape[0]
    core = parity("gy")
    target = out.at[core if own else 1 - core]
    copies = []
    done = 0
    for p in range(groups):
        rows = min(take, HALF - p * take)
        if rows > 0:
            factor = jnp.exp2(blocks[p, pl.ds(take, 1)] - 14.0) * scale
            half[pl.ds(p * take, rows)] = blocks[p, pl.ds(0, rows)] * factor
        ready = min((p + 1) * take, HALF)
        if ready - done >= HALF // 4 and ready % 8 == 0 or p == groups - 1:
            piece = pl.ds(done, ready - done)
            copies += fetching((half.at[piece], target.at[piece], sems.at[len(copies)]))
            done = ready
    for copy in copies:
        copy.wait()


def decode(take, scale, blocks, begun=None):
    rest = () if begun is None else (begun,)
    return pl.pallas_call(
        lambda *refs: decode_kernel(take, scale, not rest, *refs),
        out_shape=jax.ShapeDtypeStruct((2, HALF, C), jnp.float32),
        in_specs=[vmem()] + [hbm()] * len(rest),
        out_specs=hbm(),
        scratch_shapes=[pltpu.VMEM((HALF, C), jnp.float32), pltpu.SemaphoreType.DMA((5,))],
        input_output_aliases={1: 0} if rest else {},
        compiler_params=pltpu.CompilerParams(vmem_limit_bytes=VMEM_LIMIT),
        name="decode_other" if rest else "decode_own",
    )(blocks, *rest)


def product_kernel(f, near_hbm, mask_ref, kernel_ref, bricks, x_ref, y_ref, e0, e1, out, *refs):
    lx, ly, corners, wide, near, sem, v, *more = refs
    (table,) = fetching((near_hbm, near, sem))
    weights = kernel_ref
    if f == 0:
        fetched((bricks.at[0], more[0], more[1]))
        bricks = more[0]
    else:
        weights = more[0]
        for o in range(27):
            weights[pl.ds((26 - o) * C, C)] = kernel_ref[pl.ds(o * C, C)].T
    fill_own(bricks, lx, ly, corners)
    fill_came(f, x_ref, y_ref, (e0, e1), lx, ly, corners)
    table.wait()

    def per_slot(s, carry):
        build_columns(s, bricks, near, lx, ly, corners, wide, "all")
        stack_columns(s, wide, v)
        total = jnp.zeros((512, C), jnp.float32)
        for x in range(3):
            cells = v[s, pl.ds(x, 8)].reshape(512, 9 * C)
            total += jnp.dot(cells, weights[pl.ds(x * 9 * C, 9 * C)], preferred_element_type=jnp.float32)
        out[s] = (total * mask_columns(mask_ref, s)).astype(jnp.bfloat16)
        return carry

    lax.fori_loop(0, SLOTS, per_slot, 0)


def product(f, near, mask, kernel, bricks, x_came, y_came, edges):
    return pl.pallas_call(
        lambda *refs: product_kernel(f, *refs),
        out_shape=jax.ShapeDtypeStruct((SLOTS, 512, C), jnp.bfloat16),
        in_specs=[hbm()] + [vmem()] * 2 + [vmem() if f else hbm()] + [vmem()] * 4,
        out_specs=vmem(),
        scratch_shapes=columns_scratch()
        + [pltpu.VMEM((SLOTS, 10, 64, 9 * C), jnp.bfloat16)]
        + (
            [pltpu.VMEM((ROWS, C), jnp.bfloat16)]
            if f
            else [pltpu.VMEM((SLOTS, 512, C), jnp.bfloat16), pltpu.SemaphoreType.DMA(())]
        ),
        compiler_params=pltpu.CompilerParams(vmem_limit_bytes=VMEM_LIMIT),
        cost_estimate=pl.CostEstimate(flops=2 * 2048 * ROWS * C, bytes_accessed=4 << 20, transcendentals=0),
        name=("output_product", "input_grad_product")[f],
    )(near, mask, kernel, bricks, x_came, y_came, *edges)


def swapped(value, axis, k):
    pairs = []
    for low in range(k, lax.axis_size(axis) - 1, 2):
        pairs += [(low, low + 1), (low + 1, low)]
    return lax.ppermute(value, axis, pairs)


def hopped(value, axis):
    size = lax.axis_size(axis)
    pairs = [(i, i + 2) for i in range(1, size - 2, 2)] + [(i, i - 2) for i in range(2, size, 2)]
    return lax.ppermute(value, axis, pairs)


def local(features, out_grad, kernel, voxel_mask, neighbours, face_sends, edge_sends):
    size_x, size_y = lax.axis_size("gx"), lax.axis_size("gy")
    parts = size_x * size_y
    groups = parts // 2
    take = -(-HALF // groups)
    held = -(-(take + 1) // 16) * 16
    same_core = []
    for core in range(2):
        members = [i for i in range(parts) if i % size_y % 2 == core]
        low, high = members[: groups // 2], members[groups // 2 :]
        per_chip_row = size_y // 2
        low = [i for first in range(groups // 2 - per_chip_row, -1, -per_chip_row) for i in low[first : first + per_chip_row]]
        same_core.append([i for pair in zip(high, low) for i in pair])

    def spread(blocks):
        return lax.all_to_all(blocks, ("gx", "gy"), 0, 0, axis_index_groups=same_core, tiled=True)

    act, grd, table, y0, y1, x0, x1 = pack(
        features.reshape(SLOTS, 512, C),
        out_grad.reshape(SLOTS, 512, C),
        voxel_mask,
        neighbours,
        face_sends,
        edge_sends,
    )
    y1 = hopped(y1, "gy")
    x1 = hopped(x1, "gx")
    v = own_columns(table, act)
    x1, v = lax.optimization_barrier((x1, v))
    x_came, x_more = join(x0, x1)
    x_more, v = lax.optimization_barrier((x_more, v))
    x_came = swapped(x_came, "gx", 0)
    inner = inner_terms(v, grd)
    inner, y1 = lax.optimization_barrier((inner, y1))
    y_came, y_more = join(y0, y1)
    y_came = swapped(y_came, "gy", 0)
    keep, send = rim_terms(neighbours, inner, grd, x_came, y_came)
    blocks = merge(groups, take, held, keep, swapped(send, "gy", 0)).astype(jnp.float16)
    rows = kernel.reshape(ROWS, C)
    blocks, act, x_came, x_more, y_more = lax.optimization_barrier((blocks, act, x_came, x_more, y_more))
    x_more, y_more = swapped(x_more, "gx", 0), swapped(y_more, "gy", 0)
    e0, e1 = forward_corners(x_came)
    edges = [swapped(e0, "gy", 0), swapped(e1, "gy", 1)]
    output = product(0, neighbours, voxel_mask, rows, act, x_came, y_came, edges)
    arrived, output, x_more, y_more = lax.optimization_barrier((spread(blocks), output, x_more, y_more))
    copies = sum_blocks(take, arrived.astype(jnp.float32)).astype(jnp.float16)
    copies, grd = lax.optimization_barrier((copies, grd))
    input_grad = product(1, neighbours, voxel_mask, rows, grd, x_more, y_more, edges)
    mine, input_grad = lax.optimization_barrier((spread(copies), input_grad))
    other = swapped(mine, "gy", 0)
    scale = 1.0 / math.sqrt(parts * SLOTS * 512)
    weight = decode(take, scale, mine.astype(jnp.float32))
    weight = decode(take, scale, other.astype(jnp.float32), weight)
    shape = (SLOTS, 8, 8, 8, C)
    return output.reshape(shape), input_grad.reshape(shape), weight.reshape(27, C, C)


def solution(mesh):
    spec = P(("gx", "gy"))
    return jax.shard_map(
        local,
        mesh=mesh,
        in_specs=(spec, spec, P(), spec, spec, spec, spec),
        out_specs=(spec, spec, P()),
        check_vma=False,
    )
```

```python
import math

import jax
import jax.numpy as jnp
from jax import lax
from jax.experimental import pallas as pl
from jax.experimental.pallas import tpu as pltpu
from jax.sharding import PartitionSpec as P

FACES = ((-1, 0), (1, 0), (0, -1), (0, 1))
EDGES = ((-1, -1), (-1, 1), (1, -1), (1, 1))
C = 128
SLOTS = 4
FACE = 2
ZERO = SLOTS + 4 * FACE + 4
ROWS = 27 * C
FACE_ROWS = FACE * 64
X_ROWS = FACE_ROWS + 64
Y_ROWS = FACE_ROWS + 48
HALF = ROWS // 2
VMEM_LIMIT = 32 * 1024 * 1024
PACK_LIMIT = 60 * 1024 * 1024
ROOM_BRICKS = 48
ROOM_TABLES = 12 * 1024


def vmem():
    return pl.BlockSpec(memory_space=pltpu.VMEM)


def hbm():
    return pl.BlockSpec(memory_space=pltpu.HBM)


def fetching(*pairs):
    copies = [pltpu.make_async_copy(src, dst, sem) for src, dst, sem in pairs]
    for copy in copies:
        copy.start()
    return copies


def fetched(*pairs):
    for copy in fetching(*pairs):
        copy.wait()


def mask_columns(mask_ref, s):
    m = mask_ref[...].astype(jnp.float32).astype(jnp.bfloat16)
    pick = (lax.broadcasted_iota(jnp.int32, (SLOTS, C), 0) == s).astype(jnp.float32).astype(jnp.bfloat16)
    return lax.dot_general(m, pick, (((0,), (0,)), ((), ())), preferred_element_type=jnp.float32)


def parity(axis):
    return lax.rem(lax.axis_index(axis), 2)


def side_of(k, odd):
    return 1 - odd if k == 0 else odd


def shifts(cells, same, below, above):
    line = lax.broadcasted_iota(jnp.int32, cells.shape, cells.ndim - 2)
    axis = cells.ndim - 2
    up = jnp.where((same & (line >= 1)) | (below & (line == 0)), pltpu.roll(cells, 1, axis), 0.0)
    down = jnp.where((same & (line <= 6)) | (above & (line == 7)), pltpu.roll(cells, 7, axis), 0.0)
    return up, jnp.where(same, cells, 0.0), down


def pack_kernel(face_hbm, edge_hbm, near_hbm, feat_hbm, grad_hbm, mask_hbm, held_out, act_out, grd_out, near_out, *refs):
    sends = refs[0:4]
    y_out, x_out = refs[4:6], refs[6:8]
    face_ref, edge_ref, near, raw, mask_ref, full, sems = refs[8:]
    got_mask, got_feat, got_grad, *tables = fetching(
        (mask_hbm, mask_ref, sems.at[0]),
        (feat_hbm, raw.at[0], sems.at[1]),
        (grad_hbm, raw.at[1], sems.at[2]),
        (face_hbm, face_ref, sems.at[3]),
        (edge_hbm, edge_ref, sems.at[4]),
        (near_hbm, near, sems.at[5]),
    )
    got_mask.wait()
    got_feat.wait()
    got_grad.wait()
    for s in range(SLOTS):
        rows = mask_columns(mask_ref, s)
        for f in range(2):
            masked = raw[f, s].astype(jnp.float32) * rows
            full[f, s] = masked.reshape(8, 8, 8, C)
            raw[f, s] = masked.astype(jnp.bfloat16)
    results = fetching(
        (raw.at[0], held_out.at[0], sems.at[7]),
        (raw.at[0], act_out, sems.at[8]),
        (raw.at[1], grd_out, sems.at[9]),
    )
    for table in tables:
        table.wait()
    results += fetching((near, near_out.at[0], sems.at[6]))
    for axis, outs in enumerate((x_out, y_out)):
        odd = parity("gy" if axis else "gx")
        for k in range(2):
            side = side_of(k, odd)
            for f in range(2):
                for r in range(FACE):
                    entry = face_ref[r, 2 * axis + side]
                    slot = jnp.clip(entry, 0, SLOTS - 1)
                    layer = full[f, slot, :, 7 * side] if axis else full[f, slot, 7 * side]
                    layer = jnp.where(entry < SLOTS, layer, 0.0)
                    first = f * (Y_ROWS if axis else X_ROWS) + r * 64
                    outs[k][pl.ds(first, 64)] = layer.reshape(64, C).astype(jnp.bfloat16)
            lines = []
            for far in range(2):
                corner = 2 * far + side if axis else 2 * side + far
                entry = edge_ref[0, corner]
                slot = jnp.clip(entry, 0, SLOTS - 1)
                live = entry < SLOTS
                at_x, at_y = (7 * far, 7 * side) if axis else (7 * side, 7 * far)
                if axis == 0:
                    for f in range(2):
                        lines.append(jnp.where(live, full[f, slot, at_x, at_y], 0.0))
                    continue
                base = 18 * far + 6 * side
                low, mid, high = near[slot, base], near[slot, base + 1], near[slot, base + 2]
                up, same, down = shifts(
                    full[1, slot, at_x, at_y],
                    live & (mid < ZERO),
                    live & (high < ZERO),
                    live & (low < ZERO),
                )
                lines += [down, same, up]
            if axis == 0:
                lines.append(jnp.zeros((32, C), jnp.float32))
            lines = jnp.concatenate(lines, axis=0).astype(jnp.bfloat16)
            outs[k][pl.ds(FACE_ROWS, lines.shape[0])] = lines
    for i, (built, send) in enumerate(zip(refs[4:8], sends)):
        results += fetching((built, send, sems.at[10 + i]))
    for result in results:
        result.wait()


def pack(features, out_grad, mask, near, face_sends, edge_sends):
    sends = [
        jax.ShapeDtypeStruct((rows + FACE_ROWS, C), jnp.bfloat16) for rows in (Y_ROWS, Y_ROWS, X_ROWS, X_ROWS)
    ]
    return pl.pallas_call(
        pack_kernel,
        out_shape=[
            jax.ShapeDtypeStruct((ROOM_BRICKS, SLOTS, 512, C), jnp.bfloat16),
            jax.ShapeDtypeStruct((SLOTS, 512, C), jnp.bfloat16),
            jax.ShapeDtypeStruct((SLOTS, 512, C), jnp.bfloat16),
            jax.ShapeDtypeStruct((ROOM_TABLES, SLOTS, 27), jnp.int32),
        ]
        + sends,
        in_specs=[hbm()] * 6,
        out_specs=[hbm()] * 8,
        scratch_shapes=[pltpu.VMEM(send.shape, send.dtype) for send in sends]
        + [
            pltpu.SMEM((FACE, 4), jnp.int32),
            pltpu.SMEM((1, 4), jnp.int32),
            pltpu.SMEM((SLOTS, 27), jnp.int32),
            pltpu.VMEM((2, SLOTS, 512, C), jnp.bfloat16),
            pltpu.VMEM((SLOTS, 512), jnp.int32),
            pltpu.VMEM((2, SLOTS, 8, 8, 8, C), jnp.float32),
            pltpu.SemaphoreType.DMA((14,)),
        ],
        compiler_params=pltpu.CompilerParams(vmem_limit_bytes=PACK_LIMIT),
        name="pack",
    )(face_sends.T, edge_sends.T, near, features, out_grad, mask)


def parts_of(ref):
    rows = ref.shape[0] // 2
    return ref.at[pl.ds(0, rows)], ref.at[pl.ds(rows, rows)]


def join_kernel(first, second, out, more):
    rows = first.shape[0] - FACE_ROWS
    for k, src in enumerate((first, second)):
        out[pl.ds(k * rows, rows)] = src[pl.ds(0, rows)]
        more[pl.ds(k * FACE_ROWS, FACE_ROWS)] = src[pl.ds(rows, FACE_ROWS)]


def join(first, second):
    outs = [
        jax.ShapeDtypeStruct((2 * rows, C), jnp.bfloat16) for rows in (first.shape[0] - FACE_ROWS, FACE_ROWS)
    ]
    return pl.pallas_call(
        join_kernel,
        out_shape=outs,
        in_specs=[vmem()] * 2,
        out_specs=[vmem()] * 2,
        compiler_params=pltpu.CompilerParams(vmem_limit_bytes=VMEM_LIMIT),
        name="join_sides",
    )(first, second)


def forward_kernel(x_came, out0, out1):
    odd_x, odd_y = parity("gx"), parity("gy")
    for k, out in enumerate((out0, out1)):
        far = side_of(k, odd_y)
        for j, came in enumerate(parts_of(x_came)):
            source = side_of(j, odd_x)
            rows = came[pl.ds(pl.multiple_of(FACE_ROWS + 16 * far, 16), 16)]
            out[pl.ds(pl.multiple_of(16 * source, 16), 16)] = rows


def forward_corners(x_came):
    send = jax.ShapeDtypeStruct((32, C), jnp.bfloat16)
    return pl.pallas_call(
        forward_kernel,
        out_shape=[send] * 2,
        in_specs=[vmem()],
        out_specs=[vmem()] * 2,
        compiler_params=pltpu.CompilerParams(vmem_limit_bytes=VMEM_LIMIT),
        name="forward_corners",
    )(x_came)


def fill_own(bricks, lx, ly, corners):
    for s in range(SLOTS):
        whole = bricks[s].astype(jnp.float32).reshape(8, 8, 8, C)
        for side, at in ((0, 7), (1, 0)):
            lx[side, s] = whole[at]
            ly[side, s] = whole[:, at]
            for other, far in ((0, 7), (1, 0)):
                corners[2 * side + other, s] = whole[at, far]


def fill_zero(lx, ly, corners, first):
    for ref in (lx, ly, corners):
        count = ref.shape[1] - first
        ref[:, pl.ds(first, count)] = jnp.zeros((ref.shape[0], count) + ref.shape[2:], jnp.float32)


def fill_came(f, x_came, y_came, edges, lx, ly, corners):
    odd_x, odd_y = parity("gx"), parity("gy")
    for came, odd, dst in ((x_came, odd_x, lx), (y_came, odd_y, ly)):
        for k, part in enumerate(parts_of(came)):
            side = side_of(k, odd)
            for r in range(FACE):
                rows = part[pl.ds(r * 64, 64)]
                dst[side, SLOTS + r] = rows.astype(jnp.float32).reshape(8, 8, C)
            dst[k, SLOTS + FACE] = jnp.zeros((8, 8, C), jnp.float32)
    for k, came in enumerate(edges):
        side = side_of(k, odd_y)
        for j in range(2):
            rows = came[pl.ds(16 * j, 16)].astype(jnp.float32)
            corners[2 * j + side, SLOTS + 2 * FACE] = rows[8 * f : 8 * f + 8]
    for sx in range(2):
        for sy in range(2):
            c = 2 * sx + sy
            for r in range(FACE):
                corners[c, SLOTS + r] = lx[sx, SLOTS + r, 0 if sy else 7]
                corners[c, SLOTS + FACE + r] = ly[sy, SLOTS + r, 0 if sx else 7]
            corners[c, SLOTS + 2 * FACE + 1] = jnp.zeros((8, C), jnp.float32)


def build_columns(s, bricks, near, lx, ly, corners, wide, which):
    def spread(cells, at_x, at_y, depth):
        flat = cells.reshape(-1, 8, C)
        for k, moved in enumerate(shifts(flat, depth == 0, depth == -1, depth == 1)):
            wide[k, at_x, at_y] = moved.reshape(cells.shape)

    def column(nx, ny):
        base = 9 * (nx + 1) + 3 * (ny + 1)
        low, mid, high = near[s, base], near[s, base + 1], near[s, base + 2]
        entry = jnp.minimum(jnp.minimum(low, mid), high)
        depth = jnp.where(low < ZERO, -1, jnp.where(high < ZERO, 1, 0))
        if which == "own":
            depth = jnp.where(entry < SLOTS, depth, 2)
        if which == "rim":
            depth = jnp.where((entry >= SLOTS) & (entry < SLOTS + 4 * FACE), depth, 2)
        return entry, depth

    middle = pl.ds(1, 8)
    if which != "rim":
        spread(bricks[s].astype(jnp.float32).reshape(8, 8, 8, C), middle, middle, 0)
    for side, n in ((0, -1), (1, 1)):
        edge_at = pl.ds(0 if n < 0 else 9, 1)
        entry, depth = column(n, 0)
        place = jnp.where(entry < SLOTS, entry, jnp.clip(entry - FACE * side, 0, SLOTS + FACE))
        spread(lx[side, place].reshape(1, 8, 8, C), edge_at, middle, depth)
        entry, depth = column(0, n)
        place = jnp.where(entry < SLOTS, entry, jnp.clip(entry - FACE * (2 + side), 0, SLOTS + FACE))
        spread(ly[side, place].reshape(8, 1, 8, C), middle, edge_at, depth)
    for sx in range(2):
        for sy in range(2):
            entry, depth = column(2 * sx - 1, 2 * sy - 1)
            first_x = SLOTS + FACE * sx
            first_y = SLOTS + FACE * (2 + sy)
            own_edge = SLOTS + 4 * FACE + 2 * sx + sy
            in_x = (entry >= first_x) & (entry < first_x + FACE)
            in_y = (entry >= first_y) & (entry < first_y + FACE)
            place = jnp.where(entry == own_edge, SLOTS + 2 * FACE, SLOTS + 2 * FACE + 1)
            place = jnp.where(in_y, SLOTS + FACE + entry - first_y, place)
            place = jnp.where(in_x, SLOTS + entry - first_x, place)
            place = jnp.where(entry < SLOTS, entry, place)
            spread(corners[2 * sx + sy, place].reshape(1, 1, 8, C), pl.ds(9 * sx, 1), pl.ds(9 * sy, 1), depth)


def stack_columns(s, wide, v):
    for y in range(3):
        for z in range(3):
            cells = wide[z, :, pl.ds(y, 8)].reshape(10, 64, C).astype(jnp.bfloat16)
            v[s, :, :, pl.ds((3 * y + z) * C, C)] = cells


def columns_scratch():
    return [
        pltpu.VMEM((2, SLOTS + FACE + 1, 8, 8, C), jnp.float32),
        pltpu.VMEM((2, SLOTS + FACE + 1, 8, 8, C), jnp.float32),
        pltpu.VMEM((4, SLOTS + 2 * FACE + 2, 8, C), jnp.float32),
        pltpu.VMEM((3, 10, 10, 8, C), jnp.float32),
        pltpu.SMEM((SLOTS, 27), jnp.int32),
        pltpu.SemaphoreType.DMA(()),
    ]


def columns_kernel(near_hbm, act_hbm, v, lx, ly, corners, wide, near, sem, act, act_sem):
    table, bricks = fetching((near_hbm.at[0], near, sem), (act_hbm.at[0], act, act_sem))
    fill_zero(lx, ly, corners, SLOTS)
    bricks.wait()
    fill_own(act, lx, ly, corners)
    table.wait()

    def per_slot(s, carry):
        build_columns(s, act, near, lx, ly, corners, wide, "own")
        stack_columns(s, wide, v)
        return carry

    lax.fori_loop(0, SLOTS, per_slot, 0)


def own_columns(near, act):
    return pl.pallas_call(
        columns_kernel,
        out_shape=jax.ShapeDtypeStruct((SLOTS, 10, 64, 9 * C), jnp.bfloat16),
        in_specs=[hbm()] * 2,
        out_specs=vmem(),
        scratch_shapes=columns_scratch()
        + [pltpu.VMEM((SLOTS, 512, C), jnp.bfloat16), pltpu.SemaphoreType.DMA(())],
        compiler_params=pltpu.CompilerParams(vmem_limit_bytes=VMEM_LIMIT),
        cost_estimate=pl.CostEstimate(flops=1 << 24, bytes_accessed=6 << 20, transcendentals=0),
        name="own_columns",
    )(near, act)


def inner_kernel(v, grd, out, turned):
    for s in range(SLOTS):
        for q in range(4):
            turned[:, pl.ds((4 * s + q) * C, C)] = grd[s, pl.ds(q * C, C)].T
    for x in range(3):
        cells = v[:, pl.ds(x, 8)].reshape(SLOTS * 512, 9 * C)
        terms = jnp.dot(turned[...], cells, preferred_element_type=jnp.float32)
        for j in range(9):
            out[pl.ds((9 * x + j) * C, C)] = terms[:, j * C : (j + 1) * C].T


def inner_terms(v, grd):
    return pl.pallas_call(
        inner_kernel,
        out_shape=jax.ShapeDtypeStruct((ROWS, C), jnp.float32),
        in_specs=[vmem()] * 2,
        out_specs=vmem(),
        scratch_shapes=[pltpu.VMEM((C, SLOTS * 512), jnp.bfloat16)],
        compiler_params=pltpu.CompilerParams(vmem_limit_bytes=VMEM_LIMIT),
        cost_estimate=pl.CostEstimate(flops=2 * 2048 * ROWS * C, bytes_accessed=6 << 20, transcendentals=0),
        name="inner_terms",
    )(v, grd)


def rim_kernel(near_hbm, inner, grd, x_ref, y_ref, keep, send, lx, ly, corners, wide, near, sem, *refs):
    vx, vy, ends_a, ends_g, side_x, side_y = refs
    (table,) = fetching((near_hbm, near, sem))
    fill_came(0, x_ref, y_ref, (), lx, ly, corners)
    for k, came in enumerate(parts_of(x_ref)):
        side = side_of(k, parity("gx"))
        for j in range(2):
            ends_a[side, j] = came[pl.ds(FACE_ROWS + 16 * j, 16)].astype(jnp.float32)[0:8]
    for k, came in enumerate(parts_of(y_ref)):
        side = side_of(k, parity("gy"))
        ends_g[side] = came[pl.ds(FACE_ROWS, 48)].astype(jnp.float32).reshape(2, 3, 8, C)
    table.wait()
    for s in range(SLOTS):
        build_columns(s, None, near, lx, ly, corners, wide, "rim")
        rows = pl.ds(64 * s, 64)
        for side in range(2):
            for j in range(9):
                cells = wide[j % 3, 9 * side, pl.ds(j // 3, 8)]
                vx[side, rows, pl.ds(j * C, C)] = cells.reshape(64, C).astype(jnp.bfloat16)
        for z in range(3):
            for sx in range(2):
                for sy in range(2):
                    wide[z, 9 * sx, 9 * sy] = jnp.zeros((8, C), jnp.float32)
        for side in range(2):
            for j in range(9):
                cells = wide[j % 3, pl.ds(j // 3, 8), 9 * side]
                vy[side, rows, pl.ds(j * C, C)] = cells.reshape(64, C).astype(jnp.bfloat16)
    grads = grd[...]
    lines = grads.astype(jnp.float32).reshape(SLOTS, 8, 8, 8, C)

    def term(cells, rows):
        return lax.dot_general(cells, rows, (((0,), (0,)), ((), ())), preferred_element_type=jnp.float32)

    def end(line):
        return jnp.concatenate([line, jnp.zeros((8, C), jnp.float32)], axis=0).astype(jnp.bfloat16)

    for side in range(2):
        rows = grads[:, 448 * side : 448 * side + 64].reshape(SLOTS * 64, C)
        side_x[side] = term(vx[side], rows)
        rows = lines[:, :, 7 * side].reshape(SLOTS * 64, C).astype(jnp.bfloat16)
        side_y[side] = term(vy[side], rows)
    def write(halves):
        for x in range(3):
            for y in range(3):
                for z in range(3):
                    first = (9 * x + 3 * y + z) * C
                    value = inner[pl.ds(first, C)]
                    if x != 1:
                        value += side_x[x // 2, pl.ds((3 * y + z) * C, C)]
                    if y != 1:
                        value += side_y[y // 2, pl.ds((3 * x + z) * C, C)]
                    if x != 1 and y != 1:
                        sx, sy = x // 2, 1 - y // 2
                        value += term(end(ends_a[sx, sy]), end(ends_g[sy, sx, z]))
                    for half in range(2):
                        low = max(first, half * HALF)
                        rows = min(first + C, (half + 1) * HALF) - low
                        if rows > 0:
                            halves[half][pl.ds(low - half * HALF, rows)] = value[low - first : low - first + rows]

    core = parity("gy")

    @pl.when(core == 0)
    def _():
        write((keep, send))

    @pl.when(core == 1)
    def _():
        write((send, keep))


def rim_terms(near, inner, grd, x_came, y_came):
    half = jax.ShapeDtypeStruct((HALF, C), jnp.float32)
    side = pltpu.VMEM((2, SLOTS * 64, 9 * C), jnp.bfloat16)
    return pl.pallas_call(
        rim_kernel,
        out_shape=[half, half],
        in_specs=[hbm()] + [vmem()] * 4,
        out_specs=[vmem()] * 2,
        scratch_shapes=columns_scratch()
        + [
            side,
            side,
            pltpu.VMEM((2, 2, 8, C), jnp.float32),
            pltpu.VMEM((2, 2, 3, 8, C), jnp.float32),
            pltpu.VMEM((2, 9 * C, C), jnp.float32),
            pltpu.VMEM((2, 9 * C, C), jnp.float32),
        ],
        compiler_params=pltpu.CompilerParams(vmem_limit_bytes=VMEM_LIMIT),
        cost_estimate=pl.CostEstimate(flops=2 * 256 * 36 * C * C, bytes_accessed=6 << 20, transcendentals=0),
        name="rim_terms",
    )(near, inner, grd, x_came, y_came)


def power_of(values):
    peak = jnp.max(jnp.abs(values))
    return jnp.clip(jnp.ceil(jnp.log2(jnp.full((8, C), peak))), -100.0, 100.0)[0:1]


def merge_kernel(groups, take, keep, came, out, total):
    held = out.shape[1]
    total[pl.ds(0, HALF)] = keep[...] + came[...]
    if groups * take > HALF:
        total[pl.ds(HALF, groups * take - HALF)] = jnp.zeros((groups * take - HALF, C), jnp.float32)
    power = power_of(total[...])
    scale = jnp.exp2(14.0 - power)
    for p in range(groups):
        out[p, pl.ds(0, take)] = total[pl.ds(p * take, take)] * scale
        out[p, pl.ds(take, held - take)] = jnp.broadcast_to(power, (held - take, C))


def merge(groups, take, held, keep, came):
    return pl.pallas_call(
        lambda *refs: merge_kernel(groups, take, *refs),
        out_shape=jax.ShapeDtypeStruct((groups, held, C), jnp.float32),
        in_specs=[vmem()] * 2,
        out_specs=vmem(),
        scratch_shapes=[pltpu.VMEM((groups * take, C), jnp.float32)],
        compiler_params=pltpu.CompilerParams(vmem_limit_bytes=VMEM_LIMIT),
        name="merge",
    )(keep, came)


def sum_kernel(take, blocks, out):
    groups, held, _ = blocks.shape
    total = jnp.zeros((take, C), jnp.float32)
    for p in range(groups):
        total += blocks[p, pl.ds(0, take)] * jnp.exp2(blocks[p, pl.ds(take, 1)] - 14.0)
    power = power_of(total)
    total = total * jnp.exp2(14.0 - power)
    for p in range(groups):
        out[p, pl.ds(0, take)] = total
        out[p, pl.ds(take, held - take)] = jnp.broadcast_to(power, (held - take, C))


def sum_blocks(take, blocks):
    return pl.pallas_call(
        lambda *refs: sum_kernel(take, *refs),
        out_shape=jax.ShapeDtypeStruct(blocks.shape, jnp.float32),
        in_specs=[vmem()],
        out_specs=vmem(),
        compiler_params=pltpu.CompilerParams(vmem_limit_bytes=VMEM_LIMIT),
        name="sum_blocks",
    )(blocks)


def decode_kernel(take, scale, places, own, blocks, *refs):
    out, half, sems = refs[-3:]
    groups = blocks.shape[0]
    core = parity("gy")
    target = out.at[core if own else 1 - core]
    copies = []
    done = 0
    for p in range(groups):
        rows = min(take, HALF - p * take)
        if rows > 0:
            factor = jnp.exp2(blocks[places[p], pl.ds(take, 1)] - 14.0) * scale
            half[pl.ds(p * take, rows)] = blocks[places[p], pl.ds(0, rows)] * factor
        ready = min((p + 1) * take, HALF)
        if ready - done >= HALF // 4 and ready % 8 == 0 or p == groups - 1:
            piece = pl.ds(done, ready - done)
            copies += fetching((half.at[piece], target.at[piece], sems.at[len(copies)]))
            done = ready
    for copy in copies:
        copy.wait()


def decode(take, scale, places, blocks, begun=None):
    rest = () if begun is None else (begun,)
    return pl.pallas_call(
        lambda *refs: decode_kernel(take, scale, places, not rest, *refs),
        out_shape=jax.ShapeDtypeStruct((2, HALF, C), jnp.float32),
        in_specs=[vmem()] + [hbm()] * len(rest),
        out_specs=hbm(),
        scratch_shapes=[pltpu.VMEM((HALF, C), jnp.float32), pltpu.SemaphoreType.DMA((5,))],
        input_output_aliases={1: 0} if rest else {},
        compiler_params=pltpu.CompilerParams(vmem_limit_bytes=VMEM_LIMIT),
        name="decode_other" if rest else "decode_own",
    )(blocks, *rest)


def product_kernel(f, near_hbm, mask_ref, kernel_ref, bricks, x_ref, y_ref, e0, e1, out, *refs):
    lx, ly, corners, wide, near, sem, v, *flipped = refs
    (table,) = fetching((near_hbm, near, sem))
    weights = kernel_ref
    if f == 1:
        weights = flipped[0]
        for o in range(27):
            weights[pl.ds((26 - o) * C, C)] = kernel_ref[pl.ds(o * C, C)].T
    fill_own(bricks, lx, ly, corners)
    fill_came(f, x_ref, y_ref, (e0, e1), lx, ly, corners)
    table.wait()

    def per_slot(s, carry):
        build_columns(s, bricks, near, lx, ly, corners, wide, "all")
        stack_columns(s, wide, v)
        total = jnp.zeros((512, C), jnp.float32)
        for x in range(3):
            cells = v[s, pl.ds(x, 8)].reshape(512, 9 * C)
            total += jnp.dot(cells, weights[pl.ds(x * 9 * C, 9 * C)], preferred_element_type=jnp.float32)
        out[s] = (total * mask_columns(mask_ref, s)).astype(jnp.bfloat16)
        return carry

    lax.fori_loop(0, SLOTS, per_slot, 0)


def product(f, near, mask, kernel, bricks, x_came, y_came, edges):
    return pl.pallas_call(
        lambda *refs: product_kernel(f, *refs),
        out_shape=jax.ShapeDtypeStruct((SLOTS, 512, C), jnp.bfloat16),
        in_specs=[hbm()] + [vmem()] * 7,
        out_specs=vmem(),
        scratch_shapes=columns_scratch()
        + [pltpu.VMEM((SLOTS, 10, 64, 9 * C), jnp.bfloat16)]
        + ([pltpu.VMEM((ROWS, C), jnp.bfloat16)] if f else []),
        compiler_params=pltpu.CompilerParams(vmem_limit_bytes=VMEM_LIMIT),
        cost_estimate=pl.CostEstimate(flops=2 * 2048 * ROWS * C, bytes_accessed=4 << 20, transcendentals=0),
        name=("output_product", "input_grad_product")[f],
    )(near, mask, kernel, bricks, x_came, y_came, *edges)


def swapped(value, axis, k):
    pairs = []
    for low in range(k, lax.axis_size(axis) - 1, 2):
        pairs += [(low, low + 1), (low + 1, low)]
    return lax.ppermute(value, axis, pairs)


def hopped(value, axis):
    size = lax.axis_size(axis)
    pairs = [(i, i + 2) for i in range(1, size - 2, 2)] + [(i, i - 2) for i in range(2, size, 2)]
    return lax.ppermute(value, axis, pairs)


def local(features, out_grad, kernel, voxel_mask, neighbours, face_sends, edge_sends):
    size_x, size_y = lax.axis_size("gx"), lax.axis_size("gy")
    parts = size_x * size_y
    groups = parts // 2
    take = -(-HALF // groups)
    held = -(-(take + 1) // 16) * 16
    members = [[i for i in range(parts) if i % size_y % 2 == core] for core in range(2)]
    half, row = groups // 2, size_y // 2
    inward = [k + j for k in range(half - row, -1, -row) for j in range(row)]
    in_turn = [k for pair in zip(range(half, groups), inward) for k in pair]
    onward = [(k + half) % groups for k in range(groups)]
    places = [onward.index(k) for k in in_turn]

    def spread(blocks, order):
        same_core = [[core[k] for k in order] for core in members]
        return lax.all_to_all(blocks, ("gx", "gy"), 0, 0, axis_index_groups=same_core, tiled=True)

    held_act, act, grd, table, y0, y1, x0, x1 = pack(
        features.reshape(SLOTS, 512, C),
        out_grad.reshape(SLOTS, 512, C),
        voxel_mask,
        neighbours,
        face_sends,
        edge_sends,
    )
    y1 = hopped(y1, "gy")
    x1 = hopped(x1, "gx")
    v = own_columns(table, held_act)
    x1, v = lax.optimization_barrier((x1, v))
    x_came, x_more = join(x0, x1)
    x_more, v = lax.optimization_barrier((x_more, v))
    x_came = swapped(x_came, "gx", 0)
    inner = inner_terms(v, grd)
    inner, y1 = lax.optimization_barrier((inner, y1))
    y_came, y_more = join(y0, y1)
    y_came = swapped(y_came, "gy", 0)
    keep, send = rim_terms(neighbours, inner, grd, x_came, y_came)
    blocks = merge(groups, take, held, keep, swapped(send, "gy", 0)).astype(jnp.float16)
    rows = kernel.reshape(ROWS, C)
    blocks, act, x_came, x_more, y_more = lax.optimization_barrier((blocks, act, x_came, x_more, y_more))
    x_more, y_more = swapped(x_more, "gx", 0), swapped(y_more, "gy", 0)
    e0, e1 = forward_corners(x_came)
    edges = [swapped(e0, "gy", 0), swapped(e1, "gy", 1)]
    output = product(0, neighbours, voxel_mask, rows, act, x_came, y_came, edges)
    arrived, output, x_more, y_more = lax.optimization_barrier((spread(blocks, in_turn), output, x_more, y_more))
    copies = sum_blocks(take, arrived.astype(jnp.float32)).astype(jnp.float16)
    copies, grd = lax.optimization_barrier((copies, grd))
    input_grad = product(1, neighbours, voxel_mask, rows, grd, x_more, y_more, edges)
    mine, input_grad = lax.optimization_barrier((spread(copies, onward), input_grad))
    other = swapped(mine, "gy", 0)
    scale = 1.0 / math.sqrt(parts * SLOTS * 512)
    weight = decode(take, scale, places, mine.astype(jnp.float32))
    weight = decode(take, scale, places, other.astype(jnp.float32), weight)
    shape = (SLOTS, 8, 8, 8, C)
    return output.reshape(shape), input_grad.reshape(shape), weight.reshape(27, C, C)


def solution(mesh):
    spec = P(("gx", "gy"))
    return jax.shard_map(
        local,
        mesh=mesh,
        in_specs=(spec, spec, P(), spec, spec, spec, spec),
        out_specs=(spec, spec, P()),
        check_vma=False,
    )
```

```python
import math

import jax
import jax.numpy as jnp
from jax import lax
from jax.experimental import pallas as pl
from jax.experimental.pallas import tpu as pltpu
from jax.sharding import PartitionSpec as P

FACES = ((-1, 0), (1, 0), (0, -1), (0, 1))
EDGES = ((-1, -1), (-1, 1), (1, -1), (1, 1))
C = 128
SLOTS = 4
FACE = 2
ZERO = SLOTS + 4 * FACE + 4
ROWS = 27 * C
FACE_ROWS = FACE * 64
X_ROWS = FACE_ROWS + 64
Y_ROWS = FACE_ROWS + 48
HALF = ROWS // 2
VMEM_LIMIT = 32 * 1024 * 1024
PACK_LIMIT = 60 * 1024 * 1024
ROOM_BRICKS = 48
ROOM_TABLES = 12 * 1024


def vmem():
    return pl.BlockSpec(memory_space=pltpu.VMEM)


def hbm():
    return pl.BlockSpec(memory_space=pltpu.HBM)


def fetching(*pairs):
    copies = [pltpu.make_async_copy(src, dst, sem) for src, dst, sem in pairs]
    for copy in copies:
        copy.start()
    return copies


def fetched(*pairs):
    for copy in fetching(*pairs):
        copy.wait()


def mask_columns(mask_ref, s):
    m = mask_ref[...].astype(jnp.float32).astype(jnp.bfloat16)
    pick = (lax.broadcasted_iota(jnp.int32, (SLOTS, C), 0) == s).astype(jnp.float32).astype(jnp.bfloat16)
    return lax.dot_general(m, pick, (((0,), (0,)), ((), ())), preferred_element_type=jnp.float32)


def parity(axis):
    return lax.rem(lax.axis_index(axis), 2)


def side_of(k, odd):
    return 1 - odd if k == 0 else odd


def shifts(cells, same, below, above):
    line = lax.broadcasted_iota(jnp.int32, cells.shape, cells.ndim - 2)
    axis = cells.ndim - 2
    up = jnp.where((same & (line >= 1)) | (below & (line == 0)), pltpu.roll(cells, 1, axis), 0.0)
    down = jnp.where((same & (line <= 6)) | (above & (line == 7)), pltpu.roll(cells, 7, axis), 0.0)
    return up, jnp.where(same, cells, 0.0), down


def pack_kernel(face_hbm, edge_hbm, near_hbm, feat_hbm, grad_hbm, mask_hbm, held_out, act_out, grd_out, near_out, *refs):
    sends = refs[0:4]
    y_out, x_out = refs[4:6], refs[6:8]
    face_ref, edge_ref, near, raw, mask_ref, full, sems = refs[8:]
    got_mask, got_feat, got_grad, *tables = fetching(
        (mask_hbm, mask_ref, sems.at[0]),
        (feat_hbm, raw.at[0], sems.at[1]),
        (grad_hbm, raw.at[1], sems.at[2]),
        (face_hbm, face_ref, sems.at[3]),
        (edge_hbm, edge_ref, sems.at[4]),
        (near_hbm, near, sems.at[5]),
    )
    got_mask.wait()
    got_feat.wait()
    got_grad.wait()
    for s in range(SLOTS):
        rows = mask_columns(mask_ref, s)
        for f in range(2):
            masked = raw[f, s].astype(jnp.float32) * rows
            full[f, s] = masked.reshape(8, 8, 8, C)
            raw[f, s] = masked.astype(jnp.bfloat16)
    results = fetching(
        (raw.at[0], held_out.at[0], sems.at[7]),
        (raw.at[0], act_out, sems.at[8]),
        (raw.at[1], grd_out, sems.at[9]),
    )
    for table in tables:
        table.wait()
    results += fetching((near, near_out.at[0], sems.at[6]))
    for axis, outs in enumerate((x_out, y_out)):
        odd = parity("gy" if axis else "gx")
        for k in range(2):
            side = side_of(k, odd)
            for f in range(2):
                for r in range(FACE):
                    entry = face_ref[r, 2 * axis + side]
                    slot = jnp.clip(entry, 0, SLOTS - 1)
                    layer = full[f, slot, :, 7 * side] if axis else full[f, slot, 7 * side]
                    layer = jnp.where(entry < SLOTS, layer, 0.0)
                    first = f * (Y_ROWS if axis else X_ROWS) + r * 64
                    outs[k][pl.ds(first, 64)] = layer.reshape(64, C).astype(jnp.bfloat16)
            lines = []
            for far in range(2):
                corner = 2 * far + side if axis else 2 * side + far
                entry = edge_ref[0, corner]
                slot = jnp.clip(entry, 0, SLOTS - 1)
                live = entry < SLOTS
                at_x, at_y = (7 * far, 7 * side) if axis else (7 * side, 7 * far)
                if axis == 0:
                    for f in range(2):
                        lines.append(jnp.where(live, full[f, slot, at_x, at_y], 0.0))
                    continue
                base = 18 * far + 6 * side
                low, mid, high = near[slot, base], near[slot, base + 1], near[slot, base + 2]
                up, same, down = shifts(
                    full[1, slot, at_x, at_y],
                    live & (mid < ZERO),
                    live & (high < ZERO),
                    live & (low < ZERO),
                )
                lines += [down, same, up]
            if axis == 0:
                lines.append(jnp.zeros((32, C), jnp.float32))
            lines = jnp.concatenate(lines, axis=0).astype(jnp.bfloat16)
            outs[k][pl.ds(FACE_ROWS, lines.shape[0])] = lines
    for i, (built, send) in enumerate(zip(refs[4:8], sends)):
        results += fetching((built, send, sems.at[10 + i]))
    for result in results:
        result.wait()


def pack(features, out_grad, mask, near, face_sends, edge_sends):
    sends = [
        jax.ShapeDtypeStruct((rows + FACE_ROWS, C), jnp.bfloat16) for rows in (Y_ROWS, Y_ROWS, X_ROWS, X_ROWS)
    ]
    return pl.pallas_call(
        pack_kernel,
        out_shape=[
            jax.ShapeDtypeStruct((ROOM_BRICKS, SLOTS, 512, C), jnp.bfloat16),
            jax.ShapeDtypeStruct((SLOTS, 512, C), jnp.bfloat16),
            jax.ShapeDtypeStruct((SLOTS, 512, C), jnp.bfloat16),
            jax.ShapeDtypeStruct((ROOM_TABLES, SLOTS, 27), jnp.int32),
        ]
        + sends,
        in_specs=[hbm()] * 6,
        out_specs=[hbm()] * 8,
        scratch_shapes=[pltpu.VMEM(send.shape, send.dtype) for send in sends]
        + [
            pltpu.SMEM((FACE, 4), jnp.int32),
            pltpu.SMEM((1, 4), jnp.int32),
            pltpu.SMEM((SLOTS, 27), jnp.int32),
            pltpu.VMEM((2, SLOTS, 512, C), jnp.bfloat16),
            pltpu.VMEM((SLOTS, 512), jnp.int32),
            pltpu.VMEM((2, SLOTS, 8, 8, 8, C), jnp.float32),
            pltpu.SemaphoreType.DMA((14,)),
        ],
        compiler_params=pltpu.CompilerParams(vmem_limit_bytes=PACK_LIMIT),
        name="pack",
    )(face_sends.T, edge_sends.T, near, features, out_grad, mask)


def parts_of(ref):
    rows = ref.shape[0] // 2
    return ref.at[pl.ds(0, rows)], ref.at[pl.ds(rows, rows)]


def join_kernel(first, second, out, more):
    rows = first.shape[0] - FACE_ROWS
    for k, src in enumerate((first, second)):
        out[pl.ds(k * rows, rows)] = src[pl.ds(0, rows)]
        more[pl.ds(k * FACE_ROWS, FACE_ROWS)] = src[pl.ds(rows, FACE_ROWS)]


def join(first, second):
    outs = [
        jax.ShapeDtypeStruct((2 * rows, C), jnp.bfloat16) for rows in (first.shape[0] - FACE_ROWS, FACE_ROWS)
    ]
    return pl.pallas_call(
        join_kernel,
        out_shape=outs,
        in_specs=[vmem()] * 2,
        out_specs=[vmem()] * 2,
        compiler_params=pltpu.CompilerParams(vmem_limit_bytes=VMEM_LIMIT),
        name="join_sides",
    )(first, second)


def forward_kernel(x_came, out0, out1):
    odd_x, odd_y = parity("gx"), parity("gy")
    for k, out in enumerate((out0, out1)):
        far = side_of(k, odd_y)
        for j, came in enumerate(parts_of(x_came)):
            source = side_of(j, odd_x)
            rows = came[pl.ds(pl.multiple_of(FACE_ROWS + 16 * far, 16), 16)]
            out[pl.ds(pl.multiple_of(16 * source, 16), 16)] = rows


def forward_corners(x_came):
    send = jax.ShapeDtypeStruct((32, C), jnp.bfloat16)
    return pl.pallas_call(
        forward_kernel,
        out_shape=[send] * 2,
        in_specs=[vmem()],
        out_specs=[vmem()] * 2,
        compiler_params=pltpu.CompilerParams(vmem_limit_bytes=VMEM_LIMIT),
        name="forward_corners",
    )(x_came)


def fill_own(bricks, lx, ly, corners):
    for s in range(SLOTS):
        whole = bricks[s].astype(jnp.float32).reshape(8, 8, 8, C)
        for side, at in ((0, 7), (1, 0)):
            lx[side, s] = whole[at]
            ly[side, s] = whole[:, at]
            for other, far in ((0, 7), (1, 0)):
                corners[2 * side + other, s] = whole[at, far]


def fill_zero(lx, ly, corners, first):
    for ref in (lx, ly, corners):
        count = ref.shape[1] - first
        ref[:, pl.ds(first, count)] = jnp.zeros((ref.shape[0], count) + ref.shape[2:], jnp.float32)


def fill_came(f, x_came, y_came, edges, lx, ly, corners):
    odd_x, odd_y = parity("gx"), parity("gy")
    for came, odd, dst in ((x_came, odd_x, lx), (y_came, odd_y, ly)):
        for k, part in enumerate(parts_of(came)):
            side = side_of(k, odd)
            for r in range(FACE):
                rows = part[pl.ds(r * 64, 64)]
                dst[side, SLOTS + r] = rows.astype(jnp.float32).reshape(8, 8, C)
            dst[k, SLOTS + FACE] = jnp.zeros((8, 8, C), jnp.float32)
    for k, came in enumerate(edges):
        side = side_of(k, odd_y)
        for j in range(2):
            rows = came[pl.ds(16 * j, 16)].astype(jnp.float32)
            corners[2 * j + side, SLOTS + 2 * FACE] = rows[8 * f : 8 * f + 8]
    for sx in range(2):
        for sy in range(2):
            c = 2 * sx + sy
            for r in range(FACE):
                corners[c, SLOTS + r] = lx[sx, SLOTS + r, 0 if sy else 7]
                corners[c, SLOTS + FACE + r] = ly[sy, SLOTS + r, 0 if sx else 7]
            corners[c, SLOTS + 2 * FACE + 1] = jnp.zeros((8, C), jnp.float32)


def build_columns(s, bricks, near, lx, ly, corners, wide, which):
    def spread(cells, at_x, at_y, depth):
        flat = cells.reshape(-1, 8, C)
        for k, moved in enumerate(shifts(flat, depth == 0, depth == -1, depth == 1)):
            wide[k, at_x, at_y] = moved.reshape(cells.shape)

    def column(nx, ny):
        base = 9 * (nx + 1) + 3 * (ny + 1)
        low, mid, high = near[s, base], near[s, base + 1], near[s, base + 2]
        entry = jnp.minimum(jnp.minimum(low, mid), high)
        depth = jnp.where(low < ZERO, -1, jnp.where(high < ZERO, 1, 0))
        if which == "own":
            depth = jnp.where(entry < SLOTS, depth, 2)
        if which == "rim":
            depth = jnp.where((entry >= SLOTS) & (entry < SLOTS + 4 * FACE), depth, 2)
        return entry, depth

    middle = pl.ds(1, 8)
    if which != "rim":
        spread(bricks[s].astype(jnp.float32).reshape(8, 8, 8, C), middle, middle, 0)
    for side, n in ((0, -1), (1, 1)):
        edge_at = pl.ds(0 if n < 0 else 9, 1)
        entry, depth = column(n, 0)
        place = jnp.where(entry < SLOTS, entry, jnp.clip(entry - FACE * side, 0, SLOTS + FACE))
        spread(lx[side, place].reshape(1, 8, 8, C), edge_at, middle, depth)
        entry, depth = column(0, n)
        place = jnp.where(entry < SLOTS, entry, jnp.clip(entry - FACE * (2 + side), 0, SLOTS + FACE))
        spread(ly[side, place].reshape(8, 1, 8, C), middle, edge_at, depth)
    for sx in range(2):
        for sy in range(2):
            entry, depth = column(2 * sx - 1, 2 * sy - 1)
            first_x = SLOTS + FACE * sx
            first_y = SLOTS + FACE * (2 + sy)
            own_edge = SLOTS + 4 * FACE + 2 * sx + sy
            in_x = (entry >= first_x) & (entry < first_x + FACE)
            in_y = (entry >= first_y) & (entry < first_y + FACE)
            place = jnp.where(entry == own_edge, SLOTS + 2 * FACE, SLOTS + 2 * FACE + 1)
            place = jnp.where(in_y, SLOTS + FACE + entry - first_y, place)
            place = jnp.where(in_x, SLOTS + entry - first_x, place)
            place = jnp.where(entry < SLOTS, entry, place)
            spread(corners[2 * sx + sy, place].reshape(1, 1, 8, C), pl.ds(9 * sx, 1), pl.ds(9 * sy, 1), depth)


def stack_columns(s, wide, v):
    for y in range(3):
        for z in range(3):
            cells = wide[z, :, pl.ds(y, 8)].reshape(10, 64, C).astype(jnp.bfloat16)
            v[s, :, :, pl.ds((3 * y + z) * C, C)] = cells


def columns_scratch():
    return [
        pltpu.VMEM((2, SLOTS + FACE + 1, 8, 8, C), jnp.float32),
        pltpu.VMEM((2, SLOTS + FACE + 1, 8, 8, C), jnp.float32),
        pltpu.VMEM((4, SLOTS + 2 * FACE + 2, 8, C), jnp.float32),
        pltpu.VMEM((3, 10, 10, 8, C), jnp.float32),
        pltpu.SMEM((SLOTS, 27), jnp.int32),
        pltpu.SemaphoreType.DMA(()),
    ]


def columns_kernel(near_hbm, act_hbm, v, lx, ly, corners, wide, near, sem, act, act_sem):
    table, bricks = fetching((near_hbm.at[0], near, sem), (act_hbm.at[0], act, act_sem))
    fill_zero(lx, ly, corners, SLOTS)
    bricks.wait()
    fill_own(act, lx, ly, corners)
    table.wait()

    def per_slot(s, carry):
        build_columns(s, act, near, lx, ly, corners, wide, "own")
        stack_columns(s, wide, v)
        return carry

    lax.fori_loop(0, SLOTS, per_slot, 0)


def own_columns(near, act):
    return pl.pallas_call(
        columns_kernel,
        out_shape=jax.ShapeDtypeStruct((SLOTS, 10, 64, 9 * C), jnp.bfloat16),
        in_specs=[hbm()] * 2,
        out_specs=vmem(),
        scratch_shapes=columns_scratch()
        + [pltpu.VMEM((SLOTS, 512, C), jnp.bfloat16), pltpu.SemaphoreType.DMA(())],
        compiler_params=pltpu.CompilerParams(vmem_limit_bytes=VMEM_LIMIT),
        cost_estimate=pl.CostEstimate(flops=1 << 24, bytes_accessed=6 << 20, transcendentals=0),
        name="own_columns",
    )(near, act)


def inner_kernel(v, grd, out, turned):
    for s in range(SLOTS):
        for q in range(4):
            turned[:, pl.ds((4 * s + q) * C, C)] = grd[s, pl.ds(q * C, C)].T
    for x in range(3):
        cells = v[:, pl.ds(x, 8)].reshape(SLOTS * 512, 9 * C)
        terms = jnp.dot(turned[...], cells, preferred_element_type=jnp.float32)
        for j in range(9):
            out[pl.ds((9 * x + j) * C, C)] = terms[:, j * C : (j + 1) * C].T


def inner_terms(v, grd):
    return pl.pallas_call(
        inner_kernel,
        out_shape=jax.ShapeDtypeStruct((ROWS, C), jnp.float32),
        in_specs=[vmem()] * 2,
        out_specs=vmem(),
        scratch_shapes=[pltpu.VMEM((C, SLOTS * 512), jnp.bfloat16)],
        compiler_params=pltpu.CompilerParams(vmem_limit_bytes=VMEM_LIMIT),
        cost_estimate=pl.CostEstimate(flops=2048 * ROWS * C, bytes_accessed=3 << 20, transcendentals=0),
        name="inner_terms",
    )(v, grd)


def rim_kernel(near_hbm, inner, grd, x_ref, y_ref, keep, send, lx, ly, corners, wide, near, sem, *refs):
    vx, vy, ends_a, ends_g, side_x, side_y = refs
    (table,) = fetching((near_hbm, near, sem))
    fill_came(0, x_ref, y_ref, (), lx, ly, corners)
    for k, came in enumerate(parts_of(x_ref)):
        side = side_of(k, parity("gx"))
        for j in range(2):
            ends_a[side, j] = came[pl.ds(FACE_ROWS + 16 * j, 16)].astype(jnp.float32)[0:8]
    for k, came in enumerate(parts_of(y_ref)):
        side = side_of(k, parity("gy"))
        ends_g[side] = came[pl.ds(FACE_ROWS, 48)].astype(jnp.float32).reshape(2, 3, 8, C)
    table.wait()
    for s in range(SLOTS):
        build_columns(s, None, near, lx, ly, corners, wide, "rim")
        rows = pl.ds(64 * s, 64)
        for side in range(2):
            for j in range(9):
                cells = wide[j % 3, 9 * side, pl.ds(j // 3, 8)]
                vx[side, rows, pl.ds(j * C, C)] = cells.reshape(64, C).astype(jnp.bfloat16)
        for z in range(3):
            for sx in range(2):
                for sy in range(2):
                    wide[z, 9 * sx, 9 * sy] = jnp.zeros((8, C), jnp.float32)
        for side in range(2):
            for j in range(9):
                cells = wide[j % 3, pl.ds(j // 3, 8), 9 * side]
                vy[side, rows, pl.ds(j * C, C)] = cells.reshape(64, C).astype(jnp.bfloat16)
    grads = grd[...]
    lines = grads.astype(jnp.float32).reshape(SLOTS, 8, 8, 8, C)

    def term(cells, rows):
        return lax.dot_general(cells, rows, (((0,), (0,)), ((), ())), preferred_element_type=jnp.float32)

    def end(line):
        return jnp.concatenate([line, jnp.zeros((8, C), jnp.float32)], axis=0).astype(jnp.bfloat16)

    for side in range(2):
        rows = grads[:, 448 * side : 448 * side + 64].reshape(SLOTS * 64, C)
        side_x[side] = term(vx[side], rows)
        rows = lines[:, :, 7 * side].reshape(SLOTS * 64, C).astype(jnp.bfloat16)
        side_y[side] = term(vy[side], rows)
    def write(halves):
        for x in range(3):
            for y in range(3):
                for z in range(3):
                    first = (9 * x + 3 * y + z) * C
                    value = inner[pl.ds(first, C)]
                    if x != 1:
                        value += side_x[x // 2, pl.ds((3 * y + z) * C, C)]
                    if y != 1:
                        value += side_y[y // 2, pl.ds((3 * x + z) * C, C)]
                    if x != 1 and y != 1:
                        sx, sy = x // 2, 1 - y // 2
                        value += term(end(ends_a[sx, sy]), end(ends_g[sy, sx, z]))
                    for half in range(2):
                        low = max(first, half * HALF)
                        rows = min(first + C, (half + 1) * HALF) - low
                        if rows > 0:
                            halves[half][pl.ds(low - half * HALF, rows)] = value[low - first : low - first + rows]

    core = parity("gy")

    @pl.when(core == 0)
    def _():
        write((keep, send))

    @pl.when(core == 1)
    def _():
        write((send, keep))


def rim_terms(near, inner, grd, x_came, y_came):
    half = jax.ShapeDtypeStruct((HALF, C), jnp.float32)
    side = pltpu.VMEM((2, SLOTS * 64, 9 * C), jnp.bfloat16)
    return pl.pallas_call(
        rim_kernel,
        out_shape=[half, half],
        in_specs=[hbm()] + [vmem()] * 4,
        out_specs=[vmem()] * 2,
        scratch_shapes=columns_scratch()
        + [
            side,
            side,
            pltpu.VMEM((2, 2, 8, C), jnp.float32),
            pltpu.VMEM((2, 2, 3, 8, C), jnp.float32),
            pltpu.VMEM((2, 9 * C, C), jnp.float32),
            pltpu.VMEM((2, 9 * C, C), jnp.float32),
        ],
        compiler_params=pltpu.CompilerParams(vmem_limit_bytes=VMEM_LIMIT),
        cost_estimate=pl.CostEstimate(flops=2 * 256 * 36 * C * C, bytes_accessed=6 << 20, transcendentals=0),
        name="rim_terms",
    )(near, inner, grd, x_came, y_came)


def power_of(values):
    peak = jnp.max(jnp.abs(values))
    return jnp.clip(jnp.ceil(jnp.log2(jnp.full((8, C), peak))), -100.0, 100.0)[0:1]


def merge_kernel(groups, take, keep, came, out, total):
    held = out.shape[1]
    total[pl.ds(0, HALF)] = keep[...] + came[...]
    if groups * take > HALF:
        total[pl.ds(HALF, groups * take - HALF)] = jnp.zeros((groups * take - HALF, C), jnp.float32)
    power = power_of(total[...])
    scale = jnp.exp2(14.0 - power)
    for p in range(groups):
        out[p, pl.ds(0, take)] = total[pl.ds(p * take, take)] * scale
        out[p, pl.ds(take, held - take)] = jnp.broadcast_to(power, (held - take, C))


def merge(groups, take, held, keep, came):
    return pl.pallas_call(
        lambda *refs: merge_kernel(groups, take, *refs),
        out_shape=jax.ShapeDtypeStruct((groups, held, C), jnp.float32),
        in_specs=[vmem()] * 2,
        out_specs=vmem(),
        scratch_shapes=[pltpu.VMEM((groups * take, C), jnp.float32)],
        compiler_params=pltpu.CompilerParams(vmem_limit_bytes=VMEM_LIMIT),
        name="merge",
    )(keep, came)


def sum_kernel(take, blocks, out):
    groups, held, _ = blocks.shape
    total = jnp.zeros((take, C), jnp.float32)
    for p in range(groups):
        total += blocks[p, pl.ds(0, take)] * jnp.exp2(blocks[p, pl.ds(take, 1)] - 14.0)
    power = power_of(total)
    total = total * jnp.exp2(14.0 - power)
    for p in range(groups):
        out[p, pl.ds(0, take)] = total
        out[p, pl.ds(take, held - take)] = jnp.broadcast_to(power, (held - take, C))


def sum_blocks(take, blocks):
    return pl.pallas_call(
        lambda *refs: sum_kernel(take, *refs),
        out_shape=jax.ShapeDtypeStruct(blocks.shape, jnp.float32),
        in_specs=[vmem()],
        out_specs=vmem(),
        compiler_params=pltpu.CompilerParams(vmem_limit_bytes=VMEM_LIMIT),
        name="sum_blocks",
    )(blocks)


def decode_kernel(take, scale, places, own, blocks, *refs):
    out, half, sems = refs[-3:]
    groups = blocks.shape[0]
    core = parity("gy")
    target = out.at[core if own else 1 - core]
    copies = []
    done = 0
    for p in range(groups):
        rows = min(take, HALF - p * take)
        if rows > 0:
            factor = jnp.exp2(blocks[places[p], pl.ds(take, 1)] - 14.0) * scale
            half[pl.ds(p * take, rows)] = blocks[places[p], pl.ds(0, rows)] * factor
        ready = min((p + 1) * take, HALF)
        if ready - done >= HALF // 4 and ready % 8 == 0 or p == groups - 1:
            piece = pl.ds(done, ready - done)
            copies += fetching((half.at[piece], target.at[piece], sems.at[len(copies)]))
            done = ready
    for copy in copies:
        copy.wait()


def decode(take, scale, places, blocks, begun=None):
    rest = () if begun is None else (begun,)
    return pl.pallas_call(
        lambda *refs: decode_kernel(take, scale, places, not rest, *refs),
        out_shape=jax.ShapeDtypeStruct((2, HALF, C), jnp.float32),
        in_specs=[vmem()] + [hbm()] * len(rest),
        out_specs=hbm(),
        scratch_shapes=[pltpu.VMEM((HALF, C), jnp.float32), pltpu.SemaphoreType.DMA((5,))],
        input_output_aliases={1: 0} if rest else {},
        compiler_params=pltpu.CompilerParams(vmem_limit_bytes=VMEM_LIMIT),
        name="decode_other" if rest else "decode_own",
    )(blocks, *rest)


def product_kernel(f, near_hbm, mask_ref, kernel_ref, bricks, x_ref, y_ref, e0, e1, out, *refs):
    lx, ly, corners, wide, near, sem, v, *flipped = refs
    (table,) = fetching((near_hbm, near, sem))
    weights = kernel_ref
    if f == 1:
        weights = flipped[0]
        for o in range(27):
            weights[pl.ds((26 - o) * C, C)] = kernel_ref[pl.ds(o * C, C)].T
    fill_own(bricks, lx, ly, corners)
    fill_came(f, x_ref, y_ref, (e0, e1), lx, ly, corners)
    table.wait()

    def per_slot(s, carry):
        build_columns(s, bricks, near, lx, ly, corners, wide, "all")
        stack_columns(s, wide, v)
        total = jnp.zeros((512, C), jnp.float32)
        for x in range(3):
            cells = v[s, pl.ds(x, 8)].reshape(512, 9 * C)
            total += jnp.dot(cells, weights[pl.ds(x * 9 * C, 9 * C)], preferred_element_type=jnp.float32)
        out[s] = (total * mask_columns(mask_ref, s)).astype(jnp.bfloat16)
        return carry

    lax.fori_loop(0, SLOTS, per_slot, 0)


def product(f, near, mask, kernel, bricks, x_came, y_came, edges):
    return pl.pallas_call(
        lambda *refs: product_kernel(f, *refs),
        out_shape=jax.ShapeDtypeStruct((SLOTS, 512, C), jnp.bfloat16),
        in_specs=[hbm()] + [vmem()] * 7,
        out_specs=vmem(),
        scratch_shapes=columns_scratch()
        + [pltpu.VMEM((SLOTS, 10, 64, 9 * C), jnp.bfloat16)]
        + ([pltpu.VMEM((ROWS, C), jnp.bfloat16)] if f else []),
        compiler_params=pltpu.CompilerParams(vmem_limit_bytes=VMEM_LIMIT),
        cost_estimate=pl.CostEstimate(flops=2 * 2048 * ROWS * C, bytes_accessed=4 << 20, transcendentals=0),
        name=("output_product", "input_grad_product")[f],
    )(near, mask, kernel, bricks, x_came, y_came, *edges)


def swapped(value, axis, k):
    pairs = []
    for low in range(k, lax.axis_size(axis) - 1, 2):
        pairs += [(low, low + 1), (low + 1, low)]
    return lax.ppermute(value, axis, pairs)


def hopped(value, axis):
    size = lax.axis_size(axis)
    pairs = [(i, i + 2) for i in range(1, size - 2, 2)] + [(i, i - 2) for i in range(2, size, 2)]
    return lax.ppermute(value, axis, pairs)


def local(features, out_grad, kernel, voxel_mask, neighbours, face_sends, edge_sends):
    size_x, size_y = lax.axis_size("gx"), lax.axis_size("gy")
    parts = size_x * size_y
    groups = parts // 2
    take = -(-HALF // groups)
    held = -(-(take + 1) // 16) * 16
    members = [[i for i in range(parts) if i % size_y % 2 == core] for core in range(2)]
    half, row = groups // 2, size_y // 2
    inward = [k + j for k in range(half - row, -1, -row) for j in range(row)]
    in_turn = [k for pair in zip(range(half, groups), inward) for k in pair]
    onward = [(k + half) % groups for k in range(groups)]
    places = [onward.index(k) for k in in_turn]

    def spread(blocks, order):
        same_core = [[core[k] for k in order] for core in members]
        return lax.all_to_all(blocks, ("gx", "gy"), 0, 0, axis_index_groups=same_core, tiled=True)

    held_act, act, grd, table, y0, y1, x0, x1 = pack(
        features.reshape(SLOTS, 512, C),
        out_grad.reshape(SLOTS, 512, C),
        voxel_mask,
        neighbours,
        face_sends,
        edge_sends,
    )
    y1 = hopped(y1, "gy")
    x1 = hopped(x1, "gx")
    v = own_columns(table, held_act)
    x1, v = lax.optimization_barrier((x1, v))
    x_came, x_more = join(x0, x1)
    x_more, v = lax.optimization_barrier((x_more, v))
    x_came = swapped(x_came, "gx", 0)
    inner = inner_terms(v, grd)
    y_came, y_more = join(y0, y1)
    y_came = swapped(y_came, "gy", 0)
    keep, send = rim_terms(neighbours, inner, grd, x_came, y_came)
    blocks = merge(groups, take, held, keep, swapped(send, "gy", 0)).astype(jnp.float16)
    rows = kernel.reshape(ROWS, C)
    blocks, act, x_came, x_more, y_more = lax.optimization_barrier((blocks, act, x_came, x_more, y_more))
    x_more, y_more = swapped(x_more, "gx", 0), swapped(y_more, "gy", 0)
    e0, e1 = forward_corners(x_came)
    edges = [swapped(e0, "gy", 0), swapped(e1, "gy", 1)]
    output = product(0, neighbours, voxel_mask, rows, act, x_came, y_came, edges)
    arrived, output, x_more, y_more = lax.optimization_barrier((spread(blocks, in_turn), output, x_more, y_more))
    copies = sum_blocks(take, arrived.astype(jnp.float32)).astype(jnp.float16)
    copies, grd = lax.optimization_barrier((copies, grd))
    input_grad = product(1, neighbours, voxel_mask, rows, grd, x_more, y_more, edges)
    mine, input_grad = lax.optimization_barrier((spread(copies, onward), input_grad))
    other = swapped(mine, "gy", 0)
    scale = 1.0 / math.sqrt(parts * SLOTS * 512)
    weight = decode(take, scale, places, mine.astype(jnp.float32))
    weight = decode(take, scale, places, other.astype(jnp.float32), weight)
    shape = (SLOTS, 8, 8, 8, C)
    return output.reshape(shape), input_grad.reshape(shape), weight.reshape(27, C, C)


def solution(mesh):
    spec = P(("gx", "gy"))
    return jax.shard_map(
        local,
        mesh=mesh,
        in_specs=(spec, spec, P(), spec, spec, spec, spec),
        out_specs=(spec, spec, P()),
        check_vma=False,
    )
```

```python
import math

import jax
import jax.numpy as jnp
from jax import lax
from jax.experimental import pallas as pl
from jax.experimental.pallas import tpu as pltpu
from jax.sharding import PartitionSpec as P

FACES = ((-1, 0), (1, 0), (0, -1), (0, 1))
EDGES = ((-1, -1), (-1, 1), (1, -1), (1, 1))
C = 128
SLOTS = 4
FACE = 2
ZERO = SLOTS + 4 * FACE + 4
ROWS = 27 * C
FACE_ROWS = FACE * 64
X_ROWS = FACE_ROWS + 32
Y_ROWS = FACE_ROWS + 48
HALF = ROWS // 2
SPARE_ROWS = 32
VMEM_LIMIT = 32 * 1024 * 1024
PACK_LIMIT = 60 * 1024 * 1024
ROOM_BRICKS = 48
ROOM_TABLES = 12 * 1024


def vmem():
    return pl.BlockSpec(memory_space=pltpu.VMEM)


def hbm():
    return pl.BlockSpec(memory_space=pltpu.HBM)


def fetching(*pairs):
    copies = [pltpu.make_async_copy(src, dst, sem) for src, dst, sem in pairs]
    for copy in copies:
        copy.start()
    return copies


def fetched(*pairs):
    for copy in fetching(*pairs):
        copy.wait()


def mask_columns(mask_ref, s):
    m = mask_ref[...].astype(jnp.float32).astype(jnp.bfloat16)
    pick = (lax.broadcasted_iota(jnp.int32, (SLOTS, C), 0) == s).astype(jnp.float32).astype(jnp.bfloat16)
    return lax.dot_general(m, pick, (((0,), (0,)), ((), ())), preferred_element_type=jnp.float32)


def parity(axis):
    return lax.rem(lax.axis_index(axis), 2)


def side_of(k, odd):
    return 1 - odd if k == 0 else odd


def shifts(cells, same, below, above):
    line = lax.broadcasted_iota(jnp.int32, cells.shape, cells.ndim - 2)
    axis = cells.ndim - 2
    up = jnp.where((same & (line >= 1)) | (below & (line == 0)), pltpu.roll(cells, 1, axis), 0.0)
    down = jnp.where((same & (line <= 6)) | (above & (line == 7)), pltpu.roll(cells, 7, axis), 0.0)
    return up, jnp.where(same, cells, 0.0), down


def pack_kernel(face_hbm, edge_hbm, near_hbm, feat_hbm, grad_hbm, mask_hbm, held_out, act_out, grd_out, near_out, *refs):
    sends = refs[0:4]
    y_out, x_out = refs[4:6], refs[6:8]
    face_ref, edge_ref, near, raw, mask_ref, full, sems = refs[8:]
    got_mask, got_feat, got_grad, *tables = fetching(
        (mask_hbm, mask_ref, sems.at[0]),
        (feat_hbm, raw.at[0], sems.at[1]),
        (grad_hbm, raw.at[1], sems.at[2]),
        (face_hbm, face_ref, sems.at[3]),
        (edge_hbm, edge_ref, sems.at[4]),
        (near_hbm, near, sems.at[5]),
    )
    got_mask.wait()
    got_feat.wait()
    got_grad.wait()
    for s in range(SLOTS):
        rows = mask_columns(mask_ref, s)
        for f in range(2):
            masked = raw[f, s].astype(jnp.float32) * rows
            full[f, s] = masked.reshape(8, 8, 8, C)
            raw[f, s] = masked.astype(jnp.bfloat16)
    results = fetching(
        (raw.at[0], held_out.at[0], sems.at[7]),
        (raw.at[0], act_out, sems.at[8]),
        (raw.at[1], grd_out, sems.at[9]),
    )
    for table in tables:
        table.wait()
    results += fetching((near, near_out.at[0], sems.at[6]))
    for axis, outs in enumerate((x_out, y_out)):
        odd = parity("gy" if axis else "gx")
        for k in range(2):
            side = side_of(k, odd)
            for f in range(2):
                for r in range(FACE):
                    entry = face_ref[r, 2 * axis + side]
                    slot = jnp.clip(entry, 0, SLOTS - 1)
                    layer = full[f, slot, :, 7 * side] if axis else full[f, slot, 7 * side]
                    layer = jnp.where(entry < SLOTS, layer, 0.0)
                    first = f * (Y_ROWS if axis else X_ROWS) + r * 64
                    outs[k][pl.ds(first, 64)] = layer.reshape(64, C).astype(jnp.bfloat16)
            lines = []
            for far in range(2):
                corner = 2 * far + side if axis else 2 * side + far
                entry = edge_ref[0, corner]
                slot = jnp.clip(entry, 0, SLOTS - 1)
                live = entry < SLOTS
                at_x, at_y = (7 * far, 7 * side) if axis else (7 * side, 7 * far)
                if axis == 0:
                    for f in range(2):
                        lines.append(jnp.where(live, full[f, slot, at_x, at_y], 0.0))
                    continue
                base = 18 * far + 6 * side
                low, mid, high = near[slot, base], near[slot, base + 1], near[slot, base + 2]
                up, same, down = shifts(
                    full[1, slot, at_x, at_y],
                    live & (mid < ZERO),
                    live & (high < ZERO),
                    live & (low < ZERO),
                )
                lines += [down, same, up]
            lines = jnp.concatenate(lines, axis=0).astype(jnp.bfloat16)
            outs[k][pl.ds(FACE_ROWS, lines.shape[0])] = lines
    x_out[1][pl.ds(X_ROWS + FACE_ROWS, SPARE_ROWS)] = jnp.zeros((SPARE_ROWS, C), jnp.bfloat16)
    for i, (built, send) in enumerate(zip(refs[4:8], sends)):
        results += fetching((built, send, sems.at[10 + i]))
    for result in results:
        result.wait()


def pack(features, out_grad, mask, near, face_sends, edge_sends):
    sends = [
        jax.ShapeDtypeStruct((rows + FACE_ROWS, C), jnp.bfloat16)
        for rows in (Y_ROWS, Y_ROWS, X_ROWS, X_ROWS + SPARE_ROWS)
    ]
    return pl.pallas_call(
        pack_kernel,
        out_shape=[
            jax.ShapeDtypeStruct((ROOM_BRICKS, SLOTS, 512, C), jnp.bfloat16),
            jax.ShapeDtypeStruct((SLOTS, 512, C), jnp.bfloat16),
            jax.ShapeDtypeStruct((SLOTS, 512, C), jnp.bfloat16),
            jax.ShapeDtypeStruct((ROOM_TABLES, SLOTS, 27), jnp.int32),
        ]
        + sends,
        in_specs=[hbm()] * 6,
        out_specs=[hbm()] * 8,
        scratch_shapes=[pltpu.VMEM(send.shape, send.dtype) for send in sends]
        + [
            pltpu.SMEM((FACE, 4), jnp.int32),
            pltpu.SMEM((1, 4), jnp.int32),
            pltpu.SMEM((SLOTS, 27), jnp.int32),
            pltpu.VMEM((2, SLOTS, 512, C), jnp.bfloat16),
            pltpu.VMEM((SLOTS, 512), jnp.int32),
            pltpu.VMEM((2, SLOTS, 8, 8, 8, C), jnp.float32),
            pltpu.SemaphoreType.DMA((14,)),
        ],
        compiler_params=pltpu.CompilerParams(vmem_limit_bytes=PACK_LIMIT),
        name="pack",
    )(face_sends.T, edge_sends.T, near, features, out_grad, mask)


def parts_of(ref):
    rows = ref.shape[0] // 2
    return ref.at[pl.ds(0, rows)], ref.at[pl.ds(rows, rows)]


def join_kernel(first, second, out, more):
    rows = first.shape[0] - FACE_ROWS
    for k, src in enumerate((first, second)):
        out[pl.ds(k * rows, rows)] = src[pl.ds(0, rows)]
        more[pl.ds(k * FACE_ROWS, FACE_ROWS)] = src[pl.ds(rows, FACE_ROWS)]


def join(first, second):
    outs = [
        jax.ShapeDtypeStruct((2 * rows, C), jnp.bfloat16) for rows in (first.shape[0] - FACE_ROWS, FACE_ROWS)
    ]
    return pl.pallas_call(
        join_kernel,
        out_shape=outs,
        in_specs=[vmem()] * 2,
        out_specs=[vmem()] * 2,
        compiler_params=pltpu.CompilerParams(vmem_limit_bytes=VMEM_LIMIT),
        name="join_sides",
    )(first, second)


def forward_kernel(x_came, out0, out1):
    odd_x, odd_y = parity("gx"), parity("gy")
    for k, out in enumerate((out0, out1)):
        far = side_of(k, odd_y)
        for j, came in enumerate(parts_of(x_came)):
            source = side_of(j, odd_x)
            rows = came[pl.ds(pl.multiple_of(FACE_ROWS + 16 * far, 16), 16)]
            out[pl.ds(pl.multiple_of(16 * source, 16), 16)] = rows


def forward_corners(x_came):
    send = jax.ShapeDtypeStruct((32, C), jnp.bfloat16)
    return pl.pallas_call(
        forward_kernel,
        out_shape=[send] * 2,
        in_specs=[vmem()],
        out_specs=[vmem()] * 2,
        compiler_params=pltpu.CompilerParams(vmem_limit_bytes=VMEM_LIMIT),
        name="forward_corners",
    )(x_came)


def fill_own(bricks, lx, ly, corners):
    for s in range(SLOTS):
        whole = bricks[s].astype(jnp.float32).reshape(8, 8, 8, C)
        for side, at in ((0, 7), (1, 0)):
            lx[side, s] = whole[at]
            ly[side, s] = whole[:, at]
            for other, far in ((0, 7), (1, 0)):
                corners[2 * side + other, s] = whole[at, far]


def fill_zero(lx, ly, corners, first):
    for ref in (lx, ly, corners):
        count = ref.shape[1] - first
        ref[:, pl.ds(first, count)] = jnp.zeros((ref.shape[0], count) + ref.shape[2:], jnp.float32)


def fill_came(f, x_came, y_came, edges, lx, ly, corners):
    odd_x, odd_y = parity("gx"), parity("gy")
    for came, first, odd, dst in ((parts_of(x_came), 0, odd_x, lx), (y_came, f * Y_ROWS, odd_y, ly)):
        for k, part in enumerate(came):
            side = side_of(k, odd)
            for r in range(FACE):
                rows = part[pl.ds(first + r * 64, 64)]
                dst[side, SLOTS + r] = rows.astype(jnp.float32).reshape(8, 8, C)
            dst[k, SLOTS + FACE] = jnp.zeros((8, 8, C), jnp.float32)
    for k, came in enumerate(edges):
        side = side_of(k, odd_y)
        for j in range(2):
            rows = came[pl.ds(16 * j, 16)].astype(jnp.float32)
            corners[2 * j + side, SLOTS + 2 * FACE] = rows[8 * f : 8 * f + 8]
    for sx in range(2):
        for sy in range(2):
            c = 2 * sx + sy
            for r in range(FACE):
                corners[c, SLOTS + r] = lx[sx, SLOTS + r, 0 if sy else 7]
                corners[c, SLOTS + FACE + r] = ly[sy, SLOTS + r, 0 if sx else 7]
            corners[c, SLOTS + 2 * FACE + 1] = jnp.zeros((8, C), jnp.float32)


def build_columns(s, bricks, near, lx, ly, corners, wide, which):
    def spread(cells, at_x, at_y, depth):
        flat = cells.reshape(-1, 8, C)
        for k, moved in enumerate(shifts(flat, depth == 0, depth == -1, depth == 1)):
            wide[k, at_x, at_y] = moved.reshape(cells.shape)

    def column(nx, ny):
        base = 9 * (nx + 1) + 3 * (ny + 1)
        low, mid, high = near[s, base], near[s, base + 1], near[s, base + 2]
        entry = jnp.minimum(jnp.minimum(low, mid), high)
        depth = jnp.where(low < ZERO, -1, jnp.where(high < ZERO, 1, 0))
        if which == "own":
            depth = jnp.where(entry < SLOTS, depth, 2)
        if which == "rim":
            depth = jnp.where((entry >= SLOTS) & (entry < SLOTS + 4 * FACE), depth, 2)
        return entry, depth

    middle = pl.ds(1, 8)
    if which != "rim":
        spread(bricks[s].astype(jnp.float32).reshape(8, 8, 8, C), middle, middle, 0)
    for side, n in ((0, -1), (1, 1)):
        edge_at = pl.ds(0 if n < 0 else 9, 1)
        entry, depth = column(n, 0)
        place = jnp.where(entry < SLOTS, entry, jnp.clip(entry - FACE * side, 0, SLOTS + FACE))
        spread(lx[side, place].reshape(1, 8, 8, C), edge_at, middle, depth)
        entry, depth = column(0, n)
        place = jnp.where(entry < SLOTS, entry, jnp.clip(entry - FACE * (2 + side), 0, SLOTS + FACE))
        spread(ly[side, place].reshape(8, 1, 8, C), middle, edge_at, depth)
    for sx in range(2):
        for sy in range(2):
            entry, depth = column(2 * sx - 1, 2 * sy - 1)
            first_x = SLOTS + FACE * sx
            first_y = SLOTS + FACE * (2 + sy)
            own_edge = SLOTS + 4 * FACE + 2 * sx + sy
            in_x = (entry >= first_x) & (entry < first_x + FACE)
            in_y = (entry >= first_y) & (entry < first_y + FACE)
            place = jnp.where(entry == own_edge, SLOTS + 2 * FACE, SLOTS + 2 * FACE + 1)
            place = jnp.where(in_y, SLOTS + FACE + entry - first_y, place)
            place = jnp.where(in_x, SLOTS + entry - first_x, place)
            place = jnp.where(entry < SLOTS, entry, place)
            spread(corners[2 * sx + sy, place].reshape(1, 1, 8, C), pl.ds(9 * sx, 1), pl.ds(9 * sy, 1), depth)


def stack_columns(s, wide, v):
    for y in range(3):
        for z in range(3):
            cells = wide[z, :, pl.ds(y, 8)].reshape(10, 64, C).astype(jnp.bfloat16)
            v[s, :, :, pl.ds((3 * y + z) * C, C)] = cells


def columns_scratch():
    return [
        pltpu.VMEM((2, SLOTS + FACE + 1, 8, 8, C), jnp.float32),
        pltpu.VMEM((2, SLOTS + FACE + 1, 8, 8, C), jnp.float32),
        pltpu.VMEM((4, SLOTS + 2 * FACE + 2, 8, C), jnp.float32),
        pltpu.VMEM((3, 10, 10, 8, C), jnp.float32),
        pltpu.SMEM((SLOTS, 27), jnp.int32),
        pltpu.SemaphoreType.DMA(()),
    ]


def columns_kernel(near_hbm, act_hbm, v, lx, ly, corners, wide, near, sem, act, act_sem):
    table, bricks = fetching((near_hbm.at[0], near, sem), (act_hbm.at[0], act, act_sem))
    fill_zero(lx, ly, corners, SLOTS)
    bricks.wait()
    fill_own(act, lx, ly, corners)
    table.wait()

    def per_slot(s, carry):
        build_columns(s, act, near, lx, ly, corners, wide, "own")
        stack_columns(s, wide, v)
        return carry

    lax.fori_loop(0, SLOTS, per_slot, 0)


def own_columns(near, act):
    return pl.pallas_call(
        columns_kernel,
        out_shape=jax.ShapeDtypeStruct((SLOTS, 10, 64, 9 * C), jnp.bfloat16),
        in_specs=[hbm()] * 2,
        out_specs=vmem(),
        scratch_shapes=columns_scratch()
        + [pltpu.VMEM((SLOTS, 512, C), jnp.bfloat16), pltpu.SemaphoreType.DMA(())],
        compiler_params=pltpu.CompilerParams(vmem_limit_bytes=VMEM_LIMIT),
        cost_estimate=pl.CostEstimate(flops=1 << 24, bytes_accessed=6 << 20, transcendentals=0),
        name="own_columns",
    )(near, act)


def inner_kernel(v, grd, out, turned):
    for s in range(SLOTS):
        for q in range(4):
            turned[:, pl.ds((4 * s + q) * C, C)] = grd[s, pl.ds(q * C, C)].T
    for x in range(3):
        cells = v[:, pl.ds(x, 8)].reshape(SLOTS * 512, 9 * C)
        terms = jnp.dot(turned[...], cells, preferred_element_type=jnp.float32)
        for j in range(9):
            out[pl.ds((9 * x + j) * C, C)] = terms[:, j * C : (j + 1) * C].T


def inner_terms(v, grd):
    return pl.pallas_call(
        inner_kernel,
        out_shape=jax.ShapeDtypeStruct((ROWS, C), jnp.float32),
        in_specs=[vmem()] * 2,
        out_specs=vmem(),
        scratch_shapes=[pltpu.VMEM((C, SLOTS * 512), jnp.bfloat16)],
        compiler_params=pltpu.CompilerParams(vmem_limit_bytes=VMEM_LIMIT),
        cost_estimate=pl.CostEstimate(flops=2 * 2048 * ROWS * C, bytes_accessed=6 << 20, transcendentals=0),
        name="inner_terms",
    )(v, grd)


def rim_kernel(near_hbm, inner, grd, x_ref, y0, y1, keep, send, lx, ly, corners, wide, near, sem, *refs):
    vx, vy, ends_a, ends_g, side_x, side_y = refs
    (table,) = fetching((near_hbm, near, sem))
    fill_came(0, x_ref, (y0, y1), (), lx, ly, corners)
    for k, came in enumerate(parts_of(x_ref)):
        side = side_of(k, parity("gx"))
        for j in range(2):
            ends_a[side, j] = came[pl.ds(FACE_ROWS + 16 * j, 16)].astype(jnp.float32)[0:8]
    for k, came in enumerate((y0, y1)):
        side = side_of(k, parity("gy"))
        ends_g[side] = came[pl.ds(FACE_ROWS, 48)].astype(jnp.float32).reshape(2, 3, 8, C)
    table.wait()
    for s in range(SLOTS):
        build_columns(s, None, near, lx, ly, corners, wide, "rim")
        rows = pl.ds(64 * s, 64)
        for side in range(2):
            for j in range(9):
                cells = wide[j % 3, 9 * side, pl.ds(j // 3, 8)]
                vx[side, rows, pl.ds(j * C, C)] = cells.reshape(64, C).astype(jnp.bfloat16)
        for z in range(3):
            for sx in range(2):
                for sy in range(2):
                    wide[z, 9 * sx, 9 * sy] = jnp.zeros((8, C), jnp.float32)
        for side in range(2):
            for j in range(9):
                cells = wide[j % 3, pl.ds(j // 3, 8), 9 * side]
                vy[side, rows, pl.ds(j * C, C)] = cells.reshape(64, C).astype(jnp.bfloat16)
    grads = grd[...]
    lines = grads.astype(jnp.float32).reshape(SLOTS, 8, 8, 8, C)

    def term(cells, rows):
        return lax.dot_general(cells, rows, (((0,), (0,)), ((), ())), preferred_element_type=jnp.float32)

    def end(line):
        return jnp.concatenate([line, jnp.zeros((8, C), jnp.float32)], axis=0).astype(jnp.bfloat16)

    for side in range(2):
        rows = grads[:, 448 * side : 448 * side + 64].reshape(SLOTS * 64, C)
        side_x[side] = term(vx[side], rows)
        rows = lines[:, :, 7 * side].reshape(SLOTS * 64, C).astype(jnp.bfloat16)
        side_y[side] = term(vy[side], rows)
    def write(halves):
        for x in range(3):
            for y in range(3):
                for z in range(3):
                    first = (9 * x + 3 * y + z) * C
                    value = inner[pl.ds(first, C)]
                    if x != 1:
                        value += side_x[x // 2, pl.ds((3 * y + z) * C, C)]
                    if y != 1:
                        value += side_y[y // 2, pl.ds((3 * x + z) * C, C)]
                    if x != 1 and y != 1:
                        sx, sy = x // 2, 1 - y // 2
                        value += term(end(ends_a[sx, sy]), end(ends_g[sy, sx, z]))
                    for half in range(2):
                        low = max(first, half * HALF)
                        rows = min(first + C, (half + 1) * HALF) - low
                        if rows > 0:
                            halves[half][pl.ds(low - half * HALF, rows)] = value[low - first : low - first + rows]

    core = parity("gy")

    @pl.when(core == 0)
    def _():
        write((keep, send))

    @pl.when(core == 1)
    def _():
        write((send, keep))


def rim_terms(near, inner, grd, x_came, y_came):
    half = jax.ShapeDtypeStruct((HALF, C), jnp.float32)
    side = pltpu.VMEM((2, SLOTS * 64, 9 * C), jnp.bfloat16)
    return pl.pallas_call(
        rim_kernel,
        out_shape=[half, half],
        in_specs=[hbm()] + [vmem()] * 5,
        out_specs=[vmem()] * 2,
        scratch_shapes=columns_scratch()
        + [
            side,
            side,
            pltpu.VMEM((2, 2, 8, C), jnp.float32),
            pltpu.VMEM((2, 2, 3, 8, C), jnp.float32),
            pltpu.VMEM((2, 9 * C, C), jnp.float32),
            pltpu.VMEM((2, 9 * C, C), jnp.float32),
        ],
        compiler_params=pltpu.CompilerParams(vmem_limit_bytes=VMEM_LIMIT),
        cost_estimate=pl.CostEstimate(flops=2 * 256 * 36 * C * C, bytes_accessed=6 << 20, transcendentals=0),
        name="rim_terms",
    )(near, inner, grd, x_came, *y_came)


def power_of(values):
    peak = jnp.max(jnp.abs(values))
    return jnp.clip(jnp.ceil(jnp.log2(jnp.full((8, C), peak))), -100.0, 100.0)[0:1]


def merge_kernel(groups, take, keep, came, out, total):
    held = out.shape[1]
    total[pl.ds(0, HALF)] = keep[...] + came[...]
    if groups * take > HALF:
        total[pl.ds(HALF, groups * take - HALF)] = jnp.zeros((groups * take - HALF, C), jnp.float32)
    power = power_of(total[...])
    scale = jnp.exp2(14.0 - power)
    for p in range(groups):
        out[p, pl.ds(0, take)] = total[pl.ds(p * take, take)] * scale
        out[p, pl.ds(take, held - take)] = jnp.broadcast_to(power, (held - take, C))


def merge(groups, take, held, keep, came):
    return pl.pallas_call(
        lambda *refs: merge_kernel(groups, take, *refs),
        out_shape=jax.ShapeDtypeStruct((groups, held, C), jnp.float32),
        in_specs=[vmem()] * 2,
        out_specs=vmem(),
        scratch_shapes=[pltpu.VMEM((groups * take, C), jnp.float32)],
        compiler_params=pltpu.CompilerParams(vmem_limit_bytes=VMEM_LIMIT),
        name="merge",
    )(keep, came)


def sum_kernel(take, blocks, out):
    groups, held, _ = blocks.shape
    total = jnp.zeros((take, C), jnp.float32)
    for p in range(groups):
        total += blocks[p, pl.ds(0, take)] * jnp.exp2(blocks[p, pl.ds(take, 1)] - 14.0)
    power = power_of(total)
    total = total * jnp.exp2(14.0 - power)
    for p in range(groups):
        out[p, pl.ds(0, take)] = total
        out[p, pl.ds(take, held - take)] = jnp.broadcast_to(power, (held - take, C))


def sum_blocks(take, blocks):
    return pl.pallas_call(
        lambda *refs: sum_kernel(take, *refs),
        out_shape=jax.ShapeDtypeStruct(blocks.shape, jnp.float32),
        in_specs=[vmem()],
        out_specs=vmem(),
        compiler_params=pltpu.CompilerParams(vmem_limit_bytes=VMEM_LIMIT),
        name="sum_blocks",
    )(blocks)


def decode_kernel(take, scale, places, own, blocks, *refs):
    out, half, sems = refs[-3:]
    groups = blocks.shape[0]
    core = parity("gy")
    target = out.at[core if own else 1 - core]
    copies = []
    done = 0
    for p in range(groups):
        rows = min(take, HALF - p * take)
        if rows > 0:
            factor = jnp.exp2(blocks[places[p], pl.ds(take, 1)] - 14.0) * scale
            half[pl.ds(p * take, rows)] = blocks[places[p], pl.ds(0, rows)] * factor
        ready = min((p + 1) * take, HALF)
        if ready - done >= HALF // 4 and ready % 8 == 0 or p == groups - 1:
            piece = pl.ds(done, ready - done)
            copies += fetching((half.at[piece], target.at[piece], sems.at[len(copies)]))
            done = ready
    for copy in copies:
        copy.wait()


def decode(take, scale, places, blocks, begun=None):
    rest = () if begun is None else (begun,)
    return pl.pallas_call(
        lambda *refs: decode_kernel(take, scale, places, not rest, *refs),
        out_shape=jax.ShapeDtypeStruct((2, HALF, C), jnp.float32),
        in_specs=[vmem()] + [hbm()] * len(rest),
        out_specs=hbm(),
        scratch_shapes=[pltpu.VMEM((HALF, C), jnp.float32), pltpu.SemaphoreType.DMA((5,))],
        input_output_aliases={1: 0} if rest else {},
        compiler_params=pltpu.CompilerParams(vmem_limit_bytes=VMEM_LIMIT),
        name="decode_other" if rest else "decode_own",
    )(blocks, *rest)


def product_kernel(f, near_hbm, mask_ref, kernel_ref, bricks, x_ref, y0, y1, e0, e1, out, *refs):
    lx, ly, corners, wide, near, sem, v, *flipped = refs
    (table,) = fetching((near_hbm, near, sem))
    weights = kernel_ref
    if f == 1:
        weights = flipped[0]
        for o in range(27):
            weights[pl.ds((26 - o) * C, C)] = kernel_ref[pl.ds(o * C, C)].T
    fill_own(bricks, lx, ly, corners)
    fill_came(f, x_ref, (y0, y1), (e0, e1), lx, ly, corners)
    table.wait()

    def per_slot(s, carry):
        build_columns(s, bricks, near, lx, ly, corners, wide, "all")
        stack_columns(s, wide, v)
        total = jnp.zeros((512, C), jnp.float32)
        for x in range(3):
            cells = v[s, pl.ds(x, 8)].reshape(512, 9 * C)
            total += jnp.dot(cells, weights[pl.ds(x * 9 * C, 9 * C)], preferred_element_type=jnp.float32)
        out[s] = (total * mask_columns(mask_ref, s)).astype(jnp.bfloat16)
        return carry

    lax.fori_loop(0, SLOTS, per_slot, 0)


def product(f, near, mask, kernel, bricks, x_came, y_came, edges):
    return pl.pallas_call(
        lambda *refs: product_kernel(f, *refs),
        out_shape=jax.ShapeDtypeStruct((SLOTS, 512, C), jnp.bfloat16),
        in_specs=[hbm()] + [vmem()] * 8,
        out_specs=vmem(),
        scratch_shapes=columns_scratch()
        + [pltpu.VMEM((SLOTS, 10, 64, 9 * C), jnp.bfloat16)]
        + ([pltpu.VMEM((ROWS, C), jnp.bfloat16)] if f else []),
        compiler_params=pltpu.CompilerParams(vmem_limit_bytes=VMEM_LIMIT),
        cost_estimate=pl.CostEstimate(flops=2 * 2048 * ROWS * C, bytes_accessed=4 << 20, transcendentals=0),
        name=("output_product", "input_grad_product")[f],
    )(near, mask, kernel, bricks, x_came, *y_came, *edges)


def swapped(value, axis, k):
    pairs = []
    for low in range(k, lax.axis_size(axis) - 1, 2):
        pairs += [(low, low + 1), (low + 1, low)]
    return lax.ppermute(value, axis, pairs)


def hopped(value, axis):
    size = lax.axis_size(axis)
    pairs = [(i, i + 2) for i in range(1, size - 2, 2)] + [(i, i - 2) for i in range(2, size, 2)]
    return lax.ppermute(value, axis, pairs)


def local(features, out_grad, kernel, voxel_mask, neighbours, face_sends, edge_sends):
    size_x, size_y = lax.axis_size("gx"), lax.axis_size("gy")
    parts = size_x * size_y
    groups = parts // 2
    take = -(-HALF // groups)
    held = -(-(take + 1) // 16) * 16
    members = [[i for i in range(parts) if i % size_y % 2 == core] for core in range(2)]
    half, row = groups // 2, size_y // 2
    inward = [k + j for k in range(half - row, -1, -row) for j in range(row)]
    in_turn = [k for pair in zip(range(half, groups), inward) for k in pair]
    onward = [(k + half) % groups for k in range(groups)]
    places = [onward.index(k) for k in in_turn]

    def spread(blocks, order):
        same_core = [[core[k] for k in order] for core in members]
        return lax.all_to_all(blocks, ("gx", "gy"), 0, 0, axis_index_groups=same_core, tiled=True)

    held_act, act, grd, table, y0, y1, x0, x1 = pack(
        features.reshape(SLOTS, 512, C),
        out_grad.reshape(SLOTS, 512, C),
        voxel_mask,
        neighbours,
        face_sends,
        edge_sends,
    )
    x1 = hopped(x1, "gx")
    y_came = [swapped(y0, "gy", 0), swapped(y1, "gy", 1)]
    v = own_columns(table, held_act)
    x1, v = lax.optimization_barrier((x1, v))
    x_came, x_more = join(x0, x1)
    x_more, v = lax.optimization_barrier((x_more, v))
    x_came = swapped(x_came, "gx", 0)
    inner = inner_terms(v, grd)
    keep, send = rim_terms(neighbours, inner, grd, x_came, y_came)
    blocks = merge(groups, take, held, keep, swapped(send, "gy", 0)).astype(jnp.float16)
    rows = kernel.reshape(ROWS, C)
    blocks, act, x_came, x_more = lax.optimization_barrier((blocks, act, x_came, x_more))
    x_more = swapped(x_more, "gx", 0)
    e0, e1 = forward_corners(x_came)
    edges = [swapped(e0, "gy", 0), swapped(e1, "gy", 1)]
    output = product(0, neighbours, voxel_mask, rows, act, x_came, y_came, edges)
    arrived, output, x_more = lax.optimization_barrier((spread(blocks, in_turn), output, x_more))
    copies = sum_blocks(take, arrived.astype(jnp.float32)).astype(jnp.float16)
    copies, grd = lax.optimization_barrier((copies, grd))
    input_grad = product(1, neighbours, voxel_mask, rows, grd, x_more, y_came, edges)
    mine, input_grad = lax.optimization_barrier((spread(copies, onward), input_grad))
    other = swapped(mine, "gy", 0)
    scale = 1.0 / math.sqrt(parts * SLOTS * 512)
    weight = decode(take, scale, places, mine.astype(jnp.float32))
    weight = decode(take, scale, places, other.astype(jnp.float32), weight)
    shape = (SLOTS, 8, 8, 8, C)
    return output.reshape(shape), input_grad.reshape(shape), weight.reshape(27, C, C)


def solution(mesh):
    spec = P(("gx", "gy"))
    return jax.shard_map(
        local,
        mesh=mesh,
        in_specs=(spec, spec, P(), spec, spec, spec, spec),
        out_specs=(spec, spec, P()),
        check_vma=False,
    )
```

```python
import math

import jax
import jax.numpy as jnp
from jax import lax
from jax.experimental import pallas as pl
from jax.experimental.pallas import tpu as pltpu
from jax.sharding import PartitionSpec as P

FACES = ((-1, 0), (1, 0), (0, -1), (0, 1))
EDGES = ((-1, -1), (-1, 1), (1, -1), (1, 1))
C = 128
SLOTS = 4
FACE = 2
ZERO = SLOTS + 4 * FACE + 4
ROWS = 27 * C
FACE_ROWS = FACE * 64
X_ROWS = FACE_ROWS + 32
Y_ROWS = FACE_ROWS + 48
HALF = ROWS // 2
SPARE_ROWS = 32
VMEM_LIMIT = 32 * 1024 * 1024
PACK_LIMIT = 60 * 1024 * 1024
ROOM_BRICKS = 48
ROOM_TABLES = 12 * 1024


def vmem():
    return pl.BlockSpec(memory_space=pltpu.VMEM)


def hbm():
    return pl.BlockSpec(memory_space=pltpu.HBM)


def fetching(*pairs):
    copies = [pltpu.make_async_copy(src, dst, sem) for src, dst, sem in pairs]
    for copy in copies:
        copy.start()
    return copies


def fetched(*pairs):
    for copy in fetching(*pairs):
        copy.wait()


def mask_columns(mask_ref, s):
    m = mask_ref[...].astype(jnp.float32).astype(jnp.bfloat16)
    pick = (lax.broadcasted_iota(jnp.int32, (SLOTS, C), 0) == s).astype(jnp.float32).astype(jnp.bfloat16)
    return lax.dot_general(m, pick, (((0,), (0,)), ((), ())), preferred_element_type=jnp.float32)


def parity(axis):
    return lax.rem(lax.axis_index(axis), 2)


def side_of(k, odd):
    return 1 - odd if k == 0 else odd


def shifts(cells, same, below, above):
    line = lax.broadcasted_iota(jnp.int32, cells.shape, cells.ndim - 2)
    axis = cells.ndim - 2
    up = jnp.where((same & (line >= 1)) | (below & (line == 0)), pltpu.roll(cells, 1, axis), 0.0)
    down = jnp.where((same & (line <= 6)) | (above & (line == 7)), pltpu.roll(cells, 7, axis), 0.0)
    return up, jnp.where(same, cells, 0.0), down


def pack_kernel(face_hbm, edge_hbm, near_hbm, feat_hbm, grad_hbm, mask_hbm, held_out, act_out, grd_out, near_out, *refs):
    sends = refs[0:4]
    y_out, x_out = refs[4:6], refs[6:8]
    face_ref, edge_ref, near, raw, mask_ref, full, sems = refs[8:]
    got_mask, *tables = fetching(
        (mask_hbm, mask_ref, sems.at[0]),
        (face_hbm, face_ref, sems.at[1]),
        (edge_hbm, edge_ref, sems.at[2]),
        (near_hbm, near, sems.at[3]),
    )
    got = [
        fetching(
            (feat_hbm.at[s], raw.at[0, s], sems.at[4 + 2 * s]),
            (grad_hbm.at[s], raw.at[1, s], sems.at[5 + 2 * s]),
        )
        for s in range(SLOTS)
    ]
    got_mask.wait()
    results = []
    for s in range(SLOTS):
        rows = mask_columns(mask_ref, s)
        for f in range(2):
            got[s][f].wait()
            masked = raw[f, s].astype(jnp.float32) * rows
            full[f, s] = masked.reshape(8, 8, 8, C)
            raw[f, s] = masked.astype(jnp.bfloat16)
        first = 4 + 2 * SLOTS + 3 * s
        results += fetching(
            (raw.at[0, s], held_out.at[0, s], sems.at[first]),
            (raw.at[0, s], act_out.at[s], sems.at[first + 1]),
            (raw.at[1, s], grd_out.at[s], sems.at[first + 2]),
        )
    for table in tables:
        table.wait()
    last = 4 + 5 * SLOTS
    results += fetching((near, near_out.at[0], sems.at[last]))
    for axis, outs in enumerate((x_out, y_out)):
        odd = parity("gy" if axis else "gx")
        for k in range(2):
            side = side_of(k, odd)
            for f in range(2):
                for r in range(FACE):
                    entry = face_ref[r, 2 * axis + side]
                    slot = jnp.clip(entry, 0, SLOTS - 1)
                    layer = full[f, slot, :, 7 * side] if axis else full[f, slot, 7 * side]
                    layer = jnp.where(entry < SLOTS, layer, 0.0)
                    first = f * (Y_ROWS if axis else X_ROWS) + r * 64
                    outs[k][pl.ds(first, 64)] = layer.reshape(64, C).astype(jnp.bfloat16)
            lines = []
            for far in range(2):
                corner = 2 * far + side if axis else 2 * side + far
                entry = edge_ref[0, corner]
                slot = jnp.clip(entry, 0, SLOTS - 1)
                live = entry < SLOTS
                at_x, at_y = (7 * far, 7 * side) if axis else (7 * side, 7 * far)
                if axis == 0:
                    for f in range(2):
                        lines.append(jnp.where(live, full[f, slot, at_x, at_y], 0.0))
                    continue
                base = 18 * far + 6 * side
                low, mid, high = near[slot, base], near[slot, base + 1], near[slot, base + 2]
                up, same, down = shifts(
                    full[1, slot, at_x, at_y],
                    live & (mid < ZERO),
                    live & (high < ZERO),
                    live & (low < ZERO),
                )
                lines += [down, same, up]
            lines = jnp.concatenate(lines, axis=0).astype(jnp.bfloat16)
            outs[k][pl.ds(FACE_ROWS, lines.shape[0])] = lines
    x_out[1][pl.ds(X_ROWS + FACE_ROWS, SPARE_ROWS)] = jnp.zeros((SPARE_ROWS, C), jnp.bfloat16)
    for i, (built, send) in enumerate(zip(refs[4:8], sends)):
        results += fetching((built, send, sems.at[last + 1 + i]))
    for result in results:
        result.wait()


def pack(features, out_grad, mask, near, face_sends, edge_sends):
    sends = [
        jax.ShapeDtypeStruct((rows + FACE_ROWS, C), jnp.bfloat16)
        for rows in (Y_ROWS, Y_ROWS, X_ROWS, X_ROWS + SPARE_ROWS)
    ]
    return pl.pallas_call(
        pack_kernel,
        out_shape=[
            jax.ShapeDtypeStruct((ROOM_BRICKS, SLOTS, 512, C), jnp.bfloat16),
            jax.ShapeDtypeStruct((SLOTS, 512, C), jnp.bfloat16),
            jax.ShapeDtypeStruct((SLOTS, 512, C), jnp.bfloat16),
            jax.ShapeDtypeStruct((ROOM_TABLES, SLOTS, 27), jnp.int32),
        ]
        + sends,
        in_specs=[hbm()] * 6,
        out_specs=[hbm()] * 8,
        scratch_shapes=[pltpu.VMEM(send.shape, send.dtype) for send in sends]
        + [
            pltpu.SMEM((FACE, 4), jnp.int32),
            pltpu.SMEM((1, 4), jnp.int32),
            pltpu.SMEM((SLOTS, 27), jnp.int32),
            pltpu.VMEM((2, SLOTS, 512, C), jnp.bfloat16),
            pltpu.VMEM((SLOTS, 512), jnp.int32),
            pltpu.VMEM((2, SLOTS, 8, 8, 8, C), jnp.float32),
            pltpu.SemaphoreType.DMA((4 + 5 * SLOTS + 5,)),
        ],
        compiler_params=pltpu.CompilerParams(vmem_limit_bytes=PACK_LIMIT),
        name="pack",
    )(face_sends.T, edge_sends.T, near, features, out_grad, mask)


def parts_of(ref):
    rows = ref.shape[0] // 2
    return ref.at[pl.ds(0, rows)], ref.at[pl.ds(rows, rows)]


def join_kernel(first, second, out, more):
    rows = first.shape[0] - FACE_ROWS
    for k, src in enumerate((first, second)):
        out[pl.ds(k * rows, rows)] = src[pl.ds(0, rows)]
        more[pl.ds(k * FACE_ROWS, FACE_ROWS)] = src[pl.ds(rows, FACE_ROWS)]


def join(first, second):
    outs = [
        jax.ShapeDtypeStruct((2 * rows, C), jnp.bfloat16) for rows in (first.shape[0] - FACE_ROWS, FACE_ROWS)
    ]
    return pl.pallas_call(
        join_kernel,
        out_shape=outs,
        in_specs=[vmem()] * 2,
        out_specs=[vmem()] * 2,
        compiler_params=pltpu.CompilerParams(vmem_limit_bytes=VMEM_LIMIT),
        name="join_sides",
    )(first, second)


def forward_kernel(x_came, out0, out1):
    odd_x, odd_y = parity("gx"), parity("gy")
    for k, out in enumerate((out0, out1)):
        far = side_of(k, odd_y)
        for j, came in enumerate(parts_of(x_came)):
            source = side_of(j, odd_x)
            rows = came[pl.ds(pl.multiple_of(FACE_ROWS + 16 * far, 16), 16)]
            out[pl.ds(pl.multiple_of(16 * source, 16), 16)] = rows


def forward_corners(x_came):
    send = jax.ShapeDtypeStruct((32, C), jnp.bfloat16)
    return pl.pallas_call(
        forward_kernel,
        out_shape=[send] * 2,
        in_specs=[vmem()],
        out_specs=[vmem()] * 2,
        compiler_params=pltpu.CompilerParams(vmem_limit_bytes=VMEM_LIMIT),
        name="forward_corners",
    )(x_came)


def fill_own(bricks, lx, ly, corners):
    for s in range(SLOTS):
        whole = bricks[s].astype(jnp.float32).reshape(8, 8, 8, C)
        for side, at in ((0, 7), (1, 0)):
            lx[side, s] = whole[at]
            ly[side, s] = whole[:, at]
            for other, far in ((0, 7), (1, 0)):
                corners[2 * side + other, s] = whole[at, far]


def fill_zero(lx, ly, corners, first):
    for ref in (lx, ly, corners):
        count = ref.shape[1] - first
        ref[:, pl.ds(first, count)] = jnp.zeros((ref.shape[0], count) + ref.shape[2:], jnp.float32)


def fill_came(f, x_came, y_came, edges, lx, ly, corners):
    odd_x, odd_y = parity("gx"), parity("gy")
    for came, first, odd, dst in ((parts_of(x_came), 0, odd_x, lx), (y_came, f * Y_ROWS, odd_y, ly)):
        for k, part in enumerate(came):
            side = side_of(k, odd)
            for r in range(FACE):
                rows = part[pl.ds(first + r * 64, 64)]
                dst[side, SLOTS + r] = rows.astype(jnp.float32).reshape(8, 8, C)
            dst[k, SLOTS + FACE] = jnp.zeros((8, 8, C), jnp.float32)
    for k, came in enumerate(edges):
        side = side_of(k, odd_y)
        for j in range(2):
            rows = came[pl.ds(16 * j, 16)].astype(jnp.float32)
            corners[2 * j + side, SLOTS + 2 * FACE] = rows[8 * f : 8 * f + 8]
    for sx in range(2):
        for sy in range(2):
            c = 2 * sx + sy
            for r in range(FACE):
                corners[c, SLOTS + r] = lx[sx, SLOTS + r, 0 if sy else 7]
                corners[c, SLOTS + FACE + r] = ly[sy, SLOTS + r, 0 if sx else 7]
            corners[c, SLOTS + 2 * FACE + 1] = jnp.zeros((8, C), jnp.float32)


def build_columns(s, bricks, near, lx, ly, corners, wide, which):
    def spread(cells, at_x, at_y, depth):
        flat = cells.reshape(-1, 8, C)
        for k, moved in enumerate(shifts(flat, depth == 0, depth == -1, depth == 1)):
            wide[k, at_x, at_y] = moved.reshape(cells.shape)

    def column(nx, ny):
        base = 9 * (nx + 1) + 3 * (ny + 1)
        low, mid, high = near[s, base], near[s, base + 1], near[s, base + 2]
        entry = jnp.minimum(jnp.minimum(low, mid), high)
        depth = jnp.where(low < ZERO, -1, jnp.where(high < ZERO, 1, 0))
        if which == "own":
            depth = jnp.where(entry < SLOTS, depth, 2)
        if which == "rim":
            depth = jnp.where((entry >= SLOTS) & (entry < SLOTS + 4 * FACE), depth, 2)
        return entry, depth

    middle = pl.ds(1, 8)
    if which != "rim":
        spread(bricks[s].astype(jnp.float32).reshape(8, 8, 8, C), middle, middle, 0)
    for side, n in ((0, -1), (1, 1)):
        edge_at = pl.ds(0 if n < 0 else 9, 1)
        entry, depth = column(n, 0)
        place = jnp.where(entry < SLOTS, entry, jnp.clip(entry - FACE * side, 0, SLOTS + FACE))
        spread(lx[side, place].reshape(1, 8, 8, C), edge_at, middle, depth)
        entry, depth = column(0, n)
        place = jnp.where(entry < SLOTS, entry, jnp.clip(entry - FACE * (2 + side), 0, SLOTS + FACE))
        spread(ly[side, place].reshape(8, 1, 8, C), middle, edge_at, depth)
    for sx in range(2):
        for sy in range(2):
            entry, depth = column(2 * sx - 1, 2 * sy - 1)
            first_x = SLOTS + FACE * sx
            first_y = SLOTS + FACE * (2 + sy)
            own_edge = SLOTS + 4 * FACE + 2 * sx + sy
            in_x = (entry >= first_x) & (entry < first_x + FACE)
            in_y = (entry >= first_y) & (entry < first_y + FACE)
            place = jnp.where(entry == own_edge, SLOTS + 2 * FACE, SLOTS + 2 * FACE + 1)
            place = jnp.where(in_y, SLOTS + FACE + entry - first_y, place)
            place = jnp.where(in_x, SLOTS + entry - first_x, place)
            place = jnp.where(entry < SLOTS, entry, place)
            spread(corners[2 * sx + sy, place].reshape(1, 1, 8, C), pl.ds(9 * sx, 1), pl.ds(9 * sy, 1), depth)


def stack_columns(s, wide, v):
    for y in range(3):
        for z in range(3):
            cells = wide[z, :, pl.ds(y, 8)].reshape(10, 64, C).astype(jnp.bfloat16)
            v[s, :, :, pl.ds((3 * y + z) * C, C)] = cells


def columns_scratch():
    return [
        pltpu.VMEM((2, SLOTS + FACE + 1, 8, 8, C), jnp.float32),
        pltpu.VMEM((2, SLOTS + FACE + 1, 8, 8, C), jnp.float32),
        pltpu.VMEM((4, SLOTS + 2 * FACE + 2, 8, C), jnp.float32),
        pltpu.VMEM((3, 10, 10, 8, C), jnp.float32),
        pltpu.SMEM((SLOTS, 27), jnp.int32),
        pltpu.SemaphoreType.DMA(()),
    ]


def columns_kernel(near_hbm, act_hbm, v, lx, ly, corners, wide, near, sem, act, act_sem):
    table, bricks = fetching((near_hbm.at[0], near, sem), (act_hbm.at[0], act, act_sem))
    fill_zero(lx, ly, corners, SLOTS)
    bricks.wait()
    fill_own(act, lx, ly, corners)
    table.wait()

    def per_slot(s, carry):
        build_columns(s, act, near, lx, ly, corners, wide, "own")
        stack_columns(s, wide, v)
        return carry

    lax.fori_loop(0, SLOTS, per_slot, 0)


def own_columns(near, act):
    return pl.pallas_call(
        columns_kernel,
        out_shape=jax.ShapeDtypeStruct((SLOTS, 10, 64, 9 * C), jnp.bfloat16),
        in_specs=[hbm()] * 2,
        out_specs=vmem(),
        scratch_shapes=columns_scratch()
        + [pltpu.VMEM((SLOTS, 512, C), jnp.bfloat16), pltpu.SemaphoreType.DMA(())],
        compiler_params=pltpu.CompilerParams(vmem_limit_bytes=VMEM_LIMIT),
        cost_estimate=pl.CostEstimate(flops=1 << 24, bytes_accessed=6 << 20, transcendentals=0),
        name="own_columns",
    )(near, act)


def inner_kernel(v, grd, out, turned):
    for s in range(SLOTS):
        for q in range(4):
            turned[:, pl.ds((4 * s + q) * C, C)] = grd[s, pl.ds(q * C, C)].T
    for x in range(3):
        cells = v[:, pl.ds(x, 8)].reshape(SLOTS * 512, 9 * C)
        terms = jnp.dot(turned[...], cells, preferred_element_type=jnp.float32)
        for j in range(9):
            out[pl.ds((9 * x + j) * C, C)] = terms[:, j * C : (j + 1) * C].T


def inner_terms(v, grd):
    return pl.pallas_call(
        inner_kernel,
        out_shape=jax.ShapeDtypeStruct((ROWS, C), jnp.float32),
        in_specs=[vmem()] * 2,
        out_specs=vmem(),
        scratch_shapes=[pltpu.VMEM((C, SLOTS * 512), jnp.bfloat16)],
        compiler_params=pltpu.CompilerParams(vmem_limit_bytes=VMEM_LIMIT),
        cost_estimate=pl.CostEstimate(flops=2 * 2048 * ROWS * C, bytes_accessed=6 << 20, transcendentals=0),
        name="inner_terms",
    )(v, grd)


def rim_kernel(near_hbm, inner, grd, x_ref, y0, y1, keep, send, lx, ly, corners, wide, near, sem, *refs):
    vx, vy, ends_a, ends_g, side_x, side_y, ends = refs
    (table,) = fetching((near_hbm, near, sem))
    fill_came(0, x_ref, (y0, y1), (), lx, ly, corners)
    for k, came in enumerate(parts_of(x_ref)):
        side = side_of(k, parity("gx"))
        for j in range(2):
            ends_a[side, j] = came[pl.ds(FACE_ROWS + 16 * j, 16)].astype(jnp.float32)[0:8]
    for k, came in enumerate((y0, y1)):
        side = side_of(k, parity("gy"))
        ends_g[side] = came[pl.ds(FACE_ROWS, 48)].astype(jnp.float32).reshape(2, 3, 8, C)
    table.wait()
    for s in range(SLOTS):
        build_columns(s, None, near, lx, ly, corners, wide, "rim")
        rows = pl.ds(64 * s, 64)
        for side in range(2):
            for j in range(9):
                cells = wide[j % 3, 9 * side, pl.ds(j // 3, 8)]
                vx[side, rows, pl.ds(j * C, C)] = cells.reshape(64, C).astype(jnp.bfloat16)
        for z in range(3):
            for sx in range(2):
                for sy in range(2):
                    wide[z, 9 * sx, 9 * sy] = jnp.zeros((8, C), jnp.float32)
        for side in range(2):
            for j in range(9):
                cells = wide[j % 3, pl.ds(j // 3, 8), 9 * side]
                vy[side, rows, pl.ds(j * C, C)] = cells.reshape(64, C).astype(jnp.bfloat16)
    grads = grd[...]
    lines = grads.astype(jnp.float32).reshape(SLOTS, 8, 8, 8, C)

    def term(cells, rows):
        return lax.dot_general(cells, rows, (((0,), (0,)), ((), ())), preferred_element_type=jnp.float32)

    def end(line):
        return jnp.concatenate([line, jnp.zeros(line.shape, jnp.float32)], axis=0).astype(jnp.bfloat16)

    for side in range(2):
        rows = grads[:, 448 * side : 448 * side + 64].reshape(SLOTS * 64, C)
        side_x[side] = term(vx[side], rows)
        rows = lines[:, :, 7 * side].reshape(SLOTS * 64, C).astype(jnp.bfloat16)
        side_y[side] = term(vy[side], rows)
    for sx in range(2):
        for sy in range(2):
            lines_g = jnp.concatenate([ends_g[sy, sx, z] for z in range(3)], axis=1)
            ends[sx, sy] = term(end(ends_a[sx, sy]), end(lines_g))

    def write(halves):
        for x in range(3):
            for y in range(3):
                for z in range(3):
                    first = (9 * x + 3 * y + z) * C
                    value = inner[pl.ds(first, C)]
                    if x != 1:
                        value += side_x[x // 2, pl.ds((3 * y + z) * C, C)]
                    if y != 1:
                        value += side_y[y // 2, pl.ds((3 * x + z) * C, C)]
                    if x != 1 and y != 1:
                        sx, sy = x // 2, 1 - y // 2
                        value += ends[sx, sy, :, pl.ds(z * C, C)]
                    for half in range(2):
                        low = max(first, half * HALF)
                        rows = min(first + C, (half + 1) * HALF) - low
                        if rows > 0:
                            halves[half][pl.ds(low - half * HALF, rows)] = value[low - first : low - first + rows]

    core = parity("gy")

    @pl.when(core == 0)
    def _():
        write((keep, send))

    @pl.when(core == 1)
    def _():
        write((send, keep))


def rim_terms(near, inner, grd, x_came, y_came):
    half = jax.ShapeDtypeStruct((HALF, C), jnp.float32)
    side = pltpu.VMEM((2, SLOTS * 64, 9 * C), jnp.bfloat16)
    return pl.pallas_call(
        rim_kernel,
        out_shape=[half, half],
        in_specs=[hbm()] + [vmem()] * 5,
        out_specs=[vmem()] * 2,
        scratch_shapes=columns_scratch()
        + [
            side,
            side,
            pltpu.VMEM((2, 2, 8, C), jnp.float32),
            pltpu.VMEM((2, 2, 3, 8, C), jnp.float32),
            pltpu.VMEM((2, 9 * C, C), jnp.float32),
            pltpu.VMEM((2, 9 * C, C), jnp.float32),
            pltpu.VMEM((2, 2, C, 3 * C), jnp.float32),
        ],
        compiler_params=pltpu.CompilerParams(vmem_limit_bytes=VMEM_LIMIT),
        cost_estimate=pl.CostEstimate(flops=2 * 256 * 36 * C * C, bytes_accessed=6 << 20, transcendentals=0),
        name="rim_terms",
    )(near, inner, grd, x_came, *y_came)


def power_of(values):
    peak = jnp.max(jnp.abs(values))
    return jnp.clip(jnp.ceil(jnp.log2(jnp.full((8, C), peak))), -100.0, 100.0)[0:1]


def merge_kernel(groups, take, keep, came, out, total):
    held = out.shape[1]
    total[pl.ds(0, HALF)] = keep[...] + came[...]
    if groups * take > HALF:
        total[pl.ds(HALF, groups * take - HALF)] = jnp.zeros((groups * take - HALF, C), jnp.float32)
    power = power_of(total[...])
    scale = jnp.exp2(14.0 - power)
    for p in range(groups):
        out[p, pl.ds(0, take)] = total[pl.ds(p * take, take)] * scale
        out[p, pl.ds(take, held - take)] = jnp.broadcast_to(power, (held - take, C))


def merge(groups, take, held, keep, came):
    return pl.pallas_call(
        lambda *refs: merge_kernel(groups, take, *refs),
        out_shape=jax.ShapeDtypeStruct((groups, held, C), jnp.float32),
        in_specs=[vmem()] * 2,
        out_specs=vmem(),
        scratch_shapes=[pltpu.VMEM((groups * take, C), jnp.float32)],
        compiler_params=pltpu.CompilerParams(vmem_limit_bytes=VMEM_LIMIT),
        name="merge",
    )(keep, came)


def sum_kernel(take, blocks, out):
    groups, held, _ = blocks.shape
    total = jnp.zeros((take, C), jnp.float32)
    for p in range(groups):
        total += blocks[p, pl.ds(0, take)] * jnp.exp2(blocks[p, pl.ds(take, 1)] - 14.0)
    power = power_of(total)
    total = total * jnp.exp2(14.0 - power)
    for p in range(groups):
        out[p, pl.ds(0, take)] = total
        out[p, pl.ds(take, held - take)] = jnp.broadcast_to(power, (held - take, C))


def sum_blocks(take, blocks):
    return pl.pallas_call(
        lambda *refs: sum_kernel(take, *refs),
        out_shape=jax.ShapeDtypeStruct(blocks.shape, jnp.float32),
        in_specs=[vmem()],
        out_specs=vmem(),
        compiler_params=pltpu.CompilerParams(vmem_limit_bytes=VMEM_LIMIT),
        name="sum_blocks",
    )(blocks)


def decode_kernel(take, scale, places, own, blocks, *refs):
    out, half, sems = refs[-3:]
    groups = blocks.shape[0]
    core = parity("gy")
    target = out.at[core if own else 1 - core]
    copies = []
    done = 0
    for p in range(groups):
        rows = min(take, HALF - p * take)
        if rows > 0:
            factor = jnp.exp2(blocks[places[p], pl.ds(take, 1)] - 14.0) * scale
            half[pl.ds(p * take, rows)] = blocks[places[p], pl.ds(0, rows)] * factor
        ready = min((p + 1) * take, HALF)
        if ready - done >= HALF // 4 and ready % 8 == 0 or p == groups - 1:
            piece = pl.ds(done, ready - done)
            copies += fetching((half.at[piece], target.at[piece], sems.at[len(copies)]))
            done = ready
    for copy in copies:
        copy.wait()


def decode(take, scale, places, blocks, begun=None):
    rest = () if begun is None else (begun,)
    return pl.pallas_call(
        lambda *refs: decode_kernel(take, scale, places, not rest, *refs),
        out_shape=jax.ShapeDtypeStruct((2, HALF, C), jnp.float32),
        in_specs=[vmem()] + [hbm()] * len(rest),
        out_specs=hbm(),
        scratch_shapes=[pltpu.VMEM((HALF, C), jnp.float32), pltpu.SemaphoreType.DMA((5,))],
        input_output_aliases={1: 0} if rest else {},
        compiler_params=pltpu.CompilerParams(vmem_limit_bytes=VMEM_LIMIT),
        name="decode_other" if rest else "decode_own",
    )(blocks, *rest)


def product_kernel(f, near_hbm, mask_ref, kernel_ref, bricks, x_ref, y0, y1, e0, e1, out, *refs):
    lx, ly, corners, wide, near, sem, v, *flipped = refs
    (table,) = fetching((near_hbm, near, sem))
    weights = kernel_ref
    if f == 1:
        weights = flipped[0]
        for o in range(27):
            weights[pl.ds((26 - o) * C, C)] = kernel_ref[pl.ds(o * C, C)].T
    fill_own(bricks, lx, ly, corners)
    fill_came(f, x_ref, (y0, y1), (e0, e1), lx, ly, corners)
    table.wait()

    def per_slot(s, carry):
        build_columns(s, bricks, near, lx, ly, corners, wide, "all")
        stack_columns(s, wide, v)
        total = jnp.zeros((512, C), jnp.float32)
        for x in range(3):
            cells = v[s, pl.ds(x, 8)].reshape(512, 9 * C)
            total += jnp.dot(cells, weights[pl.ds(x * 9 * C, 9 * C)], preferred_element_type=jnp.float32)
        out[s] = (total * mask_columns(mask_ref, s)).astype(jnp.bfloat16)
        return carry

    lax.fori_loop(0, SLOTS, per_slot, 0)


def product(f, near, mask, kernel, bricks, x_came, y_came, edges):
    return pl.pallas_call(
        lambda *refs: product_kernel(f, *refs),
        out_shape=jax.ShapeDtypeStruct((SLOTS, 512, C), jnp.bfloat16),
        in_specs=[hbm()] + [vmem()] * 8,
        out_specs=vmem(),
        scratch_shapes=columns_scratch()
        + [pltpu.VMEM((SLOTS, 10, 64, 9 * C), jnp.bfloat16)]
        + ([pltpu.VMEM((ROWS, C), jnp.bfloat16)] if f else []),
        compiler_params=pltpu.CompilerParams(vmem_limit_bytes=VMEM_LIMIT),
        cost_estimate=pl.CostEstimate(flops=2 * 2048 * ROWS * C, bytes_accessed=4 << 20, transcendentals=0),
        name=("output_product", "input_grad_product")[f],
    )(near, mask, kernel, bricks, x_came, *y_came, *edges)


def swapped(value, axis, k):
    pairs = []
    for low in range(k, lax.axis_size(axis) - 1, 2):
        pairs += [(low, low + 1), (low + 1, low)]
    return lax.ppermute(value, axis, pairs)


def hopped(value, axis):
    size = lax.axis_size(axis)
    pairs = [(i, i + 2) for i in range(1, size - 2, 2)] + [(i, i - 2) for i in range(2, size, 2)]
    return lax.ppermute(value, axis, pairs)


def local(features, out_grad, kernel, voxel_mask, neighbours, face_sends, edge_sends):
    size_x, size_y = lax.axis_size("gx"), lax.axis_size("gy")
    parts = size_x * size_y
    groups = parts // 2
    take = -(-HALF // groups)
    held = -(-(take + 1) // 16) * 16
    members = [[i for i in range(parts) if i % size_y % 2 == core] for core in range(2)]
    half, row = groups // 2, size_y // 2
    inward = [k + j for k in range(half - row, -1, -row) for j in range(row)]
    in_turn = [k for pair in zip(range(half, groups), inward) for k in pair]
    onward = [(k + half) % groups for k in range(groups)]
    places = [onward.index(k) for k in in_turn]

    def spread(blocks, order):
        same_core = [[core[k] for k in order] for core in members]
        return lax.all_to_all(blocks, ("gx", "gy"), 0, 0, axis_index_groups=same_core, tiled=True)

    held_act, act, grd, table, y0, y1, x0, x1 = pack(
        features.reshape(SLOTS, 512, C),
        out_grad.reshape(SLOTS, 512, C),
        voxel_mask,
        neighbours,
        face_sends,
        edge_sends,
    )
    x1 = hopped(x1, "gx")
    y_came = [swapped(y0, "gy", 0), swapped(y1, "gy", 1)]
    v = own_columns(table, held_act)
    x1, v = lax.optimization_barrier((x1, v))
    x_came, x_more = join(x0, x1)
    x_more, v = lax.optimization_barrier((x_more, v))
    x_came = swapped(x_came, "gx", 0)
    inner = inner_terms(v, grd)
    keep, send = rim_terms(neighbours, inner, grd, x_came, y_came)
    blocks = merge(groups, take, held, keep, swapped(send, "gy", 0)).astype(jnp.float16)
    rows = kernel.reshape(ROWS, C)
    blocks, act, x_came, x_more = lax.optimization_barrier((blocks, act, x_came, x_more))
    x_more = swapped(x_more, "gx", 0)
    e0, e1 = forward_corners(x_came)
    edges = [swapped(e0, "gy", 0), swapped(e1, "gy", 1)]
    output = product(0, neighbours, voxel_mask, rows, act, x_came, y_came, edges)
    arrived, output, x_more = lax.optimization_barrier((spread(blocks, in_turn), output, x_more))
    copies = sum_blocks(take, arrived.astype(jnp.float32)).astype(jnp.float16)
    copies, grd = lax.optimization_barrier((copies, grd))
    input_grad = product(1, neighbours, voxel_mask, rows, grd, x_more, y_came, edges)
    mine, input_grad = lax.optimization_barrier((spread(copies, onward), input_grad))
    other = swapped(mine, "gy", 0)
    scale = 1.0 / math.sqrt(parts * SLOTS * 512)
    weight = decode(take, scale, places, mine.astype(jnp.float32))
    weight = decode(take, scale, places, other.astype(jnp.float32), weight)
    shape = (SLOTS, 8, 8, 8, C)
    return output.reshape(shape), input_grad.reshape(shape), weight.reshape(27, C, C)


def solution(mesh):
    spec = P(("gx", "gy"))
    return jax.shard_map(
        local,
        mesh=mesh,
        in_specs=(spec, spec, P(), spec, spec, spec, spec),
        out_specs=(spec, spec, P()),
        check_vma=False,
    )
```

```python
import math

import jax
import jax.numpy as jnp
from jax import lax
from jax.experimental import pallas as pl
from jax.experimental.pallas import tpu as pltpu
from jax.sharding import PartitionSpec as P

FACES = ((-1, 0), (1, 0), (0, -1), (0, 1))
EDGES = ((-1, -1), (-1, 1), (1, -1), (1, 1))
C = 128
SLOTS = 4
FACE = 2
ZERO = SLOTS + 4 * FACE + 4
ROWS = 27 * C
FACE_ROWS = FACE * 64
X_ROWS = FACE_ROWS + 32
Y_ROWS = FACE_ROWS + 48
HALF = ROWS // 2
SPARE_ROWS = 32
VMEM_LIMIT = 32 * 1024 * 1024
PACK_LIMIT = 60 * 1024 * 1024
ROOM_BRICKS = 48
ROOM_TABLES = 12 * 1024


def vmem():
    return pl.BlockSpec(memory_space=pltpu.VMEM)


def hbm():
    return pl.BlockSpec(memory_space=pltpu.HBM)


def fetching(*pairs):
    copies = [pltpu.make_async_copy(src, dst, sem) for src, dst, sem in pairs]
    for copy in copies:
        copy.start()
    return copies


def fetched(*pairs):
    for copy in fetching(*pairs):
        copy.wait()


def mask_columns(mask_ref, s):
    m = mask_ref[...].astype(jnp.float32).astype(jnp.bfloat16)
    pick = (lax.broadcasted_iota(jnp.int32, (SLOTS, C), 0) == s).astype(jnp.float32).astype(jnp.bfloat16)
    return lax.dot_general(m, pick, (((0,), (0,)), ((), ())), preferred_element_type=jnp.float32)


def parity(axis):
    return lax.rem(lax.axis_index(axis), 2)


def side_of(k, odd):
    return 1 - odd if k == 0 else odd


def shifts(cells, same, below, above):
    line = lax.broadcasted_iota(jnp.int32, cells.shape, cells.ndim - 2)
    axis = cells.ndim - 2
    up = jnp.where((same & (line >= 1)) | (below & (line == 0)), pltpu.roll(cells, 1, axis), 0.0)
    down = jnp.where((same & (line <= 6)) | (above & (line == 7)), pltpu.roll(cells, 7, axis), 0.0)
    return up, jnp.where(same, cells, 0.0), down


def pack_kernel(face_hbm, edge_hbm, near_hbm, feat_hbm, grad_hbm, mask_hbm, held_out, act_out, grd_out, near_out, *refs):
    sends = refs[0:4]
    y_out, x_out = refs[4:6], refs[6:8]
    face_ref, edge_ref, near, raw, mask_ref, full, sems = refs[8:]
    got_mask, *tables = fetching(
        (mask_hbm, mask_ref, sems.at[0]),
        (face_hbm, face_ref, sems.at[1]),
        (edge_hbm, edge_ref, sems.at[2]),
        (near_hbm, near, sems.at[3]),
    )
    got = [
        fetching(
            (feat_hbm.at[s], raw.at[0, s], sems.at[4 + 2 * s]),
            (grad_hbm.at[s], raw.at[1, s], sems.at[5 + 2 * s]),
        )
        for s in range(SLOTS)
    ]
    got_mask.wait()
    results = []
    for s in range(SLOTS):
        rows = mask_columns(mask_ref, s)
        for f in range(2):
            got[s][f].wait()
            masked = raw[f, s].astype(jnp.float32) * rows
            full[f, s] = masked.reshape(8, 8, 8, C)
            raw[f, s] = masked.astype(jnp.bfloat16)
        first = 4 + 2 * SLOTS + 3 * s
        results += fetching(
            (raw.at[0, s], held_out.at[0, s], sems.at[first]),
            (raw.at[0, s], act_out.at[s], sems.at[first + 1]),
            (raw.at[1, s], grd_out.at[s], sems.at[first + 2]),
        )
    for table in tables:
        table.wait()
    last = 4 + 5 * SLOTS
    results += fetching((near, near_out.at[0], sems.at[last]))
    for axis, outs in enumerate((x_out, y_out)):
        odd = parity("gy" if axis else "gx")
        for k in range(2):
            side = side_of(k, odd)
            for f in range(2):
                for r in range(FACE):
                    entry = face_ref[r, 2 * axis + side]
                    slot = jnp.clip(entry, 0, SLOTS - 1)
                    layer = full[f, slot, :, 7 * side] if axis else full[f, slot, 7 * side]
                    layer = jnp.where(entry < SLOTS, layer, 0.0)
                    first = f * (Y_ROWS if axis else X_ROWS) + r * 64
                    outs[k][pl.ds(first, 64)] = layer.reshape(64, C).astype(jnp.bfloat16)
            lines = []
            for far in range(2):
                corner = 2 * far + side if axis else 2 * side + far
                entry = edge_ref[0, corner]
                slot = jnp.clip(entry, 0, SLOTS - 1)
                live = entry < SLOTS
                at_x, at_y = (7 * far, 7 * side) if axis else (7 * side, 7 * far)
                if axis == 0:
                    for f in range(2):
                        lines.append(jnp.where(live, full[f, slot, at_x, at_y], 0.0))
                    continue
                base = 18 * far + 6 * side
                low, mid, high = near[slot, base], near[slot, base + 1], near[slot, base + 2]
                up, same, down = shifts(
                    full[1, slot, at_x, at_y],
                    live & (mid < ZERO),
                    live & (high < ZERO),
                    live & (low < ZERO),
                )
                lines += [down, same, up]
            lines = jnp.concatenate(lines, axis=0).astype(jnp.bfloat16)
            outs[k][pl.ds(FACE_ROWS, lines.shape[0])] = lines
    x_out[1][pl.ds(X_ROWS + FACE_ROWS, SPARE_ROWS)] = jnp.zeros((SPARE_ROWS, C), jnp.bfloat16)
    for i, (built, send) in enumerate(zip(refs[4:8], sends)):
        results += fetching((built, send, sems.at[last + 1 + i]))
    for result in results:
        result.wait()


def pack(features, out_grad, mask, near, face_sends, edge_sends):
    sends = [
        jax.ShapeDtypeStruct((rows + FACE_ROWS, C), jnp.bfloat16)
        for rows in (Y_ROWS, Y_ROWS, X_ROWS, X_ROWS + SPARE_ROWS)
    ]
    return pl.pallas_call(
        pack_kernel,
        out_shape=[
            jax.ShapeDtypeStruct((ROOM_BRICKS, SLOTS, 512, C), jnp.bfloat16),
            jax.ShapeDtypeStruct((SLOTS, 512, C), jnp.bfloat16),
            jax.ShapeDtypeStruct((SLOTS, 512, C), jnp.bfloat16),
            jax.ShapeDtypeStruct((ROOM_TABLES, SLOTS, 27), jnp.int32),
        ]
        + sends,
        in_specs=[hbm()] * 6,
        out_specs=[hbm()] * 8,
        scratch_shapes=[pltpu.VMEM(send.shape, send.dtype) for send in sends]
        + [
            pltpu.SMEM((FACE, 4), jnp.int32),
            pltpu.SMEM((1, 4), jnp.int32),
            pltpu.SMEM((SLOTS, 27), jnp.int32),
            pltpu.VMEM((2, SLOTS, 512, C), jnp.bfloat16),
            pltpu.VMEM((SLOTS, 512), jnp.int32),
            pltpu.VMEM((2, SLOTS, 8, 8, 8, C), jnp.float32),
            pltpu.SemaphoreType.DMA((4 + 5 * SLOTS + 5,)),
        ],
        compiler_params=pltpu.CompilerParams(vmem_limit_bytes=PACK_LIMIT),
        name="pack",
    )(face_sends.T, edge_sends.T, near, features, out_grad, mask)


def parts_of(ref):
    rows = ref.shape[0] // 2
    return ref.at[pl.ds(0, rows)], ref.at[pl.ds(rows, rows)]


def join_kernel(first, second, out, more):
    rows = first.shape[0] - FACE_ROWS
    for k, src in enumerate((first, second)):
        out[pl.ds(k * rows, rows)] = src[pl.ds(0, rows)]
        more[pl.ds(k * FACE_ROWS, FACE_ROWS)] = src[pl.ds(rows, FACE_ROWS)]


def join(first, second):
    outs = [
        jax.ShapeDtypeStruct((2 * rows, C), jnp.bfloat16) for rows in (first.shape[0] - FACE_ROWS, FACE_ROWS)
    ]
    return pl.pallas_call(
        join_kernel,
        out_shape=outs,
        in_specs=[vmem()] * 2,
        out_specs=[vmem()] * 2,
        compiler_params=pltpu.CompilerParams(vmem_limit_bytes=VMEM_LIMIT),
        name="join_sides",
    )(first, second)


def forward_kernel(x_came, out0, out1):
    odd_x, odd_y = parity("gx"), parity("gy")
    for k, out in enumerate((out0, out1)):
        far = side_of(k, odd_y)
        for j, came in enumerate(parts_of(x_came)):
            source = side_of(j, odd_x)
            rows = came[pl.ds(pl.multiple_of(FACE_ROWS + 16 * far, 16), 16)]
            out[pl.ds(pl.multiple_of(16 * source, 16), 16)] = rows


def forward_corners(x_came):
    send = jax.ShapeDtypeStruct((32, C), jnp.bfloat16)
    return pl.pallas_call(
        forward_kernel,
        out_shape=[send] * 2,
        in_specs=[vmem()],
        out_specs=[vmem()] * 2,
        compiler_params=pltpu.CompilerParams(vmem_limit_bytes=VMEM_LIMIT),
        name="forward_corners",
    )(x_came)


def fill_own(bricks, lx, ly, corners):
    for s in range(SLOTS):
        whole = bricks[s].astype(jnp.float32).reshape(8, 8, 8, C)
        for side, at in ((0, 7), (1, 0)):
            lx[side, s] = whole[at]
            ly[side, s] = whole[:, at]
            for other, far in ((0, 7), (1, 0)):
                corners[2 * side + other, s] = whole[at, far]


def fill_zero(lx, ly, corners, first):
    for ref in (lx, ly, corners):
        count = ref.shape[1] - first
        ref[:, pl.ds(first, count)] = jnp.zeros((ref.shape[0], count) + ref.shape[2:], jnp.float32)


def fill_came(f, x_came, y_came, edges, lx, ly, corners):
    odd_x, odd_y = parity("gx"), parity("gy")
    for came, first, odd, dst in ((parts_of(x_came), 0, odd_x, lx), (y_came, f * Y_ROWS, odd_y, ly)):
        for k, part in enumerate(came):
            side = side_of(k, odd)
            for r in range(FACE):
                rows = part[pl.ds(first + r * 64, 64)]
                dst[side, SLOTS + r] = rows.astype(jnp.float32).reshape(8, 8, C)
            dst[k, SLOTS + FACE] = jnp.zeros((8, 8, C), jnp.float32)
    for k, came in enumerate(edges):
        side = side_of(k, odd_y)
        for j in range(2):
            rows = came[pl.ds(16 * j, 16)].astype(jnp.float32)
            corners[2 * j + side, SLOTS + 2 * FACE] = rows[8 * f : 8 * f + 8]
    for sx in range(2):
        for sy in range(2):
            c = 2 * sx + sy
            for r in range(FACE):
                corners[c, SLOTS + r] = lx[sx, SLOTS + r, 0 if sy else 7]
                corners[c, SLOTS + FACE + r] = ly[sy, SLOTS + r, 0 if sx else 7]
            corners[c, SLOTS + 2 * FACE + 1] = jnp.zeros((8, C), jnp.float32)


def build_columns(s, bricks, near, lx, ly, corners, wide, which):
    def spread(cells, at_x, at_y, depth):
        flat = cells.reshape(-1, 8, C)
        for k, moved in enumerate(shifts(flat, depth == 0, depth == -1, depth == 1)):
            wide[k, at_x, at_y] = moved.reshape(cells.shape)

    def column(nx, ny):
        base = 9 * (nx + 1) + 3 * (ny + 1)
        low, mid, high = near[s, base], near[s, base + 1], near[s, base + 2]
        entry = jnp.minimum(jnp.minimum(low, mid), high)
        depth = jnp.where(low < ZERO, -1, jnp.where(high < ZERO, 1, 0))
        if which == "own":
            depth = jnp.where(entry < SLOTS, depth, 2)
        if which == "rim":
            depth = jnp.where((entry >= SLOTS) & (entry < SLOTS + 4 * FACE), depth, 2)
        return entry, depth

    middle = pl.ds(1, 8)
    if which != "rim":
        spread(bricks[s].astype(jnp.float32).reshape(8, 8, 8, C), middle, middle, 0)
    for side, n in ((0, -1), (1, 1)):
        edge_at = pl.ds(0 if n < 0 else 9, 1)
        entry, depth = column(n, 0)
        place = jnp.where(entry < SLOTS, entry, jnp.clip(entry - FACE * side, 0, SLOTS + FACE))
        spread(lx[side, place].reshape(1, 8, 8, C), edge_at, middle, depth)
        entry, depth = column(0, n)
        place = jnp.where(entry < SLOTS, entry, jnp.clip(entry - FACE * (2 + side), 0, SLOTS + FACE))
        spread(ly[side, place].reshape(8, 1, 8, C), middle, edge_at, depth)
    for sx in range(2):
        for sy in range(2):
            entry, depth = column(2 * sx - 1, 2 * sy - 1)
            first_x = SLOTS + FACE * sx
            first_y = SLOTS + FACE * (2 + sy)
            own_edge = SLOTS + 4 * FACE + 2 * sx + sy
            in_x = (entry >= first_x) & (entry < first_x + FACE)
            in_y = (entry >= first_y) & (entry < first_y + FACE)
            place = jnp.where(entry == own_edge, SLOTS + 2 * FACE, SLOTS + 2 * FACE + 1)
            place = jnp.where(in_y, SLOTS + FACE + entry - first_y, place)
            place = jnp.where(in_x, SLOTS + entry - first_x, place)
            place = jnp.where(entry < SLOTS, entry, place)
            spread(corners[2 * sx + sy, place].reshape(1, 1, 8, C), pl.ds(9 * sx, 1), pl.ds(9 * sy, 1), depth)


def stack_columns(s, wide, v):
    for y in range(3):
        for z in range(3):
            cells = wide[z, :, pl.ds(y, 8)].reshape(10, 64, C).astype(jnp.bfloat16)
            v[s, :, :, pl.ds((3 * y + z) * C, C)] = cells


def columns_scratch():
    return [
        pltpu.VMEM((2, SLOTS + FACE + 1, 8, 8, C), jnp.float32),
        pltpu.VMEM((2, SLOTS + FACE + 1, 8, 8, C), jnp.float32),
        pltpu.VMEM((4, SLOTS + 2 * FACE + 2, 8, C), jnp.float32),
        pltpu.VMEM((3, 10, 10, 8, C), jnp.float32),
        pltpu.SMEM((SLOTS, 27), jnp.int32),
        pltpu.SemaphoreType.DMA(()),
    ]


def columns_kernel(near_hbm, act_hbm, v, lx, ly, corners, wide, near, sem, act, act_sem):
    table, bricks = fetching((near_hbm.at[0], near, sem), (act_hbm.at[0], act, act_sem))
    fill_zero(lx, ly, corners, SLOTS)
    bricks.wait()
    fill_own(act, lx, ly, corners)
    table.wait()

    def per_slot(s, carry):
        build_columns(s, act, near, lx, ly, corners, wide, "own")
        stack_columns(s, wide, v)
        return carry

    lax.fori_loop(0, SLOTS, per_slot, 0)


def own_columns(near, act):
    return pl.pallas_call(
        columns_kernel,
        out_shape=jax.ShapeDtypeStruct((SLOTS, 10, 64, 9 * C), jnp.bfloat16),
        in_specs=[hbm()] * 2,
        out_specs=vmem(),
        scratch_shapes=columns_scratch()
        + [pltpu.VMEM((SLOTS, 512, C), jnp.bfloat16), pltpu.SemaphoreType.DMA(())],
        compiler_params=pltpu.CompilerParams(vmem_limit_bytes=VMEM_LIMIT),
        cost_estimate=pl.CostEstimate(flops=1 << 24, bytes_accessed=6 << 20, transcendentals=0),
        name="own_columns",
    )(near, act)


def inner_kernel(v, grd, out, turned):
    for s in range(SLOTS):
        for q in range(4):
            turned[:, pl.ds((4 * s + q) * C, C)] = grd[s, pl.ds(q * C, C)].T
    for x in range(3):
        cells = v[:, pl.ds(x, 8)].reshape(SLOTS * 512, 9 * C)
        terms = jnp.dot(turned[...], cells, preferred_element_type=jnp.float32)
        for j in range(9):
            out[pl.ds((9 * x + j) * C, C)] = terms[:, j * C : (j + 1) * C].T


def inner_terms(v, grd):
    return pl.pallas_call(
        inner_kernel,
        out_shape=jax.ShapeDtypeStruct((ROWS, C), jnp.float32),
        in_specs=[vmem()] * 2,
        out_specs=vmem(),
        scratch_shapes=[pltpu.VMEM((C, SLOTS * 512), jnp.bfloat16)],
        compiler_params=pltpu.CompilerParams(vmem_limit_bytes=VMEM_LIMIT),
        cost_estimate=pl.CostEstimate(flops=2 * 2048 * ROWS * C, bytes_accessed=6 << 20, transcendentals=0),
        name="inner_terms",
    )(v, grd)


def rim_kernel(near_hbm, inner, grd, x_ref, y0, y1, keep, send, lx, ly, corners, wide, near, sem, *refs):
    vx, vy, ends_a, ends_g, side_x, side_y, ends = refs
    (table,) = fetching((near_hbm, near, sem))
    fill_came(0, x_ref, (y0, y1), (), lx, ly, corners)
    for k, came in enumerate(parts_of(x_ref)):
        side = side_of(k, parity("gx"))
        for j in range(2):
            ends_a[side, j] = came[pl.ds(FACE_ROWS + 16 * j, 16)].astype(jnp.float32)[0:8]
    for k, came in enumerate((y0, y1)):
        side = side_of(k, parity("gy"))
        ends_g[side] = came[pl.ds(FACE_ROWS, 48)].astype(jnp.float32).reshape(2, 3, 8, C)
    table.wait()
    for s in range(SLOTS):
        build_columns(s, None, near, lx, ly, corners, wide, "rim")
        rows = pl.ds(64 * s, 64)
        for side in range(2):
            for j in range(9):
                cells = wide[j % 3, 9 * side, pl.ds(j // 3, 8)]
                vx[side, rows, pl.ds(j * C, C)] = cells.reshape(64, C).astype(jnp.bfloat16)
        for z in range(3):
            for sx in range(2):
                for sy in range(2):
                    wide[z, 9 * sx, 9 * sy] = jnp.zeros((8, C), jnp.float32)
        for side in range(2):
            for j in range(9):
                cells = wide[j % 3, pl.ds(j // 3, 8), 9 * side]
                vy[side, rows, pl.ds(j * C, C)] = cells.reshape(64, C).astype(jnp.bfloat16)
    grads = grd[...]
    lines = grads.astype(jnp.float32).reshape(SLOTS, 8, 8, 8, C)

    def term(cells, rows):
        return lax.dot_general(cells, rows, (((0,), (0,)), ((), ())), preferred_element_type=jnp.float32)

    def end(line):
        return jnp.concatenate([line, jnp.zeros(line.shape, jnp.float32)], axis=0).astype(jnp.bfloat16)

    for side in range(2):
        rows = grads[:, 448 * side : 448 * side + 64].reshape(SLOTS * 64, C)
        side_x[side] = term(vx[side], rows)
        rows = lines[:, :, 7 * side].reshape(SLOTS * 64, C).astype(jnp.bfloat16)
        side_y[side] = term(vy[side], rows)
    for sx in range(2):
        for sy in range(2):
            lines_g = jnp.concatenate([ends_g[sy, sx, z] for z in range(3)], axis=1)
            ends[sx, sy] = term(end(ends_a[sx, sy]), end(lines_g))

    def write(halves):
        for x in range(3):
            for y in range(3):
                for z in range(3):
                    first = (9 * x + 3 * y + z) * C
                    value = inner[pl.ds(first, C)]
                    if x != 1:
                        value += side_x[x // 2, pl.ds((3 * y + z) * C, C)]
                    if y != 1:
                        value += side_y[y // 2, pl.ds((3 * x + z) * C, C)]
                    if x != 1 and y != 1:
                        sx, sy = x // 2, 1 - y // 2
                        value += ends[sx, sy, :, pl.ds(z * C, C)]
                    for half in range(2):
                        low = max(first, half * HALF)
                        rows = min(first + C, (half + 1) * HALF) - low
                        if rows > 0:
                            halves[half][pl.ds(low - half * HALF, rows)] = value[low - first : low - first + rows]

    core = parity("gy")

    @pl.when(core == 0)
    def _():
        write((keep, send))

    @pl.when(core == 1)
    def _():
        write((send, keep))


def rim_terms(near, inner, grd, x_came, y_came):
    half = jax.ShapeDtypeStruct((HALF, C), jnp.float32)
    side = pltpu.VMEM((2, SLOTS * 64, 9 * C), jnp.bfloat16)
    return pl.pallas_call(
        rim_kernel,
        out_shape=[half, half],
        in_specs=[hbm()] + [vmem()] * 5,
        out_specs=[vmem()] * 2,
        scratch_shapes=columns_scratch()
        + [
            side,
            side,
            pltpu.VMEM((2, 2, 8, C), jnp.float32),
            pltpu.VMEM((2, 2, 3, 8, C), jnp.float32),
            pltpu.VMEM((2, 9 * C, C), jnp.float32),
            pltpu.VMEM((2, 9 * C, C), jnp.float32),
            pltpu.VMEM((2, 2, C, 3 * C), jnp.float32),
        ],
        compiler_params=pltpu.CompilerParams(vmem_limit_bytes=VMEM_LIMIT),
        cost_estimate=pl.CostEstimate(flops=2 * 256 * 36 * C * C, bytes_accessed=6 << 20, transcendentals=0),
        name="rim_terms",
    )(near, inner, grd, x_came, *y_came)


def power_of(values):
    peak = jnp.max(jnp.abs(values))
    return jnp.clip(jnp.ceil(jnp.log2(jnp.full((8, C), peak))), -100.0, 100.0)[0:1]


def merge_kernel(groups, take, keep, came, out, total):
    held = out.shape[1]
    total[pl.ds(0, HALF)] = keep[...] + came[...]
    if groups * take > HALF:
        total[pl.ds(HALF, groups * take - HALF)] = jnp.zeros((groups * take - HALF, C), jnp.float32)
    power = power_of(total[...])
    scale = jnp.exp2(14.0 - power)
    for p in range(groups):
        out[p, pl.ds(0, take)] = total[pl.ds(p * take, take)] * scale
        out[p, pl.ds(take, held - take)] = jnp.broadcast_to(power, (held - take, C))


def merge(groups, take, held, keep, came):
    return pl.pallas_call(
        lambda *refs: merge_kernel(groups, take, *refs),
        out_shape=jax.ShapeDtypeStruct((groups, held, C), jnp.float32),
        in_specs=[vmem()] * 2,
        out_specs=vmem(),
        scratch_shapes=[pltpu.VMEM((groups * take, C), jnp.float32)],
        compiler_params=pltpu.CompilerParams(vmem_limit_bytes=VMEM_LIMIT),
        name="merge",
    )(keep, came)


def sum_kernel(take, blocks, out):
    groups, held, _ = blocks.shape
    total = jnp.zeros((take, C), jnp.float32)
    for p in range(groups):
        total += blocks[p, pl.ds(0, take)] * jnp.exp2(blocks[p, pl.ds(take, 1)] - 14.0)
    power = power_of(total)
    total = total * jnp.exp2(14.0 - power)
    for p in range(groups):
        out[p, pl.ds(0, take)] = total
        out[p, pl.ds(take, held - take)] = jnp.broadcast_to(power, (held - take, C))


def sum_blocks(take, blocks):
    return pl.pallas_call(
        lambda *refs: sum_kernel(take, *refs),
        out_shape=jax.ShapeDtypeStruct(blocks.shape, jnp.float32),
        in_specs=[vmem()],
        out_specs=vmem(),
        compiler_params=pltpu.CompilerParams(vmem_limit_bytes=VMEM_LIMIT),
        name="sum_blocks",
    )(blocks)


def decode_kernel(take, scale, places, own, blocks, *refs):
    out, half, sems = refs[-3:]
    groups = blocks.shape[0]
    core = parity("gy")
    target = out.at[core if own else 1 - core]
    copies = []
    done = 0
    for p in range(groups):
        rows = min(take, HALF - p * take)
        if rows > 0:
            factor = jnp.exp2(blocks[places[p], pl.ds(take, 1)] - 14.0) * scale
            half[pl.ds(p * take, rows)] = blocks[places[p], pl.ds(0, rows)] * factor
        ready = min((p + 1) * take, HALF)
        if ready - done >= HALF // 4 and ready % 8 == 0 or p == groups - 1:
            piece = pl.ds(done, ready - done)
            copies += fetching((half.at[piece], target.at[piece], sems.at[len(copies)]))
            done = ready
    for copy in copies:
        copy.wait()


def decode(take, scale, places, blocks, begun=None):
    rest = () if begun is None else (begun,)
    return pl.pallas_call(
        lambda *refs: decode_kernel(take, scale, places, not rest, *refs),
        out_shape=jax.ShapeDtypeStruct((2, HALF, C), jnp.float32),
        in_specs=[vmem()] + [hbm()] * len(rest),
        out_specs=hbm(),
        scratch_shapes=[pltpu.VMEM((HALF, C), jnp.float32), pltpu.SemaphoreType.DMA((5,))],
        input_output_aliases={1: 0} if rest else {},
        compiler_params=pltpu.CompilerParams(vmem_limit_bytes=VMEM_LIMIT),
        name="decode_other" if rest else "decode_own",
    )(blocks, *rest)


def product_kernel(f, near_hbm, mask_ref, kernel_ref, bricks, x_ref, y0, y1, e0, e1, out, *refs):
    lx, ly, corners, wide, near, sem, v, *flipped = refs
    (table,) = fetching((near_hbm, near, sem))
    weights = kernel_ref
    if f == 1:
        weights = flipped[0]
        for o in range(27):
            weights[pl.ds((26 - o) * C, C)] = kernel_ref[pl.ds(o * C, C)].T
    fill_own(bricks, lx, ly, corners)
    fill_came(f, x_ref, (y0, y1), (e0, e1), lx, ly, corners)
    table.wait()

    def per_slot(s, carry):
        build_columns(s, bricks, near, lx, ly, corners, wide, "all")
        stack_columns(s, wide, v)
        total = jnp.zeros((512, C), jnp.float32)
        for x in range(3):
            cells = v[s, pl.ds(x, 8)].reshape(512, 9 * C)
            total += jnp.dot(cells, weights[pl.ds(x * 9 * C, 9 * C)], preferred_element_type=jnp.float32)
        out[s] = (total * mask_columns(mask_ref, s)).astype(jnp.bfloat16)
        return carry

    lax.fori_loop(0, SLOTS, per_slot, 0)


def product(f, near, mask, kernel, bricks, x_came, y_came, edges):
    return pl.pallas_call(
        lambda *refs: product_kernel(f, *refs),
        out_shape=jax.ShapeDtypeStruct((SLOTS, 512, C), jnp.bfloat16),
        in_specs=[hbm()] + [vmem()] * 8,
        out_specs=vmem(),
        scratch_shapes=columns_scratch()
        + [pltpu.VMEM((SLOTS, 10, 64, 9 * C), jnp.bfloat16)]
        + ([pltpu.VMEM((ROWS, C), jnp.bfloat16)] if f else []),
        compiler_params=pltpu.CompilerParams(vmem_limit_bytes=VMEM_LIMIT),
        cost_estimate=pl.CostEstimate(flops=2 * 2048 * ROWS * C, bytes_accessed=4 << 20, transcendentals=0),
        name=("output_product", "input_grad_product")[f],
    )(near, mask, kernel, bricks, x_came, *y_came, *edges)


def swapped(value, axis, k):
    pairs = []
    for low in range(k, lax.axis_size(axis) - 1, 2):
        pairs += [(low, low + 1), (low + 1, low)]
    return lax.ppermute(value, axis, pairs)


def hopped(value, axis):
    size = lax.axis_size(axis)
    pairs = [(i, i + 2) for i in range(1, size - 2, 2)] + [(i, i - 2) for i in range(2, size, 2)]
    return lax.ppermute(value, axis, pairs)


def local(features, out_grad, kernel, voxel_mask, neighbours, face_sends, edge_sends):
    size_x, size_y = lax.axis_size("gx"), lax.axis_size("gy")
    parts = size_x * size_y
    groups = parts // 2
    take = -(-HALF // groups)
    held = -(-(take + 1) // 16) * 16
    members = [[i for i in range(parts) if i % size_y % 2 == core] for core in range(2)]
    half, row = groups // 2, size_y // 2
    inward = [k + j for k in range(half - row, -1, -row) for j in range(row)]
    in_turn = [k for pair in zip(range(half, groups), inward) for k in pair]
    onward = [(k + half) % groups for k in range(groups)]
    places = [onward.index(k) for k in in_turn]

    def spread(blocks, order):
        same_core = [[core[k] for k in order] for core in members]
        return lax.all_to_all(blocks, ("gx", "gy"), 0, 0, axis_index_groups=same_core, tiled=True)

    held_act, act, grd, table, y0, y1, x0, x1 = pack(
        features.reshape(SLOTS, 512, C),
        out_grad.reshape(SLOTS, 512, C),
        voxel_mask,
        neighbours,
        face_sends,
        edge_sends,
    )
    x1 = hopped(x1, "gx")
    y_came = [swapped(y0, "gy", 0), swapped(y1, "gy", 1)]
    x_came, x_more = join(x0, x1)
    x_more, table = lax.optimization_barrier((x_more, table))
    x_came = swapped(x_came, "gx", 0)
    v = own_columns(table, held_act)
    inner = inner_terms(v, grd)
    keep, send = rim_terms(neighbours, inner, grd, x_came, y_came)
    blocks = merge(groups, take, held, keep, swapped(send, "gy", 0)).astype(jnp.float16)
    rows = kernel.reshape(ROWS, C)
    blocks, act, x_came, x_more = lax.optimization_barrier((blocks, act, x_came, x_more))
    x_more = swapped(x_more, "gx", 0)
    e0, e1 = forward_corners(x_came)
    edges = [swapped(e0, "gy", 0), swapped(e1, "gy", 1)]
    output = product(0, neighbours, voxel_mask, rows, act, x_came, y_came, edges)
    arrived, output, x_more = lax.optimization_barrier((spread(blocks, in_turn), output, x_more))
    copies = sum_blocks(take, arrived.astype(jnp.float32)).astype(jnp.float16)
    copies, grd = lax.optimization_barrier((copies, grd))
    input_grad = product(1, neighbours, voxel_mask, rows, grd, x_more, y_came, edges)
    mine, input_grad = lax.optimization_barrier((spread(copies, onward), input_grad))
    other = swapped(mine, "gy", 0)
    scale = 1.0 / math.sqrt(parts * SLOTS * 512)
    weight = decode(take, scale, places, mine.astype(jnp.float32))
    weight = decode(take, scale, places, other.astype(jnp.float32), weight)
    shape = (SLOTS, 8, 8, 8, C)
    return output.reshape(shape), input_grad.reshape(shape), weight.reshape(27, C, C)


def solution(mesh):
    spec = P(("gx", "gy"))
    return jax.shard_map(
        local,
        mesh=mesh,
        in_specs=(spec, spec, P(), spec, spec, spec, spec),
        out_specs=(spec, spec, P()),
        check_vma=False,
    )
```

```python
import math

import jax
import jax.numpy as jnp
from jax import lax
from jax.experimental import pallas as pl
from jax.experimental.pallas import tpu as pltpu
from jax.sharding import PartitionSpec as P

FACES = ((-1, 0), (1, 0), (0, -1), (0, 1))
EDGES = ((-1, -1), (-1, 1), (1, -1), (1, 1))
C = 128
SLOTS = 4
FACE = 2
ZERO = SLOTS + 4 * FACE + 4
ROWS = 27 * C
FACE_ROWS = FACE * 64
X_ROWS = FACE_ROWS + 32
Y_ROWS = FACE_ROWS + 48
HALF = ROWS // 2
SPARE_ROWS = 32
VMEM_LIMIT = 32 * 1024 * 1024
PACK_LIMIT = 60 * 1024 * 1024
ROOM_BRICKS = 48
ROOM_TABLES = 12 * 1024


def vmem():
    return pl.BlockSpec(memory_space=pltpu.VMEM)


def hbm():
    return pl.BlockSpec(memory_space=pltpu.HBM)


def fetching(*pairs):
    copies = [pltpu.make_async_copy(src, dst, sem) for src, dst, sem in pairs]
    for copy in copies:
        copy.start()
    return copies


def fetched(*pairs):
    for copy in fetching(*pairs):
        copy.wait()


def mask_columns(mask_ref, s):
    m = mask_ref[...].astype(jnp.float32).astype(jnp.bfloat16)
    pick = (lax.broadcasted_iota(jnp.int32, (SLOTS, C), 0) == s).astype(jnp.float32).astype(jnp.bfloat16)
    return lax.dot_general(m, pick, (((0,), (0,)), ((), ())), preferred_element_type=jnp.float32)


def parity(axis):
    return lax.rem(lax.axis_index(axis), 2)


def side_of(k, odd):
    return 1 - odd if k == 0 else odd


def shifts(cells, same, below, above):
    line = lax.broadcasted_iota(jnp.int32, cells.shape, cells.ndim - 2)
    axis = cells.ndim - 2
    up = jnp.where((same & (line >= 1)) | (below & (line == 0)), pltpu.roll(cells, 1, axis), 0.0)
    down = jnp.where((same & (line <= 6)) | (above & (line == 7)), pltpu.roll(cells, 7, axis), 0.0)
    return up, jnp.where(same, cells, 0.0), down


def pack_kernel(face_hbm, edge_hbm, near_hbm, feat_hbm, grad_hbm, mask_hbm, held_out, act_out, grd_out, near_out, *refs):
    sends = refs[0:4]
    y_out, x_out = refs[4:6], refs[6:8]
    face_ref, edge_ref, near, raw, mask_ref, full, sems = refs[8:]
    got_mask, *tables = fetching(
        (mask_hbm, mask_ref, sems.at[0]),
        (face_hbm, face_ref, sems.at[1]),
        (edge_hbm, edge_ref, sems.at[2]),
        (near_hbm, near, sems.at[3]),
    )
    got = [
        fetching(
            (feat_hbm.at[s], raw.at[0, s], sems.at[4 + 2 * s]),
            (grad_hbm.at[s], raw.at[1, s], sems.at[5 + 2 * s]),
        )
        for s in range(SLOTS)
    ]
    got_mask.wait()
    results = []
    for s in range(SLOTS):
        rows = mask_columns(mask_ref, s)
        for f in range(2):
            got[s][f].wait()
            masked = raw[f, s].astype(jnp.float32) * rows
            full[f, s] = masked.reshape(8, 8, 8, C)
            raw[f, s] = masked.astype(jnp.bfloat16)
        first = 4 + 2 * SLOTS + 3 * s
        results += fetching(
            (raw.at[0, s], held_out.at[0, s], sems.at[first]),
            (raw.at[0, s], act_out.at[s], sems.at[first + 1]),
            (raw.at[1, s], grd_out.at[s], sems.at[first + 2]),
        )
    for table in tables:
        table.wait()
    last = 4 + 5 * SLOTS
    results += fetching((near, near_out.at[0], sems.at[last]))
    for axis, outs in enumerate((x_out, y_out)):
        odd = parity("gy" if axis else "gx")
        for k in range(2):
            side = side_of(k, odd)
            for f in range(2):
                for r in range(FACE):
                    entry = face_ref[r, 2 * axis + side]
                    slot = jnp.clip(entry, 0, SLOTS - 1)
                    layer = full[f, slot, :, 7 * side] if axis else full[f, slot, 7 * side]
                    layer = jnp.where(entry < SLOTS, layer, 0.0)
                    first = f * (Y_ROWS if axis else X_ROWS) + r * 64
                    outs[k][pl.ds(first, 64)] = layer.reshape(64, C).astype(jnp.bfloat16)
            lines = []
            for far in range(2):
                corner = 2 * far + side if axis else 2 * side + far
                entry = edge_ref[0, corner]
                slot = jnp.clip(entry, 0, SLOTS - 1)
                live = entry < SLOTS
                at_x, at_y = (7 * far, 7 * side) if axis else (7 * side, 7 * far)
                if axis == 0:
                    for f in range(2):
                        lines.append(jnp.where(live, full[f, slot, at_x, at_y], 0.0))
                    continue
                base = 18 * far + 6 * side
                low, mid, high = near[slot, base], near[slot, base + 1], near[slot, base + 2]
                up, same, down = shifts(
                    full[1, slot, at_x, at_y],
                    live & (mid < ZERO),
                    live & (high < ZERO),
                    live & (low < ZERO),
                )
                lines += [down, same, up]
            lines = jnp.concatenate(lines, axis=0).astype(jnp.bfloat16)
            outs[k][pl.ds(FACE_ROWS, lines.shape[0])] = lines
    x_out[1][pl.ds(X_ROWS + FACE_ROWS, SPARE_ROWS)] = jnp.zeros((SPARE_ROWS, C), jnp.bfloat16)
    for i, (built, send) in enumerate(zip(refs[4:8], sends)):
        results += fetching((built, send, sems.at[last + 1 + i]))
    for result in results:
        result.wait()


def pack(features, out_grad, mask, near, face_sends, edge_sends):
    sends = [
        jax.ShapeDtypeStruct((rows + FACE_ROWS, C), jnp.bfloat16)
        for rows in (Y_ROWS, Y_ROWS, X_ROWS, X_ROWS + SPARE_ROWS)
    ]
    return pl.pallas_call(
        pack_kernel,
        out_shape=[
            jax.ShapeDtypeStruct((ROOM_BRICKS, SLOTS, 512, C), jnp.bfloat16),
            jax.ShapeDtypeStruct((SLOTS, 512, C), jnp.bfloat16),
            jax.ShapeDtypeStruct((SLOTS, 512, C), jnp.bfloat16),
            jax.ShapeDtypeStruct((ROOM_TABLES, SLOTS, 27), jnp.int32),
        ]
        + sends,
        in_specs=[hbm()] * 6,
        out_specs=[hbm()] * 8,
        scratch_shapes=[pltpu.VMEM(send.shape, send.dtype) for send in sends]
        + [
            pltpu.SMEM((FACE, 4), jnp.int32),
            pltpu.SMEM((1, 4), jnp.int32),
            pltpu.SMEM((SLOTS, 27), jnp.int32),
            pltpu.VMEM((2, SLOTS, 512, C), jnp.bfloat16),
            pltpu.VMEM((SLOTS, 512), jnp.int32),
            pltpu.VMEM((2, SLOTS, 8, 8, 8, C), jnp.float32),
            pltpu.SemaphoreType.DMA((4 + 5 * SLOTS + 5,)),
        ],
        compiler_params=pltpu.CompilerParams(vmem_limit_bytes=PACK_LIMIT),
        name="pack",
    )(face_sends.T, edge_sends.T, near, features, out_grad, mask)


def parts_of(ref):
    rows = ref.shape[0] // 2
    return ref.at[pl.ds(0, rows)], ref.at[pl.ds(rows, rows)]


def join_kernel(first, second, out, more):
    rows = first.shape[0] - FACE_ROWS
    for k, src in enumerate((first, second)):
        out[pl.ds(k * rows, rows)] = src[pl.ds(0, rows)]
        more[pl.ds(k * FACE_ROWS, FACE_ROWS)] = src[pl.ds(rows, FACE_ROWS)]


def join(first, second):
    outs = [
        jax.ShapeDtypeStruct((2 * rows, C), jnp.bfloat16) for rows in (first.shape[0] - FACE_ROWS, FACE_ROWS)
    ]
    return pl.pallas_call(
        join_kernel,
        out_shape=outs,
        in_specs=[vmem()] * 2,
        out_specs=[vmem()] * 2,
        compiler_params=pltpu.CompilerParams(vmem_limit_bytes=VMEM_LIMIT),
        name="join_sides",
    )(first, second)


def forward_kernel(x_came, out0, out1):
    odd_x, odd_y = parity("gx"), parity("gy")
    for k, out in enumerate((out0, out1)):
        far = side_of(k, odd_y)
        for j, came in enumerate(parts_of(x_came)):
            source = side_of(j, odd_x)
            rows = came[pl.ds(pl.multiple_of(FACE_ROWS + 16 * far, 16), 16)]
            out[pl.ds(pl.multiple_of(16 * source, 16), 16)] = rows


def forward_corners(x_came):
    send = jax.ShapeDtypeStruct((32, C), jnp.bfloat16)
    return pl.pallas_call(
        forward_kernel,
        out_shape=[send] * 2,
        in_specs=[vmem()],
        out_specs=[vmem()] * 2,
        compiler_params=pltpu.CompilerParams(vmem_limit_bytes=VMEM_LIMIT),
        name="forward_corners",
    )(x_came)


def fill_own(bricks, lx, ly, corners):
    for s in range(SLOTS):
        whole = bricks[s].astype(jnp.float32).reshape(8, 8, 8, C)
        for side, at in ((0, 7), (1, 0)):
            lx[side, s] = whole[at]
            ly[side, s] = whole[:, at]
            for other, far in ((0, 7), (1, 0)):
                corners[2 * side + other, s] = whole[at, far]


def fill_zero(lx, ly, corners, first):
    for ref in (lx, ly, corners):
        count = ref.shape[1] - first
        ref[:, pl.ds(first, count)] = jnp.zeros((ref.shape[0], count) + ref.shape[2:], jnp.float32)


def fill_came(f, x_came, y_came, edges, lx, ly, corners):
    odd_x, odd_y = parity("gx"), parity("gy")
    for came, first, odd, dst in ((parts_of(x_came), 0, odd_x, lx), (y_came, f * Y_ROWS, odd_y, ly)):
        for k, part in enumerate(came):
            side = side_of(k, odd)
            for r in range(FACE):
                rows = part[pl.ds(first + r * 64, 64)]
                dst[side, SLOTS + r] = rows.astype(jnp.float32).reshape(8, 8, C)
            dst[k, SLOTS + FACE] = jnp.zeros((8, 8, C), jnp.float32)
    for k, came in enumerate(edges):
        side = side_of(k, odd_y)
        for j in range(2):
            rows = came[pl.ds(16 * j, 16)].astype(jnp.float32)
            corners[2 * j + side, SLOTS + 2 * FACE] = rows[8 * f : 8 * f + 8]
    for sx in range(2):
        for sy in range(2):
            c = 2 * sx + sy
            for r in range(FACE):
                corners[c, SLOTS + r] = lx[sx, SLOTS + r, 0 if sy else 7]
                corners[c, SLOTS + FACE + r] = ly[sy, SLOTS + r, 0 if sx else 7]
            corners[c, SLOTS + 2 * FACE + 1] = jnp.zeros((8, C), jnp.float32)


def build_columns(s, bricks, near, lx, ly, corners, wide, which):
    def spread(cells, at_x, at_y, depth):
        flat = cells.reshape(-1, 8, C)
        for k, moved in enumerate(shifts(flat, depth == 0, depth == -1, depth == 1)):
            wide[k, at_x, at_y] = moved.reshape(cells.shape)

    def column(nx, ny):
        base = 9 * (nx + 1) + 3 * (ny + 1)
        low, mid, high = near[s, base], near[s, base + 1], near[s, base + 2]
        entry = jnp.minimum(jnp.minimum(low, mid), high)
        depth = jnp.where(low < ZERO, -1, jnp.where(high < ZERO, 1, 0))
        if which == "own":
            depth = jnp.where(entry < SLOTS, depth, 2)
        if which == "rim":
            depth = jnp.where((entry >= SLOTS) & (entry < SLOTS + 4 * FACE), depth, 2)
        return entry, depth

    middle = pl.ds(1, 8)
    if which != "rim":
        spread(bricks[s].astype(jnp.float32).reshape(8, 8, 8, C), middle, middle, 0)
    for side, n in ((0, -1), (1, 1)):
        edge_at = pl.ds(0 if n < 0 else 9, 1)
        entry, depth = column(n, 0)
        place = jnp.where(entry < SLOTS, entry, jnp.clip(entry - FACE * side, 0, SLOTS + FACE))
        spread(lx[side, place].reshape(1, 8, 8, C), edge_at, middle, depth)
        entry, depth = column(0, n)
        place = jnp.where(entry < SLOTS, entry, jnp.clip(entry - FACE * (2 + side), 0, SLOTS + FACE))
        spread(ly[side, place].reshape(8, 1, 8, C), middle, edge_at, depth)
    for sx in range(2):
        for sy in range(2):
            entry, depth = column(2 * sx - 1, 2 * sy - 1)
            first_x = SLOTS + FACE * sx
            first_y = SLOTS + FACE * (2 + sy)
            own_edge = SLOTS + 4 * FACE + 2 * sx + sy
            in_x = (entry >= first_x) & (entry < first_x + FACE)
            in_y = (entry >= first_y) & (entry < first_y + FACE)
            place = jnp.where(entry == own_edge, SLOTS + 2 * FACE, SLOTS + 2 * FACE + 1)
            place = jnp.where(in_y, SLOTS + FACE + entry - first_y, place)
            place = jnp.where(in_x, SLOTS + entry - first_x, place)
            place = jnp.where(entry < SLOTS, entry, place)
            spread(corners[2 * sx + sy, place].reshape(1, 1, 8, C), pl.ds(9 * sx, 1), pl.ds(9 * sy, 1), depth)


def stack_columns(s, wide, v):
    for y in range(3):
        for z in range(3):
            cells = wide[z, :, pl.ds(y, 8)].reshape(10, 64, C).astype(jnp.bfloat16)
            v[s, :, :, pl.ds((3 * y + z) * C, C)] = cells


def columns_scratch():
    return [
        pltpu.VMEM((2, SLOTS + FACE + 1, 8, 8, C), jnp.float32),
        pltpu.VMEM((2, SLOTS + FACE + 1, 8, 8, C), jnp.float32),
        pltpu.VMEM((4, SLOTS + 2 * FACE + 2, 8, C), jnp.float32),
        pltpu.VMEM((3, 10, 10, 8, C), jnp.float32),
        pltpu.SMEM((SLOTS, 27), jnp.int32),
        pltpu.SemaphoreType.DMA(()),
    ]


def columns_kernel(near_hbm, act_hbm, v, lx, ly, corners, wide, near, sem, act, act_sem):
    table, bricks = fetching((near_hbm.at[0], near, sem), (act_hbm.at[0], act, act_sem))
    fill_zero(lx, ly, corners, SLOTS)
    bricks.wait()
    fill_own(act, lx, ly, corners)
    table.wait()

    def per_slot(s, carry):
        build_columns(s, act, near, lx, ly, corners, wide, "own")
        stack_columns(s, wide, v)
        return carry

    lax.fori_loop(0, SLOTS, per_slot, 0)


def own_columns(near, act):
    return pl.pallas_call(
        columns_kernel,
        out_shape=jax.ShapeDtypeStruct((SLOTS, 10, 64, 9 * C), jnp.bfloat16),
        in_specs=[hbm()] * 2,
        out_specs=vmem(),
        scratch_shapes=columns_scratch()
        + [pltpu.VMEM((SLOTS, 512, C), jnp.bfloat16), pltpu.SemaphoreType.DMA(())],
        compiler_params=pltpu.CompilerParams(vmem_limit_bytes=VMEM_LIMIT),
        cost_estimate=pl.CostEstimate(flops=1 << 24, bytes_accessed=6 << 20, transcendentals=0),
        name="own_columns",
    )(near, act)


def inner_kernel(v, grd, out, turned):
    for s in range(SLOTS):
        for q in range(4):
            turned[:, pl.ds((4 * s + q) * C, C)] = grd[s, pl.ds(q * C, C)].T
    for x in range(3):
        cells = v[:, pl.ds(x, 8)].reshape(SLOTS * 512, 9 * C)
        terms = jnp.dot(turned[...], cells, preferred_element_type=jnp.float32)
        for j in range(9):
            out[pl.ds((9 * x + j) * C, C)] = terms[:, j * C : (j + 1) * C].T


def inner_terms(v, grd):
    return pl.pallas_call(
        inner_kernel,
        out_shape=jax.ShapeDtypeStruct((ROWS, C), jnp.float32),
        in_specs=[vmem()] * 2,
        out_specs=vmem(),
        scratch_shapes=[pltpu.VMEM((C, SLOTS * 512), jnp.bfloat16)],
        compiler_params=pltpu.CompilerParams(vmem_limit_bytes=VMEM_LIMIT),
        cost_estimate=pl.CostEstimate(flops=2 * 2048 * ROWS * C, bytes_accessed=6 << 20, transcendentals=0),
        name="inner_terms",
    )(v, grd)


def rim_kernel(near_hbm, inner, grd, x_ref, y0, y1, keep, send, lx, ly, corners, wide, near, sem, *refs):
    vx, vy, ends_a, ends_g, side_x, side_y, ends = refs
    (table,) = fetching((near_hbm, near, sem))
    fill_came(0, x_ref, (y0, y1), (), lx, ly, corners)
    for k, came in enumerate(parts_of(x_ref)):
        side = side_of(k, parity("gx"))
        for j in range(2):
            ends_a[side, j] = came[pl.ds(FACE_ROWS + 16 * j, 16)].astype(jnp.float32)[0:8]
    for k, came in enumerate((y0, y1)):
        side = side_of(k, parity("gy"))
        ends_g[side] = came[pl.ds(FACE_ROWS, 48)].astype(jnp.float32).reshape(2, 3, 8, C)
    table.wait()
    for s in range(SLOTS):
        build_columns(s, None, near, lx, ly, corners, wide, "rim")
        rows = pl.ds(64 * s, 64)
        for side in range(2):
            for j in range(9):
                cells = wide[j % 3, 9 * side, pl.ds(j // 3, 8)]
                vx[side, rows, pl.ds(j * C, C)] = cells.reshape(64, C).astype(jnp.bfloat16)
        for z in range(3):
            for sx in range(2):
                for sy in range(2):
                    wide[z, 9 * sx, 9 * sy] = jnp.zeros((8, C), jnp.float32)
        for side in range(2):
            for j in range(9):
                cells = wide[j % 3, pl.ds(j // 3, 8), 9 * side]
                vy[side, rows, pl.ds(j * C, C)] = cells.reshape(64, C).astype(jnp.bfloat16)
    grads = grd[...]
    lines = grads.astype(jnp.float32).reshape(SLOTS, 8, 8, 8, C)

    def term(cells, rows):
        return lax.dot_general(cells, rows, (((0,), (0,)), ((), ())), preferred_element_type=jnp.float32)

    def end(line):
        return jnp.concatenate([line, jnp.zeros(line.shape, jnp.float32)], axis=0).astype(jnp.bfloat16)

    for side in range(2):
        rows = grads[:, 448 * side : 448 * side + 64].reshape(SLOTS * 64, C)
        side_x[side] = term(vx[side], rows)
        rows = lines[:, :, 7 * side].reshape(SLOTS * 64, C).astype(jnp.bfloat16)
        side_y[side] = term(vy[side], rows)
    for sx in range(2):
        for sy in range(2):
            lines_g = jnp.concatenate([ends_g[sy, sx, z] for z in range(3)], axis=1)
            ends[sx, sy] = term(end(ends_a[sx, sy]), end(lines_g))

    def write(halves):
        for x in range(3):
            for y in range(3):
                for z in range(3):
                    first = (9 * x + 3 * y + z) * C
                    value = inner[pl.ds(first, C)]
                    if x != 1:
                        value += side_x[x // 2, pl.ds((3 * y + z) * C, C)]
                    if y != 1:
                        value += side_y[y // 2, pl.ds((3 * x + z) * C, C)]
                    if x != 1 and y != 1:
                        sx, sy = x // 2, 1 - y // 2
                        value += ends[sx, sy, :, pl.ds(z * C, C)]
                    for half in range(2):
                        low = max(first, half * HALF)
                        rows = min(first + C, (half + 1) * HALF) - low
                        if rows > 0:
                            halves[half][pl.ds(low - half * HALF, rows)] = value[low - first : low - first + rows]

    core = parity("gy")

    @pl.when(core == 0)
    def _():
        write((keep, send))

    @pl.when(core == 1)
    def _():
        write((send, keep))


def rim_terms(near, inner, grd, x_came, y_came):
    half = jax.ShapeDtypeStruct((HALF, C), jnp.float32)
    side = pltpu.VMEM((2, SLOTS * 64, 9 * C), jnp.bfloat16)
    return pl.pallas_call(
        rim_kernel,
        out_shape=[half, half],
        in_specs=[hbm()] + [vmem()] * 5,
        out_specs=[vmem()] * 2,
        scratch_shapes=columns_scratch()
        + [
            side,
            side,
            pltpu.VMEM((2, 2, 8, C), jnp.float32),
            pltpu.VMEM((2, 2, 3, 8, C), jnp.float32),
            pltpu.VMEM((2, 9 * C, C), jnp.float32),
            pltpu.VMEM((2, 9 * C, C), jnp.float32),
            pltpu.VMEM((2, 2, C, 3 * C), jnp.float32),
        ],
        compiler_params=pltpu.CompilerParams(vmem_limit_bytes=VMEM_LIMIT),
        cost_estimate=pl.CostEstimate(flops=2 * 256 * 36 * C * C, bytes_accessed=6 << 20, transcendentals=0),
        name="rim_terms",
    )(near, inner, grd, x_came, *y_came)


def power_of(values):
    peak = jnp.max(jnp.abs(values))
    return jnp.clip(jnp.ceil(jnp.log2(jnp.full((8, C), peak))), -100.0, 100.0)[0:1]


def merge_kernel(groups, take, keep, came, out, total):
    held = out.shape[1]
    total[pl.ds(0, HALF)] = keep[...] + came[...]
    if groups * take > HALF:
        total[pl.ds(HALF, groups * take - HALF)] = jnp.zeros((groups * take - HALF, C), jnp.float32)
    power = power_of(total[...])
    scale = jnp.exp2(14.0 - power)
    for p in range(groups):
        out[p, pl.ds(0, take)] = total[pl.ds(p * take, take)] * scale
        out[p, pl.ds(take, held - take)] = jnp.broadcast_to(power, (held - take, C))


def merge(groups, take, held, keep, came):
    return pl.pallas_call(
        lambda *refs: merge_kernel(groups, take, *refs),
        out_shape=jax.ShapeDtypeStruct((groups, held, C), jnp.float32),
        in_specs=[vmem()] * 2,
        out_specs=vmem(),
        scratch_shapes=[pltpu.VMEM((groups * take, C), jnp.float32)],
        compiler_params=pltpu.CompilerParams(vmem_limit_bytes=VMEM_LIMIT),
        name="merge",
    )(keep, came)


def sum_kernel(take, blocks, out):
    groups, held, _ = blocks.shape
    total = jnp.zeros((take, C), jnp.float32)
    for p in range(groups):
        total += blocks[p, pl.ds(0, take)] * jnp.exp2(blocks[p, pl.ds(take, 1)] - 14.0)
    power = power_of(total)
    total = total * jnp.exp2(14.0 - power)
    for p in range(groups):
        out[p, pl.ds(0, take)] = total
        out[p, pl.ds(take, held - take)] = jnp.broadcast_to(power, (held - take, C))


def sum_blocks(take, blocks):
    return pl.pallas_call(
        lambda *refs: sum_kernel(take, *refs),
        out_shape=jax.ShapeDtypeStruct(blocks.shape, jnp.float32),
        in_specs=[vmem()],
        out_specs=vmem(),
        compiler_params=pltpu.CompilerParams(vmem_limit_bytes=VMEM_LIMIT),
        name="sum_blocks",
    )(blocks)


def decode_kernel(take, scale, places, own, blocks, *refs):
    out, half, sems = refs[-3:]
    groups = blocks.shape[0]
    core = parity("gy")
    target = out.at[core if own else 1 - core]
    copies = []
    done = 0
    for p in range(groups):
        rows = min(take, HALF - p * take)
        if rows > 0:
            factor = jnp.exp2(blocks[places[p], pl.ds(take, 1)] - 14.0) * scale
            half[pl.ds(p * take, rows)] = blocks[places[p], pl.ds(0, rows)] * factor
        ready = min((p + 1) * take, HALF)
        if ready - done >= HALF // 4 and ready % 8 == 0 or p == groups - 1:
            piece = pl.ds(done, ready - done)
            copies += fetching((half.at[piece], target.at[piece], sems.at[len(copies)]))
            done = ready
    for copy in copies:
        copy.wait()


def decode(take, scale, places, blocks, begun=None):
    rest = () if begun is None else (begun,)
    return pl.pallas_call(
        lambda *refs: decode_kernel(take, scale, places, not rest, *refs),
        out_shape=jax.ShapeDtypeStruct((2, HALF, C), jnp.float32),
        in_specs=[vmem()] + [hbm()] * len(rest),
        out_specs=hbm(),
        scratch_shapes=[pltpu.VMEM((HALF, C), jnp.float32), pltpu.SemaphoreType.DMA((5,))],
        input_output_aliases={1: 0} if rest else {},
        compiler_params=pltpu.CompilerParams(vmem_limit_bytes=VMEM_LIMIT),
        name="decode_other" if rest else "decode_own",
    )(blocks, *rest)


def product_kernel(f, near_hbm, mask_ref, kernel_ref, bricks, x_ref, y0, y1, e0, e1, out, *refs):
    lx, ly, corners, wide, near, sem, v, *flipped = refs
    (table,) = fetching((near_hbm, near, sem))
    weights = kernel_ref
    if f == 1:
        weights = flipped[0]
        for o in range(27):
            weights[pl.ds((26 - o) * C, C)] = kernel_ref[pl.ds(o * C, C)].T
    fill_own(bricks, lx, ly, corners)
    fill_came(f, x_ref, (y0, y1), (e0, e1), lx, ly, corners)
    table.wait()

    def per_slot(s, carry):
        build_columns(s, bricks, near, lx, ly, corners, wide, "all")
        stack_columns(s, wide, v)
        total = jnp.zeros((512, C), jnp.float32)
        for x in range(3):
            cells = v[s, pl.ds(x, 8)].reshape(512, 9 * C)
            total += jnp.dot(cells, weights[pl.ds(x * 9 * C, 9 * C)], preferred_element_type=jnp.float32)
        out[s] = (total * mask_columns(mask_ref, s)).astype(jnp.bfloat16)
        return carry

    lax.fori_loop(0, SLOTS, per_slot, 0)


def product(f, near, mask, kernel, bricks, x_came, y_came, edges):
    return pl.pallas_call(
        lambda *refs: product_kernel(f, *refs),
        out_shape=jax.ShapeDtypeStruct((SLOTS, 512, C), jnp.bfloat16),
        in_specs=[hbm()] + [vmem()] * 8,
        out_specs=vmem(),
        scratch_shapes=columns_scratch()
        + [pltpu.VMEM((SLOTS, 10, 64, 9 * C), jnp.bfloat16)]
        + ([pltpu.VMEM((ROWS, C), jnp.bfloat16)] if f else []),
        compiler_params=pltpu.CompilerParams(vmem_limit_bytes=VMEM_LIMIT),
        cost_estimate=pl.CostEstimate(flops=2 * 2048 * ROWS * C, bytes_accessed=4 << 20, transcendentals=0),
        name=("output_product", "input_grad_product")[f],
    )(near, mask, kernel, bricks, x_came, *y_came, *edges)


def swapped(value, axis, k):
    pairs = []
    for low in range(k, lax.axis_size(axis) - 1, 2):
        pairs += [(low, low + 1), (low + 1, low)]
    return lax.ppermute(value, axis, pairs)


def hopped(value, axis):
    size = lax.axis_size(axis)
    pairs = [(i, i + 2) for i in range(1, size - 2, 2)] + [(i, i - 2) for i in range(2, size, 2)]
    return lax.ppermute(value, axis, pairs)


def local(features, out_grad, kernel, voxel_mask, neighbours, face_sends, edge_sends):
    size_x, size_y = lax.axis_size("gx"), lax.axis_size("gy")
    parts = size_x * size_y
    groups = parts // 2
    take = -(-HALF // groups)
    held = -(-(take + 1) // 16) * 16
    members = [[i for i in range(parts) if i % size_y % 2 == core] for core in range(2)]
    half, row = groups // 2, size_y // 2
    inward = [k + j for k in range(half - row, -1, -row) for j in range(row)]
    in_turn = [k for pair in zip(range(half, groups), inward) for k in pair]
    onward = [(k + half // 2) % groups for k in range(groups)]
    places = [onward.index(k) for k in in_turn]

    def spread(blocks, order):
        same_core = [[core[k] for k in order] for core in members]
        return lax.all_to_all(blocks, ("gx", "gy"), 0, 0, axis_index_groups=same_core, tiled=True)

    held_act, act, grd, table, y0, y1, x0, x1 = pack(
        features.reshape(SLOTS, 512, C),
        out_grad.reshape(SLOTS, 512, C),
        voxel_mask,
        neighbours,
        face_sends,
        edge_sends,
    )
    x1 = hopped(x1, "gx")
    y_came = [swapped(y0, "gy", 0), swapped(y1, "gy", 1)]
    v = own_columns(table, held_act)
    x1, v = lax.optimization_barrier((x1, v))
    x_came, x_more = join(x0, x1)
    x_more, v = lax.optimization_barrier((x_more, v))
    x_came = swapped(x_came, "gx", 0)
    inner = inner_terms(v, grd)
    keep, send = rim_terms(neighbours, inner, grd, x_came, y_came)
    blocks = merge(groups, take, held, keep, swapped(send, "gy", 0)).astype(jnp.float16)
    rows = kernel.reshape(ROWS, C)
    blocks, act, x_came, x_more = lax.optimization_barrier((blocks, act, x_came, x_more))
    x_more = swapped(x_more, "gx", 0)
    e0, e1 = forward_corners(x_came)
    edges = [swapped(e0, "gy", 0), swapped(e1, "gy", 1)]
    output = product(0, neighbours, voxel_mask, rows, act, x_came, y_came, edges)
    arrived, output, x_more = lax.optimization_barrier((spread(blocks, in_turn), output, x_more))
    copies = sum_blocks(take, arrived.astype(jnp.float32)).astype(jnp.float16)
    copies, grd = lax.optimization_barrier((copies, grd))
    input_grad = product(1, neighbours, voxel_mask, rows, grd, x_more, y_came, edges)
    mine, input_grad = lax.optimization_barrier((spread(copies, onward), input_grad))
    other = swapped(mine, "gy", 0)
    scale = 1.0 / math.sqrt(parts * SLOTS * 512)
    weight = decode(take, scale, places, mine.astype(jnp.float32))
    weight = decode(take, scale, places, other.astype(jnp.float32), weight)
    shape = (SLOTS, 8, 8, 8, C)
    return output.reshape(shape), input_grad.reshape(shape), weight.reshape(27, C, C)


def solution(mesh):
    spec = P(("gx", "gy"))
    return jax.shard_map(
        local,
        mesh=mesh,
        in_specs=(spec, spec, P(), spec, spec, spec, spec),
        out_specs=(spec, spec, P()),
        check_vma=False,
    )
```
